32 devices in a mesh: section: 2 (over x), dp: 16 (over z, y, core).
Axes of the slice: x: 2, y: 2, z: 4, core: 2. Of those that a mesh axis runs over, the one named last changes fastest.
Arguments:
- tokens: bfloat16 [3, 16, 128, 1152], P(None, 'dp'), may hold values from -6 to 6
- time_bins: int32 [3, 16], P(None, 'dp'), may hold values from 0 to 999
- labels: int32 [3, 16], P(None, 'dp'), may hold values from 0 to 1000
- dino_feats: bfloat16 [3, 16, 128, 768], P(None, 'dp'), may hold values from -6 to 6
- cotangent: bfloat16 [3, 16, 128, 1152], P(None, 'dp'), may hold values from -6 to 6
- time_table: float32 [1000, 1152], P(None, 'dp'), may hold values from -5 to 5
- class_table: float32 [1001, 1152], P(None, 'dp'), may hold values from -5 to 5
- ada_weight: float32 [2, 1152, 6912], P('section', 'dp'), may hold values from -0.1875 to 0.1875
- ada_bias: float32 [2, 6912], P('section', 'dp'), may hold values from -2 to 2
- qkv_weight: float32 [2, 1152, 3456], P('section', 'dp'), may hold values from -0.1875 to 0.1875
- qkv_bias: float32 [2, 2304], P('section', 'dp'), may hold values from -2 to 2
- out_weight: float32 [2, 1152, 1152], P('section', 'dp'), may hold values from -0.75 to 0.75
- out_bias: float32 [2, 1152], P('section', 'dp'), may hold values from -2 to 2
- mlp_in_weight: float32 [2, 1152, 4608], P('section', 'dp'), may hold values from -0.1875 to 0.1875
- mlp_in_bias: float32 [2, 4608], P('section', 'dp'), may hold values from -2 to 2
- mlp_out_weight: float32 [2, 4608, 1152], P('section', 'dp'), may hold values from -0.09375 to 0.09375
- mlp_out_bias: float32 [2, 1152], P('section', 'dp'), may hold values from -2 to 2
- align_weight_one: float32 [1152, 2048], P(('section', 'dp')), may hold values from -0.1875 to 0.1875
- align_bias_one: float32 [2048], P(('section', 'dp')), may hold values from -2 to 2
- align_weight_two: float32 [2048, 2048], P(('section', 'dp')), may hold values from -0.125 to 0.125
- align_bias_two: float32 [2048], P(('section', 'dp')), may hold values from -2 to 2
- align_weight_three: float32 [2048, 768], P(('section', 'dp')), may hold values from -0.125 to 0.125
- align_bias_three: float32 [768], P(('section', 'dp')), may hold values from -2 to 2
Outputs:
- acts: bfloat16 [2, 3, 16, 128, 1152], P('section', None, 'dp')
- in_grads: bfloat16 [2, 3, 16, 128, 1152], P('section', None, 'dp')
- grad_time_table: float32 [1000, 1152], P(None, 'dp')
- grad_class_table: float32 [1001, 1152], P(None, 'dp')
- grad_ada_weight: float32 [2, 1152, 6912], P('section', 'dp')
- grad_ada_bias: float32 [2, 6912], P('section', 'dp')
- grad_qkv_weight: float32 [2, 1152, 3456], P('section', 'dp')
- grad_qkv_bias: float32 [2, 2304], P('section', 'dp')
- grad_out_weight: float32 [2, 1152, 1152], P('section', 'dp')
- grad_out_bias: float32 [2, 1152], P('section', 'dp')
- grad_mlp_in_weight: float32 [2, 1152, 4608], P('section', 'dp')
- grad_mlp_in_bias: float32 [2, 4608], P('section', 'dp')
- grad_mlp_out_weight: float32 [2, 4608, 1152], P('section', 'dp')
- grad_mlp_out_bias: float32 [2, 1152], P('section', 'dp')
- grad_align_weight_one: float32 [1152, 2048], P(('section', 'dp'))
- grad_align_bias_one: float32 [2048], P(('section', 'dp'))
- grad_align_weight_two: float32 [2048, 2048], P(('section', 'dp'))
- grad_align_bias_two: float32 [2048], P(('section', 'dp'))
- grad_align_weight_three: float32 [2048, 768], P(('section', 'dp'))
- grad_align_bias_three: float32 [768], P(('section', 'dp'))
The draws below stay inside these ranges and needn't reach their ends.
All inputs are finite; a program needn't handle non-finite values.
Results may differ from the reference program's by a relative error of at most 0.029.
Values may be sent and summed in bfloat16 or wider, within the bound.
A program may use at most 576 MiB of HBM per device.

```python
import math
import jax
import jax.numpy as jnp
import numpy as np
from jax import lax

D = 1152
HEADS = 16
HD = 72
FF = 4608
PROJ = 2048
ZDIM = 768
CLASSES = 1001
TBINS = 1000
IMG = 128
MB = 3
IMAGES = 16
N_SECTION = 2


def place_ends(drawn, own_key, least, largest):
    extent = drawn.shape
    place = [jax.random.randint(jax.random.fold_in(own_key, axis), (), 0, extent[axis]) for axis in range(len(extent))]
    drawn = drawn.at[tuple(place)].set(least)
    longest = extent.index(max(extent))
    place[longest] = (place[longest] + 1) % extent[longest]
    return drawn.at[tuple(place)].set(largest)


def level_of(own_key, extent, cuts, least, largest):
    def one(dim, shards_of):
        steps = jax.random.uniform(jax.random.fold_in(jax.random.fold_in(own_key, 6), dim), (shards_of,), jnp.float32, least / len(cuts), largest / len(cuts))
        return jnp.repeat(jnp.exp(steps), extent[dim] // shards_of).reshape((-1,) + (1,) * (len(extent) - dim - 1))

    level = one(*cuts[0])
    for cut in cuts[1:]:
        level = level * one(*cut)
    return level


def rank_table(amount, skew):
    portions = [(1 << 20) // math.isqrt(standing ** skew) + 1 for standing in range(1, amount + 1)]
    spread = 1 + sum(portions) // (1 << 30)
    return np.cumsum(np.array([max(1, weight // spread) for weight in portions]))


def ranked(rng, extent, number_of, skew):
    grid = rank_table(number_of, skew)
    pick = jax.random.randint(jax.random.fold_in(rng, 1), extent, 0, int(grid[number_of - 1]))
    grade = jnp.searchsorted(jnp.asarray(grid, jnp.int32), pick, side="right")
    return jax.random.permutation(jax.random.fold_in(rng, 2), number_of)[grade].astype(jnp.int32)


def scatter_about(key, extent, spread, most, cuts=(), held_as=jnp.bfloat16):
    values = jax.random.normal(key, extent, jnp.float32) * spread
    if len(cuts) > 0:
        values = level_of(key, extent, cuts, -0.22, 0.18) * values
    return jnp.clip(values, min=-most, max=most).astype(held_as)


def setup_inputs(seed: int = 0) -> dict:
    streams_of = jax.random.split(jax.random.key(seed), 24)
    return {
        "tokens": scatter_about(streams_of[0], (MB, IMAGES, IMG, D), 1.0, 6.0, ((1, 16),)),
        "time_bins": place_ends(ranked(streams_of[1], (MB, IMAGES), TBINS, 2), jax.random.fold_in(streams_of[1], 3), 0, TBINS - 1).astype(jnp.int32),
        "labels": place_ends(ranked(streams_of[2], (MB, IMAGES), CLASSES, 2), jax.random.fold_in(streams_of[2], 3), 0, CLASSES - 1).astype(jnp.int32),
        "dino_feats": scatter_about(streams_of[3], (MB, IMAGES, IMG, ZDIM), 1.0, 6.0, ((1, 16),)),
        "cotangent": scatter_about(streams_of[4], (MB, IMAGES, IMG, D), 1.0, 6.0, ((1, 16),)),
        "time_table": scatter_about(streams_of[5], (TBINS, D), 0.7, 5.0, ((1, 16),), jnp.float32),
        "class_table": scatter_about(streams_of[6], (CLASSES, D), 0.7, 5.0, ((1, 16),), jnp.float32),
        "ada_weight": scatter_about(streams_of[7], (N_SECTION, D, 6 * D), D ** -0.5, 0.1875, ((0, 2), (1, 16)), jnp.float32),
        "ada_bias": scatter_about(streams_of[8], (N_SECTION, 6 * D), 0.3, 2.0, ((0, 2), (1, 16)), jnp.float32),
        "qkv_weight": scatter_about(streams_of[9], (N_SECTION, D, 3 * D), D ** -0.5, 0.1875, ((0, 2), (1, 16)), jnp.float32),
        "qkv_bias": scatter_about(streams_of[10], (N_SECTION, 2 * D), 0.3, 2.0, ((0, 2), (1, 16)), jnp.float32),
        "out_weight": scatter_about(streams_of[11], (N_SECTION, D, D), (D // 16) ** -0.5, 0.75, ((0, 2), (1, 16)), jnp.float32),
        "out_bias": scatter_about(streams_of[12], (N_SECTION, D), 0.3, 2.0, ((0, 2), (1, 16)), jnp.float32),
        "mlp_in_weight": scatter_about(streams_of[13], (N_SECTION, D, FF), D ** -0.5, 0.1875, ((0, 2), (1, 16)), jnp.float32),
        "mlp_in_bias": scatter_about(streams_of[14], (N_SECTION, FF), 0.3, 2.0, ((0, 2), (1, 16)), jnp.float32),
        "mlp_out_weight": scatter_about(streams_of[15], (N_SECTION, FF, D), FF ** -0.5, 0.09375, ((0, 2), (1, 16)), jnp.float32),
        "mlp_out_bias": scatter_about(streams_of[16], (N_SECTION, D), 0.3, 2.0, ((0, 2), (1, 16)), jnp.float32),
        "align_weight_one": scatter_about(streams_of[17], (D, PROJ), D ** -0.5, 0.1875, ((0, 32),), jnp.float32),
        "align_bias_one": scatter_about(streams_of[18], (PROJ,), 0.3, 2.0, ((0, 32),), jnp.float32),
        "align_weight_two": scatter_about(streams_of[19], (PROJ, PROJ), PROJ ** -0.5, 0.125, ((0, 32),), jnp.float32),
        "align_bias_two": scatter_about(streams_of[20], (PROJ,), 0.3, 2.0, ((0, 32),), jnp.float32),
        "align_weight_three": scatter_about(streams_of[21], (PROJ, ZDIM), PROJ ** -0.5, 0.125, ((0, 32),), jnp.float32),
        "align_bias_three": scatter_about(streams_of[22], (ZDIM,), 0.3, 2.0, ((0, 32),), jnp.float32),
    }


highest_precision = lax.Precision.HIGHEST
epsilon = 1e-06
loss_weight = 0.5

@jax.custom_vjp
def lower_precision(v):
    return lax.optimization_barrier(v.astype(jnp.bfloat16)).astype(jnp.float32)

@jax.custom_vjp
def low_back(v):
    return v

def low_keep(v):
    return (lower_precision(v), None)

def low_pass(kept, grad):
    return (grad,)

def back_keep(v):
    return (v, None)

def back_low(kept, grad):
    return (lower_precision(grad),)
lower_precision.defvjp(low_keep, low_pass)
low_back.defvjp(back_keep, back_low)

def round_both(values):
    return lower_precision(low_back(values))

def layer_norm(values):
    centred = values - lax.optimization_barrier(jnp.mean(values, -1, keepdims=True))
    return centred * lax.rsqrt(lax.optimization_barrier(jnp.mean(centred * centred, -1, keepdims=True)) + epsilon)

def product(left, right):
    return jnp.einsum('gtd,de->gte', left, right, precision=highest_precision)

def block(inputs, modulation, weights):
    qkv_weight, qkv_bias, out_weight, out_bias, in_weight, in_bias, down_weight, down_bias = weights
    groups = inputs.shape[0]
    shift_attn, scale_attn, gate_attn, shift_mlp, scale_mlp, gate_mlp = jnp.split(modulation[:, None, :], 6, axis=-1)
    attn_input = lower_precision(layer_norm(inputs) * (1.0 + scale_attn) + shift_attn)
    full_bias = jnp.concatenate([qkv_bias[:D], jnp.zeros((D,), jnp.float32), qkv_bias[D:]])
    qkv_rows = round_both(product(attn_input, qkv_weight) + full_bias)
    parts = qkv_rows.reshape(groups, IMG, 3, HEADS, HD)
    queries, key_rows, value_rows = (parts[:, :, 0], parts[:, :, 1], parts[:, :, 2])
    scores = low_back(jnp.einsum('gqhe,gkhe->ghqk', queries, key_rows, precision=highest_precision) * HD ** (-0.5))
    soft_weights = lower_precision(jax.nn.softmax(scores, axis=-1))
    mixed = jnp.einsum('ghqk,gkhe->gqhe', soft_weights, value_rows, precision=highest_precision)
    mixed = round_both(mixed.reshape(groups, IMG, D))
    attn_branch = low_back(product(mixed, out_weight) + out_bias)
    after_attn = inputs + gate_attn * attn_branch
    mlp_input = lower_precision(layer_norm(after_attn) * (1.0 + scale_mlp) + shift_mlp)
    mlp_pre = low_back(product(mlp_input, in_weight) + in_bias)
    mlp_act = lower_precision(jax.nn.gelu(mlp_pre, approximate=True))
    mlp_branch = low_back(product(mlp_act, down_weight) + down_bias)
    return after_attn + gate_mlp * mlp_branch

def align(hidden, target, pieces):
    weight_one, bias_one, weight_two, bias_two, weight_three, bias_three = pieces
    first_pre = low_back(product(hidden, weight_one) + bias_one)
    first_act = lower_precision(jax.nn.silu(first_pre))
    second_pre = low_back(product(first_act, weight_two) + bias_two)
    second_act = lower_precision(jax.nn.silu(second_pre))
    latent = low_back(product(second_act, weight_three) + bias_three)
    latent_sq = lax.optimization_barrier(jnp.sum(latent * latent, -1))
    target_sq = lax.optimization_barrier(jnp.sum(target * target, -1))
    crossed = lax.optimization_barrier(jnp.sum(latent * target, -1))
    cosine = crossed * lax.rsqrt(latent_sq + epsilon) * lax.rsqrt(target_sq + epsilon)
    return -loss_weight * jnp.sum(cosine)

def reference(tokens, time_bins, labels, dino_feats, cotangent, time_table, class_table, ada_weight, ada_bias, qkv_weight, qkv_bias, out_weight, out_bias, mlp_in_weight, mlp_in_bias, mlp_out_weight, mlp_out_bias, align_weight_one, align_bias_one, align_weight_two, align_bias_two, align_weight_three, align_bias_three):
    count = MB * IMAGES
    group = math.gcd(count, max(1, 4096 // IMG))
    blocks = count // group
    inputs = tokens.astype(jnp.float32).reshape(blocks, group, IMG, D)
    targets = dino_feats.astype(jnp.float32).reshape(blocks, group, IMG, ZDIM)
    grad_final = cotangent.astype(jnp.float32).reshape(blocks, group, IMG, D)
    bins_flat = time_bins.reshape(count).astype(jnp.int32)
    labels_flat = labels.reshape(count).astype(jnp.int32)
    model_parameters = (time_table, class_table, ada_weight, ada_bias, qkv_weight, qkv_bias, out_weight, out_bias, mlp_in_weight, mlp_in_bias, mlp_out_weight, mlp_out_bias, align_weight_one, align_bias_one, align_weight_two, align_bias_two, align_weight_three, align_bias_three)
    probe = jnp.zeros((blocks, group, IMG, D), jnp.float32)

    def forward(inputs, probe, model_parameters):
        cond = jnp.take(lower_precision(model_parameters[0]), bins_flat, axis=0) + jnp.take(lower_precision(model_parameters[1]), labels_flat, axis=0)
        activation_fn = lower_precision(jax.nn.silu(cond))
        modulation_rows = jnp.einsum('zk,bkp->bzp', activation_fn, lower_precision(model_parameters[2]), precision=highest_precision) + lower_precision(model_parameters[3])[:, None, :]
        modulation_rows = low_back(modulation_rows).reshape(2, blocks, group, 6 * D)
        layers = [tuple((lower_precision(item[which]) for item in model_parameters[4:12])) for which in range(2)]
        aligner = tuple((lower_precision(item) for item in model_parameters[12:18]))

        def group_step(total, pieces):
            block_in, block_probe, block_target, mod_first, mod_second = pieces
            hidden = round_both(block(block_in, mod_first, layers[0]) + block_probe)
            final = block(hidden, mod_second, layers[1])
            return (total + align(hidden, block_target, aligner), (hidden, final))
        total, outputs = lax.scan(jax.checkpoint(group_step), jnp.zeros((), jnp.float32), (inputs, probe, targets, modulation_rows[0], modulation_rows[1]))
        return (outputs[0], outputs[1], total)
    primal, pull = jax.vjp(forward, inputs, probe, model_parameters)
    grad_inputs, grad_probe, grads = pull((jnp.zeros_like(primal[0]), grad_final, jnp.ones_like(primal[2])))
    out_shape = (MB, IMAGES, IMG, D)
    acts = jnp.stack([primal[0].reshape(out_shape), primal[1].reshape(out_shape)]).astype(jnp.bfloat16)
    in_grads = jnp.stack([grad_inputs.reshape(out_shape), grad_probe.reshape(out_shape)]).astype(jnp.bfloat16)
    return (acts, in_grads, grads[0], grads[1], grads[2], grads[3], grads[4], grads[5], grads[6], grads[7], grads[8], grads[9], grads[10], grads[11], grads[12], grads[13], grads[14], grads[15], grads[16], grads[17])
```

```python
import functools

import jax
import jax.numpy as jnp
from jax import lax
from jax.experimental import pallas as pl
from jax.experimental.pallas import tpu as pltpu
from jax.sharding import PartitionSpec as P

HEADS = 16
HD = 72
LANES = 128
MESH = pl.DeviceIdType.MESH
DMA = pltpu.SemaphoreType.DMA

epsilon = 1e-06
loss_weight = 0.5


def norm_parts(values):
    centred = values - jnp.mean(values, -1, keepdims=True)
    inverse = lax.rsqrt(jnp.mean(centred * centred, -1, keepdims=True) + epsilon)
    return (centred * inverse, inverse)


def norm_back(grad_normed, normed, inverse):
    return inverse * (
        grad_normed
        - jnp.mean(grad_normed, -1, keepdims=True)
        - normed * jnp.mean(grad_normed * normed, -1, keepdims=True)
    )


def matmul(left, right):
    return jnp.dot(left, right, preferred_element_type=jnp.float32)


def transposed(left, right):
    return lax.dot_general(
        left, right, (((0,), (0,)), ((), ())), preferred_element_type=jnp.float32
    )


def times_transpose(grad_rows, weight):
    return lax.dot_general(
        grad_rows, weight, (((1,), (1,)), ((), ())), preferred_element_type=jnp.float32
    )


def local_grad(function, point, grad_value):
    return jax.vjp(function, point)[1](grad_value)[0]


def gelu_tanh(values):
    return jax.nn.gelu(values, approximate=True)


def half(values):
    return values.astype(jnp.bfloat16)


def wide(values):
    return values.astype(jnp.float32)


def split_heads(qkv_rows, images):
    parts = qkv_rows.reshape(images, -1, 3, HEADS, HD)
    return (parts[:, :, 0], parts[:, :, 1], parts[:, :, 2])


def score_rows(queries, key_rows):
    return jnp.einsum(
        "gqhe,gkhe->ghqk", queries, key_rows, preferred_element_type=jnp.float32
    ) * HD ** (-0.5)


def attend(qkv_rows, images):
    queries, key_rows, value_rows = split_heads(qkv_rows, images)
    scores = score_rows(queries, key_rows)
    row_max = jnp.max(scores, -1, keepdims=True)
    powers = jnp.exp(scores - row_max)
    soft = powers / jnp.sum(powers, -1, keepdims=True)
    mixed = jnp.einsum(
        "ghqk,gkhe->gqhe", half(soft), value_rows, preferred_element_type=jnp.float32
    )
    return half(mixed).reshape(qkv_rows.shape[0], HEADS * HD)


def attend_back(qkv_rows, grad_mixed, images):
    queries, key_rows, value_rows = split_heads(qkv_rows, images)
    grad_heads = grad_mixed.reshape(images, -1, HEADS, HD)
    scores = score_rows(queries, key_rows)
    row_max = jnp.max(scores, -1, keepdims=True)
    powers = jnp.exp(scores - row_max)
    soft = powers / jnp.sum(powers, -1, keepdims=True)
    grad_value = jnp.einsum(
        "ghqk,gqhe->gkhe", half(soft), grad_heads, preferred_element_type=jnp.float32
    )
    grad_soft = jnp.einsum(
        "gqhe,gkhe->ghqk", grad_heads, value_rows, preferred_element_type=jnp.float32
    )
    grad_scores = half(soft * (grad_soft - jnp.sum(soft * grad_soft, -1, keepdims=True)))
    grad_query = jnp.einsum(
        "ghqk,gkhe->gqhe", grad_scores, key_rows, preferred_element_type=jnp.float32
    ) * HD ** (-0.5)
    grad_key = jnp.einsum(
        "ghqk,gqhe->gkhe", grad_scores, queries, preferred_element_type=jnp.float32
    ) * HD ** (-0.5)
    stacked = jnp.stack([half(grad_query), half(grad_key), half(grad_value)], 2)
    return stacked.reshape(qkv_rows.shape[0], 3 * HEADS * HD)


def modulation_pieces(modulation, rows):
    images = modulation.shape[0]
    pieces = modulation.reshape(images, 6, 1, -1)
    return [
        jnp.broadcast_to(pieces[:, k], (images, rows // images, pieces.shape[-1])).reshape(rows, -1)
        for k in range(6)
    ]


def image_sums(values, images):
    return jnp.sum(values.reshape(images, -1, values.shape[1]), 1)


def block_forward(inputs, modulation, layer):
    qkv_weight, qkv_bias, out_weight, out_bias, in_weight, in_bias, down_weight, down_bias = layer
    images = modulation.shape[0]
    shift_attn, scale_attn, gate_attn, shift_mlp, scale_mlp, gate_mlp = modulation_pieces(
        modulation, inputs.shape[0]
    )
    attn_input = half(norm_parts(wide(inputs))[0] * (1.0 + scale_attn) + shift_attn)
    qkv_rows = half(matmul(attn_input, qkv_weight) + qkv_bias)
    mixed = attend(qkv_rows, images)
    attn_branch = matmul(mixed, out_weight) + out_bias
    after_attn = wide(inputs) + gate_attn * attn_branch
    mlp_input = half(norm_parts(after_attn)[0] * (1.0 + scale_mlp) + shift_mlp)
    mlp_pre = matmul(mlp_input, in_weight) + in_bias
    mlp_act = half(gelu_tanh(mlp_pre))
    mlp_branch = matmul(mlp_act, down_weight) + down_bias
    output = after_attn + gate_mlp * mlp_branch
    kept = (
        attn_input, qkv_rows, mixed, attn_branch, after_attn, mlp_input, mlp_pre, mlp_act, mlp_branch
    )
    return half(output), kept


def block_backward(inputs, modulation, kept, grad_out, layer):
    qkv_weight, qkv_bias, out_weight, out_bias, in_weight, in_bias, down_weight, down_bias = layer
    attn_input, qkv_rows, mixed, attn_branch, after_attn, mlp_input, mlp_pre, mlp_act, mlp_branch = kept
    images = modulation.shape[0]
    shift_attn, scale_attn, gate_attn, shift_mlp, scale_mlp, gate_mlp = modulation_pieces(
        modulation, inputs.shape[0]
    )
    grad_branch = half(grad_out * gate_mlp)
    grad_gate_mlp = image_sums(grad_out * mlp_branch, images)
    grad_act = times_transpose(grad_branch, down_weight)
    grad_pre = half(local_grad(gelu_tanh, mlp_pre, grad_act))
    grad_mlp_input = times_transpose(grad_pre, in_weight)
    normed_mlp, inverse_mlp = norm_parts(after_attn)
    grad_scale_mlp = image_sums(grad_mlp_input * normed_mlp, images)
    grad_shift_mlp = image_sums(grad_mlp_input, images)
    grad_after = grad_out + norm_back(grad_mlp_input * (1.0 + scale_mlp), normed_mlp, inverse_mlp)
    grad_attn = half(grad_after * gate_attn)
    grad_gate_attn = image_sums(grad_after * attn_branch, images)
    grad_mixed = half(times_transpose(grad_attn, out_weight))
    grad_qkv = attend_back(qkv_rows, grad_mixed, images)
    grad_attn_input = times_transpose(grad_qkv, qkv_weight)
    normed_attn, inverse_attn = norm_parts(wide(inputs))
    grad_scale_attn = image_sums(grad_attn_input * normed_attn, images)
    grad_shift_attn = image_sums(grad_attn_input, images)
    grad_inputs = grad_after + norm_back(
        grad_attn_input * (1.0 + scale_attn), normed_attn, inverse_attn
    )
    grad_mod = half(
        jnp.concatenate(
            [
                grad_shift_attn,
                grad_scale_attn,
                grad_gate_attn,
                grad_shift_mlp,
                grad_scale_mlp,
                grad_gate_mlp,
            ],
            1,
        )
    )
    saved = (attn_input, mixed, mlp_input, mlp_act, grad_qkv, grad_attn, grad_pre, grad_branch)
    return grad_inputs, saved + (grad_mod,)


def project_align(hidden, target, aligner):
    weight_one, bias_one, weight_two, bias_two, weight_three, bias_three = aligner
    first_pre = matmul(hidden, weight_one) + bias_one
    first_act = half(jax.nn.silu(first_pre))
    second_pre = matmul(first_act, weight_two) + bias_two
    second_act = half(jax.nn.silu(second_pre))
    latent = matmul(second_act, weight_three) + bias_three
    features = wide(target)
    source_latent = lax.rsqrt(jnp.sum(latent * latent, -1, keepdims=True) + epsilon)
    root_target = lax.rsqrt(jnp.sum(features * features, -1, keepdims=True) + epsilon)
    crossed = jnp.sum(latent * features, -1, keepdims=True)
    grad_latent = half(
        -loss_weight
        * (features * source_latent * root_target - crossed * root_target * source_latent**3 * latent)
    )
    grad_second = half(
        local_grad(jax.nn.silu, second_pre, times_transpose(grad_latent, weight_three))
    )
    grad_first = half(local_grad(jax.nn.silu, first_pre, times_transpose(grad_second, weight_two)))
    grad_hidden = times_transpose(grad_first, weight_one)
    weight_grads = (
        half(transposed(hidden, grad_first)),
        half(transposed(first_act, grad_second)),
        half(transposed(second_act, grad_latent)),
    )
    bias_grads = tuple(jnp.sum(wide(g), 0) for g in (grad_first, grad_second, grad_latent))
    return grad_hidden, weight_grads, bias_grads


def own_place():
    section = lax.axis_index("section")
    index = lax.axis_index("dp")
    return section, index, index // 4, lax.rem(index // 2, 2), lax.rem(index, 2)


def index_of(z, y, core):
    return z * 4 + y * 2 + core


def greet(targets):
    barrier = pltpu.get_barrier_semaphore()
    for target in targets:
        pl.semaphore_signal(barrier, inc=1, device_id=target, device_id_type=MESH)
    pl.semaphore_wait(barrier, len(targets))


def greet_section(count, section, index, extra=()):
    barrier = pltpu.get_barrier_semaphore()

    def one(step, carry):
        target = (section, lax.rem(index + step, count))
        pl.semaphore_signal(barrier, inc=1, device_id=target, device_id_type=MESH)
        return carry

    lax.fori_loop(1, count, one, 0)
    for target in extra:
        pl.semaphore_signal(barrier, inc=1, device_id=target, device_id_type=MESH)
    pl.semaphore_wait(barrier, count - 1 + len(extra))


class Exchange:
    def __init__(self, count, section, index, source, target, send, recv, local, own_only):
        self.count, self.section, self.index = count, section, index
        self.source, self.target = source, target
        self.send, self.recv, self.local, self.own_only = send, recv, local, own_only

    def piece(self, other):
        return self.source if self.own_only else self.source.at[other]

    def message(self, other, slot):
        return pltpu.make_async_remote_copy(
            src_ref=self.piece(other),
            dst_ref=self.target.at[slot],
            send_sem=self.send.at[other],
            recv_sem=self.recv.at[slot],
            device_id=(self.section, other),
            device_id_type=MESH,
        )

    def start(self):
        def one(step, carry):
            self.message(lax.rem(self.index + step, self.count), self.index).start()
            return carry

        lax.fori_loop(1, self.count, one, 0)
        pltpu.make_async_copy(
            self.piece(self.index), self.target.at[self.index], self.local
        ).start()

    def finish(self):
        def one(step, carry):
            other = lax.rem(self.index + step, self.count)
            self.message(other, self.index).wait_send()
            self.message(other, other).wait_recv()
            return carry

        lax.fori_loop(1, self.count, one, 0)
        pltpu.make_async_copy(
            self.piece(self.index), self.target.at[self.index], self.local
        ).wait()


def share_kernel(count, source, target, send, recv, local):
    section, index, z, y, core = own_place()
    greet_section(count, section, index)
    exchange = Exchange(count, section, index, source, target, send, recv, local, True)
    exchange.start()
    exchange.finish()


def share_small(count, values):
    return pl.pallas_call(
        functools.partial(share_kernel, count),
        out_shape=jax.ShapeDtypeStruct((count,) + values.shape, values.dtype),
        in_specs=[pl.BlockSpec(memory_space=pl.ANY)],
        out_specs=pl.BlockSpec(memory_space=pl.ANY),
        scratch_shapes=[DMA((count,)), DMA((count,)), DMA],
        compiler_params=pltpu.CompilerParams(collective_id=0, has_side_effects=True),
        name="share_small",
    )(values)


def gather_kernel(count, modes, *refs):
    total = len(modes)
    part, src = refs[0], refs[1 : total + 1]
    part_out, dst = refs[total + 1], refs[total + 2 : 2 * total + 2]
    (
        part_send, part_recv, part_local,
        local_sem, send_core, send_y, send_x, send_up, send_down, recv,
    ) = refs[2 * total + 2 :]
    depth = count // 4
    section, me, z, y, c = own_place()
    up, down = (section, me + 4), (section, me - 4)
    across, partner = (section, index_of(z, 1 - y, c)), (section, index_of(z, y, 1 - c))
    other = (1 - section, me)
    greet_section(count, section, me, (other,))
    parts = Exchange(count, section, me, part, part_out, part_send, part_recv, part_local, False)
    parts.start()

    def slot(w, sec, blk):
        return dst[w].at[sec, blk] if modes[w] else dst[w].at[blk]

    def copy(w, sec, blk, target, sem, src_ref=None):
        here = slot(w, sec, blk)
        return pltpu.make_async_remote_copy(
            src_ref=here if src_ref is None else src_ref,
            dst_ref=here,
            send_sem=sem,
            recv_sem=recv.at[w, sec if modes[w] else 0, blk],
            device_id=target,
            device_id_type=MESH,
        )

    def arrived(w, sec, blk):
        copy(w, sec, blk, partner, send_core.at[w, 0, 0, 0]).wait_recv()

    def pass_on(w, blk, zz, go_up, go_down, source=None):
        if go_up is not None:

            @pl.when(go_up)
            def _():
                copy(w, section, blk, up, send_up.at[w, zz], source).start()

        if go_down is not None:

            @pl.when(go_down)
            def _():
                copy(w, section, blk, down, send_down.at[w, zz], source).start()

        copy(w, section, blk, across, send_y.at[w, zz], source).start()
        if modes[w]:
            copy(w, section, blk, other, send_x.at[w, 0, zz], source).start()
        copy(w, section, blk, partner, send_core.at[w, 0, 0, zz], source).start()

    for w in range(total):
        pass_on(w, me, z, z < depth - 1, z > 0, src[w])
        pltpu.make_async_copy(src[w], slot(w, section, me), local_sem.at[w]).start()

    def step(k, carry):
        for w in range(total):

            @pl.when(z >= k)
            def _():
                blk = index_of(z - k, y, c)
                arrived(w, section, blk)
                pass_on(w, blk, z - k, z < depth - 1, None)

            @pl.when(z + k < depth)
            def _():
                blk = index_of(z + k, y, c)
                arrived(w, section, blk)
                pass_on(w, blk, z + k, None, z > 0)

        def from_y(w, zz):
            blk = index_of(zz, 1 - y, c)
            arrived(w, section, blk)
            if modes[w]:
                copy(w, section, blk, other, send_x.at[w, 1, zz]).start()
            copy(w, section, blk, partner, send_core.at[w, 0, 1, zz]).start()

        for w in range(total):

            @pl.when(z >= k - 1)
            def _():
                from_y(w, z - k + 1)

            @pl.when((z + k - 1 < depth) & (k > 1))
            def _():
                from_y(w, z + k - 1)

        return carry

    lax.fori_loop(1, depth + 1, step, 0)
    for w in range(total):
        if modes[w]:
            for side in range(2):

                def from_x(zz, carry):
                    blk = index_of(zz, y if side == 0 else 1 - y, c)
                    arrived(w, 1 - section, blk)
                    copy(w, 1 - section, blk, partner, send_core.at[w, 1, side, zz]).start()
                    return carry

                lax.fori_loop(0, depth, from_x, 0)
    for w in range(total):
        pltpu.make_async_copy(src[w], slot(w, section, me), local_sem.at[w]).wait()
        for far in range(2 if modes[w] else 1):
            for side in range(2):

                def finish(zz, carry):
                    blk = index_of(zz, y if side == 0 else 1 - y, 1 - c)
                    arrived(w, section if far == 0 else 1 - section, blk)
                    copy(w, section, me, partner, send_core.at[w, far, side, zz]).wait_send()
                    if far == 0:
                        if modes[w]:
                            copy(w, section, me, other, send_x.at[w, side, zz]).wait_send()
                        if side == 0:
                            copy(w, section, me, across, send_y.at[w, zz]).wait_send()

                            @pl.when((z < depth - 1) & (zz <= z))
                            def _():
                                copy(w, section, me, up, send_up.at[w, zz]).wait_send()

                            @pl.when((z > 0) & (zz >= z))
                            def _():
                                copy(w, section, me, down, send_down.at[w, zz]).wait_send()

                    return carry

                lax.fori_loop(0, depth, finish, 0)
    parts.finish()


def gather_weights(count, parts, own, both):
    items = list(own) + list(both)
    modes = [False] * len(own) + [True] * len(both)
    total, depth = len(items), count // 4
    anywhere = pl.BlockSpec(memory_space=pl.ANY)
    shapes = [((2, count) if m else (count,)) + a.shape for a, m in zip(items, modes)]
    results = pl.pallas_call(
        functools.partial(gather_kernel, count, modes),
        out_shape=[jax.ShapeDtypeStruct(parts.shape, parts.dtype)]
        + [jax.ShapeDtypeStruct(s, a.dtype) for s, a in zip(shapes, items)],
        in_specs=[anywhere] * (total + 1),
        out_specs=[anywhere] * (total + 1),
        scratch_shapes=[
            DMA((count,)),
            DMA((count,)),
            DMA,
            DMA((total,)),
            DMA((total, 2, 2, depth)),
            DMA((total, depth)),
            DMA((total, 2, depth)),
            DMA((total, depth)),
            DMA((total, depth)),
            DMA((total, 2, count)),
        ],
        compiler_params=pltpu.CompilerParams(collective_id=1, has_side_effects=True),
        name="gather_weights",
    )(parts, *items)
    return results[0], results[1:]


def reduce_kernel(count, near_counts, far_widths, *refs):
    depth = count // 4
    near_total, far_total = sum(near_counts), len(far_widths)
    n_near = len(near_counts)
    refs = list(refs)

    def take(amount):
        taken = refs[:amount]
        del refs[:amount]
        return taken

    near_src = take(n_near)
    far_src = take(far_total)
    mod_src, bias_src = take(2)
    (near_out,) = take(1)
    far_out = take(far_total)
    mod_out, bias_out = take(2)
    held, core_in, y_in, z_in = take(4)
    far_held, = take(1)
    far_core_in = take(far_total)
    far_x_in = take(far_total)
    far_y_in = take(far_total)
    far_z_in = take(far_total)
    (
        held_sem, core_send, core_recv, y_send, y_recv, z_send, z_recv,
        far_held_sem, far_core_send, far_core_recv, far_x_send, far_x_recv,
        far_y_send, far_y_recv, far_z_send, far_z_recv,
        mod_send, mod_recv, mod_local, bias_send, bias_recv, bias_local,
    ) = refs
    section, me, z, y, c = own_place()
    up, down = (section, me + 4), (section, me - 4)
    across, partner = (section, index_of(z, 1 - y, c)), (section, index_of(z, y, 1 - c))
    other = (1 - section, me)
    greet_section(count, section, me, (other,))

    near_pieces = []
    for w, amount in enumerate(near_counts):
        for j in range(amount):
            near_pieces.append((w, j))
    width = core_in.shape[-1]

    def near_slice(p, core):
        w, j = near_pieces[p]
        ref = near_src[w]
        if len(ref.shape) == 6:
            return ref.at[:, :, core, j]
        return ref.at[:, :, core, :, pl.ds(j * width, width)]

    def remote(source, target_ref, send, recv, device):
        return pltpu.make_async_remote_copy(
            src_ref=source,
            dst_ref=target_ref,
            send_sem=send,
            recv_sem=recv,
            device_id=device,
            device_id_type=MESH,
        )

    def near_core(p):
        return remote(
            near_slice(p, 1 - c), core_in.at[p], core_send.at[p], core_recv.at[p], partner
        )

    def near_load(p):
        return pltpu.make_async_copy(near_slice(p, c), held.at[p % 2], held_sem.at[p % 2])

    def far_core(i):
        return remote(
            far_src[i].at[:, :, :, 1 - c],
            far_core_in[i],
            far_core_send.at[i],
            far_core_recv.at[i],
            partner,
        )

    def far_load(i):
        return pltpu.make_async_copy(
            far_src[i].at[:, :, :, c], far_held.at[:, :, :, :, pl.ds(0, far_widths[i])], far_held_sem
        )

    near_core(0).start()
    near_load(0).start()
    far_core(0).start()
    far_load(0).start()
    for p in range(1, near_total):
        near_core(p).start()
        if p < far_total:
            far_core(p).start()
    mods = Exchange(count, section, me, mod_src, mod_out, mod_send, mod_recv, mod_local, True)
    biases = Exchange(count, section, me, bias_src, bias_out, bias_send, bias_recv, bias_local, False)
    mods.start()
    biases.start()

    def add_into(ref, place, extra_ref, extra_place):
        ref[place] = half(wide(ref[place]) + wide(extra_ref[extra_place]))

    class Chain:
        def __init__(self, sums, y_ref, z_ref, y_s, y_r, z_s, z_r, out_set):
            self.sums, self.y_ref, self.z_ref = sums, y_ref, z_ref
            self.y_s, self.y_r, self.z_s, self.z_r = y_s, y_r, z_s, z_r
            self.out_set = out_set

        def y_copy(self, p):
            ref, lead = self.sums(p)
            return remote(
                ref.at[lead + (slice(None), 1 - y)],
                self.y_ref(p),
                self.y_s.at[p],
                self.y_r.at[p],
                across,
            )

        def z_copy(self, p, to, where, device):
            ref, lead = self.sums(p)
            return remote(
                ref.at[lead + (to, y)],
                self.z_ref(p).at[where],
                self.z_s.at[p, to],
                self.z_r.at[p, where],
                device,
            )

        def z_arrived(self, p, where):
            self.z_copy(p, 0, where, across).wait_recv()

        def after_y(self, p):
            self.y_copy(p).wait_recv()
            ref, lead = self.sums(p)
            y_ref = self.y_ref(p)

            def one(to, carry):
                place = lead + (to, y)
                ref[place] = half(wide(ref[place]) + wide(y_ref[to]))
                return carry

            lax.fori_loop(0, depth, one, 0)
            self.hop(p, 0)

        def hop(self, p, h):
            ref, lead = self.sums(p)
            z_ref = self.z_ref(p)

            def arrive(to):
                if h > 0:
                    self.z_arrived(p, to)
                    place = lead + (to, y)
                    ref[place] = half(wide(ref[place]) + wide(z_ref[to]))

            @pl.when((z == h) & (z < depth - 1))
            def _():
                def one(back, carry):
                    to = depth - 1 - back
                    arrive(to)
                    self.z_copy(p, to, to, up).start()
                    return carry

                lax.fori_loop(0, depth - 1 - z, one, 0)

            @pl.when((depth - 1 - z == h) & (z > 0))
            def _():
                def one(to, carry):
                    arrive(to)
                    self.z_copy(p, to, jnp.where(to == z - 1, depth, to), down).start()
                    return carry

                lax.fori_loop(0, z, one, 0)

        def last(self, p):
            ref, lead = self.sums(p)
            z_ref = self.z_ref(p)
            total = self.out_set(p)
            total[...] = wide(ref[lead + (z, y)])

            @pl.when(z > 0)
            def _():
                self.z_arrived(p, z)
                total[...] += wide(z_ref[z])

            @pl.when(z < depth - 1)
            def _():
                self.z_arrived(p, depth)
                total[...] += wide(z_ref[depth])

        def finish(self, p):
            self.y_copy(p).wait_send()

            def one(to, carry):
                @pl.when(to != z)
                def _():
                    self.z_copy(p, to, to, across).wait_send()

                return carry

            lax.fori_loop(0, depth, one, 0)

    near = Chain(
        lambda p: (core_in, (p,)),
        lambda p: y_in.at[p],
        lambda p: z_in.at[p],
        y_send, y_recv, z_send, z_recv,
        lambda p: near_out.at[p],
    )
    far = Chain(
        lambda i: (far_core_in[i], (section,)),
        lambda i: far_y_in[i],
        lambda i: far_z_in[i],
        far_y_send, far_y_recv, far_z_send, far_z_recv,
        lambda i: far_out[i],
    )

    def near_start(p):
        for i in range(near_total):

            @pl.when(p == i)
            def _():
                near_load(i).wait()
                if i + 1 < near_total:
                    near_load(i + 1).start()
                near_core(i).wait_recv()

        place = lax.rem(p, 2)

        def add_side(side):
            def one(to, carry):
                add_into(core_in, (p, to, side), held, (place, to, side))
                return carry

            lax.fori_loop(0, depth, one, 0)

        add_side(1 - y)
        near.y_copy(p).start()
        add_side(y)

    def far_x(i):
        return remote(
            far_core_in[i].at[1 - section], far_x_in[i], far_x_send.at[i], far_x_recv.at[i], other
        )

    def far_start(i):
        far_load(i).wait()
        far_core(i).wait_recv()
        lanes = pl.ds(0, far_widths[i])

        def add_section(sec):
            def one(at, carry):
                to, side = at // 2, lax.rem(at, 2)
                add_into(
                    far_core_in[i], (sec, to, side),
                    far_held, (sec, to, side, slice(None), lanes),
                )
                return carry

            lax.fori_loop(0, 2 * depth, one, 0)

        add_section(1 - section)
        far_x(i).start()
        add_section(section)
        if i + 1 < far_total:
            far_load(i + 1).start()

    def far_after_x(i):
        far_x(i).wait_recv()

        def add_side(side):
            def one(to, carry):
                add_into(far_core_in[i], (section, to, side), far_x_in[i], (to, side))
                return carry

            lax.fori_loop(0, depth, one, 0)

        add_side(1 - y)
        far.y_copy(i).start()
        add_side(y)

    def stage(p, total, action):
        @pl.when((p >= 0) & (p < total))
        def _():
            action(p)

    def step(t, carry):
        stage(t, near_total, near_start)
        for i in range(far_total):
            base = 2 * i + 3

            @pl.when(t == i)
            def _():
                far_start(i)

            @pl.when(t == base)
            def _():
                far_after_x(i)

            @pl.when(t == base + 1)
            def _():
                far.after_y(i)

            for h in range(1, depth - 1):

                @pl.when(t == base + 1 + h)
                def _():
                    far.hop(i, h)

            @pl.when(t == base + depth)
            def _():
                far.last(i)

        stage(t - 1, near_total, near.after_y)
        for h in range(1, depth - 1):
            stage(t - 1 - h, near_total, lambda p: near.hop(p, h))
        stage(t - depth, near_total, near.last)
        return carry

    steps = max(near_total + depth, 2 * far_total + 2 + depth)
    lax.fori_loop(0, steps, step, 0)
    for p in range(near_total):
        near_core(p).wait_send()
    for i in range(far_total):
        far_core(i).wait_send()
        far_x(i).wait_send()
        far.finish(i)

    def near_finish(p, carry):
        near.finish(p)
        return carry

    lax.fori_loop(0, near_total, near_finish, 0)
    mods.finish()
    biases.finish()


def reduce_grads(count, near, far, mods, biases):
    depth = count // 4
    rows, width = near[1].shape[3], near[1].shape[4]
    near_counts = [a.shape[3] if a.ndim == 6 else a.shape[4] // width for a in near]
    near_total = sum(near_counts)
    far_shapes = [a.shape[4:] for a in far]
    far_rows, far_wide = far_shapes[0][0], max(s[1] for s in far_shapes)
    kind = jnp.bfloat16
    anywhere, vmem = pl.BlockSpec(memory_space=pl.ANY), pl.BlockSpec(memory_space=pltpu.VMEM)
    n_far = len(far)
    results = pl.pallas_call(
        functools.partial(reduce_kernel, count, near_counts, [s[1] for s in far_shapes]),
        out_shape=[jax.ShapeDtypeStruct((near_total, rows, width), jnp.float32)]
        + [jax.ShapeDtypeStruct(s, jnp.float32) for s in far_shapes]
        + [
            jax.ShapeDtypeStruct((count,) + mods.shape, mods.dtype),
            jax.ShapeDtypeStruct(biases.shape, biases.dtype),
        ],
        in_specs=[anywhere] * (len(near) + n_far + 2),
        out_specs=[vmem] * (1 + n_far) + [anywhere] * 2,
        scratch_shapes=[
            pltpu.VMEM((2, depth, 2, rows, width), kind),
            pltpu.VMEM((near_total, depth, 2, rows, width), kind),
            pltpu.VMEM((near_total, depth, rows, width), kind),
            pltpu.VMEM((near_total, depth + 1, rows, width), kind),
            pltpu.VMEM((2, depth, 2, far_rows, far_wide), kind),
        ]
        + [pltpu.VMEM((2, depth, 2) + s, kind) for s in far_shapes]
        + [pltpu.VMEM((depth, 2) + s, kind) for s in far_shapes]
        + [pltpu.VMEM((depth,) + s, kind) for s in far_shapes]
        + [pltpu.VMEM((depth + 1,) + s, kind) for s in far_shapes]
        + [
            DMA((2,)),
            DMA((near_total,)),
            DMA((near_total,)),
            DMA((near_total,)),
            DMA((near_total,)),
            DMA((near_total, depth)),
            DMA((near_total, depth + 1)),
            DMA,
            DMA((n_far,)),
            DMA((n_far,)),
            DMA((n_far,)),
            DMA((n_far,)),
            DMA((n_far,)),
            DMA((n_far,)),
            DMA((n_far, depth)),
            DMA((n_far, depth + 1)),
            DMA((count,)),
            DMA((count,)),
            DMA,
            DMA((count,)),
            DMA((count,)),
            DMA,
        ],
        compiler_params=pltpu.CompilerParams(
            collective_id=2, has_side_effects=True, vmem_limit_bytes=63 * 2**20
        ),
        name="reduce_grads",
    )(*near, *far, mods, biases)
    return results[0], results[1 : 1 + n_far], results[1 + n_far], results[2 + n_far]


def padded(values, rows):
    flat = values.reshape(values.shape[0], -1)
    room = rows * LANES - flat.shape[1]
    return jnp.pad(flat, ((0, 0), (0, room))).reshape(values.shape[0], rows, LANES)


def rows_for(amount, unit):
    rows = -(-amount // LANES)
    return -(-rows // unit) * unit


def split_at(flat, sizes):
    pieces, start = [], 0
    for size in sizes:
        pieces.append(flat[..., start : start + size])
        start += size
    return pieces


def body(
    tokens,
    time_bins,
    labels,
    dino_feats,
    cotangent,
    time_table,
    class_table,
    ada_weight,
    ada_bias,
    qkv_weight,
    qkv_bias,
    out_weight,
    out_bias,
    mlp_in_weight,
    mlp_in_bias,
    mlp_out_weight,
    mlp_out_bias,
    align_weight_one,
    align_bias_one,
    align_weight_two,
    align_bias_two,
    align_weight_three,
    align_bias_three,
):
    count = lax.axis_size("dp")
    first_section = lax.axis_index("section") == 0
    index = lax.axis_index("dp")
    images, _, image_rows, model_width = tokens.shape
    rows_all = images * image_rows
    shard = out_weight.shape[1]
    kernels = count % 4 == 0 and shard % 8 == 0

    indices = jnp.concatenate([time_bins, labels], 1).reshape(1, 2 * images)
    if kernels:
        indices_all = share_small(count, jnp.pad(indices, ((0, 7), (0, LANES - 2 * images))))
        indices_all = indices_all[:, 0, : 2 * images]
    else:
        indices_all = lax.all_gather(indices[0], "dp")
    pairs = indices_all.reshape(count * images, 2)
    time_hot = pairs[:, :1] == jnp.arange(time_table.shape[0], dtype=jnp.int32)[None]
    class_hot = pairs[:, 1:] == jnp.arange(class_table.shape[0], dtype=jnp.int32)[None]
    cond = matmul(half(time_hot), half(time_table)) + matmul(half(class_hot), half(class_table))
    cond_act = half(jax.nn.silu(cond))
    ada_half = half(ada_weight[0])
    mod_parts = half(matmul(cond_act, ada_half)).reshape(count, -1)
    mod_wide = ada_half.shape[1]
    mod_rows = rows_for(images * mod_wide, 16)

    block_biases = (qkv_bias, out_bias, mlp_in_bias, mlp_out_bias, ada_bias)
    align_biases = (align_bias_one, align_bias_two, align_bias_three)
    bias_flat = jnp.concatenate([b.reshape(-1) for b in block_biases + align_biases])
    block_sizes = [b.size for b in block_biases]
    align_sizes = [b.size for b in align_biases]
    bias_rows = rows_for(bias_flat.size, 16)
    own = [half(w[0]) for w in (qkv_weight, out_weight, mlp_in_weight, mlp_out_weight)]
    both = [half(w) for w in (align_weight_one, align_weight_two, align_weight_three)]
    bias_pack = padded(half(bias_flat)[None], bias_rows)[0]
    if kernels:
        fold = both[0].shape[0] * both[0].shape[1] // model_width
        first_shape = both[0].shape
        if fold % 8 == 0:
            both[0] = both[0].reshape(fold, model_width)
        parts, gathered = gather_weights(
            count, padded(mod_parts, mod_rows), own, [bias_pack] + both
        )
        modulation = jnp.sum(wide(parts), 0).reshape(-1)[: images * mod_wide]
        biases_full = gathered[len(own)].reshape(2, count, -1)
        align_full = [g.reshape((2 * count,) + g.shape[2:]) for g in gathered[len(own) + 1 :]]
        align_full[0] = align_full[0].reshape((2 * count,) + first_shape)
    else:
        modulation = lax.psum_scatter(wide(mod_parts), "dp", scatter_dimension=0, tiled=True)
        gathered = [lax.all_gather(w, "dp") for w in own]
        align_full = [lax.all_gather(w, ("section", "dp")) for w in both]
        biases_full = lax.all_gather(bias_pack.reshape(-1), ("section", "dp"))
        biases_full = biases_full.reshape(2, count, -1)
    own_biases = jnp.where(first_section, biases_full[0], biases_full[1])
    block_full = [
        wide(b).reshape(-1)
        for b in split_at(own_biases[:, : sum(block_sizes)], block_sizes)
    ]
    align_bias_full = [
        wide(b).reshape(-1)
        for b in split_at(
            biases_full[:, :, sum(block_sizes) : sum(block_sizes + align_sizes)], align_sizes
        )
    ]
    modulation = modulation.reshape(images, mod_wide) + block_full[4]
    weights = [g.reshape(-1, g.shape[-1]) for g in gathered[:4]]
    qkv_full_bias = jnp.concatenate(
        [block_full[0][:model_width], jnp.zeros((model_width,), jnp.float32), block_full[0][model_width:]]
    )
    layer = (
        weights[0], qkv_full_bias, weights[1], block_full[1],
        weights[2], block_full[2], weights[3], block_full[3],
    )
    align_weights = [g.reshape(-1, g.shape[-1]) for g in align_full]
    aligner = (
        align_weights[0], align_bias_full[0], align_weights[1], align_bias_full[1],
        align_weights[2], align_bias_full[2],
    )

    start_rows = tokens.reshape(rows_all, model_width)
    hidden, kept_first = block_forward(start_rows, modulation, layer)
    to_second = [(0, 1)]
    to_first = [(1, 0)]
    received = lax.ppermute(hidden, "section", to_second)
    target = dino_feats.reshape(rows_all, -1)
    grad_final = cotangent.reshape(rows_all, model_width)

    def run_align(values):
        grad_hidden, weight_grads, bias_grads = project_align(values, target, aligner)
        saved = (
            kept_first[0], kept_first[2], kept_first[5], kept_first[7],
            jnp.zeros((rows_all, 3 * model_width), jnp.bfloat16),
            jnp.zeros((rows_all, model_width), jnp.bfloat16),
            jnp.zeros(kept_first[7].shape, jnp.bfloat16),
            jnp.zeros((rows_all, model_width), jnp.bfloat16),
            jnp.zeros((images, mod_wide), jnp.bfloat16),
        )
        return values, grad_hidden, saved, weight_grads, bias_grads

    def run_second(values):
        final, kept = block_forward(values, modulation, layer)
        grad_inputs, saved = block_backward(values, modulation, kept, wide(grad_final), layer)
        weight_grads = tuple(jnp.zeros(w.shape, jnp.bfloat16) for w in align_weights)
        bias_grads = tuple(jnp.zeros(b.shape, jnp.float32) for b in align_bias_full)
        return final, grad_inputs, saved, weight_grads, bias_grads

    own_hidden = jnp.where(first_section, hidden, received)
    outputs, grad_part, saved_second, align_grads, align_bias_grads = lax.cond(
        first_section, run_align, run_second, own_hidden
    )
    grad_align = lax.ppermute(half(grad_part), "section", to_second)
    grad_hidden = half(grad_part + wide(grad_align))
    grad_received = lax.ppermute(grad_hidden, "section", to_first)

    def run_first(values):
        grad_inputs, saved = block_backward(start_rows, modulation, kept_first, wide(values), layer)
        return half(grad_inputs), saved

    def keep_second(values):
        return grad_hidden, saved_second

    in_grads, saved = lax.cond(first_section, run_first, keep_second, grad_received)
    attn_input, mixed, mlp_input, mlp_act, grad_qkv, grad_attn, grad_pre, grad_branch, grad_mod = saved
    weight_grads = (
        half(transposed(attn_input, grad_qkv)),
        half(transposed(mixed, grad_attn)),
        half(transposed(mlp_input, grad_pre)),
        half(transposed(mlp_act, grad_branch)),
    )
    sums = [jnp.sum(wide(g), 0) for g in (grad_qkv, grad_attn, grad_pre, grad_branch)]
    sums[0] = jnp.concatenate([sums[0][:model_width], sums[0][2 * model_width :]])
    align_sums = [jnp.moveaxis(g.reshape(2, count, -1), 0, 1).reshape(count, -1) for g in align_bias_grads]
    bias_flat = jnp.concatenate([g.reshape(count, -1) for g in sums] + align_sums, 1)
    if kernels:
        tall = weight_grads[3].shape[0] // (count * shard)
        near = [
            g.reshape(count // 4, 2, 2, shard, g.shape[1]) for g in weight_grads[:3]
        ] + [weight_grads[3].reshape(count // 4, 2, 2, tall, shard, model_width)]
        far_first = align_grads[0].reshape((2 * count,) + first_shape)
        far_first = far_first.reshape(2, count // 4, 2, 2, *both[0].shape)
        far = [far_first] + [
            g.reshape(2, count // 4, 2, 2, *w.shape) for g, w in zip(align_grads[1:], both[1:])
        ]
        bias_grad_rows = rows_for(bias_flat.shape[1], 8)
        near_sum, far_sum, mods, bias_parts = reduce_grads(
            count, near, far, padded(grad_mod.reshape(1, -1), mod_rows)[0], padded(bias_flat, bias_grad_rows)
        )
        grad_mods = mods.reshape(count, -1)[:, : images * mod_wide]
        bias_sum = jnp.sum(bias_parts, 0).reshape(-1)
        n_qkv, n_in = 3, weights[2].shape[1] // model_width
        grad_qkv_weight = jnp.concatenate([near_sum[j] for j in range(n_qkv)], 1)
        grad_out_weight = near_sum[n_qkv]
        grad_in_weight = jnp.concatenate([near_sum[n_qkv + 1 + j] for j in range(n_in)], 1)
        grad_down_weight = near_sum[n_qkv + 1 + n_in :].reshape(-1, model_width)
        align_out = [far_sum[0].reshape(first_shape), far_sum[1], far_sum[2]]
    else:
        grad_mods = lax.all_gather(grad_mod.reshape(-1), "dp")
        bias_sum = lax.psum_scatter(bias_flat, "dp", scatter_dimension=0, tiled=True).reshape(-1)
        reduced = [
            lax.psum_scatter(wide(g), "dp", scatter_dimension=0, tiled=True) for g in weight_grads
        ]
        grad_qkv_weight, grad_out_weight, grad_in_weight, grad_down_weight = reduced
        align_out = [
            lax.psum_scatter(wide(g), ("section", "dp"), scatter_dimension=0, tiled=True)
            for g in align_grads
        ]

    grad_mods = grad_mods.reshape(count * images, mod_wide)
    grad_ada = transposed(cond_act, grad_mods)
    mod_sums = jnp.sum(wide(grad_mods), 0)
    ada_share = mod_wide // count
    grad_ada_bias = lax.dynamic_slice(mod_sums, (index * ada_share,), (ada_share,))
    cond_part = times_transpose(grad_mods, ada_half)
    block_sum = sum(block_sizes[:4])
    grad_biases = split_at(bias_sum[:block_sum], block_sizes[:4])
    align_share = split_at(bias_sum[block_sum : block_sum + 2 * sum(align_sizes)], [2 * a for a in align_sizes])
    align_share = jnp.concatenate([a.reshape(2, -1) for a in align_share], 1)
    packet = jnp.concatenate([cond_part.reshape(-1), align_share.reshape(-1)])
    packet = packet + lax.ppermute(packet, "section", [(0, 1), (1, 0)])
    cond_grad = packet[: cond_part.size].reshape(cond_part.shape)
    align_share = packet[cond_part.size :].reshape(2, -1)
    align_share = jnp.where(first_section, align_share[0], align_share[1])
    align_bias_out = split_at(align_share, align_sizes)
    cond_grad = local_grad(jax.nn.silu, cond, cond_grad)

    def table_grad(hot):
        return lax.dot_general(
            wide(hot),
            cond_grad,
            (((0,), (0,)), ((), ())),
            precision=lax.Precision.HIGHEST,
            preferred_element_type=jnp.float32,
        )

    whole_rows = (1, images, 1, image_rows, model_width)
    return (
        outputs.reshape(whole_rows),
        in_grads.reshape(whole_rows),
        table_grad(time_hot),
        table_grad(class_hot),
        grad_ada[None],
        grad_ada_bias[None],
        grad_qkv_weight[None],
        grad_biases[0][None],
        grad_out_weight[None],
        grad_biases[1][None],
        grad_in_weight[None],
        grad_biases[2][None],
        grad_down_weight[None],
        grad_biases[3][None],
        align_out[0],
        align_bias_out[0],
        align_out[1],
        align_bias_out[1],
        align_out[2],
        align_bias_out[2],
    )


def solution(mesh):
    placed = (
        P(None, "dp", None, None),
        P(None, "dp"),
        P(None, "dp"),
        P(None, "dp", None, None),
        P(None, "dp", None, None),
        P(None, "dp"),
        P(None, "dp"),
        P("section", "dp", None),
        P("section", "dp"),
        P("section", "dp", None),
        P("section", "dp"),
        P("section", "dp", None),
        P("section", "dp"),
        P("section", "dp", None),
        P("section", "dp"),
        P("section", "dp", None),
        P("section", "dp"),
        P(("section", "dp"), None),
        P(("section", "dp")),
        P(("section", "dp"), None),
        P(("section", "dp")),
        P(("section", "dp"), None),
        P(("section", "dp")),
    )
    return jax.shard_map(
        body,
        mesh=mesh,
        in_specs=placed,
        out_specs=(
            P("section", None, "dp", None, None),
            P("section", None, "dp", None, None),
        )
        + placed[5:],
        check_vma=False,
    )
```

```python
import functools

import jax
import jax.numpy as jnp
from jax import lax
from jax.experimental import pallas as pl
from jax.experimental.pallas import tpu as pltpu
from jax.sharding import PartitionSpec as P

HEADS = 16
HD = 72
LANES = 128
MESH = pl.DeviceIdType.MESH
DMA = pltpu.SemaphoreType.DMA

epsilon = 1e-06
loss_weight = 0.5


def matmul(left, right):
    return jnp.dot(left, right, preferred_element_type=jnp.float32)


def transposed(left, right):
    return lax.dot_general(
        left, right, (((0,), (0,)), ((), ())), preferred_element_type=jnp.float32
    )


def times_transpose(grad_rows, weight):
    return lax.dot_general(
        grad_rows, weight, (((1,), (1,)), ((), ())), preferred_element_type=jnp.float32
    )


def local_grad(function, point, grad_value):
    return jax.vjp(function, point)[1](grad_value)[0]


def half(values):
    return values.astype(jnp.bfloat16)


def wide(values):
    return values.astype(jnp.float32)


GELU_SLOPE = 0.7978845608028654
GELU_CUBE = 0.044715


def dot_plain(left, right):
    return lax.dot_general(left, right, (((1,), (0,)), ((), ())), preferred_element_type=jnp.float32)


def dot_across(left, right):
    return lax.dot_general(left, right, (((1,), (1,)), ((), ())), preferred_element_type=jnp.float32)


def dot_down(left, right):
    return lax.dot_general(left, right, (((0,), (0,)), ((), ())), preferred_element_type=jnp.float32)


class Loads:
    def __init__(self, sems):
        self.sems, self.copies = sems, []

    def add(self, source, target, axis, tiles):
        size = source.shape[axis] // tiles
        first = len(self.copies)
        for j in range(tiles):
            place = (pl.ds(j * size, size),) if axis == 0 else (slice(None), pl.ds(j * size, size))
            self.copies.append(
                pltpu.make_async_copy(source.at[place], target.at[place], self.sems.at[first + j])
            )
        return list(range(first, first + tiles))

    def start(self):
        for copy in self.copies:
            copy.start()

    def wait(self, places):
        for place in places:
            self.copies[place].wait()


def head_window(head):
    low = head * HD
    start = low // LANES * LANES
    stop = -(-(low + HD) // LANES) * LANES
    return low, start, stop - start


def head_mask(head, rows):
    low, start, size = head_window(head)
    lane = lax.broadcasted_iota(jnp.int32, (rows, size), 1) + start
    return (lane >= low) & (lane < low + HD)


def masked(mask, values):
    return jnp.where(mask, values, jnp.zeros_like(values))


def row_norm(values):
    centred = values - jnp.mean(values, -1, keepdims=True)
    inverse = lax.rsqrt(jnp.mean(centred * centred, -1, keepdims=True) + epsilon)
    return centred * inverse, inverse


def row_norm_back(grad, normed, inverse):
    return inverse * (
        grad
        - jnp.mean(grad, -1, keepdims=True)
        - normed * jnp.mean(grad * normed, -1, keepdims=True)
    )


def column_tiles(total, tile):
    return [(at, min(tile, total - at)) for at in range(0, total, tile)]


def forward_kernel(
    images,
    x_ref, mod_ref, qkv_bias, out_bias, in_bias, down_bias, qkv_hbm, out_hbm, in_hbm, down_hbm,
    y_ref, attn_in, qkv_ref, probs, mixed, attn_branch, after, mlp_in, slope, act, mlp_branch,
    qkv_w, out_w, in_w, down_w, blend, sems,
):
    rows, width = x_ref.shape
    each = rows // images
    hidden_width = in_w.shape[1]
    loads = Loads(sems)
    parts = qkv_w.shape[1] // width
    in_tile = 512
    in_parts = hidden_width // in_tile
    qkv_at = loads.add(qkv_hbm, qkv_w, 1, parts)
    out_at = loads.add(out_hbm, out_w, 0, 1)
    in_at = loads.add(in_hbm, in_w, 1, 3)
    down_at = loads.add(down_hbm, down_w, 0, 3)
    loads.start()

    def per_image(action):
        def one(image, carry):
            action(image, pl.ds(pl.multiple_of(image * each, each), each))
            return carry

        lax.fori_loop(0, images, one, 0)

    def mod(image, k):
        return mod_ref[image, pl.ds(k, 1), :]

    def enter(image, at):
        normed, _ = row_norm(wide(x_ref[at, :]))
        attn_in[at, :] = half(normed * (1.0 + mod(image, 1)) + mod(image, 0))

    per_image(enter)
    for j in range(parts):
        loads.wait([qkv_at[j]])
        cols = slice(j * width, (j + 1) * width)
        qkv_ref[:, cols] = half(dot_plain(attn_in[...], qkv_w[:, cols]) + qkv_bias[:, cols])

    def attend(image, at):
        for head in range(HEADS):
            low, start, size = head_window(head)
            mask = head_mask(head, each)
            cols = [slice(part * width + start, part * width + start + size) for part in range(3)]
            queries = masked(mask, qkv_ref[at, cols[0]])
            scores = dot_across(queries, qkv_ref[at, cols[1]]) * HD ** (-0.5)
            powers = jnp.exp(scores - jnp.max(scores, -1, keepdims=True))
            soft = half(powers / jnp.sum(powers, -1, keepdims=True))
            probs[image, head] = soft
            fresh = dot_plain(soft, qkv_ref[at, cols[2]])
            window = slice(start, start + size)
            blend[:, window] = jnp.where(mask, fresh, blend[:, window])
        mixed[at, :] = half(blend[...])

    per_image(attend)
    loads.wait(out_at)
    attn_branch[...] = half(dot_plain(mixed[...], out_w[...]) + out_bias[...])

    def middle(image, at):
        joined = wide(x_ref[at, :]) + mod(image, 2) * wide(attn_branch[at, :])
        after[at, :] = joined
        normed, _ = row_norm(joined)
        mlp_in[at, :] = half(normed * (1.0 + mod(image, 4)) + mod(image, 3))

    per_image(middle)
    loads.wait(in_at)

    def feed(j, carry):
        cols = pl.ds(pl.multiple_of(j * in_tile, in_tile), in_tile)
        pre = dot_plain(mlp_in[...], in_w[:, cols]) + in_bias[:, cols]
        square = pre * pre
        bend = jnp.tanh(GELU_SLOPE * pre * (1.0 + GELU_CUBE * square))
        act[:, cols] = half(0.5 * pre * (1.0 + bend))
        slope[:, cols] = half(
            0.5 * (1.0 + bend)
            + 0.5 * pre * (1.0 - bend * bend) * (GELU_SLOPE + 3.0 * GELU_SLOPE * GELU_CUBE * square)
        )
        return carry

    lax.fori_loop(0, in_parts, feed, 0)
    loads.wait(down_at)
    mlp_branch[...] = half(dot_plain(act[...], down_w[...]) + down_bias[...])

    def leave(image, at):
        y_ref[at, :] = half(after[at, :] + mod(image, 5) * wide(mlp_branch[at, :]))

    per_image(leave)


def block_forward(inputs, modulation, layer):
    qkv_weight, qkv_bias, out_weight, out_bias, in_weight, in_bias, down_weight, down_bias = layer
    rows, width = inputs.shape
    images = modulation.shape[0]
    each = rows // images
    hidden_width = in_weight.shape[1]
    vmem, anywhere = pl.BlockSpec(memory_space=pltpu.VMEM), pl.BlockSpec(memory_space=pl.ANY)
    thin = jax.ShapeDtypeStruct((rows, width), jnp.bfloat16)
    fat = jax.ShapeDtypeStruct((rows, hidden_width), jnp.bfloat16)
    return pl.pallas_call(
        functools.partial(forward_kernel, images),
        out_shape=[
            thin, thin, jax.ShapeDtypeStruct((rows, 3 * width), jnp.bfloat16),
            jax.ShapeDtypeStruct((images, HEADS, each, each), jnp.bfloat16),
            thin, thin, jax.ShapeDtypeStruct((rows, width), jnp.float32), thin, fat, fat, thin,
        ],
        in_specs=[vmem] * 6 + [anywhere] * 4,
        out_specs=[vmem] * 11,
        scratch_shapes=[pltpu.VMEM(w.shape, w.dtype) for w in (qkv_weight, out_weight, in_weight, down_weight)]
        + [pltpu.VMEM((each, width), jnp.float32), DMA((10,))],
        compiler_params=pltpu.CompilerParams(vmem_limit_bytes=62 * 2**20),
        name="block_forward",
    )(
        inputs, modulation, qkv_bias[None], out_bias[None], in_bias[None], down_bias[None],
        qkv_weight, out_weight, in_weight, down_weight,
    )


def backward_kernel(
    images,
    x_ref, mod_ref, qkv_ref, probs, attn_branch, after, slope, mlp_branch, dout,
    qkv_hbm, out_hbm, in_hbm, down_hbm,
    dx_ref, d_qkv, d_attn, d_pre, d_branch, d_mod, qkv_sum, attn_sum, pre_sum, branch_sum,
    qkv_w, out_w, in_w, down_w, wide_grad, half_grad, blend, sems,
):
    rows, width = x_ref.shape
    each = rows // images
    hidden_width = in_w.shape[1]
    loads = Loads(sems)
    tile = 512
    down_at = loads.add(down_hbm, down_w, 0, 3)
    in_at = loads.add(in_hbm, in_w, 0, 3)
    out_at = loads.add(out_hbm, out_w, 0, 1)
    qkv_at = loads.add(qkv_hbm, qkv_w, 0, 3)
    loads.start()

    def per_image(action):
        def one(image, carry):
            action(image, pl.ds(pl.multiple_of(image * each, each), each))
            return carry

        lax.fori_loop(0, images, one, 0)

    def mod(image, k):
        return mod_ref[image, pl.ds(k, 1), :]

    def sums(image, k, values):
        d_mod[image, pl.ds(k, 1), :] = jnp.sum(values, 0, keepdims=True)

    def enter(image, at):
        grad = wide(dout[at, :])
        d_branch[at, :] = half(grad * mod(image, 5))
        sums(image, 5, grad * wide(mlp_branch[at, :]))

    per_image(enter)
    loads.wait(down_at)

    def feed(j, carry):
        cols = pl.ds(pl.multiple_of(j * tile, tile), tile)
        grad = half(dot_across(d_branch[...], down_w[cols, :]) * wide(slope[:, cols]))
        d_pre[:, cols] = grad
        pre_sum[:, cols] = jnp.sum(wide(grad), 0, keepdims=True)
        return carry

    lax.fori_loop(0, hidden_width // tile, feed, 0)
    loads.wait(in_at)
    for start, size in column_tiles(width, 512):
        wide_grad[:, start : start + size] = dot_across(d_pre[...], in_w[start : start + size, :])

    def middle(image, at):
        grad_in = wide_grad[at, :]
        normed, inverse = row_norm(after[at, :])
        sums(image, 4, grad_in * normed)
        sums(image, 3, grad_in)
        grad = wide(dout[at, :]) + row_norm_back(grad_in * (1.0 + mod(image, 4)), normed, inverse)
        dx_ref[at, :] = grad
        d_attn[at, :] = half(grad * mod(image, 2))
        sums(image, 2, grad * wide(attn_branch[at, :]))

    per_image(middle)
    loads.wait(out_at)
    half_grad[...] = half(dot_across(d_attn[...], out_w[...]))

    def attend(image, at):
        for head in range(HEADS):
            low, start, size = head_window(head)
            mask = head_mask(head, each)
            window = slice(start, start + size)
            cols = [slice(part * width + start, part * width + start + size) for part in range(3)]
            grad = masked(mask, half_grad[at, window])
            soft = probs[image, head]
            grad_soft = dot_across(grad, qkv_ref[at, cols[2]])
            weighed = wide(soft) * grad_soft
            grad_scores = half(weighed - wide(soft) * jnp.sum(weighed, -1, keepdims=True))
            fresh = (
                dot_plain(grad_scores, qkv_ref[at, cols[1]]) * HD ** (-0.5),
                dot_down(grad_scores, qkv_ref[at, cols[0]]) * HD ** (-0.5),
                dot_down(soft, grad),
            )
            for part in range(3):
                blend[:, cols[part]] = jnp.where(mask, fresh[part], blend[:, cols[part]])
        d_qkv[at, :] = half(blend[...])

    per_image(attend)
    loads.wait(qkv_at)
    for start, size in column_tiles(width, 512):
        wide_grad[:, start : start + size] = dot_across(d_qkv[...], qkv_w[start : start + size, :])

    def leave(image, at):
        grad_in = wide_grad[at, :]
        normed, inverse = row_norm(wide(x_ref[at, :]))
        sums(image, 1, grad_in * normed)
        sums(image, 0, grad_in)
        dx_ref[at, :] += row_norm_back(grad_in * (1.0 + mod(image, 1)), normed, inverse)

    per_image(leave)
    qkv_sum[...] = jnp.sum(wide(d_qkv[...]), 0, keepdims=True)
    attn_sum[...] = jnp.sum(wide(d_attn[...]), 0, keepdims=True)
    branch_sum[...] = jnp.sum(wide(d_branch[...]), 0, keepdims=True)


def block_backward(inputs, modulation, kept, grad_out, layer):
    qkv_weight, qkv_bias, out_weight, out_bias, in_weight, in_bias, down_weight, down_bias = layer
    attn_in, qkv_rows, probs, mixed, attn_branch, after, mlp_in, slope, act, mlp_branch = kept
    rows, width = inputs.shape
    images = modulation.shape[0]
    each = rows // images
    hidden_width = in_weight.shape[1]
    vmem, anywhere = pl.BlockSpec(memory_space=pltpu.VMEM), pl.BlockSpec(memory_space=pl.ANY)

    def shape(columns, kind=jnp.bfloat16, count=rows):
        return jax.ShapeDtypeStruct((count, columns), kind)

    results = pl.pallas_call(
        functools.partial(backward_kernel, images),
        out_shape=[
            shape(width, jnp.float32), shape(3 * width), shape(width), shape(hidden_width), shape(width),
            jax.ShapeDtypeStruct((images, 6, width), jnp.float32),
            shape(3 * width, jnp.float32, 1), shape(width, jnp.float32, 1),
            shape(hidden_width, jnp.float32, 1), shape(width, jnp.float32, 1),
        ],
        in_specs=[vmem] * 9 + [anywhere] * 4,
        out_specs=[vmem] * 10,
        scratch_shapes=[pltpu.VMEM(w.shape, w.dtype) for w in (qkv_weight, out_weight, in_weight, down_weight)]
        + [
            pltpu.VMEM((rows, width), jnp.float32), pltpu.VMEM((rows, width), jnp.bfloat16),
            pltpu.VMEM((each, 3 * width), jnp.float32), DMA((10,)),
        ],
        compiler_params=pltpu.CompilerParams(vmem_limit_bytes=62 * 2**20),
        name="block_backward",
    )(
        inputs, modulation, qkv_rows, probs, attn_branch, after, slope, mlp_branch, grad_out,
        qkv_weight, out_weight, in_weight, down_weight,
    )
    return results[0], tuple(results[1:5]), half(results[5]), tuple(results[6:])


def sigmoid_parts(values):
    gate = 1.0 / (1.0 + jnp.exp(-values))
    return values * gate, gate * (1.0 + values * (1.0 - gate))


def align_kernel(
    loss,
    x_ref, target, bias_one, bias_two, bias_three, one_hbm, two_hbm, three_hbm,
    dx_ref, act_one, act_two, d_one, d_two, d_latent, one_sum, two_sum, three_sum,
    one_w, two_w, three_w, slope_one, slope_two, sems,
):
    loads = Loads(sems)
    tile = 512
    one_at = loads.add(one_hbm, one_w, 0, 1)
    two_at = loads.add(two_hbm, two_w, 0, 1)
    three_at = loads.add(three_hbm, three_w, 0, 1)
    loads.start()

    def layer(source, weight, bias, act, slope):
        def one(j, carry):
            cols = pl.ds(pl.multiple_of(j * tile, tile), tile)
            pre = dot_plain(source[...], weight[:, cols]) + bias[:, cols]
            value, bend = sigmoid_parts(pre)
            act[:, cols] = half(value)
            slope[:, cols] = half(bend)
            return carry

        lax.fori_loop(0, weight.shape[1] // tile, one, 0)

    def back(grad, weight, slope, target_ref, sum_ref):
        def one(j, carry):
            cols = pl.ds(pl.multiple_of(j * tile, tile), tile)
            value = half(dot_across(grad[...], weight[cols, :]) * wide(slope[:, cols]))
            target_ref[:, cols] = value
            sum_ref[:, cols] = jnp.sum(wide(value), 0, keepdims=True)
            return carry

        lax.fori_loop(0, weight.shape[0] // tile, one, 0)

    loads.wait(one_at)
    layer(x_ref, one_w, bias_one, act_one, slope_one)
    loads.wait(two_at)
    layer(act_one, two_w, bias_two, act_two, slope_two)
    loads.wait(three_at)
    latent = dot_plain(act_two[...], three_w[...]) + bias_three[...]
    features = wide(target[...])
    root_latent = lax.rsqrt(jnp.sum(latent * latent, -1, keepdims=True) + epsilon)
    root_target = lax.rsqrt(jnp.sum(features * features, -1, keepdims=True) + epsilon)
    crossed = jnp.sum(latent * features, -1, keepdims=True)
    grad = half(
        -loss
        * (
            features * (root_latent * root_target)
            - (crossed * root_target * root_latent * root_latent * root_latent) * latent
        )
    )
    d_latent[...] = grad
    three_sum[...] = jnp.sum(wide(grad), 0, keepdims=True)
    back(d_latent, three_w, slope_two, d_two, two_sum)
    back(d_two, two_w, slope_one, d_one, one_sum)
    for start, size in column_tiles(x_ref.shape[1], 512):
        dx_ref[:, start : start + size] = half(dot_across(d_one[...], one_w[start : start + size, :]))


def project_align(hidden, target, aligner, loss):
    weight_one, bias_one, weight_two, bias_two, weight_three, bias_three = aligner
    rows, width = hidden.shape
    first, second, third = weight_one.shape[1], weight_two.shape[1], weight_three.shape[1]
    vmem, anywhere = pl.BlockSpec(memory_space=pltpu.VMEM), pl.BlockSpec(memory_space=pl.ANY)

    def shape(columns, kind=jnp.bfloat16, count=rows):
        return jax.ShapeDtypeStruct((count, columns), kind)

    results = pl.pallas_call(
        functools.partial(align_kernel, loss),
        out_shape=[
            shape(width), shape(first), shape(second), shape(first), shape(second), shape(third),
            shape(first, jnp.float32, 1), shape(second, jnp.float32, 1), shape(third, jnp.float32, 1),
        ],
        in_specs=[vmem] * 5 + [anywhere] * 3,
        out_specs=[vmem] * 9,
        scratch_shapes=[pltpu.VMEM(w.shape, w.dtype) for w in (weight_one, weight_two, weight_three)]
        + [pltpu.VMEM((rows, first), jnp.bfloat16), pltpu.VMEM((rows, second), jnp.bfloat16), DMA((3,))],
        compiler_params=pltpu.CompilerParams(vmem_limit_bytes=62 * 2**20),
        name="project_align",
    )(
        hidden, target, bias_one[None], bias_two[None], bias_three[None],
        weight_one, weight_two, weight_three,
    )
    return results[0], tuple(results[1:6]), results[6:]


def own_place():
    section = lax.axis_index("section")
    index = lax.axis_index("dp")
    return section, index, index // 4, lax.rem(index // 2, 2), lax.rem(index, 2)


def index_of(z, y, core):
    return z * 4 + y * 2 + core


def greet(targets):
    barrier = pltpu.get_barrier_semaphore()
    for target in targets:
        pl.semaphore_signal(barrier, inc=1, device_id=target, device_id_type=MESH)
    pl.semaphore_wait(barrier, len(targets))


def greet_section(count, section, index, extra=()):
    barrier = pltpu.get_barrier_semaphore()

    def one(step, carry):
        target = (section, lax.rem(index + step, count))
        pl.semaphore_signal(barrier, inc=1, device_id=target, device_id_type=MESH)
        return carry

    lax.fori_loop(1, count, one, 0)
    for target in extra:
        pl.semaphore_signal(barrier, inc=1, device_id=target, device_id_type=MESH)
    pl.semaphore_wait(barrier, count - 1 + len(extra))


class Exchange:
    def __init__(self, count, section, index, source, target, send, recv, local, own_only):
        self.count, self.section, self.index = count, section, index
        self.source, self.target = source, target
        self.send, self.recv, self.local, self.own_only = send, recv, local, own_only

    def piece(self, other):
        return self.source if self.own_only else self.source.at[other]

    def message(self, other, slot):
        return pltpu.make_async_remote_copy(
            src_ref=self.piece(other),
            dst_ref=self.target.at[slot],
            send_sem=self.send.at[other],
            recv_sem=self.recv.at[slot],
            device_id=(self.section, other),
            device_id_type=MESH,
        )

    def start(self):
        def one(step, carry):
            self.message(lax.rem(self.index + step, self.count), self.index).start()
            return carry

        lax.fori_loop(1, self.count, one, 0)
        pltpu.make_async_copy(
            self.piece(self.index), self.target.at[self.index], self.local
        ).start()

    def finish(self):
        def one(step, carry):
            other = lax.rem(self.index + step, self.count)
            self.message(other, self.index).wait_send()
            self.message(other, other).wait_recv()
            return carry

        lax.fori_loop(1, self.count, one, 0)
        pltpu.make_async_copy(
            self.piece(self.index), self.target.at[self.index], self.local
        ).wait()


def share_kernel(count, source, target, send, recv, local):
    section, index, z, y, core = own_place()
    greet_section(count, section, index)
    exchange = Exchange(count, section, index, source, target, send, recv, local, True)
    exchange.start()
    exchange.finish()


def share_small(count, values):
    return pl.pallas_call(
        functools.partial(share_kernel, count),
        out_shape=jax.ShapeDtypeStruct((count,) + values.shape, values.dtype),
        in_specs=[pl.BlockSpec(memory_space=pl.ANY)],
        out_specs=pl.BlockSpec(memory_space=pl.ANY),
        scratch_shapes=[DMA((count,)), DMA((count,)), DMA],
        compiler_params=pltpu.CompilerParams(collective_id=0, has_side_effects=True),
        name="share_small",
    )(values)


def gather_kernel(count, modes, first, order, *refs):
    total = len(modes)
    part, src = refs[0], refs[1 : total + 1]
    part_out, dst = refs[total + 1], refs[total + 2 : 2 * total + 2]
    (
        part_send, part_recv, part_local,
        local_sem, send_core, send_y, send_x, send_up, send_down, recv,
    ) = refs[2 * total + 2 :]
    depth = count // 4
    section, me, z, y, c = own_place()
    up, down = (section, me + 4), (section, me - 4)
    across, partner = (section, index_of(z, 1 - y, c)), (section, index_of(z, y, 1 - c))
    other = (1 - section, me)
    greet_section(count, section, me, (other,))
    parts = Exchange(count, section, me, part, part_out, part_send, part_recv, part_local, False)
    parts.start()

    def slot(w, sec, blk):
        return dst[w].at[sec, blk] if modes[w] else dst[w].at[blk]

    def copy(w, sec, blk, target, sem, src_ref=None):
        here = slot(w, sec, blk)
        return pltpu.make_async_remote_copy(
            src_ref=here if src_ref is None else src_ref,
            dst_ref=here,
            send_sem=sem,
            recv_sem=recv.at[w, sec if modes[w] else 0, blk],
            device_id=target,
            device_id_type=MESH,
        )

    def arrived(w, sec, blk):
        copy(w, sec, blk, partner, send_core.at[w, 0, 0, 0]).wait_recv()

    def pass_on(w, zz, side, go_up, go_down, go_across, source=None):
        blk = index_of(zz, y if side == 0 else 1 - y, c)
        if go_up is not None:

            @pl.when(go_up)
            def _():
                copy(w, section, blk, up, send_up.at[w, side, zz], source).start()

        if go_down is not None:

            @pl.when(go_down)
            def _():
                copy(w, section, blk, down, send_down.at[w, side, zz], source).start()

        if go_across:
            copy(w, section, blk, across, send_y.at[w, zz], source).start()
        if modes[w]:
            copy(w, section, blk, other, send_x.at[w, side, zz], source).start()
        copy(w, section, blk, partner, send_core.at[w, 0, side, zz], source).start()

    for w in order:
        pass_on(w, z, 0, z < depth - 1, z > 0, True, src[w])
        pltpu.make_async_copy(src[w], slot(w, section, me), local_sem.at[w]).start()

    def near(w, k):
        @pl.when(z >= k)
        def _():
            arrived(w, section, index_of(z - k, y, c))
            pass_on(w, z - k, 0, z < depth - 1, None, not first[w])

        @pl.when(z + k < depth)
        def _():
            arrived(w, section, index_of(z + k, y, c))
            pass_on(w, z + k, 0, None, z > 0, not first[w])

    def far(w, k):
        @pl.when(z >= k)
        def _():
            arrived(w, section, index_of(z - k, 1 - y, c))
            if first[w]:
                pass_on(w, z - k, 1, z < depth - 1, (z > 0) & (k == 0), False)
            else:
                pass_on(w, z - k, 1, None, None, False)

        @pl.when((z + k < depth) & (k > 0))
        def _():
            arrived(w, section, index_of(z + k, 1 - y, c))
            pass_on(w, z + k, 1, None, (z > 0) if first[w] else None, False)

    def step(k, carry):
        for w in order:
            if first[w]:
                far(w, k - 1)
                near(w, k)
        for w in order:
            if not first[w]:
                near(w, k)
        for w in order:
            if not first[w]:
                far(w, k - 1)
        return carry

    lax.fori_loop(1, depth + 1, step, 0)
    for w in order:
        if modes[w]:
            for side in range(2):

                def from_x(zz, carry):
                    blk = index_of(zz, y if side == 0 else 1 - y, c)
                    arrived(w, 1 - section, blk)
                    copy(w, 1 - section, blk, partner, send_core.at[w, 1, side, zz]).start()
                    return carry

                lax.fori_loop(0, depth, from_x, 0)
    for w in order:
        pltpu.make_async_copy(src[w], slot(w, section, me), local_sem.at[w]).wait()
        for other_section in range(2 if modes[w] else 1):
            for side in range(2):

                def finish(zz, carry):
                    blk = index_of(zz, y if side == 0 else 1 - y, 1 - c)
                    arrived(w, section if other_section == 0 else 1 - section, blk)
                    copy(w, section, me, partner, send_core.at[w, other_section, side, zz]).wait_send()
                    if other_section == 0:
                        if modes[w]:
                            copy(w, section, me, other, send_x.at[w, side, zz]).wait_send()
                        if side == 0:
                            @pl.when((zz == z) if first[w] else (zz >= 0))
                            def _():
                                copy(w, section, me, across, send_y.at[w, zz]).wait_send()

                        if side == 0 or first[w]:

                            @pl.when((z < depth - 1) & (zz <= z))
                            def _():
                                copy(w, section, me, up, send_up.at[w, side, zz]).wait_send()

                            @pl.when((z > 0) & (zz >= z))
                            def _():
                                copy(w, section, me, down, send_down.at[w, side, zz]).wait_send()

                    return carry

                lax.fori_loop(0, depth, finish, 0)
    parts.finish()


def gather_weights(count, parts, own, both, first=(), order=None):
    items = list(own) + list(both)
    modes = [False] * len(own) + [True] * len(both)
    total, depth = len(items), count // 4
    anywhere = pl.BlockSpec(memory_space=pl.ANY)
    shapes = [((2, count) if m else (count,)) + a.shape for a, m in zip(items, modes)]
    results = pl.pallas_call(
        functools.partial(gather_kernel, count, modes, [w in first for w in range(total)], order or list(range(total))),
        out_shape=[jax.ShapeDtypeStruct(parts.shape, parts.dtype)]
        + [jax.ShapeDtypeStruct(s, a.dtype) for s, a in zip(shapes, items)],
        in_specs=[anywhere] * (total + 1),
        out_specs=[anywhere] * (total + 1),
        scratch_shapes=[
            DMA((count,)),
            DMA((count,)),
            DMA,
            DMA((total,)),
            DMA((total, 2, 2, depth)),
            DMA((total, depth)),
            DMA((total, 2, depth)),
            DMA((total, 2, depth)),
            DMA((total, 2, depth)),
            DMA((total, 2, count)),
        ],
        compiler_params=pltpu.CompilerParams(collective_id=1, has_side_effects=True),
        name="gather_weights",
    )(parts, *items)
    return results[0], results[1:]


class Chain:
    def __init__(self, place, depth, z_first, sums, y_in, z_in, sems, out):
        self.section, self.z, self.y, self.c = place
        self.depth, self.z_first = depth, z_first
        self.sums, self.y_in, self.z_in, self.out = sums, y_in, z_in, out
        self.y_send, self.y_recv, self.z_send, self.z_recv = sems
        me = index_of(self.z, self.y, self.c)
        self.up, self.down = (self.section, me + 4), (self.section, me - 4)
        self.across = (self.section, index_of(self.z, 1 - self.y, self.c))

    def part(self, p, to):
        ref, lead = self.sums(p)
        return ref, lead + ((to,) if self.z_first else (to, self.y))

    def y_copy(self, p):
        ref, lead = self.sums(p)
        whole = self.z if self.z_first else slice(None)
        return remote_copy(
            ref.at[lead + (whole, 1 - self.y)],
            self.y_in(p),
            self.y_send.at[p],
            self.y_recv.at[p],
            self.across,
        )

    def z_copy(self, p, to, where, device):
        ref, place = self.part(p, to)
        return remote_copy(
            ref.at[place], self.z_in(p).at[where], self.z_send.at[p, to], self.z_recv.at[p, where], device
        )

    def add_z(self, p, to, where):
        self.z_copy(p, 0, where, self.across).wait_recv()
        ref, place = self.part(p, to)
        z_in = self.z_in(p)
        if self.z_first:
            for side in range(2):
                ref[place + (side,)] = half(wide(ref[place + (side,)]) + wide(z_in[where, side]))
        else:
            ref[place] = half(wide(ref[place]) + wide(z_in[where]))

    def hop(self, p, h):
        @pl.when((self.z == h) & (self.z < self.depth - 1))
        def _():
            def one(back, carry):
                to = self.depth - 1 - back
                if h > 0:
                    self.add_z(p, to, to)
                self.z_copy(p, to, to, self.up).start()
                return carry

            lax.fori_loop(0, self.depth - 1 - self.z, one, 0)

        @pl.when((self.depth - 1 - self.z == h) & (self.z > 0))
        def _():
            def one(to, carry):
                if h > 0:
                    self.add_z(p, to, to)
                self.z_copy(p, to, jnp.where(to == self.z - 1, self.depth, to), self.down).start()
                return carry

            lax.fori_loop(0, self.z, one, 0)

    def join(self, p):
        @pl.when(self.z > 0)
        def _():
            self.add_z(p, self.z, self.z)

        @pl.when(self.z < self.depth - 1)
        def _():
            self.add_z(p, self.z, self.depth)

    def begin(self, p):
        if self.z_first:
            self.hop(p, 0)
        else:
            self.y_copy(p).start()

    def move(self, p, step):
        if self.z_first:
            if step < self.depth - 1:
                self.hop(p, step)
            else:
                self.join(p)
                self.y_copy(p).start()
            return
        if step == 1:
            self.y_copy(p).wait_recv()
            y_in = self.y_in(p)

            def one(to, carry):
                ref, place = self.part(p, to)
                ref[place] = half(wide(ref[place]) + wide(y_in[to]))
                return carry

            lax.fori_loop(0, self.depth, one, 0)
        self.hop(p, step - 1)

    def last(self, p):
        ref, lead = self.sums(p)
        if self.z_first:
            self.y_copy(p).wait_recv()
            total = wide(ref[lead + (self.z, self.y)]) + wide(self.y_in(p)[...])
            self.out(p)[...] = half(total)
        else:
            self.join(p)
            self.out(p)[...] = ref[lead + (self.z, self.y)]

    def finish(self, p):
        self.y_copy(p).wait_send()

        def one(to, carry):
            @pl.when(to != self.z)
            def _():
                self.z_copy(p, to, to, self.across).wait_send()

            return carry

        lax.fori_loop(0, self.depth, one, 0)


def remote_copy(source, target, send, recv, device):
    return pltpu.make_async_remote_copy(
        src_ref=source,
        dst_ref=target,
        send_sem=send,
        recv_sem=recv,
        device_id=device,
        device_id_type=MESH,
    )


def reduce_kernel(count, ready, pairs, plan, far_first, far_steps, *refs):
    depth = count // 4
    far_total = len(far_first)
    near_total = ready + len(plan)
    refs = list(refs)

    def take(amount):
        taken = refs[:amount]
        del refs[:amount]
        return taken

    (ready_src,) = take(1)
    left_src, right_src = take(pairs), take(pairs)
    far_src = take(far_total)
    mod_src, bias_src = take(2)
    (near_out,) = take(1)
    far_out = take(far_total)
    mod_out, bias_out = take(2)
    left, right, made, core_in, y_in, z_in, tail_y_in, tail_z_in, far_held = take(9)
    far_core_in, far_y_in, far_z_in = take(far_total), take(far_total), take(far_total)
    (
        left_sem, right_sem, ready_sem, core_send, core_recv, y_send, y_recv, z_send, z_recv,
        far_held_sem, far_core_send, far_core_recv, far_x_send, far_x_recv,
        far_y_send, far_y_recv, far_z_send, far_z_recv,
        mod_send, mod_recv, mod_local, bias_send, bias_recv, bias_local,
    ) = refs
    section, me, z, y, c = own_place()
    partner = (section, index_of(z, y, 1 - c))
    other = (1 - section, me)
    greet_section(count, section, me, (other,))
    rows, width = made.shape[-2:]
    mods = Exchange(count, section, me, mod_src, mod_out, mod_send, mod_recv, mod_local, True)
    biases = Exchange(count, section, me, bias_src, bias_out, bias_send, bias_recv, bias_local, False)

    order = [near_total - 1] + list(range(near_total - 1))

    def operands(p, slot):
        pair, row, column = plan[p - ready]
        return (
            pltpu.make_async_copy(
                left_src[pair].at[:, pl.ds(row * width, width)], left.at[slot], left_sem.at[slot]
            ),
            pltpu.make_async_copy(
                right_src[pair].at[:, pl.ds(column * width, width)], right.at[slot], right_sem.at[slot]
            ),
        )

    def ready_copy(p, slot):
        return pltpu.make_async_copy(
            ready_src.at[:, :, :, p], made.at[slot], ready_sem
        )

    def core_copy(p, slot):
        return remote_copy(
            made.at[slot, :, :, 1 - c], core_in.at[p], core_send.at[p], core_recv.at[p], partner
        )

    def fetch(t, slot):
        for i, p in enumerate(order):
            if p >= ready:

                @pl.when(t == i)
                def _():
                    for copy in operands(p, slot):
                        copy.start()

    def piece_of(t):
        return jnp.where(t == 0, near_total - 1, t - 1)

    def make(t):
        slot = lax.rem(t, 2)
        p = piece_of(t)

        @pl.when(t >= 2)
        def _():
            core_copy(piece_of(t - 2), slot).wait_send()

        @pl.when(t + 1 < near_total)
        def _():
            fetch(t + 1, 1 - slot)

        @pl.when(p < ready)
        def _():
            copy = ready_copy(p, slot)
            copy.start()
            copy.wait()

        @pl.when(p >= ready)
        def _():
            for copy in operands(ready, slot):
                copy.wait()
            tile = 3 * LANES
            for at in range(0, width, tile):
                cols = slice(at, at + tile)
                product = dot_down(left[slot], right[slot, :, cols])
                made[slot, :, :, :, :, cols] = half(product).reshape(depth, 2, 2, rows, tile)

        core_copy(p, slot).start()

    near = Chain(
        (section, z, y, c), depth, False,
        lambda p: (core_in, (p,)), lambda p: y_in.at[p], lambda p: z_in.at[p],
        (y_send, y_recv, z_send, z_recv), lambda p: near_out.at[p],
    )
    tail = Chain(
        (section, z, y, c), depth, True,
        lambda p: (core_in, (p,)), lambda p: tail_y_in, lambda p: tail_z_in,
        (y_send, y_recv, z_send, z_recv), lambda p: near_out.at[p],
    )
    far = [
        Chain(
            (section, z, y, c), depth, far_first[i],
            lambda p: (far_core_in[p], (section,)), lambda p: far_y_in[p], lambda p: far_z_in[p],
            (far_y_send, far_y_recv, far_z_send, far_z_recv), lambda p: far_out[p],
        )
        for i in range(far_total)
    ]

    def begin(t):
        slot = lax.rem(t, 2)
        p = piece_of(t)
        core_copy(p, slot).wait_recv()

        def add_side(side):
            def one(to, carry):
                core_in[p, to, side] = half(
                    wide(core_in[p, to, side]) + wide(made[slot, to, side, c])
                )
                return carry

            lax.fori_loop(0, depth, one, 0)

        add_side(1 - y)

        @pl.when(p < near_total - 1)
        def _():
            near.begin(p)

        add_side(y)

        @pl.when(p == near_total - 1)
        def _():
            tail.begin(near_total - 1)

    def far_core(i):
        return remote_copy(
            far_src[i].at[:, :, :, 1 - c],
            far_core_in[i],
            far_core_send.at[i],
            far_core_recv.at[i],
            partner,
        )

    def far_load(i):
        wide_i = far_core_in[i].shape[-1]
        return pltpu.make_async_copy(
            far_src[i].at[:, :, :, c], far_held.at[:, :, :, :, pl.ds(0, wide_i)], far_held_sem
        )

    def far_x(i):
        return remote_copy(
            far_core_in[i].at[1], far_core_in[i].at[1], far_x_send.at[i], far_x_recv.at[i], other
        )

    def far_add(i):
        far_load(i).wait()
        far_core(i).wait_recv()
        lanes = pl.ds(0, far_core_in[i].shape[-1])
        ref = far_core_in[i]
        for owner in (1, 0):

            def one(at, carry):
                to, side = at // 2, lax.rem(at, 2)
                ref[owner, to, side] = half(
                    wide(ref[owner, to, side]) + wide(far_held[owner, to, side, :, lanes])
                )
                return carry

            lax.fori_loop(0, 2 * depth, one, 0)
            if owner == 1:
                far_x(i).start()
        if i + 1 < far_total:
            far_load(i + 1).start()

    fetch(0, 0)

    @pl.when(section == 0)
    def _():
        far_load(0).start()
        for i in range(far_total):
            far_core(i).start()

    mods.start()
    biases.start()

    def step(t, carry):
        @pl.when(t < near_total)
        def _():
            make(t)

        @pl.when((t >= 1) & (t <= near_total))
        def _():
            begin(t - 1)

        for i in range(far_total):

            @pl.when((t == i + 1) & (section == 0))
            def _():
                far_add(i)

            @pl.when(t == far_steps[i])
            def _():
                @pl.when(section == 1)
                def _():
                    far_x(i).wait_recv()

                far[i].begin(i)

            for k in range(1, depth):

                @pl.when(t == far_steps[i] + k)
                def _():
                    far[i].move(i, k)

            @pl.when(t == far_steps[i] + depth)
            def _():
                far[i].last(i)

        for k in range(1, depth):
            p = t - 2 - k

            @pl.when((p >= 0) & (p < near_total - 1))
            def _():
                near.move(p, k)

            @pl.when(t == 1 + k)
            def _():
                tail.move(near_total - 1, k)

        p = t - 2 - depth

        @pl.when((p >= 0) & (p < near_total - 1))
        def _():
            near.last(p)

        @pl.when(t == 1 + depth)
        def _():
            tail.last(near_total - 1)

        return carry

    lax.fori_loop(0, near_total + 1 + depth, step, 0)
    for t in (near_total - 2, near_total - 1):
        core_copy(order[t], t % 2).wait_send()

    @pl.when(section == 0)
    def _():
        for i in range(far_total):
            far_core(i).wait_send()
            far_x(i).wait_send()

    for i in range(far_total):
        far[i].finish(i)

    def near_finish(p, carry):
        near.finish(p)
        return carry

    lax.fori_loop(0, near_total - 1, near_finish, 0)
    tail.finish(near_total - 1)
    mods.finish()
    biases.finish()


def reduce_grads(count, ready, pairs, plan, far, far_first, far_steps, mods, biases):
    depth = count // 4
    pieces, rows, width = ready.shape[3:]
    near_total = pieces + len(plan)
    tokens = pairs[0][0].shape[0]
    far_shapes = [a.shape[4:] for a in far]
    far_rows, far_wide = far_shapes[0][0], max(s[1] for s in far_shapes)
    kind = jnp.bfloat16
    anywhere, vmem = pl.BlockSpec(memory_space=pl.ANY), pl.BlockSpec(memory_space=pltpu.VMEM)
    n_far = len(far)
    lefts, rights = [a for a, _ in pairs], [b for _, b in pairs]

    def slots(first, shape):
        y_shape = shape if first else (depth,) + shape
        z_shape = (depth + 1, 2) + shape if first else (depth + 1,) + shape
        return y_shape, z_shape

    far_slots = [slots(f, s) for f, s in zip(far_first, far_shapes)]
    results = pl.pallas_call(
        functools.partial(reduce_kernel, count, pieces, len(pairs), plan, far_first, far_steps),
        out_shape=[jax.ShapeDtypeStruct((near_total, rows, width), kind)]
        + [jax.ShapeDtypeStruct(s, kind) for s in far_shapes]
        + [
            jax.ShapeDtypeStruct((count,) + mods.shape, mods.dtype),
            jax.ShapeDtypeStruct(biases.shape, biases.dtype),
        ],
        in_specs=[anywhere] * (1 + 2 * len(pairs) + n_far + 2),
        out_specs=[vmem] * (1 + n_far) + [anywhere] * 2,
        scratch_shapes=[
            pltpu.VMEM((2, tokens, width), kind),
            pltpu.VMEM((2, tokens, width), kind),
            pltpu.VMEM((2, depth, 2, 2, rows, width), kind),
            pltpu.VMEM((near_total, depth, 2, rows, width), kind),
            pltpu.VMEM((near_total - 1, depth, rows, width), kind),
            pltpu.VMEM((near_total - 1, depth + 1, rows, width), kind),
            pltpu.VMEM((rows, width), kind),
            pltpu.VMEM((depth + 1, 2, rows, width), kind),
            pltpu.VMEM((2, depth, 2, far_rows, far_wide), kind),
        ]
        + [pltpu.VMEM((2, depth, 2) + s, kind) for s in far_shapes]
        + [pltpu.VMEM(s[0], kind) for s in far_slots]
        + [pltpu.VMEM(s[1], kind) for s in far_slots]
        + [
            DMA((2,)),
            DMA((2,)),
            DMA,
            DMA((near_total,)),
            DMA((near_total,)),
            DMA((near_total,)),
            DMA((near_total,)),
            DMA((near_total, depth)),
            DMA((near_total, depth + 1)),
            DMA,
            DMA((n_far,)),
            DMA((n_far,)),
            DMA((n_far,)),
            DMA((n_far,)),
            DMA((n_far,)),
            DMA((n_far,)),
            DMA((n_far, depth)),
            DMA((n_far, depth + 1)),
            DMA((count,)),
            DMA((count,)),
            DMA,
            DMA((count,)),
            DMA((count,)),
            DMA,
        ],
        compiler_params=pltpu.CompilerParams(
            collective_id=2, has_side_effects=True, vmem_limit_bytes=63 * 2**20
        ),
        name="reduce_grads",
    )(ready, *lefts, *rights, *far, mods, biases)
    return results[0], results[1 : 1 + n_far], results[1 + n_far], results[2 + n_far]


def padded(values, rows):
    flat = values.reshape(values.shape[0], -1)
    room = rows * LANES - flat.shape[1]
    return jnp.pad(flat, ((0, 0), (0, room))).reshape(values.shape[0], rows, LANES)


def rows_for(amount, unit):
    rows = -(-amount // LANES)
    return -(-rows // unit) * unit


def split_at(flat, sizes):
    pieces, start = [], 0
    for size in sizes:
        pieces.append(flat[..., start : start + size])
        start += size
    return pieces


def body(
    tokens,
    time_bins,
    labels,
    dino_feats,
    cotangent,
    time_table,
    class_table,
    ada_weight,
    ada_bias,
    qkv_weight,
    qkv_bias,
    out_weight,
    out_bias,
    mlp_in_weight,
    mlp_in_bias,
    mlp_out_weight,
    mlp_out_bias,
    align_weight_one,
    align_bias_one,
    align_weight_two,
    align_bias_two,
    align_weight_three,
    align_bias_three,
):
    count = lax.axis_size("dp")
    first_section = lax.axis_index("section") == 0
    index = lax.axis_index("dp")
    images, _, image_rows, model_width = tokens.shape
    rows_all = images * image_rows
    shard = out_weight.shape[1]
    kernels = count % 4 == 0 and shard % 8 == 0

    indices = jnp.concatenate([time_bins, labels], 1).reshape(1, 2 * images)
    if kernels:
        indices_all = share_small(count, jnp.pad(indices, ((0, 7), (0, LANES - 2 * images))))
        indices_all = indices_all[:, 0, : 2 * images]
    else:
        indices_all = lax.all_gather(indices[0], "dp")
    pairs = indices_all.reshape(count * images, 2)
    time_hot = pairs[:, :1] == jnp.arange(time_table.shape[0], dtype=jnp.int32)[None]
    class_hot = pairs[:, 1:] == jnp.arange(class_table.shape[0], dtype=jnp.int32)[None]
    cond = matmul(half(time_hot), half(time_table)) + matmul(half(class_hot), half(class_table))
    cond_act = half(jax.nn.silu(cond))
    ada_half = half(ada_weight[0])
    mod_parts = half(matmul(cond_act, ada_half)).reshape(count, -1)
    mod_wide = ada_half.shape[1]
    mod_rows = rows_for(images * mod_wide, 16)

    block_biases = (qkv_bias, out_bias, mlp_in_bias, mlp_out_bias, ada_bias)
    align_biases = (align_bias_one, align_bias_two, align_bias_three)
    bias_flat = jnp.concatenate([b.reshape(-1) for b in block_biases + align_biases])
    block_sizes = [b.size for b in block_biases]
    align_sizes = [b.size for b in align_biases]
    bias_rows = rows_for(bias_flat.size, 16)
    own = [half(w[0]) for w in (qkv_weight, out_weight, mlp_in_weight, mlp_out_weight)]
    both = [half(w) for w in (align_weight_one, align_weight_two, align_weight_three)]
    bias_pack = padded(half(bias_flat)[None], bias_rows)[0]
    if kernels:
        fold = both[0].shape[0] * both[0].shape[1] // model_width
        first_shape = both[0].shape
        if fold % 8 == 0:
            both[0] = both[0].reshape(fold, model_width)
        parts, gathered = gather_weights(
            count, padded(mod_parts, mod_rows), own, [bias_pack] + both, (1, 6), (4, 6, 5, 7, 0, 1, 2, 3)
        )
        modulation = jnp.sum(wide(parts), 0).reshape(-1)[: images * mod_wide]
        biases_full = gathered[len(own)].reshape(2, count, -1)
        align_full = [g.reshape((2 * count,) + g.shape[2:]) for g in gathered[len(own) + 1 :]]
        align_full[0] = align_full[0].reshape((2 * count,) + first_shape)
    else:
        modulation = lax.psum_scatter(wide(mod_parts), "dp", scatter_dimension=0, tiled=True)
        gathered = [lax.all_gather(w, "dp") for w in own]
        align_full = [lax.all_gather(w, ("section", "dp")) for w in both]
        biases_full = lax.all_gather(bias_pack.reshape(-1), ("section", "dp"))
        biases_full = biases_full.reshape(2, count, -1)
    own_biases = jnp.where(first_section, biases_full[0], biases_full[1])
    block_full = [
        wide(b).reshape(-1)
        for b in split_at(own_biases[:, : sum(block_sizes)], block_sizes)
    ]
    align_bias_full = [
        wide(b).reshape(-1)
        for b in split_at(
            biases_full[:, :, sum(block_sizes) : sum(block_sizes + align_sizes)], align_sizes
        )
    ]
    modulation = modulation.reshape(images, mod_wide) + block_full[4]
    weights = [g.reshape(-1, g.shape[-1]) for g in gathered[:4]]
    qkv_full_bias = jnp.concatenate(
        [block_full[0][:model_width], jnp.zeros((model_width,), jnp.float32), block_full[0][model_width:]]
    )
    layer = (
        weights[0], qkv_full_bias, weights[1], block_full[1],
        weights[2], block_full[2], weights[3], block_full[3],
    )
    align_weights = [g.reshape(-1, g.shape[-1]) for g in align_full]
    aligner = (
        align_weights[0], align_bias_full[0], align_weights[1], align_bias_full[1],
        align_weights[2], align_bias_full[2],
    )

    modulation = modulation.reshape(images, 6, model_width)
    start_rows = tokens.reshape(rows_all, model_width)
    hidden, *kept_first = block_forward(start_rows, modulation, layer)
    to_second = [(0, 1)]
    to_first = [(1, 0)]
    received = lax.ppermute(hidden, "section", to_second)
    target = dino_feats.reshape(rows_all, -1)
    grad_final = cotangent.reshape(rows_all, model_width)
    widths = [w.shape[1] for w in align_weights]

    def run_align(values):
        grad_hidden, acts, sums = project_align(hidden, target, aligner, loss_weight)
        return hidden, tuple(kept_first), grad_hidden, acts, tuple(sums)

    def run_second(values):
        final, *kept = block_forward(values, modulation, layer)
        empty = tuple(
            jnp.zeros((rows_all, k), jnp.bfloat16) for k in (widths[0], widths[1], *widths)
        )
        sums = tuple(jnp.zeros((1, k), jnp.float32) for k in widths)
        return final, tuple(kept), jnp.zeros_like(values), empty, sums

    outputs, kept, grad_align, align_acts, align_bias_grads = lax.cond(
        first_section, run_align, run_second, received
    )
    grad_align = lax.ppermute(grad_align, "section", to_second)

    def grad_shapes(kind):
        shapes = [(rows_all, 3 * model_width), (rows_all, model_width), kept[8].shape, (rows_all, model_width)]
        return tuple(jnp.zeros(s, kind) for s in shapes)

    def align_weight_grads(values):
        pairs = zip((hidden, align_acts[0], align_acts[1]), align_acts[2:])
        return (
            jnp.zeros((rows_all, model_width), jnp.float32),
            grad_shapes(jnp.bfloat16),
            jnp.zeros((images, 6, model_width), jnp.bfloat16),
            tuple(jnp.zeros((1, g.shape[1]), jnp.float32) for g in grad_shapes(jnp.bfloat16)),
            tuple(half(transposed(a, g)) for a, g in pairs),
        )

    def back_second(values):
        grad_inputs, grads, grad_mod, sums = block_backward(values, modulation, kept, grad_final, layer)
        empty = tuple(jnp.zeros(w.shape, jnp.bfloat16) for w in align_weights)
        return grad_inputs, grads, grad_mod, sums, empty

    grad_part, grads_second, mod_second, sums_second, align_grads = lax.cond(
        first_section, align_weight_grads, back_second, received
    )
    grad_hidden = half(grad_part + wide(grad_align))
    grad_received = lax.ppermute(grad_hidden, "section", to_first)

    def back_first(values):
        grad_inputs, grads, grad_mod, sums = block_backward(start_rows, modulation, kept, values, layer)
        return half(grad_inputs), grads, grad_mod, sums

    def keep_second(values):
        return grad_hidden, grads_second, mod_second, sums_second

    in_grads, grads, grad_mod, sums = lax.cond(first_section, back_first, keep_second, grad_received)
    attn_input, mixed, mlp_input, mlp_act = kept[0], kept[3], kept[6], kept[8]
    grad_qkv, grad_attn, grad_pre, grad_branch = grads
    sums = [g[0] for g in sums]
    sums[0] = jnp.concatenate([sums[0][:model_width], sums[0][2 * model_width :]])
    align_sums = [jnp.moveaxis(g.reshape(2, count, -1), 0, 1).reshape(count, -1) for g in align_bias_grads]
    bias_flat = jnp.concatenate([g.reshape(count, -1) for g in sums] + align_sums, 1)
    grad_down = half(transposed(mlp_act, grad_branch))
    if kernels:
        tall = grad_down.shape[0] // (count * shard)
        n_qkv, n_in = 3, weights[2].shape[1] // model_width
        ready = grad_down.reshape(count // 4, 2, 2, tall, shard, model_width)
        pairs = ((mlp_input, grad_pre), (attn_input, grad_qkv), (mixed, grad_attn))
        plan = [(0, 0, j) for j in range(n_in)] + [(1, 0, j) for j in range(n_qkv)] + [(2, 0, 0)]
        far = [g.reshape(2, count // 4, 2, 2, *w.shape) for g, w in zip(align_grads, both)]
        far = [far[2], far[0], far[1]]
        bias_grad_rows = rows_for(bias_flat.shape[1], 8)
        near_sum, far_sum, mods, bias_parts = reduce_grads(
            count, ready, pairs, plan, far, (False, False, True), (3, 5, 8),
            padded(grad_mod.reshape(1, -1), mod_rows)[0], padded(bias_flat, bias_grad_rows),
        )
        grad_mods = mods.reshape(count, -1)[:, : images * mod_wide]
        bias_sum = jnp.sum(bias_parts, 0).reshape(-1)
        grad_down_weight = wide(near_sum[:tall]).reshape(-1, model_width)
        grad_in_weight = wide(jnp.concatenate([near_sum[tall + j] for j in range(n_in)], 1))
        grad_qkv_weight = wide(jnp.concatenate([near_sum[tall + n_in + j] for j in range(n_qkv)], 1))
        grad_out_weight = wide(near_sum[tall + n_in + n_qkv])
        align_out = [wide(far_sum[1]).reshape(first_shape), wide(far_sum[2]), wide(far_sum[0])]
    else:
        grad_mods = lax.all_gather(grad_mod.reshape(-1), "dp")
        bias_sum = lax.psum_scatter(bias_flat, "dp", scatter_dimension=0, tiled=True).reshape(-1)
        weight_grads = (
            transposed(attn_input, grad_qkv),
            transposed(mixed, grad_attn),
            transposed(mlp_input, grad_pre),
            wide(grad_down),
        )
        reduced = [
            lax.psum_scatter(g, "dp", scatter_dimension=0, tiled=True) for g in weight_grads
        ]
        grad_qkv_weight, grad_out_weight, grad_in_weight, grad_down_weight = reduced
        align_out = [
            lax.psum_scatter(wide(g), ("section", "dp"), scatter_dimension=0, tiled=True)
            for g in align_grads
        ]

    grad_mods = grad_mods.reshape(count * images, mod_wide)
    grad_ada = transposed(cond_act, grad_mods)
    mod_sums = jnp.sum(wide(grad_mods), 0)
    ada_share = mod_wide // count
    grad_ada_bias = lax.dynamic_slice(mod_sums, (index * ada_share,), (ada_share,))
    cond_part = times_transpose(grad_mods, ada_half)
    block_sum = sum(block_sizes[:4])
    grad_biases = split_at(bias_sum[:block_sum], block_sizes[:4])
    align_share = split_at(bias_sum[block_sum : block_sum + 2 * sum(align_sizes)], [2 * a for a in align_sizes])
    align_share = jnp.concatenate([a.reshape(2, -1) for a in align_share], 1)
    packet = jnp.concatenate([cond_part.reshape(-1), align_share.reshape(-1)])
    packet = packet + lax.ppermute(packet, "section", [(0, 1), (1, 0)])
    cond_grad = packet[: cond_part.size].reshape(cond_part.shape)
    align_share = packet[cond_part.size :].reshape(2, -1)
    align_share = jnp.where(first_section, align_share[0], align_share[1])
    align_bias_out = split_at(align_share, align_sizes)
    cond_grad = local_grad(jax.nn.silu, cond, cond_grad)

    def table_grad(hot):
        return lax.dot_general(
            wide(hot),
            cond_grad,
            (((0,), (0,)), ((), ())),
            precision=lax.Precision.HIGHEST,
            preferred_element_type=jnp.float32,
        )

    whole_rows = (1, images, 1, image_rows, model_width)
    return (
        outputs.reshape(whole_rows),
        in_grads.reshape(whole_rows),
        table_grad(time_hot),
        table_grad(class_hot),
        grad_ada[None],
        grad_ada_bias[None],
        grad_qkv_weight[None],
        grad_biases[0][None],
        grad_out_weight[None],
        grad_biases[1][None],
        grad_in_weight[None],
        grad_biases[2][None],
        grad_down_weight[None],
        grad_biases[3][None],
        align_out[0],
        align_bias_out[0],
        align_out[1],
        align_bias_out[1],
        align_out[2],
        align_bias_out[2],
    )


def solution(mesh):
    placed = (
        P(None, "dp", None, None),
        P(None, "dp"),
        P(None, "dp"),
        P(None, "dp", None, None),
        P(None, "dp", None, None),
        P(None, "dp"),
        P(None, "dp"),
        P("section", "dp", None),
        P("section", "dp"),
        P("section", "dp", None),
        P("section", "dp"),
        P("section", "dp", None),
        P("section", "dp"),
        P("section", "dp", None),
        P("section", "dp"),
        P("section", "dp", None),
        P("section", "dp"),
        P(("section", "dp"), None),
        P(("section", "dp")),
        P(("section", "dp"), None),
        P(("section", "dp")),
        P(("section", "dp"), None),
        P(("section", "dp")),
    )
    return jax.shard_map(
        body,
        mesh=mesh,
        in_specs=placed,
        out_specs=(
            P("section", None, "dp", None, None),
            P("section", None, "dp", None, None),
        )
        + placed[5:],
        check_vma=False,
    )
```

```python
import functools

import jax
import jax.numpy as jnp
from jax import lax
from jax.experimental import pallas as pl
from jax.experimental.pallas import tpu as pltpu
from jax.sharding import PartitionSpec as P

HEADS = 16
HD = 72
LANES = 128
MESH = pl.DeviceIdType.MESH
DMA = pltpu.SemaphoreType.DMA

epsilon = 1e-06
loss_weight = 0.5


def matmul(left, right):
    return jnp.dot(left, right, preferred_element_type=jnp.float32)


def transposed(left, right):
    return lax.dot_general(
        left, right, (((0,), (0,)), ((), ())), preferred_element_type=jnp.float32
    )


def times_transpose(grad_rows, weight):
    return lax.dot_general(
        grad_rows, weight, (((1,), (1,)), ((), ())), preferred_element_type=jnp.float32
    )


def local_grad(function, point, grad_value):
    return jax.vjp(function, point)[1](grad_value)[0]


def half(values):
    return values.astype(jnp.bfloat16)


def wide(values):
    return values.astype(jnp.float32)


GELU_SLOPE = 0.7978845608028654
GELU_CUBE = 0.044715


def dot_plain(left, right):
    return lax.dot_general(left, right, (((1,), (0,)), ((), ())), preferred_element_type=jnp.float32)


def dot_across(left, right):
    return lax.dot_general(left, right, (((1,), (1,)), ((), ())), preferred_element_type=jnp.float32)


def dot_down(left, right):
    return lax.dot_general(left, right, (((0,), (0,)), ((), ())), preferred_element_type=jnp.float32)


class Loads:
    def __init__(self, sems):
        self.sems, self.copies = sems, []

    def add(self, source, target, axis, tiles):
        size = source.shape[axis] // tiles
        first = len(self.copies)
        for j in range(tiles):
            place = (pl.ds(j * size, size),) if axis == 0 else (slice(None), pl.ds(j * size, size))
            self.copies.append(
                pltpu.make_async_copy(source.at[place], target.at[place], self.sems.at[first + j])
            )
        return list(range(first, first + tiles))

    def start(self):
        for copy in self.copies:
            copy.start()

    def wait(self, places):
        for place in places:
            self.copies[place].wait()


def head_window(head):
    low = head * HD
    start = low // LANES * LANES
    stop = -(-(low + HD) // LANES) * LANES
    return low, start, stop - start


def head_mask(head, rows):
    low, start, size = head_window(head)
    lane = lax.broadcasted_iota(jnp.int32, (rows, size), 1) + start
    return (lane >= low) & (lane < low + HD)


def masked(mask, values):
    return jnp.where(mask, values, jnp.zeros_like(values))


def row_norm(values):
    centred = values - jnp.mean(values, -1, keepdims=True)
    inverse = lax.rsqrt(jnp.mean(centred * centred, -1, keepdims=True) + epsilon)
    return centred * inverse, inverse


def row_norm_back(grad, normed, inverse):
    return inverse * (
        grad
        - jnp.mean(grad, -1, keepdims=True)
        - normed * jnp.mean(grad * normed, -1, keepdims=True)
    )


def column_tiles(total, tile):
    return [(at, min(tile, total - at)) for at in range(0, total, tile)]


class Forward:
    def __init__(self, images, x_ref, mod_ref, biases, kept, blend, weights, store):
        self.images, self.x_ref, self.mod_ref = images, x_ref, mod_ref
        self.qkv_bias, self.out_bias, self.in_bias, self.down_bias = biases
        (
            self.attn_in, self.qkv, self.probs, self.mixed, self.attn_branch, self.after,
            self.mlp_in, self.slope, self.act, self.mlp_branch, self.output,
        ) = kept
        self.blend, self.weights, self.store = blend, weights, store
        self.rows, self.width = x_ref.shape
        self.each = self.rows // images

    def at(self, image):
        return pl.ds(pl.multiple_of(image * self.each, self.each), self.each)

    def mod(self, image, k):
        return self.mod_ref[image, pl.ds(k, 1), :]

    def per_image(self, action):
        def one(image, carry):
            action(image, self.at(image))
            return carry

        lax.fori_loop(0, self.images, one, 0)

    def enter(self):
        def one(image, at):
            normed, _ = row_norm(wide(self.x_ref[at, :]))
            self.attn_in[at, :] = half(normed * (1.0 + self.mod(image, 1)) + self.mod(image, 0))

        self.per_image(one)
        self.store(0)

    def project(self, part):
        cols = slice(part * self.width, (part + 1) * self.width)
        product = dot_plain(self.attn_in[...], self.weights[0](cols))
        self.qkv[:, cols] = half(product + self.qkv_bias[:, cols])
        if part == 2:
            self.store(1)

    def attend(self, image):
        at, each, width = self.at(image), self.each, self.width
        for head in range(HEADS):
            low, start, size = head_window(head)
            mask = head_mask(head, each)
            cols = [slice(part * width + start, part * width + start + size) for part in range(3)]
            queries = masked(mask, self.qkv[at, cols[0]])
            scores = dot_across(queries, self.qkv[at, cols[1]]) * HD ** (-0.5)
            powers = jnp.exp(scores - jnp.max(scores, -1, keepdims=True))
            soft = half(powers / jnp.sum(powers, -1, keepdims=True))
            self.probs[image, head] = soft
            fresh = dot_plain(soft, self.qkv[at, cols[2]])
            window = slice(start, start + size)
            self.blend[:, window] = jnp.where(mask, fresh, self.blend[:, window])
        self.mixed[at, :] = half(self.blend[...])

    def attend_all(self):
        def one(image, carry):
            self.attend(image)
            return carry

        lax.fori_loop(0, self.images, one, 0)
        self.attended()

    def attended(self):
        self.store(2)
        self.store(3)

    def middle(self):
        branch = dot_plain(self.mixed[...], self.weights[1](slice(0, self.width))) + self.out_bias[...]
        self.attn_branch[...] = half(branch)
        self.store(4)

        def one(image, at):
            joined = wide(self.x_ref[at, :]) + self.mod(image, 2) * wide(self.attn_branch[at, :])
            self.after[at, :] = joined
            normed, _ = row_norm(joined)
            self.mlp_in[at, :] = half(normed * (1.0 + self.mod(image, 4)) + self.mod(image, 3))

        self.per_image(one)
        self.store(5)
        self.store(6)

    def feed(self, first, last, tile=512):
        def one(j, carry):
            cols = pl.ds(pl.multiple_of(j * tile, tile), tile)
            pre = dot_plain(self.mlp_in[...], self.weights[2](cols)) + self.in_bias[:, cols]
            square = pre * pre
            bend = jnp.tanh(GELU_SLOPE * pre * (1.0 + GELU_CUBE * square))
            self.act[:, cols] = half(0.5 * pre * (1.0 + bend))
            self.slope[:, cols] = half(
                0.5 * (1.0 + bend)
                + 0.5 * pre * (1.0 - bend * bend) * (GELU_SLOPE + 3.0 * GELU_SLOPE * GELU_CUBE * square)
            )
            return carry

        lax.fori_loop(first, last, one, 0)
        if last * tile == self.act.shape[1]:
            self.store(7)
            self.store(8)

    def leave(self):
        branch = dot_plain(self.act[...], self.weights[3](slice(0, self.width))) + self.down_bias[...]
        self.mlp_branch[...] = half(branch)
        self.store(9)

        def one(image, at):
            self.output[at, :] = half(
                self.after[at, :] + self.mod(image, 5) * wide(self.mlp_branch[at, :])
            )

        self.per_image(one)
        self.store(10)


def kept_shapes(rows, width, images, hidden_width):
    each = rows // images
    thin = jax.ShapeDtypeStruct((rows, width), jnp.bfloat16)
    fat = jax.ShapeDtypeStruct((rows, hidden_width), jnp.bfloat16)
    return [
        thin, jax.ShapeDtypeStruct((rows, 3 * width), jnp.bfloat16),
        jax.ShapeDtypeStruct((images, HEADS, each, each), jnp.bfloat16), thin, thin,
        jax.ShapeDtypeStruct((rows, width), jnp.float32), thin, fat, fat, thin, thin,
    ]


def stored(refs, places, sems):
    copies = [pltpu.make_async_copy(a, b, sems.at[k]) for k, (a, b) in enumerate(zip(refs, places))]

    def wait():
        for copy in copies:
            copy.wait()

    return lambda k: copies[k].start(), wait


def flat(ref):
    def columns(cols):
        values = ref[:, :, cols]
        return values.reshape(values.shape[0] * values.shape[1], values.shape[2])

    return columns


def forward_kernel(images, own_section, *refs):
    x_hbm, mod_ref, bias = refs[:3]
    weights_hbm = refs[3:7]
    kept_out = refs[17:28]
    weights = refs[28:32]
    x_ref, *kept = refs[32:44]
    blend, load_sem, kept_sem = refs[44:]

    @pl.when(lax.axis_index("section") == own_section)
    def _():
        loads = Loads(load_sem)
        x_at = loads.add(x_hbm, x_ref, 0, 1)
        qkv_at = loads.add(weights_hbm[0], weights[0], 1, 3)
        out_at = loads.add(weights_hbm[1], weights[1], 0, 1)
        in_at = loads.add(weights_hbm[2], weights[2], 1, 3)
        down_at = loads.add(weights_hbm[3], weights[3], 0, 3)
        loads.start()
        store, wait_stored = stored(kept, kept_out, kept_sem)
        columns = [functools.partial(lambda ref, cols: ref[:, cols], ref) for ref in weights]
        forward = Forward(images, x_ref, mod_ref, bias_parts(bias), kept, blend, columns, store)
        loads.wait(x_at)
        forward.enter()
        for part in range(3):
            loads.wait([qkv_at[part]])
            forward.project(part)
        forward.attend_all()
        loads.wait(out_at)
        forward.middle()
        feeds = kept[8].shape[1] // 512
        for third in range(3):
            loads.wait([in_at[third]])
            forward.feed(feeds * third // 3, feeds * (third + 1) // 3)
        loads.wait(down_at)
        forward.leave()
        wait_stored()


def bias_parts(bias):
    width = bias.shape[1] // 15
    places = ((0, 3), (3, 1), (4, 4), (8, 1))
    return [bias.at[:, start * width : (start + size) * width] for start, size in places]


def block_forward(own_section, inputs, modulation, bias, weights, previous):
    rows, width = inputs.shape
    images = modulation.shape[0]
    each = rows // images
    kept = kept_shapes(rows, width, images, weights[2].shape[1])
    vmem, anywhere = pl.BlockSpec(memory_space=pltpu.VMEM), pl.BlockSpec(memory_space=pl.ANY)
    return pl.pallas_call(
        functools.partial(forward_kernel, images, own_section),
        out_shape=kept,
        in_specs=[anywhere, vmem, vmem] + [anywhere] * 14,
        out_specs=[anywhere] * 11,
        scratch_shapes=[pltpu.VMEM(w.shape, w.dtype) for w in weights]
        + [pltpu.VMEM(inputs.shape, inputs.dtype)]
        + [pltpu.VMEM(s.shape, s.dtype) for s in kept]
        + [pltpu.VMEM((each, width), jnp.float32), DMA((11,)), DMA((11,))],
        input_output_aliases={7 + k: k for k in range(10)},
        compiler_params=pltpu.CompilerParams(vmem_limit_bytes=63 * 2**20),
        name="block_forward",
    )(inputs, modulation, bias, *weights, *previous)


def backward_kernel(images, own_section, fresh, *refs):
    refs = list(refs)

    def take(amount):
        taken = refs[:amount]
        del refs[:amount]
        return taken

    (mod_ref,) = take(1)
    sources = take(8)
    weights_hbm = take(4)
    if not fresh:
        take(10)
    out_hbm = take(10)
    held = take(8)
    weights = take(4)
    outs = take(9)
    half_grad, wide_grad, blend, load_sem, out_sem = refs
    x_ref, dout, mlp_branch, slope, after, attn_branch, probs, qkv_ref = held
    qkv_w, out_w, in_w, down_w = weights
    dx_half, d_qkv, d_attn, d_branch, d_mod, qkv_sum, attn_sum, pre_sum, branch_sum = outs
    d_pre = slope
    out_refs = [dx_half, d_qkv, d_attn, d_pre, d_branch, d_mod, qkv_sum, attn_sum, pre_sum, branch_sum]
    rows, width = x_ref.shape
    each = rows // images
    hidden_width = in_w.shape[1]
    tile = 512
    section = lax.axis_index("section")
    dx_ref = wide_grad.at[1]
    grad_ref = wide_grad.at[0]

    feeds = hidden_width // tile

    @pl.when(section == own_section)
    def _():
        loads = Loads(load_sem)
        places = {}
        for name in (1, 2, "down", 3, "in", 4, 5, "out", 6, 7, "qkv", 0):
            if name == "down":
                places[name] = loads.add(weights_hbm[3], down_w, 0, 3)
            elif name == "in":
                places[name] = loads.add(weights_hbm[2], in_w, 0, 3)
            elif name == "out":
                places[name] = loads.add(weights_hbm[1], out_w, 0, 1)
            elif name == "qkv":
                places[name] = loads.add(weights_hbm[0], qkv_w, 0, 3)
            else:
                places[name] = loads.add(sources[name], held[name], 0, 1)
        loads.start()
        store, wait_stored = stored(out_refs, out_hbm, out_sem)

        def per_image(action):
            def one(image, carry):
                action(image, pl.ds(pl.multiple_of(image * each, each), each))
                return carry

            lax.fori_loop(0, images, one, 0)

        def mod(image, k):
            return mod_ref[image, pl.ds(k, 1), :]

        def sums(image, k, values):
            d_mod[image, pl.ds(k, 1), :] = jnp.sum(values, 0, keepdims=True)

        def enter(image, at):
            grad = wide(dout[at, :])
            d_branch[at, :] = half(grad * mod(image, 5))
            sums(image, 5, grad * wide(mlp_branch[at, :]))

        loads.wait(places[1] + places[2])
        per_image(enter)
        branch_sum[...] = jnp.sum(wide(d_branch[...]), 0, keepdims=True)
        store(4)
        store(9)
        loads.wait(places[3])

        def feed(j, carry):
            cols = pl.ds(pl.multiple_of(j * tile, tile), tile)
            grad = half(dot_across(d_branch[...], down_w[cols, :]) * wide(slope[:, cols]))
            d_pre[:, cols] = grad
            pre_sum[:, cols] = jnp.sum(wide(grad), 0, keepdims=True)
            return carry

        for third in range(3):
            loads.wait([places["down"][third]])
            lax.fori_loop(feeds * third // 3, feeds * (third + 1) // 3, feed, 0)
        store(3)
        store(8)
        loads.wait(places["in"])
        for start, size in column_tiles(width, 512):
            grad_ref[:, start : start + size] = dot_across(d_pre[...], in_w[start : start + size, :])

        def middle(image, at):
            grad_in = grad_ref[at, :]
            normed, inverse = row_norm(after[at, :])
            sums(image, 4, grad_in * normed)
            sums(image, 3, grad_in)
            grad = wide(dout[at, :]) + row_norm_back(grad_in * (1.0 + mod(image, 4)), normed, inverse)
            dx_ref[at, :] = grad
            d_attn[at, :] = half(grad * mod(image, 2))
            sums(image, 2, grad * wide(attn_branch[at, :]))

        loads.wait(places[4] + places[5])
        per_image(middle)
        attn_sum[...] = jnp.sum(wide(d_attn[...]), 0, keepdims=True)
        store(2)
        store(7)
        loads.wait(places["out"])
        half_grad[...] = half(dot_across(d_attn[...], out_w[...]))
        loads.wait(places[6] + places[7])

        def attend(image, at):
            for head in range(HEADS):
                low, start, size = head_window(head)
                mask = head_mask(head, each)
                window = slice(start, start + size)
                cols = [slice(part * width + start, part * width + start + size) for part in range(3)]
                grad = masked(mask, half_grad[at, window])
                soft = probs[image, head]
                grad_soft = dot_across(grad, qkv_ref[at, cols[2]])
                weighed = wide(soft) * grad_soft
                grad_scores = half(weighed - wide(soft) * jnp.sum(weighed, -1, keepdims=True))
                made = (
                    dot_plain(grad_scores, qkv_ref[at, cols[1]]) * HD ** (-0.5),
                    dot_down(grad_scores, qkv_ref[at, cols[0]]) * HD ** (-0.5),
                    dot_down(soft, grad),
                )
                for part in range(3):
                    blend[:, cols[part]] = jnp.where(mask, made[part], blend[:, cols[part]])
            d_qkv[at, :] = half(blend[...])

        per_image(attend)
        store(1)
        loads.wait(places["qkv"])
        for start, size in column_tiles(width, 512):
            grad_ref[:, start : start + size] = dot_across(d_qkv[...], qkv_w[start : start + size, :])
        loads.wait(places[0])

        def leave(image, at):
            grad_in = grad_ref[at, :]
            normed, inverse = row_norm(wide(x_ref[at, :]))
            sums(image, 1, grad_in * normed)
            sums(image, 0, grad_in)
            grad = dx_ref[at, :] + row_norm_back(grad_in * (1.0 + mod(image, 1)), normed, inverse)
            dx_half[at, :] = half(grad)

        per_image(leave)
        store(0)
        qkv_sum[...] = jnp.sum(wide(d_qkv[...]), 0, keepdims=True)
        store(5)
        store(6)
        wait_stored()


def block_backward(own_section, modulation, sources, weights, previous=None):
    fresh = previous is None
    rows, width = sources[0].shape
    images = modulation.shape[0]
    each = rows // images
    hidden_width = weights[2].shape[1]
    vmem, anywhere = pl.BlockSpec(memory_space=pltpu.VMEM), pl.BlockSpec(memory_space=pl.ANY)

    def shape(columns, kind=jnp.bfloat16, count=rows):
        return jax.ShapeDtypeStruct((count, columns), kind)

    outs = [
        shape(width), shape(3 * width), shape(width), shape(hidden_width), shape(width),
        jax.ShapeDtypeStruct((images, 8, width), jnp.float32),
        shape(3 * width, jnp.float32, 1), shape(width, jnp.float32, 1),
        shape(hidden_width, jnp.float32, 1), shape(width, jnp.float32, 1),
    ]
    scratch = [pltpu.VMEM(a.shape, a.dtype) for a in list(sources) + list(weights)]
    scratch += [pltpu.VMEM(s.shape, s.dtype) for k, s in enumerate(outs) if k != 3]
    scratch += [
        pltpu.VMEM((rows, width), jnp.bfloat16), pltpu.VMEM((2, rows, width), jnp.float32),
        pltpu.VMEM((each, 3 * width), jnp.float32), DMA((18,)), DMA((10,)),
    ]
    extra_in, aliases = [], {}
    if not fresh:
        extra_in = list(previous)
        aliases = {13 + k: k for k in range(10)}
    return pl.pallas_call(
        functools.partial(backward_kernel, images, own_section, fresh),
        out_shape=outs,
        in_specs=[vmem] + [anywhere] * (12 + len(extra_in)),
        out_specs=[anywhere] * 10,
        scratch_shapes=scratch,
        input_output_aliases=aliases,
        compiler_params=pltpu.CompilerParams(vmem_limit_bytes=63 * 2**20),
        name="block_backward",
    )(modulation, *sources, *weights, *extra_in)


def sigmoid_parts(values):
    gate = 1.0 / (1.0 + jnp.exp(-values))
    return values * gate, gate * (1.0 + values * (1.0 - gate))


def align_kernel(
    loss,
    x_ref, target, wanted, bias_one, bias_two, bias_three, one_hbm, two_hbm, three_hbm,
    dx_ref, one_sum, two_sum, three_sum, one_grad, two_grad, three_grad,
    one_w, two_w, three_w, padded_x, act_one, act_two, d_one, d_two, d_latent, slope_one, slope_two,
    product, sems, product_sem,
):
    tile = 512

    def layer(source, weight, bias, act, slope):
        def one(j, carry):
            cols = pl.ds(pl.multiple_of(j * tile, tile), tile)
            pre = dot_plain(source[...], weight[:, cols]) + bias[:, cols]
            value, bend = sigmoid_parts(pre)
            act[:, cols] = half(value)
            slope[:, cols] = half(bend)
            return carry

        lax.fori_loop(0, weight.shape[1] // tile, one, 0)

    def back(grad, weight, slope, target_ref, sum_ref):
        def one(j, carry):
            cols = pl.ds(pl.multiple_of(j * tile, tile), tile)
            value = half(dot_across(grad[...], weight[cols, :]) * wide(slope[:, cols]))
            target_ref[:, cols] = value
            sum_ref[:, cols] = jnp.sum(wide(value), 0, keepdims=True)
            return carry

        lax.fori_loop(0, weight.shape[0] // tile, one, 0)

    def picks(cols, size):
        row = lax.broadcasted_iota(jnp.int32, (x_ref.shape[1], size), 0)
        return half(jnp.where(row == wanted[:, cols], 1.0, 0.0))

    @pl.when(lax.axis_index("section") == 0)
    def _():
        loads = Loads(sems)
        one_at = loads.add(one_hbm, one_w, 0, 1)
        two_at = loads.add(two_hbm, two_w, 0, 1)
        three_at = loads.add(three_hbm, three_w, 0, 1)
        loads.start()
        padded_width = one_w.shape[0]
        for start, size in column_tiles(padded_width, tile):
            cols = slice(start, start + size)
            padded_x[:, cols] = half(dot_plain(x_ref[...], picks(cols, size)))
        loads.wait(one_at)
        layer(padded_x, one_w, bias_one, act_one, slope_one)
        loads.wait(two_at)
        layer(act_one, two_w, bias_two, act_two, slope_two)
        loads.wait(three_at)
        latent = dot_plain(act_two[...], three_w[...]) + bias_three[...]
        features = wide(target[...])
        root_latent = lax.rsqrt(jnp.sum(latent * latent, -1, keepdims=True) + epsilon)
        root_target = lax.rsqrt(jnp.sum(features * features, -1, keepdims=True) + epsilon)
        crossed = jnp.sum(latent * features, -1, keepdims=True)
        grad = half(
            -loss
            * (
                features * (root_latent * root_target)
                - (crossed * root_target * root_latent * root_latent * root_latent) * latent
            )
        )
        d_latent[...] = grad
        three_sum[...] = jnp.sum(wide(grad), 0, keepdims=True)
        back(d_latent, three_w, slope_two, d_two, two_sum)
        back(d_two, two_w, slope_one, d_one, one_sum)
        total = jnp.zeros(x_ref.shape, jnp.float32)
        for start, size in column_tiles(padded_width, tile):
            cols = slice(start, start + size)
            value = half(dot_across(d_one[...], one_w[start : start + size, :]))
            total = total + dot_across(value, picks(cols, size))
        dx_ref[...] = half(total)

        jobs = []
        for left, right, place in (
            (act_two, d_latent, three_grad), (padded_x, d_one, one_grad), (act_one, d_two, two_grad),
        ):
            for start, size in column_tiles(left.shape[1], tile):
                jobs.append((left, right, place, start, size))
        copies = []
        for k, (left, right, place, start, size) in enumerate(jobs):
            if k >= 2:
                copies[k - 2].wait()
            held = product.at[k % 2, pl.ds(0, size), pl.ds(0, right.shape[1])]
            held[...] = half(dot_down(left[:, start : start + size], right[...]))
            copies.append(
                pltpu.make_async_copy(held, place.at[pl.ds(start, size)], product_sem.at[k % 2])
            )
            copies[k].start()
        copies[-2].wait()
        copies[-1].wait()


def project_align(hidden, target, wanted, aligner, loss):
    weight_one, bias_one, weight_two, bias_two, weight_three, bias_three = aligner
    rows, width = hidden.shape
    first, second, third = weight_one.shape[1], weight_two.shape[1], weight_three.shape[1]
    vmem, anywhere = pl.BlockSpec(memory_space=pltpu.VMEM), pl.BlockSpec(memory_space=pl.ANY)

    def shape(columns, kind=jnp.bfloat16, count=rows):
        return jax.ShapeDtypeStruct((count, columns), kind)

    weights = (weight_one, weight_two, weight_three)
    results = pl.pallas_call(
        functools.partial(align_kernel, loss),
        out_shape=[
            shape(width),
            shape(first, jnp.float32, 1), shape(second, jnp.float32, 1), shape(third, jnp.float32, 1),
        ]
        + [jax.ShapeDtypeStruct(w.shape, jnp.bfloat16) for w in weights],
        in_specs=[vmem] * 6 + [anywhere] * 3,
        out_specs=[vmem] * 4 + [anywhere] * 3,
        scratch_shapes=[pltpu.VMEM(w.shape, w.dtype) for w in weights]
        + [
            pltpu.VMEM((rows, k), jnp.bfloat16)
            for k in (weight_one.shape[0], first, second, first, second, third, first, second)
        ]
        + [pltpu.VMEM((2, 512, max(first, second, third)), jnp.bfloat16), DMA((3,)), DMA((2,))],
        compiler_params=pltpu.CompilerParams(vmem_limit_bytes=62 * 2**20),
        name="project_align",
    )(
        hidden, target, wanted, bias_one[None], bias_two[None], bias_three[None], *weights
    )
    return results[0], results[1:4], results[4:]


def own_place():
    section = lax.axis_index("section")
    index = lax.axis_index("dp")
    return section, index, index // 4, lax.rem(index // 2, 2), lax.rem(index, 2)


def index_of(z, y, core):
    return z * 4 + y * 2 + core


def greet(targets):
    barrier = pltpu.get_barrier_semaphore()
    for target in targets:
        pl.semaphore_signal(barrier, inc=1, device_id=target, device_id_type=MESH)
    pl.semaphore_wait(barrier, len(targets))


def greet_section(count, section, index, extra=()):
    barrier = pltpu.get_barrier_semaphore()

    def one(step, carry):
        target = (section, lax.rem(index + step, count))
        pl.semaphore_signal(barrier, inc=1, device_id=target, device_id_type=MESH)
        return carry

    lax.fori_loop(1, count, one, 0)
    for target in extra:
        pl.semaphore_signal(barrier, inc=1, device_id=target, device_id_type=MESH)
    pl.semaphore_wait(barrier, count - 1 + len(extra))


class Exchange:
    def __init__(self, count, section, index, source, target, send, recv, local, own_only):
        self.count, self.section, self.index = count, section, index
        self.source, self.target = source, target
        self.send, self.recv, self.local, self.own_only = send, recv, local, own_only

    def piece(self, other):
        return self.source if self.own_only else self.source.at[other]

    def message(self, other, slot):
        return pltpu.make_async_remote_copy(
            src_ref=self.piece(other),
            dst_ref=self.target.at[slot],
            send_sem=self.send.at[other],
            recv_sem=self.recv.at[slot],
            device_id=(self.section, other),
            device_id_type=MESH,
        )

    def start(self):
        def one(step, carry):
            self.message(lax.rem(self.index + step, self.count), self.index).start()
            return carry

        lax.fori_loop(1, self.count, one, 0)
        pltpu.make_async_copy(
            self.piece(self.index), self.target.at[self.index], self.local
        ).start()

    def finish(self):
        def one(step, carry):
            other = lax.rem(self.index + step, self.count)
            self.message(other, self.index).wait_send()
            self.message(other, other).wait_recv()
            return carry

        lax.fori_loop(1, self.count, one, 0)
        pltpu.make_async_copy(
            self.piece(self.index), self.target.at[self.index], self.local
        ).wait()


def share_kernel(count, source, target, send, recv, local):
    section, index, z, y, core = own_place()
    me = section * count + index
    everybody = 2 * count

    def device(step):
        other = lax.rem(me + step, everybody)
        return other, (other // count, lax.rem(other, count))

    def message(other, where, slot):
        return remote_copy(
            source, target.at[slot // count, lax.rem(slot, count)], send.at[other], recv.at[slot], where
        )

    barrier = pltpu.get_barrier_semaphore()

    def greet_one(step, carry):
        pl.semaphore_signal(barrier, inc=1, device_id=device(step)[1], device_id_type=MESH)
        return carry

    def start_one(step, carry):
        other, where = device(step)
        message(other, where, me).start()
        return carry

    def finish_one(step, carry):
        other, where = device(step)
        message(other, where, me).wait_send()
        message(other, where, other).wait_recv()
        return carry

    lax.fori_loop(1, everybody, greet_one, 0)
    pl.semaphore_wait(barrier, everybody - 1)
    own = pltpu.make_async_copy(source, target.at[section, index], local)
    own.start()
    lax.fori_loop(1, everybody, start_one, 0)
    lax.fori_loop(1, everybody, finish_one, 0)
    own.wait()


def share_small(count, values):
    return pl.pallas_call(
        functools.partial(share_kernel, count),
        out_shape=jax.ShapeDtypeStruct((2, count) + values.shape, values.dtype),
        in_specs=[pl.BlockSpec(memory_space=pl.ANY)],
        out_specs=pl.BlockSpec(memory_space=pl.ANY),
        scratch_shapes=[DMA((2 * count,)), DMA((2 * count,)), DMA],
        compiler_params=pltpu.CompilerParams(collective_id=0, has_side_effects=True),
        name="share_small",
    )(values)


def gather_kernel(count, images, arrays, items, stride, *refs):
    total = len(items)
    modes = [item[0] >= 4 for item in items]
    first = [item[4] for item in items]
    starts = [item[5] for item in items]
    refs = list(refs)

    def take(amount):
        taken = refs[:amount]
        del refs[:amount]
        return taken

    part, x_ref, bias = take(3)
    src = take(arrays)
    part_out, mod_out = take(2)
    dst = take(arrays)
    kept_out = take(11)
    part_send, part_recv, part_local, local_sem, send_core, send_y, send_x, send_up, send_down, recv = take(10)
    weight_refs = take(4)
    kept = take(11)
    part_in, blend, part_sem, weight_sem, kept_sem, hidden_send, hidden_recv = refs
    depth = count // 4
    section, me, z, y, c = own_place()
    up, down = (section, me + 4), (section, me - 4)
    across, partner = (section, index_of(z, 1 - y, c)), (section, index_of(z, y, 1 - c))
    other = (1 - section, me)
    greet_section(count, section, me, (other,))
    parts = Exchange(count, section, me, part, part_out, part_send, part_recv, part_local, False)
    parts.start()

    def cut(w):
        _, axis, start, size = items[w][:4]
        return (pl.ds(start, size),) if axis == 0 else (slice(None), pl.ds(start, size))

    def slot(w, sec, blk):
        place = (sec, blk) if modes[w] else (blk,)
        return dst[items[w][0]].at[place + cut(w)]

    def source_of(w):
        return src[items[w][0]].at[cut(w)]

    def copy(w, sec, blk, target, sem, src_ref=None):
        here = slot(w, sec, blk)
        return pltpu.make_async_remote_copy(
            src_ref=here if src_ref is None else src_ref,
            dst_ref=here,
            send_sem=sem,
            recv_sem=recv.at[w, sec if modes[w] else 0, blk],
            device_id=target,
            device_id_type=MESH,
        )

    def arrived(w, sec, blk):
        copy(w, sec, blk, partner, send_core.at[w, 0, 0, 0]).wait_recv()

    def pass_on(w, zz, side, go_up, go_down, go_across, source=None):
        blk = index_of(zz, y if side == 0 else 1 - y, c)
        if go_up is not None:

            @pl.when(go_up)
            def _():
                copy(w, section, blk, up, send_up.at[w, side, zz], source).start()

        if go_down is not None:

            @pl.when(go_down)
            def _():
                copy(w, section, blk, down, send_down.at[w, side, zz], source).start()

        if go_across:
            copy(w, section, blk, across, send_y.at[w, zz], source).start()
        if modes[w]:

            @pl.when(section == 1)
            def _():
                copy(w, section, blk, other, send_x.at[w, side, zz], source).start()

        copy(w, section, blk, partner, send_core.at[w, 0, side, zz], source).start()

    def depart(w):
        pass_on(w, z, 0, z < depth - 1, z > 0, True, source_of(w))
        pltpu.make_async_copy(source_of(w), slot(w, section, me), local_sem.at[w]).start()

    def near(w, k):
        if k >= depth:
            return

        @pl.when(z >= k)
        def _():
            arrived(w, section, index_of(z - k, y, c))
            pass_on(w, z - k, 0, z < depth - 1, None, not first[w])

        @pl.when(z + k < depth)
        def _():
            arrived(w, section, index_of(z + k, y, c))
            pass_on(w, z + k, 0, None, z > 0, not first[w])

    def far(w, k):
        @pl.when(z >= k)
        def _():
            arrived(w, section, index_of(z - k, 1 - y, c))
            if first[w]:
                pass_on(w, z - k, 1, z < depth - 1, (z > 0) if k == 0 else None, False)
            else:
                pass_on(w, z - k, 1, None, None, False)

        if k > 0:

            @pl.when(z + k < depth)
            def _():
                arrived(w, section, index_of(z + k, 1 - y, c))
                pass_on(w, z + k, 1, None, (z > 0) if first[w] else None, False)

    def complete(w):
        pltpu.make_async_copy(source_of(w), slot(w, section, me), local_sem.at[w]).wait()
        for side in range(2):

            def one(zz, carry):
                arrived(w, section, index_of(zz, y if side == 0 else 1 - y, 1 - c))
                return carry

            lax.fori_loop(0, depth, one, 0)

    def load(w):
        return pltpu.make_async_copy(dst[w], weight_refs[w], weight_sem.at[w])

    def modulate():
        parts.finish()
        copy_in = pltpu.make_async_copy(part_out, part_in, part_sem)
        copy_in.start()
        copy_in.wait()
        total_mod = wide(part_in[0])
        for device in range(1, count):
            total_mod = total_mod + wide(part_in[device])
        chunks = x_ref.shape[1] // LANES
        for image in range(images):
            for q in range(chunks):
                at = (image * chunks + q) * 6
                cols = slice(q * LANES, (q + 1) * LANES)
                mod_out[image, 0:6, cols] = total_mod[at : at + 6]
            for k in range(6):
                start = (9 + k) * x_ref.shape[1]
                mod_out[image, k : k + 1, :] += bias[:, start : start + x_ref.shape[1]]

    store, wait_stored = stored(kept, kept_out, kept_sem)
    forward = Forward(
        images, x_ref, mod_out, bias_parts(bias), kept, blend,
        [flat(ref) for ref in weight_refs], store,
    )

    def on_first(action):
        @pl.when(section == 0)
        def _():
            action()

    def load_array(a):
        on_first(lambda: load(a).start())

    last_item = [max(w for w in range(total) if items[w][0] == a) for a in range(4)]
    events = []
    for t in range(max(starts) + stride * depth + 1):
        for w in range(total):
            k, rest = divmod(t - starts[w], stride)
            if rest or k < 0 or k > depth:
                continue
            if k == 0:
                events.append((t, functools.partial(depart, w), None))
                continue
            if first[w]:
                events.append((t, functools.partial(far, w, k - 1), None))
                events.append((t, functools.partial(near, w, k), None))
            else:
                events.append((t, functools.partial(near, w, k), None))
                events.append((t, functools.partial(far, w, k - 1), None))
            if k == depth and not modes[w]:
                events.append((t, functools.partial(complete, w), None))
                a = items[w][0]
                if w == last_item[a]:
                    events.append((t, functools.partial(load_array, a), a))
    feeds = kept[8].shape[1] // 512

    def finish_block():
        forward.leave()
        remote_copy(kept[10], kept_out[10], hidden_send, hidden_recv, other).start()

    groups = [
        [functools.partial(forward.project, part) for part in range(3)]
        + [functools.partial(forward.attend, image) for image in range(images)]
        + [forward.attended],
        [forward.middle],
        [functools.partial(forward.feed, 0, feeds)],
        [finish_block],
    ]

    def run_group(w):
        load(w).wait()
        for chunk in groups[w]:
            chunk()

    modulated = False
    for i, (t, event, ready) in enumerate(events):
        event()
        if not modulated and t == stride and events[i + 1][0] > stride:
            modulated = True
            modulate()
            on_first(forward.enter)
        if ready is not None:
            on_first(functools.partial(run_group, ready))

    for w in range(total):
        if modes[w]:
            complete(w)

            @pl.when(section == 0)
            def _():
                for side in range(2):

                    def from_x(zz, carry):
                        blk = index_of(zz, y if side == 0 else 1 - y, c)
                        arrived(w, 1, blk)
                        copy(w, 1, blk, partner, send_core.at[w, 1, side, zz]).start()
                        return carry

                    lax.fori_loop(0, depth, from_x, 0)

    for w in range(total):
        for side in range(2):

            def finish(zz, carry):
                copy(w, section, me, partner, send_core.at[w, 0, side, zz]).wait_send()
                if modes[w]:

                    @pl.when(section == 1)
                    def _():
                        copy(w, section, me, other, send_x.at[w, side, zz]).wait_send()

                    @pl.when(section == 0)
                    def _():
                        blk = index_of(zz, y if side == 0 else 1 - y, 1 - c)
                        arrived(w, 1, blk)
                        copy(w, 1, blk, partner, send_core.at[w, 1, side, zz]).wait_send()

                if side == 0:

                    @pl.when((zz == z) if first[w] else (zz >= 0))
                    def _():
                        copy(w, section, me, across, send_y.at[w, zz]).wait_send()

                if side == 0 or first[w]:

                    @pl.when((z < depth - 1) & (zz <= z))
                    def _():
                        copy(w, section, me, up, send_up.at[w, side, zz]).wait_send()

                    @pl.when((z > 0) & (zz >= z))
                    def _():
                        copy(w, section, me, down, send_down.at[w, side, zz]).wait_send()

                return carry

            lax.fori_loop(0, depth, finish, 0)
    hidden_copy = remote_copy(kept[10], kept_out[10], hidden_send, hidden_recv, other)

    @pl.when(section == 0)
    def _():
        hidden_copy.wait_send()
        wait_stored()

    @pl.when(section == 1)
    def _():
        hidden_copy.wait_recv()


def gather_forward(count, parts, inputs, images, bias, own, both, items, stride):
    arrays = list(own) + list(both)
    modes = [False] * len(own) + [True] * len(both)
    total, depth, n_arrays = len(items), count // 4, len(arrays)
    rows, width = inputs.shape
    anywhere, vmem = pl.BlockSpec(memory_space=pl.ANY), pl.BlockSpec(memory_space=pltpu.VMEM)
    shapes = [((2, count) if m else (count,)) + a.shape for a, m in zip(arrays, modes)]
    kept = kept_shapes(rows, width, images, own[2].shape[1])
    results = pl.pallas_call(
        functools.partial(gather_kernel, count, images, n_arrays, items, stride),
        out_shape=[
            jax.ShapeDtypeStruct(parts.shape, parts.dtype),
            jax.ShapeDtypeStruct((images, 8, width), jnp.float32),
        ]
        + [jax.ShapeDtypeStruct(s, a.dtype) for s, a in zip(shapes, arrays)]
        + kept,
        in_specs=[anywhere] + [vmem] * 2 + [anywhere] * n_arrays,
        out_specs=[anywhere, vmem] + [anywhere] * (n_arrays + 11),
        scratch_shapes=[
            DMA((count,)),
            DMA((count,)),
            DMA,
            DMA((total,)),
            DMA((total, 2, 2, depth)),
            DMA((total, depth)),
            DMA((total, 2, depth)),
            DMA((total, 2, depth)),
            DMA((total, 2, depth)),
            DMA((total, 2, count)),
        ]
        + [pltpu.VMEM((count,) + a.shape, a.dtype) for a in own]
        + [pltpu.VMEM(s.shape, s.dtype) for s in kept]
        + [
            pltpu.VMEM(parts.shape, parts.dtype),
            pltpu.VMEM((rows // images, width), jnp.float32),
            DMA,
            DMA((4,)),
            DMA((11,)),
            DMA,
            DMA,
        ],
        compiler_params=pltpu.CompilerParams(
            collective_id=1, has_side_effects=True, vmem_limit_bytes=63 * 2**20
        ),
        name="gather_forward",
    )(parts, inputs, bias, *arrays)
    return results[1], results[2 : 2 + n_arrays], results[2 + n_arrays :]


class Chain:
    def __init__(self, place, depth, z_first, sums, y_in, z_in, sems, out):
        self.section, self.z, self.y, self.c = place
        self.depth, self.z_first = depth, z_first
        self.sums, self.y_in, self.z_in, self.out = sums, y_in, z_in, out
        self.y_send, self.y_recv, self.z_send, self.z_recv = sems
        me = index_of(self.z, self.y, self.c)
        self.up, self.down = (self.section, me + 4), (self.section, me - 4)
        self.across = (self.section, index_of(self.z, 1 - self.y, self.c))

    def part(self, p, to):
        ref, lead = self.sums(p)
        return ref, lead + ((to,) if self.z_first else (to, self.y))

    def y_copy(self, p):
        ref, lead = self.sums(p)
        whole = self.z if self.z_first else slice(None)
        return remote_copy(
            ref.at[lead + (whole, 1 - self.y)],
            self.y_in(p),
            self.y_send.at[p],
            self.y_recv.at[p],
            self.across,
        )

    def z_copy(self, p, to, where, device):
        ref, place = self.part(p, to)
        return remote_copy(
            ref.at[place], self.z_in(p).at[where], self.z_send.at[p, to], self.z_recv.at[p, where], device
        )

    def add_z(self, p, to, where):
        self.z_copy(p, 0, where, self.across).wait_recv()
        ref, place = self.part(p, to)
        z_in = self.z_in(p)
        if self.z_first:
            for side in range(2):
                ref[place + (side,)] = half(wide(ref[place + (side,)]) + wide(z_in[where, side]))
        else:
            ref[place] = half(wide(ref[place]) + wide(z_in[where]))

    def hop(self, p, h):
        @pl.when((self.z == h) & (self.z < self.depth - 1))
        def _():
            def one(back, carry):
                to = self.depth - 1 - back
                if h > 0:
                    self.add_z(p, to, to)
                self.z_copy(p, to, to, self.up).start()
                return carry

            lax.fori_loop(0, self.depth - 1 - self.z, one, 0)

        @pl.when((self.depth - 1 - self.z == h) & (self.z > 0))
        def _():
            def one(to, carry):
                if h > 0:
                    self.add_z(p, to, to)
                self.z_copy(p, to, jnp.where(to == self.z - 1, self.depth, to), self.down).start()
                return carry

            lax.fori_loop(0, self.z, one, 0)

    def join(self, p):
        @pl.when(self.z > 0)
        def _():
            self.add_z(p, self.z, self.z)

        @pl.when(self.z < self.depth - 1)
        def _():
            self.add_z(p, self.z, self.depth)

    def begin(self, p):
        if self.z_first:
            self.hop(p, 0)
        else:
            self.y_copy(p).start()

    def move(self, p, step):
        if self.z_first:
            if step < self.depth - 1:
                self.hop(p, step)
            else:
                self.join(p)
                self.y_copy(p).start()
            return
        if step == 1:
            self.y_copy(p).wait_recv()
            y_in = self.y_in(p)

            def one(to, carry):
                ref, place = self.part(p, to)
                ref[place] = half(wide(ref[place]) + wide(y_in[to]))
                return carry

            lax.fori_loop(0, self.depth, one, 0)
        self.hop(p, step - 1)

    def last(self, p):
        ref, lead = self.sums(p)
        if self.z_first:
            self.y_copy(p).wait_recv()
            total = wide(ref[lead + (self.z, self.y)]) + wide(self.y_in(p)[...])
            self.out(p)[...] = half(total)
        else:
            self.join(p)
            self.out(p)[...] = ref[lead + (self.z, self.y)]

    def finish(self, p):
        self.y_copy(p).wait_send()

        def one(to, carry):
            @pl.when(to != self.z)
            def _():
                self.z_copy(p, to, to, self.across).wait_send()

            return carry

        lax.fori_loop(0, self.depth, one, 0)


def remote_copy(source, target, send, recv, device):
    return pltpu.make_async_remote_copy(
        src_ref=source,
        dst_ref=target,
        send_sem=send,
        recv_sem=recv,
        device_id=device,
        device_id_type=MESH,
    )


def reduce_kernel(count, ready, pairs, plan, far_first, far_steps, stride, *refs):
    depth = count // 4
    far_total = len(far_first)
    near_total = ready + len(plan)
    refs = list(refs)

    def take(amount):
        taken = refs[:amount]
        del refs[:amount]
        return taken

    (ready_src,) = take(1)
    left_src, right_src = take(pairs), take(pairs)
    far_src = take(far_total)
    mod_src, bias_src = take(2)
    (near_out,) = take(1)
    far_out = take(far_total)
    mod_out, bias_out = take(2)
    left, right, made, core_in, y_in, z_in, tail_y_in, tail_z_in, far_held = take(9)
    far_core_in, far_y_in, far_z_in = take(far_total), take(far_total), take(far_total)
    (
        left_sem, right_sem, ready_sem, core_send, core_recv, y_send, y_recv, z_send, z_recv,
        far_held_sem, far_core_send, far_core_recv, far_x_send, far_x_recv,
        far_y_send, far_y_recv, far_z_send, far_z_recv,
        mod_send, mod_recv, mod_local, bias_send, bias_recv, bias_local,
    ) = refs
    section, me, z, y, c = own_place()
    partner = (section, index_of(z, y, 1 - c))
    other = (1 - section, me)
    greet_section(count, section, me, (other,))
    rows, width = made.shape[-2:]
    mods = Exchange(count, section, me, mod_src, mod_out, mod_send, mod_recv, mod_local, True)
    biases = Exchange(count, section, me, bias_src, bias_out, bias_send, bias_recv, bias_local, False)

    order = [near_total - 1] + list(range(near_total - 1))

    def operands(p, slot):
        pair, row, column = plan[p - ready]
        return (
            pltpu.make_async_copy(
                left_src[pair].at[:, pl.ds(row * width, width)], left.at[slot], left_sem.at[slot]
            ),
            pltpu.make_async_copy(
                right_src[pair].at[:, pl.ds(column * width, width)], right.at[slot], right_sem.at[slot]
            ),
        )

    def ready_copy(p, slot):
        return pltpu.make_async_copy(
            ready_src.at[:, :, :, p], made.at[slot], ready_sem
        )

    def core_copy(p, slot):
        return remote_copy(
            made.at[slot, :, :, 1 - c], core_in.at[p], core_send.at[p], core_recv.at[p], partner
        )

    def fetch(t, slot):
        for i, p in enumerate(order):
            if p >= ready:

                @pl.when(t == i)
                def _():
                    for copy in operands(p, slot):
                        copy.start()

    def piece_of(t):
        return jnp.where(t == 0, near_total - 1, t - 1)

    def make(t):
        slot = lax.rem(t, 2)
        p = piece_of(t)

        @pl.when(t >= 2)
        def _():
            core_copy(piece_of(t - 2), slot).wait_send()

        @pl.when(t + 1 < near_total)
        def _():
            fetch(t + 1, 1 - slot)

        @pl.when(p < ready)
        def _():
            copy = ready_copy(p, slot)
            copy.start()
            copy.wait()

        @pl.when(p >= ready)
        def _():
            for copy in operands(ready, slot):
                copy.wait()
            tile = 3 * LANES
            for at in range(0, width, tile):
                cols = slice(at, at + tile)
                product = dot_down(left[slot], right[slot, :, cols])
                made[slot, :, :, :, :, cols] = half(product).reshape(depth, 2, 2, rows, tile)

        core_copy(p, slot).start()

    near = Chain(
        (section, z, y, c), depth, False,
        lambda p: (core_in, (p,)), lambda p: y_in.at[p], lambda p: z_in.at[p],
        (y_send, y_recv, z_send, z_recv), lambda p: near_out.at[p],
    )
    tail = Chain(
        (section, z, y, c), depth, True,
        lambda p: (core_in, (p,)), lambda p: tail_y_in, lambda p: tail_z_in,
        (y_send, y_recv, z_send, z_recv), lambda p: near_out.at[p],
    )
    far = [
        Chain(
            (section, z, y, c), depth, far_first[i],
            lambda p: (far_core_in[p], (section,)), lambda p: far_y_in[p], lambda p: far_z_in[p],
            (far_y_send, far_y_recv, far_z_send, far_z_recv), lambda p: far_out[p],
        )
        for i in range(far_total)
    ]

    def begin(t):
        slot = lax.rem(t, 2)
        p = piece_of(t)
        core_copy(p, slot).wait_recv()

        def add_side(side):
            def one(to, carry):
                core_in[p, to, side] = half(
                    wide(core_in[p, to, side]) + wide(made[slot, to, side, c])
                )
                return carry

            lax.fori_loop(0, depth, one, 0)

        add_side(1 - y)

        @pl.when(p < near_total - 1)
        def _():
            near.begin(p)

        add_side(y)

        @pl.when(p == near_total - 1)
        def _():
            tail.begin(near_total - 1)

    def far_core(i):
        return remote_copy(
            far_src[i].at[:, :, :, 1 - c],
            far_core_in[i],
            far_core_send.at[i],
            far_core_recv.at[i],
            partner,
        )

    def far_load(i):
        tall_i, wide_i = far_core_in[i].shape[-2:]
        return pltpu.make_async_copy(
            far_src[i].at[:, :, :, c],
            far_held.at[:, :, :, pl.ds(0, tall_i), pl.ds(0, wide_i)],
            far_held_sem,
        )

    def far_x(i):
        return remote_copy(
            far_core_in[i].at[1], far_core_in[i].at[1], far_x_send.at[i], far_x_recv.at[i], other
        )

    def far_add(i):
        far_load(i).wait()
        far_core(i).wait_recv()
        tall_i, wide_i = far_core_in[i].shape[-2:]
        tile = (pl.ds(0, tall_i), pl.ds(0, wide_i))
        ref = far_core_in[i]
        for owner in (1, 0):

            def one(at, carry):
                to, side = at // 2, lax.rem(at, 2)
                ref[owner, to, side] = half(
                    wide(ref[owner, to, side]) + wide(far_held[(owner, to, side) + tile])
                )
                return carry

            lax.fori_loop(0, 2 * depth, one, 0)
            if owner == 1:
                far_x(i).start()
        if i + 1 < far_total:
            far_load(i + 1).start()

    fetch(0, 0)

    @pl.when(section == 0)
    def _():
        far_load(0).start()
        for i in range(far_total):
            far_core(i).start()

    mods.start()
    biases.start()

    def step(t, carry):
        @pl.when(t < near_total)
        def _():
            make(t)

        @pl.when((t >= 1) & (t <= near_total))
        def _():
            begin(t - 1)

        for i in range(far_total):

            @pl.when((t == i + 1) & (section == 0))
            def _():
                far_add(i)

            @pl.when(t == far_steps[i])
            def _():
                @pl.when(section == 1)
                def _():
                    far_x(i).wait_recv()

                far[i].begin(i)

            for k in range(1, depth):

                @pl.when(t == far_steps[i] + stride * k)
                def _():
                    far[i].move(i, k)

            @pl.when(t == far_steps[i] + stride * depth)
            def _():
                far[i].last(i)

        for k in range(1, depth):
            p = t - 2 - stride * k

            @pl.when((p >= 0) & (p < near_total - 1))
            def _():
                near.move(p, k)

            @pl.when(t == 1 + stride * k)
            def _():
                tail.move(near_total - 1, k)

        p = t - 2 - stride * depth

        @pl.when((p >= 0) & (p < near_total - 1))
        def _():
            near.last(p)

        @pl.when(t == 1 + stride * depth)
        def _():
            tail.last(near_total - 1)

        return carry

    lax.fori_loop(0, max(near_total + 1, max(far_steps) + 1) + stride * depth, step, 0)
    for t in (near_total - 2, near_total - 1):
        core_copy(order[t], t % 2).wait_send()

    @pl.when(section == 0)
    def _():
        for i in range(far_total):
            far_core(i).wait_send()
            far_x(i).wait_send()

    for i in range(far_total):
        far[i].finish(i)

    def near_finish(p, carry):
        near.finish(p)
        return carry

    lax.fori_loop(0, near_total - 1, near_finish, 0)
    tail.finish(near_total - 1)
    mods.finish()
    biases.finish()


def reduce_grads(count, ready, pairs, plan, far, far_first, far_steps, stride, mods, biases):
    depth = count // 4
    pieces, rows, width = ready.shape[3:]
    near_total = pieces + len(plan)
    tokens = pairs[0][0].shape[0]
    far_shapes = [a.shape[4:] for a in far]
    far_rows, far_wide = max(s[0] for s in far_shapes), max(s[1] for s in far_shapes)
    kind = jnp.bfloat16
    anywhere, vmem = pl.BlockSpec(memory_space=pl.ANY), pl.BlockSpec(memory_space=pltpu.VMEM)
    n_far = len(far)
    lefts, rights = [a for a, _ in pairs], [b for _, b in pairs]

    def slots(first, shape):
        y_shape = shape if first else (depth,) + shape
        z_shape = (depth + 1, 2) + shape if first else (depth + 1,) + shape
        return y_shape, z_shape

    far_slots = [slots(f, s) for f, s in zip(far_first, far_shapes)]
    results = pl.pallas_call(
        functools.partial(reduce_kernel, count, pieces, len(pairs), plan, far_first, far_steps, stride),
        out_shape=[jax.ShapeDtypeStruct((near_total, rows, width), kind)]
        + [jax.ShapeDtypeStruct(s, kind) for s in far_shapes]
        + [
            jax.ShapeDtypeStruct((count,) + mods.shape, mods.dtype),
            jax.ShapeDtypeStruct(biases.shape, biases.dtype),
        ],
        in_specs=[anywhere] * (1 + 2 * len(pairs) + n_far + 2),
        out_specs=[vmem] * (1 + n_far) + [anywhere] * 2,
        scratch_shapes=[
            pltpu.VMEM((2, tokens, width), kind),
            pltpu.VMEM((2, tokens, width), kind),
            pltpu.VMEM((2, depth, 2, 2, rows, width), kind),
            pltpu.VMEM((near_total, depth, 2, rows, width), kind),
            pltpu.VMEM((near_total - 1, depth, rows, width), kind),
            pltpu.VMEM((near_total - 1, depth + 1, rows, width), kind),
            pltpu.VMEM((rows, width), kind),
            pltpu.VMEM((depth + 1, 2, rows, width), kind),
            pltpu.VMEM((2, depth, 2, far_rows, far_wide), kind),
        ]
        + [pltpu.VMEM((2, depth, 2) + s, kind) for s in far_shapes]
        + [pltpu.VMEM(s[0], kind) for s in far_slots]
        + [pltpu.VMEM(s[1], kind) for s in far_slots]
        + [
            DMA((2,)),
            DMA((2,)),
            DMA,
            DMA((near_total,)),
            DMA((near_total,)),
            DMA((near_total,)),
            DMA((near_total,)),
            DMA((near_total, depth)),
            DMA((near_total, depth + 1)),
            DMA,
            DMA((n_far,)),
            DMA((n_far,)),
            DMA((n_far,)),
            DMA((n_far,)),
            DMA((n_far,)),
            DMA((n_far,)),
            DMA((n_far, depth)),
            DMA((n_far, depth + 1)),
            DMA((count,)),
            DMA((count,)),
            DMA,
            DMA((count,)),
            DMA((count,)),
            DMA,
        ],
        compiler_params=pltpu.CompilerParams(
            collective_id=2, has_side_effects=True, vmem_limit_bytes=63 * 2**20
        ),
        name="reduce_grads",
    )(ready, *lefts, *rights, *far, mods, biases)
    return results[0], results[1 : 1 + n_far], results[1 + n_far], results[2 + n_far]


def padded(values, rows):
    flat = values.reshape(values.shape[0], -1)
    room = rows * LANES - flat.shape[1]
    return jnp.pad(flat, ((0, 0), (0, room))).reshape(values.shape[0], rows, LANES)


def rows_for(amount, unit):
    rows = -(-amount // LANES)
    return -(-rows // unit) * unit


def split_at(flat, sizes):
    pieces, start = [], 0
    for size in sizes:
        pieces.append(flat[..., start : start + size])
        start += size
    return pieces


def gather_plan(own, both):
    width = own[1].shape[1]
    parts = [(0, 1, j * width, width, False) for j in range(own[0].shape[1] // width)]
    parts.append((1, 1, 0, width, True))
    parts += [(2, 1, j * width, width, False) for j in range(own[2].shape[1] // width)]
    third = own[3].shape[0] // 3
    parts += [(3, 0, j * third, third, False) for j in range(3)]
    parts.append((4, 1, 0, both[0].shape[1], False))
    wide_two = both[1].shape[1] // 2
    parts += [(5, 1, j * wide_two, wide_two, True) for j in range(2)]
    parts.append((6, 1, 0, both[2].shape[1], False))
    return tuple(part + (i // 2,) for i, part in enumerate(parts))


def body(
    tokens,
    time_bins,
    labels,
    dino_feats,
    cotangent,
    time_table,
    class_table,
    ada_weight,
    ada_bias,
    qkv_weight,
    qkv_bias,
    out_weight,
    out_bias,
    mlp_in_weight,
    mlp_in_bias,
    mlp_out_weight,
    mlp_out_bias,
    align_weight_one,
    align_bias_one,
    align_weight_two,
    align_bias_two,
    align_weight_three,
    align_bias_three,
):
    count = lax.axis_size("dp")
    first_section = lax.axis_index("section") == 0
    index = lax.axis_index("dp")
    images, _, image_rows, model_width = tokens.shape
    rows_all = images * image_rows
    shard = out_weight.shape[1]
    kernels = count % 4 == 0 and shard % 8 == 0

    block_biases = (qkv_bias, out_bias, mlp_in_bias, mlp_out_bias, ada_bias)
    align_biases = (align_bias_one, align_bias_two, align_bias_three)
    block_sizes = [b.size for b in block_biases]
    align_sizes = [b.size for b in align_biases]
    indices = jnp.concatenate([time_bins, labels], 1).reshape(-1)
    pack = jnp.concatenate(
        [wide(half(b.reshape(-1))) for b in block_biases + align_biases] + [wide(indices)]
    )
    pack = padded(pack[None], rows_for(pack.size, 8))[0]
    if kernels:
        packs = share_small(count, pack).reshape(2, count, -1)
    else:
        packs = lax.all_gather(pack.reshape(-1), ("section", "dp")).reshape(2, count, -1)
    own_pack = jnp.where(first_section, packs[0], packs[1])
    block_full = [b.reshape(-1) for b in split_at(own_pack[:, : sum(block_sizes)], block_sizes)]
    bias_row = jnp.concatenate(
        [block_full[0][:model_width], jnp.zeros((model_width,), jnp.float32), block_full[0][model_width:]]
        + block_full[1:]
    )[None]
    start = sum(block_sizes)
    align_bias_full = [
        b.reshape(-1) for b in split_at(packs[:, :, start : start + sum(align_sizes)], align_sizes)
    ]
    start = start + sum(align_sizes)
    pairs = own_pack[:, start : start + 2 * images].astype(jnp.int32).reshape(count * images, 2)

    time_hot = pairs[:, :1] == jnp.arange(time_table.shape[0], dtype=jnp.int32)[None]
    class_hot = pairs[:, 1:] == jnp.arange(class_table.shape[0], dtype=jnp.int32)[None]
    cond = matmul(half(time_hot), half(time_table)) + matmul(half(class_hot), half(class_table))
    cond_act = half(jax.nn.silu(cond))
    ada_half = half(ada_weight[0])
    mod_wide = ada_half.shape[1]
    mod_parts = half(matmul(cond_act, ada_half)).reshape(count, images, mod_wide)
    mod_rows = rows_for(images * mod_wide, 16)

    start_rows = tokens.reshape(rows_all, model_width)
    own = [half(w[0]) for w in (qkv_weight, out_weight, mlp_in_weight, mlp_out_weight)]
    both = [half(w) for w in (align_weight_one, align_weight_two, align_weight_three)]
    one_rows = both[0].shape[0]
    one_padded = -(-one_rows // 16) * 16
    both[0] = jnp.pad(both[0], ((0, one_padded - one_rows), (0, 0)))
    place = jnp.arange(2 * count * one_padded, dtype=jnp.int32)
    owner, row = place // one_padded, place % one_padded
    wanted = jnp.where(row < one_rows, owner * one_rows + row, -1)[None]
    if kernels:
        chunked = mod_parts.reshape(count, images, 6, model_width // LANES, LANES)
        parts = padded(jnp.swapaxes(chunked, 2, 3).reshape(count, -1), mod_rows)
        modulation, gathered, kept = gather_forward(
            count, parts, start_rows, images, bias_row, own, both, gather_plan(own, both), 2
        )
        weights = [g.reshape(-1, g.shape[-1]) for g in gathered[:4]]
        align_weights = [g.reshape(-1, g.shape[-1]) for g in gathered[4:]]
        hidden = kept[10]
    else:
        modulation = lax.psum_scatter(wide(mod_parts), "dp", scatter_dimension=0, tiled=True)
        modulation = modulation.reshape(images, 6, model_width) + block_full[4].reshape(6, model_width)
        modulation = jnp.pad(modulation, ((0, 0), (0, 2), (0, 0)))
        weights = [lax.all_gather(w, "dp", axis=0, tiled=True) for w in own]
        align_weights = [lax.all_gather(w, ("section", "dp"), axis=0, tiled=True) for w in both]
        blank = kept_shapes(rows_all, model_width, images, weights[2].shape[1])
        blank = [jnp.zeros(b.shape, b.dtype) for b in blank[:10]]
        kept = block_forward(0, start_rows, modulation, bias_row, weights, blank)
        received = lax.ppermute(kept[10], "section", [(0, 1)])
        hidden = jnp.where(first_section, kept[10], received)
    aligner = (
        align_weights[0], align_bias_full[0], align_weights[1], align_bias_full[1],
        align_weights[2], align_bias_full[2],
    )

    target = dino_feats.reshape(rows_all, -1)
    *kept, final = block_forward(1, hidden, modulation, bias_row, weights, kept[:10])
    grad_align, align_sums, align_grads = project_align(hidden, target, wanted, aligner, loss_weight)
    grad_align = lax.ppermute(grad_align, "section", [(0, 1)])
    attn_input, qkv_rows, probs, mixed, attn_branch, after, mlp_input, slope, mlp_act, mlp_branch = kept

    def sources(block_input, grad):
        return (block_input, grad, mlp_branch, slope, after, attn_branch, probs, qkv_rows)

    grads = block_backward(
        1, modulation, sources(hidden, cotangent.reshape(rows_all, model_width)), weights
    )
    grad_hidden = half(wide(grads[0]) + wide(grad_align))
    received = lax.ppermute(grad_hidden, "section", [(1, 0)])
    grads = block_backward(
        0, modulation, sources(start_rows, received), weights, [grad_hidden] + list(grads[1:])
    )
    in_grads, grad_qkv, grad_attn, grad_pre, grad_branch, grad_mod = grads[:6]
    grad_down = half(transposed(mlp_act, grad_branch))
    outputs = jnp.where(first_section, hidden, final)
    grad_mod = half(grad_mod[:, :6])
    sums = [g[0] for g in grads[6:]]
    sums[0] = jnp.concatenate([sums[0][:model_width], sums[0][2 * model_width :]])
    align_bias_grads = [jnp.where(first_section, g, 0.0) for g in align_sums]
    align_sums = [jnp.moveaxis(g.reshape(2, count, -1), 0, 1).reshape(count, -1) for g in align_bias_grads]
    bias_flat = jnp.concatenate([g.reshape(count, -1) for g in sums] + align_sums, 1)
    if kernels:
        tall = grad_down.shape[0] // (count * shard)
        n_qkv, n_in = 3, weights[2].shape[1] // model_width
        ready = grad_down.reshape(count // 4, 2, 2, tall, shard, model_width)
        products = ((mlp_input, grad_pre), (attn_input, grad_qkv), (mixed, grad_attn))
        plan = [(0, 0, j) for j in range(n_in)] + [(1, 0, j) for j in range(n_qkv)] + [(2, 0, 0)]
        far = [g.reshape(2, count // 4, 2, 2, *w.shape) for g, w in zip(align_grads, both)]
        far = [far[2], far[0], far[1]]
        bias_grad_rows = rows_for(bias_flat.shape[1], 8)
        near_sum, far_sum, mods, bias_parts_sum = reduce_grads(
            count, ready, products, plan, far, (False, True, False), (3, 5, 8), 2,
            padded(grad_mod.reshape(1, -1), mod_rows)[0], padded(bias_flat, bias_grad_rows),
        )
        grad_mods = mods.reshape(count, -1)[:, : images * mod_wide]
        bias_sum = jnp.sum(bias_parts_sum, 0).reshape(-1)
        grad_down_weight = wide(near_sum[:tall]).reshape(-1, model_width)
        grad_in_weight = wide(jnp.concatenate([near_sum[tall + j] for j in range(n_in)], 1))
        grad_qkv_weight = wide(jnp.concatenate([near_sum[tall + n_in + j] for j in range(n_qkv)], 1))
        grad_out_weight = wide(near_sum[tall + n_in + n_qkv])
        align_out = [wide(far_sum[1])[:one_rows], wide(far_sum[2]), wide(far_sum[0])]
    else:
        grad_mods = lax.all_gather(grad_mod.reshape(-1), "dp")
        bias_sum = lax.psum_scatter(bias_flat, "dp", scatter_dimension=0, tiled=True).reshape(-1)
        weight_grads = (
            transposed(attn_input, grad_qkv),
            transposed(mixed, grad_attn),
            transposed(mlp_input, grad_pre),
            wide(grad_down),
        )
        reduced = [
            lax.psum_scatter(g, "dp", scatter_dimension=0, tiled=True) for g in weight_grads
        ]
        grad_qkv_weight, grad_out_weight, grad_in_weight, grad_down_weight = reduced
        align_out = [
            lax.psum_scatter(
                jnp.where(first_section, wide(g), 0.0), ("section", "dp"), scatter_dimension=0, tiled=True
            )
            for g in align_grads
        ]
        align_out[0] = align_out[0][:one_rows]

    grad_mods = grad_mods.reshape(count * images, mod_wide)
    grad_ada = transposed(cond_act, grad_mods)
    mod_sums = jnp.sum(wide(grad_mods), 0)
    ada_share = mod_wide // count
    grad_ada_bias = lax.dynamic_slice(mod_sums, (index * ada_share,), (ada_share,))
    cond_part = times_transpose(grad_mods, ada_half)
    block_sum = sum(block_sizes[:4])
    grad_biases = split_at(bias_sum[:block_sum], block_sizes[:4])
    align_share = split_at(bias_sum[block_sum : block_sum + 2 * sum(align_sizes)], [2 * a for a in align_sizes])
    align_share = jnp.concatenate([a.reshape(2, -1) for a in align_share], 1)
    packet = jnp.concatenate([cond_part.reshape(-1), align_share.reshape(-1)])
    packet = packet + lax.ppermute(packet, "section", [(0, 1), (1, 0)])
    cond_grad = packet[: cond_part.size].reshape(cond_part.shape)
    align_share = packet[cond_part.size :].reshape(2, -1)
    align_share = jnp.where(first_section, align_share[0], align_share[1])
    align_bias_out = split_at(align_share, align_sizes)
    cond_grad = local_grad(jax.nn.silu, cond, cond_grad)

    def table_grad(hot):
        return lax.dot_general(
            wide(hot),
            cond_grad,
            (((0,), (0,)), ((), ())),
            precision=lax.Precision.HIGHEST,
            preferred_element_type=jnp.float32,
        )

    whole_rows = (1, images, 1, image_rows, model_width)
    return (
        outputs.reshape(whole_rows),
        in_grads.reshape(whole_rows),
        table_grad(time_hot),
        table_grad(class_hot),
        grad_ada[None],
        grad_ada_bias[None],
        grad_qkv_weight[None],
        grad_biases[0][None],
        grad_out_weight[None],
        grad_biases[1][None],
        grad_in_weight[None],
        grad_biases[2][None],
        grad_down_weight[None],
        grad_biases[3][None],
        align_out[0],
        align_bias_out[0],
        align_out[1],
        align_bias_out[1],
        align_out[2],
        align_bias_out[2],
    )


def solution(mesh):
    placed = (
        P(None, "dp", None, None),
        P(None, "dp"),
        P(None, "dp"),
        P(None, "dp", None, None),
        P(None, "dp", None, None),
        P(None, "dp"),
        P(None, "dp"),
        P("section", "dp", None),
        P("section", "dp"),
        P("section", "dp", None),
        P("section", "dp"),
        P("section", "dp", None),
        P("section", "dp"),
        P("section", "dp", None),
        P("section", "dp"),
        P("section", "dp", None),
        P("section", "dp"),
        P(("section", "dp"), None),
        P(("section", "dp")),
        P(("section", "dp"), None),
        P(("section", "dp")),
        P(("section", "dp"), None),
        P(("section", "dp")),
    )
    return jax.shard_map(
        body,
        mesh=mesh,
        in_specs=placed,
        out_specs=(
            P("section", None, "dp", None, None),
            P("section", None, "dp", None, None),
        )
        + placed[5:],
        check_vma=False,
    )
```

```python
import functools

import jax
import jax.numpy as jnp
from jax import lax
from jax.experimental import pallas as pl
from jax.experimental.pallas import tpu as pltpu
from jax.sharding import PartitionSpec as P

HEADS = 16
HD = 72
LANES = 128
MESH = pl.DeviceIdType.MESH
DMA = pltpu.SemaphoreType.DMA

epsilon = 1e-06
loss_weight = 0.5


def matmul(left, right):
    return jnp.dot(left, right, preferred_element_type=jnp.float32)


def transposed(left, right):
    return lax.dot_general(
        left, right, (((0,), (0,)), ((), ())), preferred_element_type=jnp.float32
    )


def times_transpose(grad_rows, weight):
    return lax.dot_general(
        grad_rows, weight, (((1,), (1,)), ((), ())), preferred_element_type=jnp.float32
    )


def local_grad(function, point, grad_value):
    return jax.vjp(function, point)[1](grad_value)[0]


def half(values):
    return values.astype(jnp.bfloat16)


def wide(values):
    return values.astype(jnp.float32)


GELU_SLOPE = 0.7978845608028654
GELU_CUBE = 0.044715


def dot_plain(left, right):
    return lax.dot_general(left, right, (((1,), (0,)), ((), ())), preferred_element_type=jnp.float32)


def dot_across(left, right):
    return lax.dot_general(left, right, (((1,), (1,)), ((), ())), preferred_element_type=jnp.float32)


def dot_down(left, right):
    return lax.dot_general(left, right, (((0,), (0,)), ((), ())), preferred_element_type=jnp.float32)


class Loads:
    def __init__(self, sems):
        self.sems, self.copies = sems, []

    def add(self, source, target, axis, tiles):
        size = source.shape[axis] // tiles
        first = len(self.copies)
        for j in range(tiles):
            place = (pl.ds(j * size, size),) if axis == 0 else (slice(None), pl.ds(j * size, size))
            self.copies.append(
                pltpu.make_async_copy(source.at[place], target.at[place], self.sems.at[first + j])
            )
        return list(range(first, first + tiles))

    def start(self):
        for copy in self.copies:
            copy.start()

    def wait(self, places):
        for place in places:
            self.copies[place].wait()


def head_window(head):
    low = head * HD
    start = low // LANES * LANES
    stop = -(-(low + HD) // LANES) * LANES
    return low, start, stop - start


def head_mask(head, rows):
    low, start, size = head_window(head)
    lane = lax.broadcasted_iota(jnp.int32, (rows, size), 1) + start
    return (lane >= low) & (lane < low + HD)


def masked(mask, values):
    return jnp.where(mask, values, jnp.zeros_like(values))


def row_norm(values):
    centred = values - jnp.mean(values, -1, keepdims=True)
    inverse = lax.rsqrt(jnp.mean(centred * centred, -1, keepdims=True) + epsilon)
    return centred * inverse, inverse


def row_norm_back(grad, normed, inverse):
    return inverse * (
        grad
        - jnp.mean(grad, -1, keepdims=True)
        - normed * jnp.mean(grad * normed, -1, keepdims=True)
    )


def column_tiles(total, tile):
    return [(at, min(tile, total - at)) for at in range(0, total, tile)]


class Forward:
    def __init__(self, images, x_ref, mod_ref, biases, kept, blend, weights, store):
        self.images, self.x_ref, self.mod_ref = images, x_ref, mod_ref
        self.qkv_bias, self.out_bias, self.in_bias, self.down_bias = biases
        (
            self.attn_in, self.qkv, self.probs, self.mixed, self.attn_branch, self.after,
            self.mlp_in, self.slope, self.act, self.mlp_branch, self.output,
        ) = kept
        self.blend, self.weights, self.store = blend, weights, store
        self.rows, self.width = x_ref.shape
        self.each = self.rows // images

    def at(self, image):
        return pl.ds(pl.multiple_of(image * self.each, self.each), self.each)

    def mod(self, image, k):
        return self.mod_ref[image, pl.ds(k, 1), :]

    def per_image(self, action):
        def one(image, carry):
            action(image, self.at(image))
            return carry

        lax.fori_loop(0, self.images, one, 0)

    def enter(self):
        def one(image, at):
            normed, _ = row_norm(wide(self.x_ref[at, :]))
            self.attn_in[at, :] = half(normed * (1.0 + self.mod(image, 1)) + self.mod(image, 0))

        self.per_image(one)
        self.store(0)

    def project(self, part):
        cols = slice(part * self.width, (part + 1) * self.width)
        product = dot_plain(self.attn_in[...], self.weights[0](cols))
        self.qkv[:, cols] = half(product + self.qkv_bias[:, cols])
        if part == 2:
            self.store(1)

    def attend(self, image):
        at, each, width = self.at(image), self.each, self.width
        for head in range(HEADS):
            low, start, size = head_window(head)
            mask = head_mask(head, each)
            cols = [slice(part * width + start, part * width + start + size) for part in range(3)]
            queries = masked(mask, self.qkv[at, cols[0]])
            scores = dot_across(queries, self.qkv[at, cols[1]]) * HD ** (-0.5)
            powers = jnp.exp(scores - jnp.max(scores, -1, keepdims=True))
            soft = half(powers * (1.0 / jnp.sum(powers, -1, keepdims=True)))
            self.probs[image, head] = soft
            fresh = dot_plain(soft, self.qkv[at, cols[2]])
            window = slice(start, start + size)
            self.blend[:, window] = jnp.where(mask, fresh, self.blend[:, window])
        self.mixed[at, :] = half(self.blend[...])

    def attend_all(self):
        def one(image, carry):
            self.attend(image)
            return carry

        lax.fori_loop(0, self.images, one, 0)
        self.attended()

    def attended(self):
        self.store(2)
        self.store(3)

    def middle(self):
        branch = dot_plain(self.mixed[...], self.weights[1](slice(0, self.width))) + self.out_bias[...]
        self.attn_branch[...] = half(branch)
        self.store(4)

        def one(image, at):
            joined = wide(self.x_ref[at, :]) + self.mod(image, 2) * wide(self.attn_branch[at, :])
            self.after[at, :] = joined
            normed, _ = row_norm(joined)
            self.mlp_in[at, :] = half(normed * (1.0 + self.mod(image, 4)) + self.mod(image, 3))

        self.per_image(one)
        self.store(5)
        self.store(6)

    def feed(self, first, last, tile=512):
        def one(j, carry):
            cols = pl.ds(pl.multiple_of(j * tile, tile), tile)
            pre = dot_plain(self.mlp_in[...], self.weights[2](cols)) + self.in_bias[:, cols]
            square = pre * pre
            bend = jnp.tanh(GELU_SLOPE * pre * (1.0 + GELU_CUBE * square))
            self.act[:, cols] = half(0.5 * pre * (1.0 + bend))
            self.slope[:, cols] = half(
                0.5 * (1.0 + bend)
                + 0.5 * pre * (1.0 - bend * bend) * (GELU_SLOPE + 3.0 * GELU_SLOPE * GELU_CUBE * square)
            )
            return carry

        lax.fori_loop(first, last, one, 0)
        if last * tile == self.act.shape[1]:
            self.store(7)
            self.store(8)

    def leave(self):
        branch = dot_plain(self.act[...], self.weights[3](slice(0, self.width))) + self.down_bias[...]
        self.mlp_branch[...] = half(branch)
        self.store(9)

        def one(image, at):
            self.output[at, :] = half(
                self.after[at, :] + self.mod(image, 5) * wide(self.mlp_branch[at, :])
            )

        self.per_image(one)
        self.store(10)


def kept_shapes(rows, width, images, hidden_width):
    each = rows // images
    thin = jax.ShapeDtypeStruct((rows, width), jnp.bfloat16)
    fat = jax.ShapeDtypeStruct((rows, hidden_width), jnp.bfloat16)
    return [
        thin, jax.ShapeDtypeStruct((rows, 3 * width), jnp.bfloat16),
        jax.ShapeDtypeStruct((images, HEADS, each, each), jnp.bfloat16), thin, thin,
        jax.ShapeDtypeStruct((rows, width), jnp.float32), thin, fat, fat, thin, thin,
    ]


def stored(refs, places, sems):
    copies = [pltpu.make_async_copy(a, b, sems.at[k]) for k, (a, b) in enumerate(zip(refs, places))]

    def wait():
        for copy in copies:
            copy.wait()

    return lambda k: copies[k].start(), wait


def flat(ref):
    def columns(cols):
        values = ref[:, :, cols]
        return values.reshape(values.shape[0] * values.shape[1], values.shape[2])

    return columns


def forward_kernel(images, own_section, *refs):
    x_hbm, mod_ref, bias = refs[:3]
    weights_hbm = refs[3:7]
    kept_out = refs[17:28]
    weights = refs[28:32]
    x_ref, *kept = refs[32:44]
    blend, load_sem, kept_sem = refs[44:]

    @pl.when(lax.axis_index("section") == own_section)
    def _():
        loads = Loads(load_sem)
        x_at = loads.add(x_hbm, x_ref, 0, 1)
        qkv_at = loads.add(weights_hbm[0], weights[0], 1, 3)
        out_at = loads.add(weights_hbm[1], weights[1], 0, 1)
        in_at = loads.add(weights_hbm[2], weights[2], 1, 3)
        down_at = loads.add(weights_hbm[3], weights[3], 0, 3)
        loads.start()
        store, wait_stored = stored(kept, kept_out, kept_sem)
        columns = [functools.partial(lambda ref, cols: ref[:, cols], ref) for ref in weights]
        forward = Forward(images, x_ref, mod_ref, bias_parts(bias), kept, blend, columns, store)
        loads.wait(x_at)
        forward.enter()
        for part in range(3):
            loads.wait([qkv_at[part]])
            forward.project(part)
        forward.attend_all()
        loads.wait(out_at)
        forward.middle()
        feeds = kept[8].shape[1] // 512
        for third in range(3):
            loads.wait([in_at[third]])
            forward.feed(feeds * third // 3, feeds * (third + 1) // 3)
        loads.wait(down_at)
        forward.leave()
        wait_stored()


def bias_parts(bias):
    width = bias.shape[1] // 15
    places = ((0, 3), (3, 1), (4, 4), (8, 1))
    return [bias.at[:, start * width : (start + size) * width] for start, size in places]


def block_forward(own_section, inputs, modulation, bias, weights, previous):
    rows, width = inputs.shape
    images = modulation.shape[0]
    each = rows // images
    kept = kept_shapes(rows, width, images, weights[2].shape[1])
    vmem, anywhere = pl.BlockSpec(memory_space=pltpu.VMEM), pl.BlockSpec(memory_space=pl.ANY)
    return pl.pallas_call(
        functools.partial(forward_kernel, images, own_section),
        out_shape=kept,
        in_specs=[anywhere, vmem, vmem] + [anywhere] * 14,
        out_specs=[anywhere] * 11,
        scratch_shapes=[pltpu.VMEM(w.shape, w.dtype) for w in weights]
        + [pltpu.VMEM(inputs.shape, inputs.dtype)]
        + [pltpu.VMEM(s.shape, s.dtype) for s in kept]
        + [pltpu.VMEM((each, width), jnp.float32), DMA((11,)), DMA((11,))],
        input_output_aliases={7 + k: k for k in range(10)},
        compiler_params=pltpu.CompilerParams(vmem_limit_bytes=63 * 2**20),
        name="block_forward",
    )(inputs, modulation, bias, *weights, *previous)


def backward_kernel(count, images, own_section, fresh, kept, *refs):
    refs = list(refs)

    def take(amount):
        taken = refs[:amount]
        del refs[:amount]
        return taken

    (mod_ref,) = take(1)
    sources = take(8)
    weights_hbm = take(4)
    if fresh:
        (extra_hbm,) = take(1)
        far_src = take(3)
    if kept:
        take(10)
    out_hbm = take(10)
    if fresh:
        far_out, half_out = take(3), take(3)
    held = take(8)
    in_w, down_w = take(2)
    outs = take(9)
    wide_grad, blend, load_sem, out_sem, late_sem = take(5)
    x_ref, dout, mlp_branch, slope, after, attn_branch, probs, qkv_ref = held
    dx_half, d_qkv, d_attn, d_branch, d_mod, qkv_sum, attn_sum, pre_sum, branch_sum = outs
    d_pre, half_grad = slope, dx_half
    out_refs = [dx_half, d_qkv, d_attn, d_pre, d_branch, d_mod, qkv_sum, attn_sum, pre_sum, branch_sum]
    rows, width = x_ref.shape
    each = rows // images
    hidden_width = in_w.shape[1]
    tile = 512
    section = lax.axis_index("section")
    dx_ref = wide_grad.at[1]
    grad_ref = wide_grad.at[0]

    feeds = hidden_width // tile
    if fresh:
        extra, extra_send, extra_recv, grad_send, grad_recv = take(5)
        place = own_place()
        other = (1 - section, place[1])
        greet_section(count, section, place[1], (other,))
        extra_copy = remote_copy(extra_hbm, extra, extra_send, extra_recv, other)

        def grad_copy(image):
            at = pl.ds(pl.multiple_of(image * each, each), each)
            return remote_copy(
                dx_half.at[at], out_hbm[0].at[at], grad_send.at[image], grad_recv.at[image], other
            )

        @pl.when(section != own_section)
        def _():
            extra_copy.start()
            far_sums(count, place, far_src, far_out, half_out, refs)
            extra_copy.wait_send()

            def one(image, carry):
                grad_copy(image).wait_recv()
                return carry

            lax.fori_loop(0, images, one, 0)

    @pl.when(section == own_section)
    def _():
        loads = Loads(load_sem)
        places = {}
        qkv_w = in_w.at[:, pl.ds(0, weights_hbm[0].shape[1])]
        out_w = down_w.at[pl.ds(0, width)]
        out_load = pltpu.make_async_copy(weights_hbm[1], out_w, late_sem.at[0])
        qkv_load = pltpu.make_async_copy(weights_hbm[0], qkv_w, late_sem.at[1])
        for name in (1, 2, "down", 3, "in", 4, 5, 6, 7, 0):
            if name == "down":
                places[name] = loads.add(weights_hbm[3], down_w, 0, 3)
            elif name == "in":
                places[name] = loads.add(weights_hbm[2], in_w, 0, 3)
            else:
                places[name] = loads.add(sources[name], held[name], 0, 1)
        loads.start()
        store, wait_stored = stored(out_refs, out_hbm, out_sem)

        def per_image(action):
            def one(image, carry):
                action(image, pl.ds(pl.multiple_of(image * each, each), each))
                return carry

            lax.fori_loop(0, images, one, 0)

        def mod(image, k):
            return mod_ref[image, pl.ds(k, 1), :]

        def sums(image, k, values):
            d_mod[image, pl.ds(k, 1), :] = jnp.sum(values, 0, keepdims=True)

        def enter(image, at):
            grad = wide(dout[at, :])
            d_branch[at, :] = half(grad * mod(image, 5))
            sums(image, 5, grad * wide(mlp_branch[at, :]))

        loads.wait(places[1] + places[2])
        per_image(enter)
        branch_sum[...] = jnp.sum(wide(d_branch[...]), 0, keepdims=True)
        store(4)
        store(9)
        loads.wait(places[3])

        def feed(j, carry):
            cols = pl.ds(pl.multiple_of(j * tile, tile), tile)
            grad = half(dot_across(d_branch[...], down_w[cols, :]) * wide(slope[:, cols]))
            d_pre[:, cols] = grad
            pre_sum[:, cols] = jnp.sum(wide(grad), 0, keepdims=True)
            return carry

        for third in range(3):
            loads.wait([places["down"][third]])
            lax.fori_loop(feeds * third // 3, feeds * (third + 1) // 3, feed, 0)
        out_load.start()
        store(3)
        store(8)
        loads.wait(places["in"])
        for start, size in column_tiles(width, 512):
            grad_ref[:, start : start + size] = dot_across(d_pre[...], in_w[start : start + size, :])
        qkv_load.start()

        def middle(image, at):
            grad_in = grad_ref[at, :]
            normed, inverse = row_norm(after[at, :])
            sums(image, 4, grad_in * normed)
            sums(image, 3, grad_in)
            grad = wide(dout[at, :]) + row_norm_back(grad_in * (1.0 + mod(image, 4)), normed, inverse)
            dx_ref[at, :] = grad
            d_attn[at, :] = half(grad * mod(image, 2))
            sums(image, 2, grad * wide(attn_branch[at, :]))

        loads.wait(places[4] + places[5])
        per_image(middle)
        attn_sum[...] = jnp.sum(wide(d_attn[...]), 0, keepdims=True)
        store(2)
        store(7)
        out_load.wait()
        half_grad[...] = half(dot_across(d_attn[...], out_w[...]))
        loads.wait(places[6] + places[7])

        def attend(image, at):
            for head in range(HEADS):
                low, start, size = head_window(head)
                mask = head_mask(head, each)
                window = slice(start, start + size)
                cols = [slice(part * width + start, part * width + start + size) for part in range(3)]
                grad = masked(mask, half_grad[at, window])
                soft = probs[image, head]
                grad_soft = dot_across(grad, qkv_ref[at, cols[2]])
                weighed = wide(soft) * grad_soft
                grad_scores = half(weighed - wide(soft) * jnp.sum(weighed, -1, keepdims=True))
                made = (
                    dot_plain(grad_scores, qkv_ref[at, cols[1]]) * HD ** (-0.5),
                    dot_down(grad_scores, qkv_ref[at, cols[0]]) * HD ** (-0.5),
                    dot_down(soft, grad),
                )
                for part in range(3):
                    blend[:, cols[part]] = jnp.where(mask, made[part], blend[:, cols[part]])
            d_qkv[at, :] = half(blend[...])

        def leave(image, at):
            grad_in = grad_ref[at, :]
            normed, inverse = row_norm(wide(x_ref[at, :]))
            sums(image, 1, grad_in * normed)
            sums(image, 0, grad_in)
            grad = dx_ref[at, :] + row_norm_back(grad_in * (1.0 + mod(image, 1)), normed, inverse)
            if fresh:
                grad = grad + wide(extra[at, :])
            dx_half[at, :] = half(grad)

        loads.wait(places[0])
        qkv_load.wait()
        if fresh:
            extra_copy.wait_recv()

            def finish(image, at):
                attend(image, at)
                for start, size in column_tiles(width, 512):
                    grad_ref[at, start : start + size] = dot_across(
                        d_qkv[at, :], qkv_w[start : start + size, :]
                    )
                leave(image, at)
                grad_copy(image).start()

            per_image(finish)
            store(1)
        else:
            per_image(attend)
            store(1)
            for start, size in column_tiles(width, 512):
                grad_ref[:, start : start + size] = dot_across(
                    d_qkv[...], qkv_w[start : start + size, :]
                )
            per_image(leave)
        store(0)
        qkv_sum[...] = jnp.sum(wide(d_qkv[...]), 0, keepdims=True)
        store(5)
        store(6)
        wait_stored()
        if fresh:

            def one(image, carry):
                grad_copy(image).wait_send()
                return carry

            lax.fori_loop(0, images, one, 0)
            total = len(FAR_CUTS)
            sems = refs[3 * total + 4 : 3 * total + 6]
            for i in range(total):
                if i in FAR_EARLY:
                    far_half_copy(i, None, half_out, sems, other).wait_recv()


FAR_CUTS = ((2, 2, 0, False), (2, 2, 1, False), (1, 2, 0, False), (1, 2, 1, False), (0, 1, 0, True))
FAR_EARLY = (0, 4)


def far_shape(cut, shapes):
    rows, columns = shapes[cut[0]]
    return (rows, columns // cut[1])


def far_place(cut, shapes):
    size = far_shape(cut, shapes)[1]
    return (slice(None), pl.ds(cut[2] * size, size))


def far_scratch(count, shapes):
    depth, kind, total = count // 4, jnp.bfloat16, len(FAR_CUTS)
    parts = [far_shape(cut, shapes) for cut in FAR_CUTS]
    tall, wide_most = max(s[0] for s in parts), max(s[1] for s in parts)
    slots = [chain_slots(depth, cut[3], s) for cut, s in zip(FAR_CUTS, parts)]
    return (
        [pltpu.VMEM((2, depth, 2) + s, kind) for s in parts]
        + [pltpu.VMEM((depth, 2, tall, wide_most), kind)]
        + [pltpu.VMEM(s[0], kind) for s in slots]
        + [pltpu.VMEM(s[1], kind) for s in slots]
        + [DMA, DMA((2, total)), DMA((2, total)), DMA((total,)), DMA((total,))]
        + [DMA((total,)), DMA((total,)), DMA((total, depth)), DMA((total, depth + 1))]
    )


def far_half_copy(i, source, half_out, sems, other):
    cut = FAR_CUTS[i]
    shapes = [ref.shape[2:] for ref in half_out]
    place = half_out[cut[0]].at[(slice(None), slice(None)) + far_place(cut, shapes)]
    if i not in FAR_EARLY:
        return pltpu.make_async_copy(place if source is None else source, place, sems[0].at[i])
    return remote_copy(
        place if source is None else source, place, sems[0].at[i], sems[1].at[i], other
    )


def far_sums(count, place, far_src, far_out, half_out, refs):
    depth, total = count // 4, len(FAR_CUTS)
    refs = list(refs)

    def take(amount):
        taken = refs[:amount]
        del refs[:amount]
        return taken

    core_in, held, y_in, z_in = take(total), take(1)[0], take(total), take(total)
    held_sem, core_send, core_recv, x_send, x_recv, y_send, y_recv, z_send, z_recv = refs
    section, me, z, y, c = place
    partner, other = (section, index_of(z, y, 1 - c)), (1 - section, me)
    shapes = [ref.shape for ref in far_out]
    places = [far_place(cut, shapes) for cut in FAR_CUTS]
    chains = [
        Chain(
            (section, z, y, c), depth, cut[3],
            lambda p: (core_in[p], (0,)), lambda p: y_in[p], lambda p: z_in[p],
            (y_send, y_recv, z_send, z_recv), lambda p: far_out[FAR_CUTS[p][0]].at[places[p]],
        )
        for cut in FAR_CUTS
    ]

    def core_copy(i, owner):
        source = far_src[FAR_CUTS[i][0]].at[(owner, slice(None), slice(None), 1 - c) + places[i]]
        return remote_copy(
            source, core_in[i].at[owner], core_send.at[owner, i], core_recv.at[owner, i], partner
        )

    def add_core(i, owner):
        ref = core_in[i]
        tile = (pl.ds(0, ref.shape[-2]), pl.ds(0, ref.shape[-1]))
        load = pltpu.make_async_copy(
            far_src[FAR_CUTS[i][0]].at[(owner, slice(None), slice(None), c) + places[i]],
            held.at[(slice(None), slice(None)) + tile],
            held_sem,
        )
        load.start()
        load.wait()
        core_copy(i, owner).wait_recv()

        def one(at, carry):
            to, side = at // 2, lax.rem(at, 2)
            ref[owner, to, side] = half(wide(ref[owner, to, side]) + wide(held[(to, side) + tile]))
            return carry

        lax.fori_loop(0, 2 * depth, one, 0)

    def leave(i):
        return far_half_copy(i, core_in[i].at[1], half_out, (x_send, x_recv), other)

    for owner in (0, 1):
        for i in range(total):
            core_copy(i, owner).start()
    for i in range(total):
        add_core(i, 0)
        chains[i].begin(i)
    for i in FAR_EARLY:
        add_core(i, 1)
        leave(i).start()
    later = [i for i in range(total) if i not in FAR_EARLY]
    for step in range(total + depth):
        for i in range(total):
            k = step - i + 1
            if 1 <= k < depth:
                chains[i].move(i, k)
            elif k == depth:
                chains[i].last(i)
        if later:
            i = later.pop(0)
            add_core(i, 1)
            leave(i).start()
    for i in range(total):
        chains[i].finish(i)
        core_copy(i, 0).wait_send()
        core_copy(i, 1).wait_send()
        if i in FAR_EARLY:
            leave(i).wait_send()
        else:
            leave(i).wait()


def block_backward(count, own_section, modulation, sources, weights, extra=None, far=(), previous=None):
    fresh = extra is not None
    rows, width = sources[0].shape
    images = modulation.shape[0]
    each = rows // images
    hidden_width = weights[2].shape[1]
    vmem, anywhere = pl.BlockSpec(memory_space=pltpu.VMEM), pl.BlockSpec(memory_space=pl.ANY)

    def shape(columns, kind=jnp.bfloat16, count=rows):
        return jax.ShapeDtypeStruct((count, columns), kind)

    outs = [
        shape(width), shape(3 * width), shape(width), shape(hidden_width), shape(width),
        jax.ShapeDtypeStruct((images, 8, width), jnp.float32),
        shape(3 * width, jnp.float32, 1), shape(width, jnp.float32, 1),
        shape(hidden_width, jnp.float32, 1), shape(width, jnp.float32, 1),
    ]
    scratch = [pltpu.VMEM(a.shape, a.dtype) for a in list(sources) + list(weights[2:])]
    scratch += [pltpu.VMEM(s.shape, s.dtype) for k, s in enumerate(outs) if k != 3]
    scratch += [
        pltpu.VMEM((2, rows, width), jnp.float32),
        pltpu.VMEM((each, 3 * width), jnp.float32), DMA((14,)), DMA((10,)), DMA((2,)),
    ]
    extra_in, extra_out, aliases = [], [], {}
    params = {}
    if fresh:
        extra_in = [extra] + list(far)
        scratch += [pltpu.VMEM(extra.shape, extra.dtype), DMA, DMA, DMA((images,)), DMA((images,))]
        shapes = [a.shape[4:] for a in far]
        extra_out = [jax.ShapeDtypeStruct(s, jnp.bfloat16) for s in shapes]
        extra_out += [jax.ShapeDtypeStruct((count // 4, 2) + s, jnp.bfloat16) for s in shapes]
        scratch += far_scratch(count, shapes)
        params = {"collective_id": 3, "has_side_effects": True}
    elif previous is not None:
        extra_in = list(previous)
        aliases = {13 + k: k for k in range(10)}
    return pl.pallas_call(
        functools.partial(
            backward_kernel, count, images, own_section, fresh, previous is not None
        ),
        out_shape=outs + extra_out,
        in_specs=[vmem] + [anywhere] * (12 + len(extra_in)),
        out_specs=[anywhere] * 10 + ([vmem] * 3 + [anywhere] * 3 if fresh else []),
        scratch_shapes=scratch,
        input_output_aliases=aliases,
        compiler_params=pltpu.CompilerParams(vmem_limit_bytes=63 * 2**20, **params),
        name="block_backward",
    )(modulation, *sources, *weights, *extra_in)


def sigmoid_parts(values):
    gate = 1.0 / (1.0 + jnp.exp(-values))
    return values * gate, gate * (1.0 + values * (1.0 - gate))


def align_kernel(
    loss,
    wanted, bias_one, bias_two, bias_three, x_hbm, target_hbm, one_hbm, two_hbm, three_hbm,
    dx_hbm, one_sum, two_sum, three_sum, one_grad, two_grad, three_grad,
    x_ref, target, dx_ref, one_w, two_w, three_w, padded_x, act_one, act_two, d_one, d_two, d_latent, slope_one, slope_two,
    product, sems, product_sem, dx_sem,
):
    tile = 512

    def layer(source, weight, bias, act, slope):
        def one(j, carry):
            cols = pl.ds(pl.multiple_of(j * tile, tile), tile)
            pre = dot_plain(source[...], weight[:, cols]) + bias[:, cols]
            value, bend = sigmoid_parts(pre)
            act[:, cols] = half(value)
            slope[:, cols] = half(bend)
            return carry

        lax.fori_loop(0, weight.shape[1] // tile, one, 0)

    def back(grad, weight, slope, target_ref, sum_ref):
        def one(j, carry):
            cols = pl.ds(pl.multiple_of(j * tile, tile), tile)
            value = half(dot_across(grad[...], weight[cols, :]) * wide(slope[:, cols]))
            target_ref[:, cols] = value
            sum_ref[:, cols] = jnp.sum(wide(value), 0, keepdims=True)
            return carry

        lax.fori_loop(0, weight.shape[0] // tile, one, 0)

    def picks(cols, size):
        row = lax.broadcasted_iota(jnp.int32, (x_ref.shape[1], size), 0)
        return half(jnp.where(row == wanted[:, cols], 1.0, 0.0))

    @pl.when(lax.axis_index("section") == 0)
    def _():
        loads = Loads(sems)
        x_at = loads.add(x_hbm, x_ref, 0, 1)
        target_at = loads.add(target_hbm, target, 0, 1)
        one_at = loads.add(one_hbm, one_w, 0, 1)
        two_at = loads.add(two_hbm, two_w, 0, 1)
        three_at = loads.add(three_hbm, three_w, 0, 1)
        loads.start()
        loads.wait(x_at)
        padded_width = one_w.shape[0]
        for start, size in column_tiles(padded_width, tile):
            cols = slice(start, start + size)
            padded_x[:, cols] = half(dot_plain(x_ref[...], picks(cols, size)))
        loads.wait(one_at)
        layer(padded_x, one_w, bias_one, act_one, slope_one)
        loads.wait(two_at)
        layer(act_one, two_w, bias_two, act_two, slope_two)
        loads.wait(three_at + target_at)
        latent = dot_plain(act_two[...], three_w[...]) + bias_three[...]
        features = wide(target[...])
        root_latent = lax.rsqrt(jnp.sum(latent * latent, -1, keepdims=True) + epsilon)
        root_target = lax.rsqrt(jnp.sum(features * features, -1, keepdims=True) + epsilon)
        crossed = jnp.sum(latent * features, -1, keepdims=True)
        grad = half(
            -loss
            * (
                features * (root_latent * root_target)
                - (crossed * root_target * root_latent * root_latent * root_latent) * latent
            )
        )
        d_latent[...] = grad
        three_sum[...] = jnp.sum(wide(grad), 0, keepdims=True)
        back(d_latent, three_w, slope_two, d_two, two_sum)
        back(d_two, two_w, slope_one, d_one, one_sum)
        total = jnp.zeros(x_ref.shape, jnp.float32)
        for start, size in column_tiles(padded_width, tile):
            cols = slice(start, start + size)
            value = half(dot_across(d_one[...], one_w[start : start + size, :]))
            total = total + dot_across(value, picks(cols, size))
        dx_ref[...] = half(total)
        dx_copy = pltpu.make_async_copy(dx_ref, dx_hbm, dx_sem)
        dx_copy.start()

        jobs = []
        for left, right, place in (
            (act_two, d_latent, three_grad), (padded_x, d_one, one_grad), (act_one, d_two, two_grad),
        ):
            for start, size in column_tiles(left.shape[1], tile):
                jobs.append((left, right, place, start, size))
        copies = []
        for k, (left, right, place, start, size) in enumerate(jobs):
            if k >= 2:
                copies[k - 2].wait()
            held = product.at[k % 2, pl.ds(0, size), pl.ds(0, right.shape[1])]
            held[...] = half(dot_down(left[:, start : start + size], right[...]))
            copies.append(
                pltpu.make_async_copy(held, place.at[pl.ds(start, size)], product_sem.at[k % 2])
            )
            copies[k].start()
        copies[-2].wait()
        copies[-1].wait()
        dx_copy.wait()


def project_align(hidden, target, wanted, aligner, loss):
    weight_one, bias_one, weight_two, bias_two, weight_three, bias_three = aligner
    rows, width = hidden.shape
    first, second, third = weight_one.shape[1], weight_two.shape[1], weight_three.shape[1]
    vmem, anywhere = pl.BlockSpec(memory_space=pltpu.VMEM), pl.BlockSpec(memory_space=pl.ANY)

    def shape(columns, kind=jnp.bfloat16, count=rows):
        return jax.ShapeDtypeStruct((count, columns), kind)

    weights = (weight_one, weight_two, weight_three)
    results = pl.pallas_call(
        functools.partial(align_kernel, loss),
        out_shape=[
            shape(width),
            shape(first, jnp.float32, 1), shape(second, jnp.float32, 1), shape(third, jnp.float32, 1),
        ]
        + [jax.ShapeDtypeStruct(w.shape, jnp.bfloat16) for w in weights],
        in_specs=[vmem] * 4 + [anywhere] * 5,
        out_specs=[anywhere] + [vmem] * 3 + [anywhere] * 3,
        scratch_shapes=[pltpu.VMEM(a.shape, a.dtype) for a in (hidden, target, hidden) + weights]
        + [
            pltpu.VMEM((rows, k), jnp.bfloat16)
            for k in (weight_one.shape[0], first, second, first, second, third, first, second)
        ]
        + [pltpu.VMEM((2, 512, max(first, second, third)), jnp.bfloat16), DMA((5,)), DMA((2,)), DMA],
        compiler_params=pltpu.CompilerParams(vmem_limit_bytes=62 * 2**20),
        name="project_align",
    )(
        wanted, bias_one[None], bias_two[None], bias_three[None], hidden, target, *weights
    )
    return results[0], results[1:4], results[4:]


def own_place():
    section = lax.axis_index("section")
    index = lax.axis_index("dp")
    return section, index, index // 4, lax.rem(index // 2, 2), lax.rem(index, 2)


def index_of(z, y, core):
    return z * 4 + y * 2 + core


def greet(targets):
    barrier = pltpu.get_barrier_semaphore()
    for target in targets:
        pl.semaphore_signal(barrier, inc=1, device_id=target, device_id_type=MESH)
    pl.semaphore_wait(barrier, len(targets))


def greet_section(count, section, index, extra=()):
    barrier = pltpu.get_barrier_semaphore()

    def one(step, carry):
        target = (section, lax.rem(index + step, count))
        pl.semaphore_signal(barrier, inc=1, device_id=target, device_id_type=MESH)
        return carry

    lax.fori_loop(1, count, one, 0)
    for target in extra:
        pl.semaphore_signal(barrier, inc=1, device_id=target, device_id_type=MESH)
    pl.semaphore_wait(barrier, count - 1 + len(extra))


class Exchange:
    def __init__(self, count, section, index, source, target, send, recv, local, own_only):
        self.count, self.section, self.index = count, section, index
        self.source, self.target = source, target
        self.send, self.recv, self.local, self.own_only = send, recv, local, own_only

    def piece(self, other):
        return self.source if self.own_only else self.source.at[other]

    def message(self, other, slot):
        return pltpu.make_async_remote_copy(
            src_ref=self.piece(other),
            dst_ref=self.target.at[slot],
            send_sem=self.send.at[other],
            recv_sem=self.recv.at[slot],
            device_id=(self.section, other),
            device_id_type=MESH,
        )

    def start(self):
        def one(step, carry):
            self.message(lax.rem(self.index + step, self.count), self.index).start()
            return carry

        lax.fori_loop(1, self.count, one, 0)
        pltpu.make_async_copy(
            self.piece(self.index), self.target.at[self.index], self.local
        ).start()

    def finish(self):
        def one(step, carry):
            other = lax.rem(self.index + step, self.count)
            self.message(other, self.index).wait_send()
            self.message(other, other).wait_recv()
            return carry

        lax.fori_loop(1, self.count, one, 0)
        pltpu.make_async_copy(
            self.piece(self.index), self.target.at[self.index], self.local
        ).wait()


def share_kernel(count, source, target, send, recv, local):
    section, index, z, y, core = own_place()
    me = section * count + index
    everybody = 2 * count

    def device(step):
        other = lax.rem(me + step, everybody)
        return other, (other // count, lax.rem(other, count))

    def message(other, where, slot):
        return remote_copy(
            source, target.at[slot // count, lax.rem(slot, count)], send.at[other], recv.at[slot], where
        )

    barrier = pltpu.get_barrier_semaphore()

    def greet_one(step, carry):
        pl.semaphore_signal(barrier, inc=1, device_id=device(step)[1], device_id_type=MESH)
        return carry

    def start_one(step, carry):
        other, where = device(step)
        message(other, where, me).start()
        return carry

    def finish_one(step, carry):
        other, where = device(step)
        message(other, where, me).wait_send()
        message(other, where, other).wait_recv()
        return carry

    lax.fori_loop(1, everybody, greet_one, 0)
    pl.semaphore_wait(barrier, everybody - 1)
    own = pltpu.make_async_copy(source, target.at[section, index], local)
    own.start()
    lax.fori_loop(1, everybody, start_one, 0)
    lax.fori_loop(1, everybody, finish_one, 0)
    own.wait()


def share_small(count, values):
    return pl.pallas_call(
        functools.partial(share_kernel, count),
        out_shape=jax.ShapeDtypeStruct((2, count) + values.shape, values.dtype),
        in_specs=[pl.BlockSpec(memory_space=pl.ANY)],
        out_specs=pl.BlockSpec(memory_space=pl.ANY),
        scratch_shapes=[DMA((2 * count,)), DMA((2 * count,)), DMA],
        compiler_params=pltpu.CompilerParams(collective_id=0, has_side_effects=True),
        name="share_small",
    )(values)


def gather_kernel(count, images, arrays, items, stride, *refs):
    total = len(items)
    modes = [item[0] >= 4 for item in items]
    first = [item[4] for item in items]
    starts = [item[5] for item in items]
    refs = list(refs)

    def take(amount):
        taken = refs[:amount]
        del refs[:amount]
        return taken

    part, x_ref, bias = take(3)
    src = take(arrays)
    part_out, mod_out = take(2)
    dst = take(arrays)
    kept_out = take(11)
    part_send, part_recv, part_local, local_sem, send_core, send_y, send_x, send_up, send_down, recv = take(10)
    weight_refs = take(4)
    kept = take(11)
    part_in, blend, part_sem, weight_sem, kept_sem, hidden_send, hidden_recv = refs
    depth = count // 4
    section, me, z, y, c = own_place()
    up, down = (section, me + 4), (section, me - 4)
    across, partner = (section, index_of(z, 1 - y, c)), (section, index_of(z, y, 1 - c))
    other = (1 - section, me)
    greet_section(count, section, me, (other,))
    parts = Exchange(count, section, me, part, part_out, part_send, part_recv, part_local, False)
    parts.start()

    def cut(w):
        _, axis, start, size = items[w][:4]
        return (pl.ds(start, size),) if axis == 0 else (slice(None), pl.ds(start, size))

    def slot(w, sec, blk):
        place = (sec, blk) if modes[w] else (blk,)
        return dst[items[w][0]].at[place + cut(w)]

    def source_of(w):
        return src[items[w][0]].at[cut(w)]

    def copy(w, sec, blk, target, sem, src_ref=None):
        here = slot(w, sec, blk)
        return pltpu.make_async_remote_copy(
            src_ref=here if src_ref is None else src_ref,
            dst_ref=here,
            send_sem=sem,
            recv_sem=recv.at[w, sec if modes[w] else 0, blk],
            device_id=target,
            device_id_type=MESH,
        )

    def arrived(w, sec, blk):
        copy(w, sec, blk, partner, send_core.at[w, 0, 0, 0]).wait_recv()

    def pass_on(w, zz, side, go_up, go_down, go_across, source=None):
        blk = index_of(zz, y if side == 0 else 1 - y, c)
        if go_up is not None:

            @pl.when(go_up)
            def _():
                copy(w, section, blk, up, send_up.at[w, side, zz], source).start()

        if go_down is not None:

            @pl.when(go_down)
            def _():
                copy(w, section, blk, down, send_down.at[w, side, zz], source).start()

        if go_across:
            copy(w, section, blk, across, send_y.at[w, zz], source).start()
        if modes[w]:

            @pl.when(section == 1)
            def _():
                copy(w, section, blk, other, send_x.at[w, side, zz], source).start()

        copy(w, section, blk, partner, send_core.at[w, 0, side, zz], source).start()

    def depart(w):
        pass_on(w, z, 0, z < depth - 1, z > 0, True, source_of(w))
        pltpu.make_async_copy(source_of(w), slot(w, section, me), local_sem.at[w]).start()

    def near(w, k):
        if k >= depth:
            return

        @pl.when(z >= k)
        def _():
            arrived(w, section, index_of(z - k, y, c))
            pass_on(w, z - k, 0, z < depth - 1, None, not first[w])

        @pl.when(z + k < depth)
        def _():
            arrived(w, section, index_of(z + k, y, c))
            pass_on(w, z + k, 0, None, z > 0, not first[w])

    def far(w, k):
        @pl.when(z >= k)
        def _():
            arrived(w, section, index_of(z - k, 1 - y, c))
            if first[w]:
                pass_on(w, z - k, 1, z < depth - 1, (z > 0) if k == 0 else None, False)
            else:
                pass_on(w, z - k, 1, None, None, False)

        if k > 0:

            @pl.when(z + k < depth)
            def _():
                arrived(w, section, index_of(z + k, 1 - y, c))
                pass_on(w, z + k, 1, None, (z > 0) if first[w] else None, False)

    def complete(w):
        pltpu.make_async_copy(source_of(w), slot(w, section, me), local_sem.at[w]).wait()
        for side in range(2):

            def one(zz, carry):
                arrived(w, section, index_of(zz, y if side == 0 else 1 - y, 1 - c))
                return carry

            lax.fori_loop(0, depth, one, 0)

    def load(w):
        return pltpu.make_async_copy(dst[w], weight_refs[w], weight_sem.at[w])

    def modulate():
        parts.finish()
        copy_in = pltpu.make_async_copy(part_out, part_in, part_sem)
        copy_in.start()
        copy_in.wait()
        total_mod = wide(part_in[0])
        for device in range(1, count):
            total_mod = total_mod + wide(part_in[device])
        chunks = x_ref.shape[1] // LANES
        for image in range(images):
            for q in range(chunks):
                at = (image * chunks + q) * 6
                cols = slice(q * LANES, (q + 1) * LANES)
                mod_out[image, 0:6, cols] = total_mod[at : at + 6]
            for k in range(6):
                start = (9 + k) * x_ref.shape[1]
                mod_out[image, k : k + 1, :] += bias[:, start : start + x_ref.shape[1]]

    store, wait_stored = stored(kept, kept_out, kept_sem)
    forward = Forward(
        images, x_ref, mod_out, bias_parts(bias), kept, blend,
        [flat(ref) for ref in weight_refs], store,
    )

    def on_first(action):
        @pl.when(section == 0)
        def _():
            action()

    def load_array(a):
        on_first(lambda: load(a).start())

    last_item = [max(w for w in range(total) if items[w][0] == a) for a in range(4)]
    events = []
    for t in range(max(starts) + stride * depth + 1):
        for w in range(total):
            k, rest = divmod(t - starts[w], stride)
            if rest or k < 0 or k > depth:
                continue
            if k == 0:
                events.append((t, functools.partial(depart, w), None))
                continue
            if first[w]:
                events.append((t, functools.partial(far, w, k - 1), None))
                events.append((t, functools.partial(near, w, k), None))
            else:
                events.append((t, functools.partial(near, w, k), None))
                events.append((t, functools.partial(far, w, k - 1), None))
            if k == depth and not modes[w]:
                events.append((t, functools.partial(complete, w), None))
                a = items[w][0]
                if w == last_item[a]:
                    events.append((t, functools.partial(load_array, a), a))
    feeds = kept[8].shape[1] // 512

    def finish_block():
        forward.leave()
        remote_copy(kept[10], kept_out[10], hidden_send, hidden_recv, other).start()

    groups = [
        [functools.partial(forward.project, part) for part in range(3)]
        + [functools.partial(forward.attend, image) for image in range(images)]
        + [forward.attended],
        [forward.middle],
        [functools.partial(forward.feed, 0, feeds)],
        [finish_block],
    ]

    def run_group(w):
        load(w).wait()
        for chunk in groups[w]:
            chunk()

    modulated = False
    for i, (t, event, ready) in enumerate(events):
        event()
        if not modulated and t == stride and events[i + 1][0] > stride:
            modulated = True
            modulate()
            on_first(forward.enter)
        if ready is not None:
            on_first(functools.partial(run_group, ready))

    for w in range(total):
        if modes[w]:
            complete(w)

            @pl.when(section == 0)
            def _():
                for side in range(2):

                    def from_x(zz, carry):
                        blk = index_of(zz, y if side == 0 else 1 - y, c)
                        arrived(w, 1, blk)
                        copy(w, 1, blk, partner, send_core.at[w, 1, side, zz]).start()
                        return carry

                    lax.fori_loop(0, depth, from_x, 0)

    for w in range(total):
        for side in range(2):

            def finish(zz, carry):
                copy(w, section, me, partner, send_core.at[w, 0, side, zz]).wait_send()
                if modes[w]:

                    @pl.when(section == 1)
                    def _():
                        copy(w, section, me, other, send_x.at[w, side, zz]).wait_send()

                    @pl.when(section == 0)
                    def _():
                        blk = index_of(zz, y if side == 0 else 1 - y, 1 - c)
                        arrived(w, 1, blk)
                        copy(w, 1, blk, partner, send_core.at[w, 1, side, zz]).wait_send()

                if side == 0:

                    @pl.when((zz == z) if first[w] else (zz >= 0))
                    def _():
                        copy(w, section, me, across, send_y.at[w, zz]).wait_send()

                if side == 0 or first[w]:

                    @pl.when((z < depth - 1) & (zz <= z))
                    def _():
                        copy(w, section, me, up, send_up.at[w, side, zz]).wait_send()

                    @pl.when((z > 0) & (zz >= z))
                    def _():
                        copy(w, section, me, down, send_down.at[w, side, zz]).wait_send()

                return carry

            lax.fori_loop(0, depth, finish, 0)
    hidden_copy = remote_copy(kept[10], kept_out[10], hidden_send, hidden_recv, other)

    @pl.when(section == 0)
    def _():
        hidden_copy.wait_send()
        wait_stored()

    @pl.when(section == 1)
    def _():
        hidden_copy.wait_recv()


def gather_forward(count, parts, inputs, images, bias, own, both, items, stride):
    arrays = list(own) + list(both)
    modes = [False] * len(own) + [True] * len(both)
    total, depth, n_arrays = len(items), count // 4, len(arrays)
    rows, width = inputs.shape
    anywhere, vmem = pl.BlockSpec(memory_space=pl.ANY), pl.BlockSpec(memory_space=pltpu.VMEM)
    shapes = [((2, count) if m else (count,)) + a.shape for a, m in zip(arrays, modes)]
    kept = kept_shapes(rows, width, images, own[2].shape[1])
    results = pl.pallas_call(
        functools.partial(gather_kernel, count, images, n_arrays, items, stride),
        out_shape=[
            jax.ShapeDtypeStruct(parts.shape, parts.dtype),
            jax.ShapeDtypeStruct((images, 8, width), jnp.float32),
        ]
        + [jax.ShapeDtypeStruct(s, a.dtype) for s, a in zip(shapes, arrays)]
        + kept,
        in_specs=[anywhere] + [vmem] * 2 + [anywhere] * n_arrays,
        out_specs=[anywhere, vmem] + [anywhere] * (n_arrays + 11),
        scratch_shapes=[
            DMA((count,)),
            DMA((count,)),
            DMA,
            DMA((total,)),
            DMA((total, 2, 2, depth)),
            DMA((total, depth)),
            DMA((total, 2, depth)),
            DMA((total, 2, depth)),
            DMA((total, 2, depth)),
            DMA((total, 2, count)),
        ]
        + [pltpu.VMEM((count,) + a.shape, a.dtype) for a in own]
        + [pltpu.VMEM(s.shape, s.dtype) for s in kept]
        + [
            pltpu.VMEM(parts.shape, parts.dtype),
            pltpu.VMEM((rows // images, width), jnp.float32),
            DMA,
            DMA((4,)),
            DMA((11,)),
            DMA,
            DMA,
        ],
        compiler_params=pltpu.CompilerParams(
            collective_id=1, has_side_effects=True, vmem_limit_bytes=63 * 2**20
        ),
        name="gather_forward",
    )(parts, inputs, bias, *arrays)
    return results[1], results[2 : 2 + n_arrays], results[2 + n_arrays :]


class Chain:
    def __init__(self, place, depth, z_first, sums, y_in, z_in, sems, out):
        self.section, self.z, self.y, self.c = place
        self.depth, self.z_first = depth, z_first
        self.sums, self.y_in, self.z_in, self.out = sums, y_in, z_in, out
        self.y_send, self.y_recv, self.z_send, self.z_recv = sems
        me = index_of(self.z, self.y, self.c)
        self.up, self.down = (self.section, me + 4), (self.section, me - 4)
        self.across = (self.section, index_of(self.z, 1 - self.y, self.c))

    def part(self, p, to):
        ref, lead = self.sums(p)
        return ref, lead + ((to,) if self.z_first else (to, self.y))

    def y_copy(self, p):
        ref, lead = self.sums(p)
        whole = self.z if self.z_first else slice(None)
        return remote_copy(
            ref.at[lead + (whole, 1 - self.y)],
            self.y_in(p),
            self.y_send.at[p],
            self.y_recv.at[p],
            self.across,
        )

    def z_copy(self, p, to, where, device):
        ref, place = self.part(p, to)
        return remote_copy(
            ref.at[place], self.z_in(p).at[where], self.z_send.at[p, to], self.z_recv.at[p, where], device
        )

    def add_z(self, p, to, where):
        self.z_copy(p, 0, where, self.across).wait_recv()
        ref, place = self.part(p, to)
        z_in = self.z_in(p)
        if self.z_first:
            for side in range(2):
                ref[place + (side,)] = half(wide(ref[place + (side,)]) + wide(z_in[where, side]))
        else:
            ref[place] = half(wide(ref[place]) + wide(z_in[where]))

    def hop(self, p, h):
        @pl.when((self.z == h) & (self.z < self.depth - 1))
        def _():
            def one(back, carry):
                to = self.depth - 1 - back
                if h > 0:
                    self.add_z(p, to, to)
                self.z_copy(p, to, to, self.up).start()
                return carry

            lax.fori_loop(0, self.depth - 1 - self.z, one, 0)

        @pl.when((self.depth - 1 - self.z == h) & (self.z > 0))
        def _():
            def one(to, carry):
                if h > 0:
                    self.add_z(p, to, to)
                self.z_copy(p, to, jnp.where(to == self.z - 1, self.depth, to), self.down).start()
                return carry

            lax.fori_loop(0, self.z, one, 0)

    def join(self, p):
        @pl.when(self.z > 0)
        def _():
            self.add_z(p, self.z, self.z)

        @pl.when(self.z < self.depth - 1)
        def _():
            self.add_z(p, self.z, self.depth)

    def begin(self, p):
        if self.z_first:
            self.hop(p, 0)
        else:
            self.y_copy(p).start()

    def move(self, p, step):
        if self.z_first:
            if step < self.depth - 1:
                self.hop(p, step)
            else:
                self.join(p)
                self.y_copy(p).start()
            return
        if step == 1:
            self.y_copy(p).wait_recv()
            y_in = self.y_in(p)

            def one(to, carry):
                ref, place = self.part(p, to)
                ref[place] = half(wide(ref[place]) + wide(y_in[to]))
                return carry

            lax.fori_loop(0, self.depth, one, 0)
        self.hop(p, step - 1)

    def last(self, p):
        ref, lead = self.sums(p)
        if self.z_first:
            self.y_copy(p).wait_recv()
            total = wide(ref[lead + (self.z, self.y)]) + wide(self.y_in(p)[...])
            self.out(p)[...] = half(total)
        else:
            self.join(p)
            self.out(p)[...] = ref[lead + (self.z, self.y)]

    def finish(self, p):
        self.y_copy(p).wait_send()

        def one(to, carry):
            @pl.when(to != self.z)
            def _():
                self.z_copy(p, to, to, self.across).wait_send()

            return carry

        lax.fori_loop(0, self.depth, one, 0)


def chain_slots(depth, first, shape):
    y_shape = shape if first else (depth,) + shape
    z_shape = (depth + 1, 2) + shape if first else (depth + 1,) + shape
    return y_shape, z_shape


def remote_copy(source, target, send, recv, device):
    return pltpu.make_async_remote_copy(
        src_ref=source,
        dst_ref=target,
        send_sem=send,
        recv_sem=recv,
        device_id=device,
        device_id_type=MESH,
    )


def reduce_kernel(count, ready, pairs, plan, far_first, far_steps, stride, *refs):
    depth = count // 4
    far_total = len(far_first)
    near_total = ready + len(plan)
    refs = list(refs)

    def take(amount):
        taken = refs[:amount]
        del refs[:amount]
        return taken

    (ready_src,) = take(1)
    left_src, right_src = take(pairs), take(pairs)
    far_src = take(far_total)
    mod_src, bias_src = take(2)
    (near_out,) = take(1)
    far_out = take(far_total)
    mod_out, bias_out = take(2)
    left, right, made, core_in, y_in, z_in, tail_y_in, tail_z_in = take(8)
    far_core_in, far_y_in, far_z_in = take(far_total), take(far_total), take(far_total)
    (
        left_sem, right_sem, ready_sem, core_send, core_recv, y_send, y_recv, z_send, z_recv,
        far_local, far_send, far_recv,
        far_y_send, far_y_recv, far_z_send, far_z_recv,
        mod_send, mod_recv, mod_local, bias_send, bias_recv, bias_local,
    ) = refs
    section, me, z, y, c = own_place()
    partner = (section, index_of(z, y, 1 - c))
    other = (1 - section, me)
    barrier = pltpu.get_barrier_semaphore()

    def greet_one(step, carry):
        target = (section, lax.rem(me + step, count))
        pl.semaphore_signal(barrier, inc=1, device_id=target, device_id_type=MESH)
        return carry

    lax.fori_loop(1, count, greet_one, 0)

    @pl.when(section == 1)
    def _():
        pl.semaphore_signal(barrier, inc=1, device_id=other, device_id_type=MESH)
        pl.semaphore_wait(barrier, count - 1)

    @pl.when(section == 0)
    def _():
        pl.semaphore_wait(barrier, count)

    rows, width = made.shape[-2:]
    mods = Exchange(count, section, me, mod_src, mod_out, mod_send, mod_recv, mod_local, True)
    biases = Exchange(count, section, me, bias_src, bias_out, bias_send, bias_recv, bias_local, False)

    order = [near_total - 1] + list(range(near_total - 1))

    def operands(p, slot):
        pair, row, column = plan[p - ready]
        return (
            pltpu.make_async_copy(
                left_src[pair].at[:, pl.ds(row * width, width)], left.at[slot], left_sem.at[slot]
            ),
            pltpu.make_async_copy(
                right_src[pair].at[:, pl.ds(column * width, width)], right.at[slot], right_sem.at[slot]
            ),
        )

    def ready_copy(p, slot):
        return pltpu.make_async_copy(
            ready_src.at[:, :, :, p], made.at[slot], ready_sem
        )

    def core_copy(p, slot):
        return remote_copy(
            made.at[slot, :, :, 1 - c], core_in.at[p], core_send.at[p], core_recv.at[p], partner
        )

    def fetch(t, slot):
        for i, p in enumerate(order):
            if p >= ready:

                @pl.when(t == i)
                def _():
                    for copy in operands(p, slot):
                        copy.start()

    def piece_of(t):
        return jnp.where(t == 0, near_total - 1, t - 1)

    def make(t):
        slot = lax.rem(t, 2)
        p = piece_of(t)

        @pl.when(t >= 2)
        def _():
            core_copy(piece_of(t - 2), slot).wait_send()

        @pl.when(t + 1 < near_total)
        def _():
            fetch(t + 1, 1 - slot)

        @pl.when(p < ready)
        def _():
            copy = ready_copy(p, slot)
            copy.start()
            copy.wait()

        @pl.when(p >= ready)
        def _():
            for copy in operands(ready, slot):
                copy.wait()
            tile = 3 * LANES
            for at in range(0, width, tile):
                cols = slice(at, at + tile)
                product = dot_down(left[slot], right[slot, :, cols])
                made[slot, :, :, :, :, cols] = half(product).reshape(depth, 2, 2, rows, tile)

        core_copy(p, slot).start()

    near = Chain(
        (section, z, y, c), depth, False,
        lambda p: (core_in, (p,)), lambda p: y_in.at[p], lambda p: z_in.at[p],
        (y_send, y_recv, z_send, z_recv), lambda p: near_out.at[p],
    )
    tail = Chain(
        (section, z, y, c), depth, True,
        lambda p: (core_in, (p,)), lambda p: tail_y_in, lambda p: tail_z_in,
        (y_send, y_recv, z_send, z_recv), lambda p: near_out.at[p],
    )
    far = [
        Chain(
            (section, z, y, c), depth, far_first[i],
            lambda p: (far_core_in[p], ()), lambda p: far_y_in[p], lambda p: far_z_in[p],
            (far_y_send, far_y_recv, far_z_send, far_z_recv), lambda p: far_out[p],
        )
        for i in range(far_total)
    ]

    def begin(t):
        slot = lax.rem(t, 2)
        p = piece_of(t)
        core_copy(p, slot).wait_recv()

        def add_side(side):
            def one(to, carry):
                core_in[p, to, side] = half(
                    wide(core_in[p, to, side]) + wide(made[slot, to, side, c])
                )
                return carry

            lax.fori_loop(0, depth, one, 0)

        add_side(1 - y)

        @pl.when(p < near_total - 1)
        def _():
            near.begin(p)

        add_side(y)

        @pl.when(p == near_total - 1)
        def _():
            tail.begin(near_total - 1)

    def far_columns(i, late):
        size = far_core_in[i].shape[-1]
        start, stop = {0: (size, size), 1: (0, size), 2: (size // 2, size)}[i]
        start, stop = (start, stop) if late else (0, start)
        return (slice(None),) * 3 + (pl.ds(start, stop - start),)

    def far_lies(i):
        at = far_columns(i, False)
        return pltpu.make_async_copy(far_src[i].at[at], far_core_in[i].at[at], far_local.at[i])

    def far_comes(i):
        at = far_columns(i, True)
        return remote_copy(
            far_src[i].at[at], far_core_in[i].at[at], far_send.at[i], far_recv.at[i], other
        )

    fetch(0, 0)

    @pl.when(section == 0)
    def _():
        for i in (1, 2):
            far_comes(i).start()

    @pl.when(section == 1)
    def _():
        for i in (0, 2):
            far_lies(i).start()

    mods.start()
    biases.start()

    def step(t, carry):
        @pl.when(t < near_total)
        def _():
            make(t)

        @pl.when((t >= 1) & (t <= near_total))
        def _():
            begin(t - 1)

        for i in range(far_total):

            @pl.when((t == far_steps[i]) & (section == 1))
            def _():
                if i != 1:
                    far_lies(i).wait()
                if i != 0:
                    far_comes(i).wait_recv()
                far[i].begin(i)

            for k in range(1, depth):

                @pl.when((t == far_steps[i] + stride * k) & (section == 1))
                def _():
                    far[i].move(i, k)

            @pl.when((t == far_steps[i] + stride * depth) & (section == 1))
            def _():
                far[i].last(i)

        for k in range(1, depth):
            p = t - 2 - stride * k

            @pl.when((p >= 0) & (p < near_total - 1))
            def _():
                near.move(p, k)

            @pl.when(t == 1 + stride * k)
            def _():
                tail.move(near_total - 1, k)

        p = t - 2 - stride * depth

        @pl.when((p >= 0) & (p < near_total - 1))
        def _():
            near.last(p)

        @pl.when(t == 1 + stride * depth)
        def _():
            tail.last(near_total - 1)

        return carry

    lax.fori_loop(0, max(near_total + 1, max(far_steps) + 1) + stride * depth, step, 0)
    for t in (near_total - 2, near_total - 1):
        core_copy(order[t], t % 2).wait_send()

    @pl.when(section == 0)
    def _():
        for i in (1, 2):
            far_comes(i).wait_send()

    @pl.when(section == 1)
    def _():
        for i in range(far_total):
            far[i].finish(i)

    def near_finish(p, carry):
        near.finish(p)
        return carry

    lax.fori_loop(0, near_total - 1, near_finish, 0)
    tail.finish(near_total - 1)
    mods.finish()
    biases.finish()


def reduce_grads(count, ready, pairs, plan, far, far_first, far_steps, stride, mods, biases):
    depth = count // 4
    pieces, rows, width = ready.shape[3:]
    near_total = pieces + len(plan)
    tokens = pairs[0][0].shape[0]
    far_shapes = [a.shape[2:] for a in far]
    kind = jnp.bfloat16
    anywhere, vmem = pl.BlockSpec(memory_space=pl.ANY), pl.BlockSpec(memory_space=pltpu.VMEM)
    n_far = len(far)
    lefts, rights = [a for a, _ in pairs], [b for _, b in pairs]

    far_slots = [chain_slots(depth, f, s) for f, s in zip(far_first, far_shapes)]
    results = pl.pallas_call(
        functools.partial(reduce_kernel, count, pieces, len(pairs), plan, far_first, far_steps, stride),
        out_shape=[jax.ShapeDtypeStruct((near_total, rows, width), kind)]
        + [jax.ShapeDtypeStruct(s, kind) for s in far_shapes]
        + [
            jax.ShapeDtypeStruct((count,) + mods.shape, mods.dtype),
            jax.ShapeDtypeStruct(biases.shape, biases.dtype),
        ],
        in_specs=[anywhere] * (1 + 2 * len(pairs) + n_far + 2),
        out_specs=[vmem] * (1 + n_far) + [anywhere] * 2,
        scratch_shapes=[
            pltpu.VMEM((2, tokens, width), kind),
            pltpu.VMEM((2, tokens, width), kind),
            pltpu.VMEM((2, depth, 2, 2, rows, width), kind),
            pltpu.VMEM((near_total, depth, 2, rows, width), kind),
            pltpu.VMEM((near_total - 1, depth, rows, width), kind),
            pltpu.VMEM((near_total - 1, depth + 1, rows, width), kind),
            pltpu.VMEM((rows, width), kind),
            pltpu.VMEM((depth + 1, 2, rows, width), kind),
        ]
        + [pltpu.VMEM((depth, 2) + s, kind) for s in far_shapes]
        + [pltpu.VMEM(s[0], kind) for s in far_slots]
        + [pltpu.VMEM(s[1], kind) for s in far_slots]
        + [
            DMA((2,)),
            DMA((2,)),
            DMA,
            DMA((near_total,)),
            DMA((near_total,)),
            DMA((near_total,)),
            DMA((near_total,)),
            DMA((near_total, depth)),
            DMA((near_total, depth + 1)),
            DMA((n_far,)),
            DMA((n_far,)),
            DMA((n_far,)),
            DMA((n_far,)),
            DMA((n_far,)),
            DMA((n_far, depth)),
            DMA((n_far, depth + 1)),
            DMA((count,)),
            DMA((count,)),
            DMA,
            DMA((count,)),
            DMA((count,)),
            DMA,
        ],
        compiler_params=pltpu.CompilerParams(
            collective_id=2, has_side_effects=True, vmem_limit_bytes=63 * 2**20
        ),
        name="reduce_grads",
    )(ready, *lefts, *rights, *far, mods, biases)
    return results[0], results[1 : 1 + n_far], results[1 + n_far], results[2 + n_far]


def padded(values, rows):
    flat = values.reshape(values.shape[0], -1)
    room = rows * LANES - flat.shape[1]
    return jnp.pad(flat, ((0, 0), (0, room))).reshape(values.shape[0], rows, LANES)


def rows_for(amount, unit):
    rows = -(-amount // LANES)
    return -(-rows // unit) * unit


def split_at(flat, sizes):
    pieces, start = [], 0
    for size in sizes:
        pieces.append(flat[..., start : start + size])
        start += size
    return pieces


def gather_plan(own, both):
    width = own[1].shape[1]
    parts = [(0, 1, j * width, width, False) for j in range(own[0].shape[1] // width)]
    parts.append((1, 1, 0, width, True))
    parts += [(2, 1, j * width, width, False) for j in range(own[2].shape[1] // width)]
    third = own[3].shape[0] // 3
    parts += [(3, 0, j * third, third, False) for j in range(3)]
    parts.append((4, 1, 0, both[0].shape[1], False))
    wide_two = both[1].shape[1] // 2
    parts += [(5, 1, j * wide_two, wide_two, True) for j in range(2)]
    parts.append((6, 1, 0, both[2].shape[1], False))
    return tuple(part + (i // 2,) for i, part in enumerate(parts))


def body(
    tokens,
    time_bins,
    labels,
    dino_feats,
    cotangent,
    time_table,
    class_table,
    ada_weight,
    ada_bias,
    qkv_weight,
    qkv_bias,
    out_weight,
    out_bias,
    mlp_in_weight,
    mlp_in_bias,
    mlp_out_weight,
    mlp_out_bias,
    align_weight_one,
    align_bias_one,
    align_weight_two,
    align_bias_two,
    align_weight_three,
    align_bias_three,
):
    count = lax.axis_size("dp")
    first_section = lax.axis_index("section") == 0
    index = lax.axis_index("dp")
    images, _, image_rows, model_width = tokens.shape
    rows_all = images * image_rows
    shard = out_weight.shape[1]
    kernels = count % 4 == 0 and shard % 8 == 0

    block_biases = (qkv_bias, out_bias, mlp_in_bias, mlp_out_bias, ada_bias)
    align_biases = (align_bias_one, align_bias_two, align_bias_three)
    block_sizes = [b.size for b in block_biases]
    align_sizes = [b.size for b in align_biases]
    indices = jnp.concatenate([time_bins, labels], 1).reshape(-1)
    pack = jnp.concatenate(
        [wide(half(b.reshape(-1))) for b in block_biases + align_biases] + [wide(indices)]
    )
    pack = padded(pack[None], rows_for(pack.size, 8))[0]
    if kernels:
        packs = share_small(count, pack).reshape(2, count, -1)
    else:
        packs = lax.all_gather(pack.reshape(-1), ("section", "dp")).reshape(2, count, -1)
    own_pack = jnp.where(first_section, packs[0], packs[1])
    block_full = [b.reshape(-1) for b in split_at(own_pack[:, : sum(block_sizes)], block_sizes)]
    bias_row = jnp.concatenate(
        [block_full[0][:model_width], jnp.zeros((model_width,), jnp.float32), block_full[0][model_width:]]
        + block_full[1:]
    )[None]
    start = sum(block_sizes)
    align_bias_full = [
        b.reshape(-1) for b in split_at(packs[:, :, start : start + sum(align_sizes)], align_sizes)
    ]
    start = start + sum(align_sizes)
    pairs = own_pack[:, start : start + 2 * images].astype(jnp.int32).reshape(count * images, 2)

    time_hot = pairs[:, :1] == jnp.arange(time_table.shape[0], dtype=jnp.int32)[None]
    class_hot = pairs[:, 1:] == jnp.arange(class_table.shape[0], dtype=jnp.int32)[None]
    cond = matmul(half(time_hot), half(time_table)) + matmul(half(class_hot), half(class_table))
    cond_act = half(jax.nn.silu(cond))
    ada_half = half(ada_weight[0])
    mod_wide = ada_half.shape[1]
    mod_parts = half(matmul(cond_act, ada_half)).reshape(count, images, mod_wide)
    mod_rows = rows_for(images * mod_wide, 16)

    start_rows = tokens.reshape(rows_all, model_width)
    own = [half(w[0]) for w in (qkv_weight, out_weight, mlp_in_weight, mlp_out_weight)]
    both = [half(w) for w in (align_weight_one, align_weight_two, align_weight_three)]
    one_rows = both[0].shape[0]
    one_padded = -(-one_rows // 16) * 16
    both[0] = jnp.pad(both[0], ((0, one_padded - one_rows), (0, 0)))
    place = jnp.arange(2 * count * one_padded, dtype=jnp.int32)
    owner, row = place // one_padded, place % one_padded
    wanted = jnp.where(row < one_rows, owner * one_rows + row, -1)[None]
    if kernels:
        chunked = mod_parts.reshape(count, images, 6, model_width // LANES, LANES)
        parts = padded(jnp.swapaxes(chunked, 2, 3).reshape(count, -1), mod_rows)
        modulation, gathered, kept = gather_forward(
            count, parts, start_rows, images, bias_row, own, both, gather_plan(own, both), 2
        )
        weights = [g.reshape(-1, g.shape[-1]) for g in gathered[:4]]
        align_weights = [g.reshape(-1, g.shape[-1]) for g in gathered[4:]]
        hidden = kept[10]
    else:
        modulation = lax.psum_scatter(wide(mod_parts), "dp", scatter_dimension=0, tiled=True)
        modulation = modulation.reshape(images, 6, model_width) + block_full[4].reshape(6, model_width)
        modulation = jnp.pad(modulation, ((0, 0), (0, 2), (0, 0)))
        weights = [lax.all_gather(w, "dp", axis=0, tiled=True) for w in own]
        align_weights = [lax.all_gather(w, ("section", "dp"), axis=0, tiled=True) for w in both]
        blank = kept_shapes(rows_all, model_width, images, weights[2].shape[1])
        blank = [jnp.zeros(b.shape, b.dtype) for b in blank[:10]]
        kept = block_forward(0, start_rows, modulation, bias_row, weights, blank)
        received = lax.ppermute(kept[10], "section", [(0, 1)])
        hidden = jnp.where(first_section, kept[10], received)
    aligner = (
        align_weights[0], align_bias_full[0], align_weights[1], align_bias_full[1],
        align_weights[2], align_bias_full[2],
    )

    target = dino_feats.reshape(rows_all, -1)
    *kept, final = block_forward(1, hidden, modulation, bias_row, weights, kept[:10])
    align_hidden, final = lax.optimization_barrier((hidden, final))
    grad_align, align_sums, align_grads = project_align(align_hidden, target, wanted, aligner, loss_weight)
    attn_input, qkv_rows, probs, mixed, attn_branch, after, mlp_input, slope, mlp_act, mlp_branch = kept

    def sources(block_input, grad):
        return (block_input, grad, mlp_branch, slope, after, attn_branch, probs, qkv_rows)

    last_sources = sources(hidden, cotangent.reshape(rows_all, model_width))
    if kernels:
        far = [g.reshape(2, count // 4, 2, 2, *w.shape) for g, w in zip(align_grads, both)]
        far = [far[2], far[0], far[1]]
        results = block_backward(count, 1, modulation, last_sources, weights, grad_align, far)
        grads, far_first_sum, far_halves = results[:10], results[10:13], results[13:]
    else:
        blank = block_backward(count, 0, modulation, last_sources, weights)
        grads = block_backward(count, 1, modulation, last_sources, weights, previous=blank)
        received = lax.ppermute(grad_align, "section", [(0, 1)])
        grad_hidden = half(wide(grads[0]) + wide(received))
        received = lax.ppermute(grad_hidden, "section", [(1, 0)])
        grads = [jnp.where(first_section, received, grad_hidden)] + list(grads[1:])
    grads = block_backward(
        count, 0, modulation, sources(start_rows, grads[0]), weights, previous=grads
    )
    in_grads, grad_qkv, grad_attn, grad_pre, grad_branch, grad_mod = grads[:6]
    grad_down = half(transposed(mlp_act, grad_branch))
    outputs = jnp.where(first_section, hidden, final)
    grad_mod = half(grad_mod[:, :6])
    sums = [g[0] for g in grads[6:]]
    sums[0] = jnp.concatenate([sums[0][:model_width], sums[0][2 * model_width :]])
    align_bias_grads = [jnp.where(first_section, g, 0.0) for g in align_sums]
    align_sums = [jnp.moveaxis(g.reshape(2, count, -1), 0, 1).reshape(count, -1) for g in align_bias_grads]
    bias_flat = jnp.concatenate([g.reshape(count, -1) for g in sums] + align_sums, 1)
    if kernels:
        tall = grad_down.shape[0] // (count * shard)
        n_qkv, n_in = 3, weights[2].shape[1] // model_width
        ready = grad_down.reshape(count // 4, 2, 2, tall, shard, model_width)
        products = ((mlp_input, grad_pre), (attn_input, grad_qkv), (mixed, grad_attn))
        plan = [(0, 0, j) for j in range(n_in)] + [(1, 0, j) for j in range(n_qkv)] + [(2, 0, 0)]
        bias_grad_rows = rows_for(bias_flat.shape[1], 8)
        near_sum, far_sum, mods, bias_parts_sum = reduce_grads(
            count, ready, products, plan, far_halves, (False, True, False), (3, 7, 9), 2,
            padded(grad_mod.reshape(1, -1), mod_rows)[0], padded(bias_flat, bias_grad_rows),
        )
        grad_mods = mods.reshape(count, -1)[:, : images * mod_wide]
        bias_sum = jnp.sum(bias_parts_sum, 0).reshape(-1)
        grad_down_weight = wide(near_sum[:tall]).reshape(-1, model_width)
        grad_in_weight = wide(jnp.concatenate([near_sum[tall + j] for j in range(n_in)], 1))
        grad_qkv_weight = wide(jnp.concatenate([near_sum[tall + n_in + j] for j in range(n_qkv)], 1))
        grad_out_weight = wide(near_sum[tall + n_in + n_qkv])
        far_sum = [wide(jnp.where(first_section, a, b)) for a, b in zip(far_first_sum, far_sum)]
        align_out = [far_sum[1][:one_rows], far_sum[2], far_sum[0]]
    else:
        grad_mods = lax.all_gather(grad_mod.reshape(-1), "dp")
        bias_sum = lax.psum_scatter(bias_flat, "dp", scatter_dimension=0, tiled=True).reshape(-1)
        weight_grads = (
            transposed(attn_input, grad_qkv),
            transposed(mixed, grad_attn),
            transposed(mlp_input, grad_pre),
            wide(grad_down),
        )
        reduced = [
            lax.psum_scatter(g, "dp", scatter_dimension=0, tiled=True) for g in weight_grads
        ]
        grad_qkv_weight, grad_out_weight, grad_in_weight, grad_down_weight = reduced
        align_out = [
            lax.psum_scatter(
                jnp.where(first_section, wide(g), 0.0), ("section", "dp"), scatter_dimension=0, tiled=True
            )
            for g in align_grads
        ]
        align_out[0] = align_out[0][:one_rows]

    grad_mods = grad_mods.reshape(count * images, mod_wide)
    grad_ada = transposed(cond_act, grad_mods)
    mod_sums = jnp.sum(wide(grad_mods), 0)
    ada_share = mod_wide // count
    grad_ada_bias = lax.dynamic_slice(mod_sums, (index * ada_share,), (ada_share,))
    cond_part = times_transpose(grad_mods, ada_half)
    block_sum = sum(block_sizes[:4])
    grad_biases = split_at(bias_sum[:block_sum], block_sizes[:4])
    align_share = split_at(bias_sum[block_sum : block_sum + 2 * sum(align_sizes)], [2 * a for a in align_sizes])
    align_share = jnp.concatenate([a.reshape(2, -1) for a in align_share], 1)
    packet = jnp.concatenate([cond_part.reshape(-1), align_share.reshape(-1)])
    packet = packet + lax.ppermute(packet, "section", [(0, 1), (1, 0)])
    cond_grad = packet[: cond_part.size].reshape(cond_part.shape)
    align_share = packet[cond_part.size :].reshape(2, -1)
    align_share = jnp.where(first_section, align_share[0], align_share[1])
    align_bias_out = split_at(align_share, align_sizes)
    cond_grad = local_grad(jax.nn.silu, cond, cond_grad)

    def table_grad(hot):
        return lax.dot_general(
            wide(hot),
            cond_grad,
            (((0,), (0,)), ((), ())),
            precision=lax.Precision.HIGHEST,
            preferred_element_type=jnp.float32,
        )

    whole_rows = (1, images, 1, image_rows, model_width)
    return (
        outputs.reshape(whole_rows),
        in_grads.reshape(whole_rows),
        table_grad(time_hot),
        table_grad(class_hot),
        grad_ada[None],
        grad_ada_bias[None],
        grad_qkv_weight[None],
        grad_biases[0][None],
        grad_out_weight[None],
        grad_biases[1][None],
        grad_in_weight[None],
        grad_biases[2][None],
        grad_down_weight[None],
        grad_biases[3][None],
        align_out[0],
        align_bias_out[0],
        align_out[1],
        align_bias_out[1],
        align_out[2],
        align_bias_out[2],
    )


def solution(mesh):
    placed = (
        P(None, "dp", None, None),
        P(None, "dp"),
        P(None, "dp"),
        P(None, "dp", None, None),
        P(None, "dp", None, None),
        P(None, "dp"),
        P(None, "dp"),
        P("section", "dp", None),
        P("section", "dp"),
        P("section", "dp", None),
        P("section", "dp"),
        P("section", "dp", None),
        P("section", "dp"),
        P("section", "dp", None),
        P("section", "dp"),
        P("section", "dp", None),
        P("section", "dp"),
        P(("section", "dp"), None),
        P(("section", "dp")),
        P(("section", "dp"), None),
        P(("section", "dp")),
        P(("section", "dp"), None),
        P(("section", "dp")),
    )
    return jax.shard_map(
        body,
        mesh=mesh,
        in_specs=placed,
        out_specs=(
            P("section", None, "dp", None, None),
            P("section", None, "dp", None, None),
        )
        + placed[5:],
        check_vma=False,
    )
```

```python
import functools

import jax
import jax.numpy as jnp
from jax import lax
from jax.experimental import pallas as pl
from jax.experimental.pallas import tpu as pltpu
from jax.sharding import PartitionSpec as P

HEADS = 16
HD = 72
LANES = 128
MESH = pl.DeviceIdType.MESH
DMA = pltpu.SemaphoreType.DMA

epsilon = 1e-06
loss_weight = 0.5


def matmul(left, right):
    return jnp.dot(left, right, preferred_element_type=jnp.float32)


def transposed(left, right):
    return lax.dot_general(
        left, right, (((0,), (0,)), ((), ())), preferred_element_type=jnp.float32
    )


def times_transpose(grad_rows, weight):
    return lax.dot_general(
        grad_rows, weight, (((1,), (1,)), ((), ())), preferred_element_type=jnp.float32
    )


def local_grad(function, point, grad_value):
    return jax.vjp(function, point)[1](grad_value)[0]


def half(values):
    return values.astype(jnp.bfloat16)


def wide(values):
    return values.astype(jnp.float32)


GELU_SLOPE = 0.7978845608028654
GELU_CUBE = 0.044715


def dot_plain(left, right):
    return lax.dot_general(left, right, (((1,), (0,)), ((), ())), preferred_element_type=jnp.float32)


def dot_across(left, right):
    return lax.dot_general(left, right, (((1,), (1,)), ((), ())), preferred_element_type=jnp.float32)


def dot_down(left, right):
    return lax.dot_general(left, right, (((0,), (0,)), ((), ())), preferred_element_type=jnp.float32)


class Loads:
    def __init__(self, sems):
        self.sems, self.copies = sems, []

    def add(self, source, target, axis, tiles):
        size = source.shape[axis] // tiles
        first = len(self.copies)
        for j in range(tiles):
            place = (pl.ds(j * size, size),) if axis == 0 else (slice(None), pl.ds(j * size, size))
            self.copies.append(
                pltpu.make_async_copy(source.at[place], target.at[place], self.sems.at[first + j])
            )
        return list(range(first, first + tiles))

    def start(self):
        for copy in self.copies:
            copy.start()

    def wait(self, places):
        for place in places:
            self.copies[place].wait()


def head_window(head):
    low = head * HD
    start = low // LANES * LANES
    stop = -(-(low + HD) // LANES) * LANES
    return low, start, stop - start


def head_mask(head, rows):
    low, start, size = head_window(head)
    lane = lax.broadcasted_iota(jnp.int32, (rows, size), 1) + start
    return (lane >= low) & (lane < low + HD)


def masked(mask, values):
    return jnp.where(mask, values, jnp.zeros_like(values))


def row_norm(values):
    centred = values - jnp.mean(values, -1, keepdims=True)
    inverse = lax.rsqrt(jnp.mean(centred * centred, -1, keepdims=True) + epsilon)
    return centred * inverse, inverse


def row_norm_back(grad, normed, inverse):
    return inverse * (
        grad
        - jnp.mean(grad, -1, keepdims=True)
        - normed * jnp.mean(grad * normed, -1, keepdims=True)
    )


def column_tiles(total, tile):
    return [(at, min(tile, total - at)) for at in range(0, total, tile)]


class Forward:
    def __init__(self, images, x_ref, mod_ref, biases, kept, blend, weights, store):
        self.images, self.x_ref, self.mod_ref = images, x_ref, mod_ref
        self.qkv_bias, self.out_bias, self.in_bias, self.down_bias = biases
        (
            self.attn_in, self.qkv, self.probs, self.mixed, self.attn_branch, self.after,
            self.mlp_in, self.slope, self.act, self.mlp_branch, self.output,
        ) = kept
        self.blend, self.weights, self.store = blend, weights, store
        self.rows, self.width = x_ref.shape
        self.each = self.rows // images

    def at(self, image):
        return pl.ds(pl.multiple_of(image * self.each, self.each), self.each)

    def mod(self, image, k):
        return self.mod_ref[image, pl.ds(k, 1), :]

    def per_image(self, action):
        def one(image, carry):
            action(image, self.at(image))
            return carry

        lax.fori_loop(0, self.images, one, 0)

    def enter(self):
        def one(image, at):
            normed, _ = row_norm(wide(self.x_ref[at, :]))
            self.attn_in[at, :] = half(normed * (1.0 + self.mod(image, 1)) + self.mod(image, 0))

        self.per_image(one)
        self.store(0)

    def project_all(self, ready=None):
        def one(part, carry):
            if ready is not None:
                for third in range(3):

                    @pl.when(part == third)
                    def _():
                        ready(third)

            cols = pl.ds(pl.multiple_of(part * self.width, LANES), self.width)
            product = dot_plain(self.attn_in[...], self.weights[0](cols))
            self.qkv[:, cols] = half(product + self.qkv_bias[:, cols])
            return carry

        lax.fori_loop(0, 3, one, 0)
        self.store(1)

    def attend(self, image):
        at, each, width = self.at(image), self.each, self.width
        for head in range(HEADS):
            low, start, size = head_window(head)
            mask = head_mask(head, each)
            cols = [slice(part * width + start, part * width + start + size) for part in range(3)]
            queries = masked(mask, self.qkv[at, cols[0]])
            scores = dot_across(queries, self.qkv[at, cols[1]]) * HD ** (-0.5)
            powers = jnp.exp(scores - jnp.max(scores, -1, keepdims=True))
            soft = half(powers * (1.0 / jnp.sum(powers, -1, keepdims=True)))
            self.probs[image, head] = soft
            fresh = dot_plain(soft, self.qkv[at, cols[2]])
            window = slice(start, start + size)
            self.blend[:, window] = jnp.where(mask, fresh, self.blend[:, window])
        self.mixed[at, :] = half(self.blend[...])

    def attend_all(self):
        def one(image, carry):
            self.attend(image)
            return carry

        lax.fori_loop(0, self.images, one, 0)
        self.attended()

    def attended(self):
        self.store(2)
        self.store(3)

    def middle(self):
        branch = dot_plain(self.mixed[...], self.weights[1](slice(0, self.width))) + self.out_bias[...]
        self.attn_branch[...] = half(branch)
        self.store(4)

        def one(image, at):
            joined = wide(self.x_ref[at, :]) + self.mod(image, 2) * wide(self.attn_branch[at, :])
            self.after[at, :] = joined
            normed, _ = row_norm(joined)
            self.mlp_in[at, :] = half(normed * (1.0 + self.mod(image, 4)) + self.mod(image, 3))

        self.per_image(one)
        self.store(5)
        self.store(6)

    def feed(self, ready=None, tile=512):
        feeds = self.act.shape[1] // tile

        def one(j, carry):
            if ready is not None:
                for third in range(3):

                    @pl.when(j == feeds * third // 3)
                    def _():
                        ready(third)

            cols = pl.ds(pl.multiple_of(j * tile, tile), tile)
            pre = dot_plain(self.mlp_in[...], self.weights[2](cols)) + self.in_bias[:, cols]
            square = pre * pre
            bend = jnp.tanh(GELU_SLOPE * pre * (1.0 + GELU_CUBE * square))
            self.act[:, cols] = half(0.5 * pre * (1.0 + bend))
            self.slope[:, cols] = half(
                0.5 * (1.0 + bend)
                + 0.5 * pre * (1.0 - bend * bend) * (GELU_SLOPE + 3.0 * GELU_SLOPE * GELU_CUBE * square)
            )
            return carry

        lax.fori_loop(0, feeds, one, 0)
        self.store(7)
        self.store(8)

    def leave(self):
        branch = dot_plain(self.act[...], self.weights[3](slice(0, self.width))) + self.down_bias[...]
        self.mlp_branch[...] = half(branch)
        self.store(9)

        def one(image, at):
            self.output[at, :] = half(
                self.after[at, :] + self.mod(image, 5) * wide(self.mlp_branch[at, :])
            )

        self.per_image(one)
        self.store(10)


def kept_shapes(rows, width, images, hidden_width):
    each = rows // images
    thin = jax.ShapeDtypeStruct((rows, width), jnp.bfloat16)
    fat = jax.ShapeDtypeStruct((rows, hidden_width), jnp.bfloat16)
    return [
        thin, jax.ShapeDtypeStruct((rows, 3 * width), jnp.bfloat16),
        jax.ShapeDtypeStruct((images, HEADS, each, each), jnp.bfloat16), thin, thin,
        jax.ShapeDtypeStruct((rows, width), jnp.float32), thin, fat, fat, thin, thin,
    ]


def stored(refs, places, sems):
    copies = [pltpu.make_async_copy(a, b, sems.at[k]) for k, (a, b) in enumerate(zip(refs, places))]

    def wait():
        for copy in copies:
            copy.wait()

    return lambda k: copies[k].start(), wait


def flat(ref):
    def columns(cols):
        values = ref[:, :, cols]
        return values.reshape(values.shape[0] * values.shape[1], values.shape[2])

    return columns


def forward_kernel(images, own_section, *refs):
    x_hbm, mod_ref, bias = refs[:3]
    weights_hbm = refs[3:7]
    kept_out = refs[17:28]
    weights = refs[28:32]
    x_ref, *kept = refs[32:44]
    blend, load_sem, kept_sem = refs[44:]

    @pl.when(lax.axis_index("section") == own_section)
    def _():
        loads = Loads(load_sem)
        x_at = loads.add(x_hbm, x_ref, 0, 1)
        qkv_at = loads.add(weights_hbm[0], weights[0], 1, 3)
        out_at = loads.add(weights_hbm[1], weights[1], 0, 1)
        in_at = loads.add(weights_hbm[2], weights[2], 1, 3)
        down_at = loads.add(weights_hbm[3], weights[3], 0, 3)
        loads.start()
        store, wait_stored = stored(kept, kept_out, kept_sem)
        columns = [functools.partial(lambda ref, cols: ref[:, cols], ref) for ref in weights]
        forward = Forward(images, x_ref, mod_ref, bias_parts(bias), kept, blend, columns, store)
        loads.wait(x_at)
        forward.enter()
        forward.project_all(lambda part: loads.wait([qkv_at[part]]))
        forward.attend_all()
        loads.wait(out_at)
        forward.middle()
        forward.feed(lambda third: loads.wait([in_at[third]]))
        loads.wait(down_at)
        forward.leave()
        wait_stored()


def bias_parts(bias):
    width = bias.shape[1] // 15
    places = ((0, 3), (3, 1), (4, 4), (8, 1))
    return [bias.at[:, start * width : (start + size) * width] for start, size in places]


def block_forward(own_section, inputs, modulation, bias, weights, previous):
    rows, width = inputs.shape
    images = modulation.shape[0]
    each = rows // images
    kept = kept_shapes(rows, width, images, weights[2].shape[1])
    vmem, anywhere = pl.BlockSpec(memory_space=pltpu.VMEM), pl.BlockSpec(memory_space=pl.ANY)
    return pl.pallas_call(
        functools.partial(forward_kernel, images, own_section),
        out_shape=kept,
        in_specs=[anywhere, vmem, vmem] + [anywhere] * 14,
        out_specs=[anywhere] * 11,
        scratch_shapes=[pltpu.VMEM(w.shape, w.dtype) for w in weights]
        + [pltpu.VMEM(inputs.shape, inputs.dtype)]
        + [pltpu.VMEM(s.shape, s.dtype) for s in kept]
        + [pltpu.VMEM((each, width), jnp.float32), DMA((11,)), DMA((11,))],
        input_output_aliases={7 + k: k for k in range(10)},
        compiler_params=pltpu.CompilerParams(vmem_limit_bytes=63 * 2**20),
        name="block_forward",
    )(inputs, modulation, bias, *weights, *previous)


def backward_kernel(count, images, own_section, fresh, kept, *refs):
    refs = list(refs)

    def take(amount):
        taken = refs[:amount]
        del refs[:amount]
        return taken

    (mod_ref,) = take(1)
    sources = take(8)
    weights_hbm = take(4)
    if fresh:
        (extra_hbm,) = take(1)
        far_src = take(3)
    if kept:
        take(10)
    out_hbm = take(10)
    if fresh:
        far_out, half_out = take(3), take(3)
    held = take(8)
    in_w, down_w = take(2)
    outs = take(9)
    wide_grad, blend, load_sem, out_sem, late_sem = take(5)
    x_ref, dout, mlp_branch, slope, after, attn_branch, probs, qkv_ref = held
    dx_half, d_qkv, d_attn, d_branch, d_mod, qkv_sum, attn_sum, pre_sum, branch_sum = outs
    d_pre, half_grad = slope, dx_half
    out_refs = [dx_half, d_qkv, d_attn, d_pre, d_branch, d_mod, qkv_sum, attn_sum, pre_sum, branch_sum]
    rows, width = x_ref.shape
    each = rows // images
    hidden_width = in_w.shape[1]
    tile = 512
    section = lax.axis_index("section")
    dx_ref = wide_grad.at[1]
    grad_ref = wide_grad.at[0]

    feeds = hidden_width // tile
    if fresh:
        extra, extra_send, extra_recv, grad_send, grad_recv = take(5)
        place = own_place()
        other = (1 - section, place[1])
        greet_section(count, section, place[1], (other,))
        extra_copy = remote_copy(extra_hbm, extra, extra_send, extra_recv, other)

        def grad_copy(image):
            at = pl.ds(pl.multiple_of(image * each, each), each)
            return remote_copy(
                dx_half.at[at], out_hbm[0].at[at], grad_send.at[image], grad_recv.at[image], other
            )

        @pl.when(section != own_section)
        def _():
            extra_copy.start()
            far_sums(count, place, far_src, far_out, half_out, refs)
            extra_copy.wait_send()

            def one(image, carry):
                grad_copy(image).wait_recv()
                return carry

            lax.fori_loop(0, images, one, 0)

    @pl.when(section == own_section)
    def _():
        loads = Loads(load_sem)
        places = {}
        qkv_w = in_w.at[:, pl.ds(0, weights_hbm[0].shape[1])]
        out_w = down_w.at[pl.ds(0, width)]
        out_load = pltpu.make_async_copy(weights_hbm[1], out_w, late_sem.at[0])
        qkv_load = pltpu.make_async_copy(weights_hbm[0], qkv_w, late_sem.at[1])
        for name in (1, 2, "down", 3, "in", 4, 5, 6, 7, 0):
            if name == "down":
                places[name] = loads.add(weights_hbm[3], down_w, 0, 3)
            elif name == "in":
                places[name] = loads.add(weights_hbm[2], in_w, 0, 3)
            else:
                places[name] = loads.add(sources[name], held[name], 0, 1)
        loads.start()
        store, wait_stored = stored(out_refs, out_hbm, out_sem)

        def per_image(action):
            def one(image, carry):
                action(image, pl.ds(pl.multiple_of(image * each, each), each))
                return carry

            lax.fori_loop(0, images, one, 0)

        def mod(image, k):
            return mod_ref[image, pl.ds(k, 1), :]

        def sums(image, k, values):
            d_mod[image, pl.ds(k, 1), :] = jnp.sum(values, 0, keepdims=True)

        def enter(image, at):
            grad = wide(dout[at, :])
            d_branch[at, :] = half(grad * mod(image, 5))
            sums(image, 5, grad * wide(mlp_branch[at, :]))

        loads.wait(places[1] + places[2])
        per_image(enter)
        branch_sum[...] = jnp.sum(wide(d_branch[...]), 0, keepdims=True)
        store(4)
        store(9)
        loads.wait(places[3])

        def feed(j, carry):
            for third in range(3):

                @pl.when(j == feeds * third // 3)
                def _():
                    loads.wait([places["down"][third]])

            cols = pl.ds(pl.multiple_of(j * tile, tile), tile)
            grad = half(dot_across(d_branch[...], down_w[cols, :]) * wide(slope[:, cols]))
            d_pre[:, cols] = grad
            pre_sum[:, cols] = jnp.sum(wide(grad), 0, keepdims=True)
            return carry

        lax.fori_loop(0, feeds, feed, 0)
        out_load.start()
        store(3)
        store(8)
        loads.wait(places["in"])
        for start, size in column_tiles(width, 512):
            grad_ref[:, start : start + size] = dot_across(d_pre[...], in_w[start : start + size, :])
        qkv_load.start()

        def middle(image, at):
            grad_in = grad_ref[at, :]
            normed, inverse = row_norm(after[at, :])
            sums(image, 4, grad_in * normed)
            sums(image, 3, grad_in)
            grad = wide(dout[at, :]) + row_norm_back(grad_in * (1.0 + mod(image, 4)), normed, inverse)
            dx_ref[at, :] = grad
            d_attn[at, :] = half(grad * mod(image, 2))
            sums(image, 2, grad * wide(attn_branch[at, :]))

        loads.wait(places[4] + places[5])
        per_image(middle)
        attn_sum[...] = jnp.sum(wide(d_attn[...]), 0, keepdims=True)
        store(2)
        store(7)
        out_load.wait()
        half_grad[...] = half(dot_across(d_attn[...], out_w[...]))
        loads.wait(places[6] + places[7])

        def attend(image, at):
            for head in range(HEADS):
                low, start, size = head_window(head)
                mask = head_mask(head, each)
                window = slice(start, start + size)
                cols = [slice(part * width + start, part * width + start + size) for part in range(3)]
                grad = masked(mask, half_grad[at, window])
                soft = probs[image, head]
                grad_soft = dot_across(grad, qkv_ref[at, cols[2]])
                weighed = wide(soft) * grad_soft
                grad_scores = half(weighed - wide(soft) * jnp.sum(weighed, -1, keepdims=True))
                made = (
                    dot_plain(grad_scores, qkv_ref[at, cols[1]]) * HD ** (-0.5),
                    dot_down(grad_scores, qkv_ref[at, cols[0]]) * HD ** (-0.5),
                    dot_down(soft, grad),
                )
                for part in range(3):
                    blend[:, cols[part]] = jnp.where(mask, made[part], blend[:, cols[part]])
            d_qkv[at, :] = half(blend[...])

        def leave(image, at):
            grad_in = grad_ref[at, :]
            normed, inverse = row_norm(wide(x_ref[at, :]))
            sums(image, 1, grad_in * normed)
            sums(image, 0, grad_in)
            grad = dx_ref[at, :] + row_norm_back(grad_in * (1.0 + mod(image, 1)), normed, inverse)
            if fresh:
                grad = grad + wide(extra[at, :])
            dx_half[at, :] = half(grad)

        loads.wait(places[0])
        qkv_load.wait()
        if fresh:
            extra_copy.wait_recv()

            def finish(image, at):
                attend(image, at)
                for start, size in column_tiles(width, 512):
                    grad_ref[at, start : start + size] = dot_across(
                        d_qkv[at, :], qkv_w[start : start + size, :]
                    )
                leave(image, at)
                grad_copy(image).start()

            per_image(finish)
            store(1)
        else:
            per_image(attend)
            store(1)
            for start, size in column_tiles(width, 512):
                grad_ref[:, start : start + size] = dot_across(
                    d_qkv[...], qkv_w[start : start + size, :]
                )
            per_image(leave)
        store(0)
        qkv_sum[...] = jnp.sum(wide(d_qkv[...]), 0, keepdims=True)
        store(5)
        store(6)
        wait_stored()
        if fresh:

            def one(image, carry):
                grad_copy(image).wait_send()
                return carry

            lax.fori_loop(0, images, one, 0)
            total = len(FAR_CUTS)
            sems = refs[3 * total + 4 : 3 * total + 6]
            for i in range(total):
                if i in FAR_EARLY:
                    far_half_copy(i, None, half_out, sems, other).wait_recv()


FAR_CUTS = ((2, 2, 0, False), (2, 2, 1, False), (1, 2, 0, False), (1, 2, 1, False), (0, 1, 0, True))
FAR_EARLY = (0, 4)


def far_shape(cut, shapes):
    rows, columns = shapes[cut[0]]
    return (rows, columns // cut[1])


def far_place(cut, shapes):
    size = far_shape(cut, shapes)[1]
    return (slice(None), pl.ds(cut[2] * size, size))


def far_scratch(count, shapes):
    depth, kind, total = count // 4, jnp.bfloat16, len(FAR_CUTS)
    parts = [far_shape(cut, shapes) for cut in FAR_CUTS]
    tall, wide_most = max(s[0] for s in parts), max(s[1] for s in parts)
    slots = [chain_slots(depth, cut[3], s) for cut, s in zip(FAR_CUTS, parts)]
    return (
        [pltpu.VMEM((2, depth, 2) + s, kind) for s in parts]
        + [pltpu.VMEM((depth, 2, tall, wide_most), kind)]
        + [pltpu.VMEM(s[0], kind) for s in slots]
        + [pltpu.VMEM(s[1], kind) for s in slots]
        + [DMA, DMA((2, total)), DMA((2, total)), DMA((total,)), DMA((total,))]
        + [DMA((total,)), DMA((total,)), DMA((total, depth)), DMA((total, depth + 1))]
    )


def far_half_copy(i, source, half_out, sems, other):
    cut = FAR_CUTS[i]
    shapes = [ref.shape[2:] for ref in half_out]
    place = half_out[cut[0]].at[(slice(None), slice(None)) + far_place(cut, shapes)]
    if i not in FAR_EARLY:
        return pltpu.make_async_copy(place if source is None else source, place, sems[0].at[i])
    return remote_copy(
        place if source is None else source, place, sems[0].at[i], sems[1].at[i], other
    )


def far_sums(count, place, far_src, far_out, half_out, refs):
    depth, total = count // 4, len(FAR_CUTS)
    refs = list(refs)

    def take(amount):
        taken = refs[:amount]
        del refs[:amount]
        return taken

    core_in, held, y_in, z_in = take(total), take(1)[0], take(total), take(total)
    held_sem, core_send, core_recv, x_send, x_recv, y_send, y_recv, z_send, z_recv = refs
    section, me, z, y, c = place
    partner, other = (section, index_of(z, y, 1 - c)), (1 - section, me)
    shapes = [ref.shape for ref in far_out]
    places = [far_place(cut, shapes) for cut in FAR_CUTS]
    chains = [
        Chain(
            (section, z, y, c), depth, cut[3],
            lambda p: (core_in[p], (0,)), lambda p: y_in[p], lambda p: z_in[p],
            (y_send, y_recv, z_send, z_recv), lambda p: far_out[FAR_CUTS[p][0]].at[places[p]],
        )
        for cut in FAR_CUTS
    ]

    def core_copy(i, owner):
        source = far_src[FAR_CUTS[i][0]].at[(owner, slice(None), slice(None), 1 - c) + places[i]]
        return remote_copy(
            source, core_in[i].at[owner], core_send.at[owner, i], core_recv.at[owner, i], partner
        )

    def add_core(i, owner):
        ref = core_in[i]
        tile = (pl.ds(0, ref.shape[-2]), pl.ds(0, ref.shape[-1]))
        load = pltpu.make_async_copy(
            far_src[FAR_CUTS[i][0]].at[(owner, slice(None), slice(None), c) + places[i]],
            held.at[(slice(None), slice(None)) + tile],
            held_sem,
        )
        load.start()
        load.wait()
        core_copy(i, owner).wait_recv()

        def one(at, carry):
            to, side = at // 2, lax.rem(at, 2)
            ref[owner, to, side] = half(wide(ref[owner, to, side]) + wide(held[(to, side) + tile]))
            return carry

        lax.fori_loop(0, 2 * depth, one, 0)

    def leave(i):
        return far_half_copy(i, core_in[i].at[1], half_out, (x_send, x_recv), other)

    for owner in (0, 1):
        for i in range(total):
            core_copy(i, owner).start()
    for i in range(total):
        add_core(i, 0)
        chains[i].begin(i)
    for i in FAR_EARLY:
        add_core(i, 1)
        leave(i).start()
    later = [i for i in range(total) if i not in FAR_EARLY]
    for step in range(total + depth):
        for i in range(total):
            k = step - i + 1
            if 1 <= k < depth:
                chains[i].move(i, k)
            elif k == depth:
                chains[i].last(i)
        if later:
            i = later.pop(0)
            add_core(i, 1)
            leave(i).start()
    for i in range(total):
        chains[i].finish(i)
        core_copy(i, 0).wait_send()
        core_copy(i, 1).wait_send()
        if i in FAR_EARLY:
            leave(i).wait_send()
        else:
            leave(i).wait()


def block_backward(count, own_section, modulation, sources, weights, extra=None, far=(), previous=None):
    fresh = extra is not None
    rows, width = sources[0].shape
    images = modulation.shape[0]
    each = rows // images
    hidden_width = weights[2].shape[1]
    vmem, anywhere = pl.BlockSpec(memory_space=pltpu.VMEM), pl.BlockSpec(memory_space=pl.ANY)

    def shape(columns, kind=jnp.bfloat16, count=rows):
        return jax.ShapeDtypeStruct((count, columns), kind)

    outs = [
        shape(width), shape(3 * width), shape(width), shape(hidden_width), shape(width),
        jax.ShapeDtypeStruct((images, 8, width), jnp.float32),
        shape(3 * width, jnp.float32, 1), shape(width, jnp.float32, 1),
        shape(hidden_width, jnp.float32, 1), shape(width, jnp.float32, 1),
    ]
    scratch = [pltpu.VMEM(a.shape, a.dtype) for a in list(sources) + list(weights[2:])]
    scratch += [pltpu.VMEM(s.shape, s.dtype) for k, s in enumerate(outs) if k != 3]
    scratch += [
        pltpu.VMEM((2, rows, width), jnp.float32),
        pltpu.VMEM((each, 3 * width), jnp.float32), DMA((14,)), DMA((10,)), DMA((2,)),
    ]
    extra_in, extra_out, aliases = [], [], {}
    params = {}
    if fresh:
        extra_in = [extra] + list(far)
        scratch += [pltpu.VMEM(extra.shape, extra.dtype), DMA, DMA, DMA((images,)), DMA((images,))]
        shapes = [a.shape[4:] for a in far]
        extra_out = [jax.ShapeDtypeStruct(s, jnp.bfloat16) for s in shapes]
        extra_out += [jax.ShapeDtypeStruct((count // 4, 2) + s, jnp.bfloat16) for s in shapes]
        scratch += far_scratch(count, shapes)
        params = {"collective_id": 3, "has_side_effects": True}
    elif previous is not None:
        extra_in = list(previous)
        aliases = {13 + k: k for k in range(10)}
    return pl.pallas_call(
        functools.partial(
            backward_kernel, count, images, own_section, fresh, previous is not None
        ),
        out_shape=outs + extra_out,
        in_specs=[vmem] + [anywhere] * (12 + len(extra_in)),
        out_specs=[anywhere] * 10 + ([vmem] * 3 + [anywhere] * 3 if fresh else []),
        scratch_shapes=scratch,
        input_output_aliases=aliases,
        compiler_params=pltpu.CompilerParams(vmem_limit_bytes=63 * 2**20, **params),
        name="block_backward",
    )(modulation, *sources, *weights, *extra_in)


def sigmoid_parts(values):
    gate = 1.0 / (1.0 + jnp.exp(-values))
    return values * gate, gate * (1.0 + values * (1.0 - gate))


def align_kernel(
    loss,
    wanted, bias_one, bias_two, bias_three, x_hbm, target_hbm, one_hbm, two_hbm, three_hbm,
    dx_hbm, one_sum, two_sum, three_sum, one_grad, two_grad, three_grad,
    x_ref, target, dx_ref, one_w, two_w, three_w, padded_x, act_one, act_two, d_one, d_two, d_latent, slope_one, slope_two,
    product, sems, product_sem, dx_sem,
):
    tile = 512

    def layer(source, weight, bias, act, slope):
        def one(j, carry):
            cols = pl.ds(pl.multiple_of(j * tile, tile), tile)
            pre = dot_plain(source[...], weight[:, cols]) + bias[:, cols]
            value, bend = sigmoid_parts(pre)
            act[:, cols] = half(value)
            slope[:, cols] = half(bend)
            return carry

        lax.fori_loop(0, weight.shape[1] // tile, one, 0)

    def back(grad, weight, slope, target_ref, sum_ref):
        def one(j, carry):
            cols = pl.ds(pl.multiple_of(j * tile, tile), tile)
            value = half(dot_across(grad[...], weight[cols, :]) * wide(slope[:, cols]))
            target_ref[:, cols] = value
            sum_ref[:, cols] = jnp.sum(wide(value), 0, keepdims=True)
            return carry

        lax.fori_loop(0, weight.shape[0] // tile, one, 0)

    def picks(cols, size):
        row = lax.broadcasted_iota(jnp.int32, (x_ref.shape[1], size), 0)
        return half(jnp.where(row == wanted[:, cols], 1.0, 0.0))

    @pl.when(lax.axis_index("section") == 0)
    def _():
        loads = Loads(sems)
        x_at = loads.add(x_hbm, x_ref, 0, 1)
        target_at = loads.add(target_hbm, target, 0, 1)
        one_at = loads.add(one_hbm, one_w, 0, 1)
        two_at = loads.add(two_hbm, two_w, 0, 1)
        three_at = loads.add(three_hbm, three_w, 0, 1)
        loads.start()
        loads.wait(x_at)
        padded_width = one_w.shape[0]
        for start, size in column_tiles(padded_width, tile):
            cols = slice(start, start + size)
            padded_x[:, cols] = half(dot_plain(x_ref[...], picks(cols, size)))
        loads.wait(one_at)
        layer(padded_x, one_w, bias_one, act_one, slope_one)
        loads.wait(two_at)
        layer(act_one, two_w, bias_two, act_two, slope_two)
        loads.wait(three_at + target_at)
        latent = dot_plain(act_two[...], three_w[...]) + bias_three[...]
        features = wide(target[...])
        root_latent = lax.rsqrt(jnp.sum(latent * latent, -1, keepdims=True) + epsilon)
        root_target = lax.rsqrt(jnp.sum(features * features, -1, keepdims=True) + epsilon)
        crossed = jnp.sum(latent * features, -1, keepdims=True)
        grad = half(
            -loss
            * (
                features * (root_latent * root_target)
                - (crossed * root_target * root_latent * root_latent * root_latent) * latent
            )
        )
        d_latent[...] = grad
        three_sum[...] = jnp.sum(wide(grad), 0, keepdims=True)
        back(d_latent, three_w, slope_two, d_two, two_sum)
        back(d_two, two_w, slope_one, d_one, one_sum)
        total = jnp.zeros(x_ref.shape, jnp.float32)
        for start, size in column_tiles(padded_width, tile):
            cols = slice(start, start + size)
            value = half(dot_across(d_one[...], one_w[start : start + size, :]))
            total = total + dot_across(value, picks(cols, size))
        dx_ref[...] = half(total)
        dx_copy = pltpu.make_async_copy(dx_ref, dx_hbm, dx_sem)
        dx_copy.start()

        jobs = []
        for left, right, place in (
            (act_two, d_latent, three_grad), (padded_x, d_one, one_grad), (act_one, d_two, two_grad),
        ):
            for start, size in column_tiles(left.shape[1], tile):
                jobs.append((left, right, place, start, size))
        copies = []
        for k, (left, right, place, start, size) in enumerate(jobs):
            if k >= 2:
                copies[k - 2].wait()
            held = product.at[k % 2, pl.ds(0, size), pl.ds(0, right.shape[1])]
            held[...] = half(dot_down(left[:, start : start + size], right[...]))
            copies.append(
                pltpu.make_async_copy(held, place.at[pl.ds(start, size)], product_sem.at[k % 2])
            )
            copies[k].start()
        copies[-2].wait()
        copies[-1].wait()
        dx_copy.wait()


def project_align(hidden, target, wanted, aligner, loss):
    weight_one, bias_one, weight_two, bias_two, weight_three, bias_three = aligner
    rows, width = hidden.shape
    first, second, third = weight_one.shape[1], weight_two.shape[1], weight_three.shape[1]
    vmem, anywhere = pl.BlockSpec(memory_space=pltpu.VMEM), pl.BlockSpec(memory_space=pl.ANY)

    def shape(columns, kind=jnp.bfloat16, count=rows):
        return jax.ShapeDtypeStruct((count, columns), kind)

    weights = (weight_one, weight_two, weight_three)
    results = pl.pallas_call(
        functools.partial(align_kernel, loss),
        out_shape=[
            shape(width),
            shape(first, jnp.float32, 1), shape(second, jnp.float32, 1), shape(third, jnp.float32, 1),
        ]
        + [jax.ShapeDtypeStruct(w.shape, jnp.bfloat16) for w in weights],
        in_specs=[vmem] * 4 + [anywhere] * 5,
        out_specs=[anywhere] + [vmem] * 3 + [anywhere] * 3,
        scratch_shapes=[pltpu.VMEM(a.shape, a.dtype) for a in (hidden, target, hidden) + weights]
        + [
            pltpu.VMEM((rows, k), jnp.bfloat16)
            for k in (weight_one.shape[0], first, second, first, second, third, first, second)
        ]
        + [pltpu.VMEM((2, 512, max(first, second, third)), jnp.bfloat16), DMA((5,)), DMA((2,)), DMA],
        compiler_params=pltpu.CompilerParams(vmem_limit_bytes=62 * 2**20),
        name="project_align",
    )(
        wanted, bias_one[None], bias_two[None], bias_three[None], hidden, target, *weights
    )
    return results[0], results[1:4], results[4:]


def own_place():
    section = lax.axis_index("section")
    index = lax.axis_index("dp")
    return section, index, index // 4, lax.rem(index // 2, 2), lax.rem(index, 2)


def index_of(z, y, core):
    return z * 4 + y * 2 + core


def greet(targets):
    barrier = pltpu.get_barrier_semaphore()
    for target in targets:
        pl.semaphore_signal(barrier, inc=1, device_id=target, device_id_type=MESH)
    pl.semaphore_wait(barrier, len(targets))


def greet_section(count, section, index, extra=()):
    barrier = pltpu.get_barrier_semaphore()

    def one(step, carry):
        target = (section, lax.rem(index + step, count))
        pl.semaphore_signal(barrier, inc=1, device_id=target, device_id_type=MESH)
        return carry

    lax.fori_loop(1, count, one, 0)
    for target in extra:
        pl.semaphore_signal(barrier, inc=1, device_id=target, device_id_type=MESH)
    pl.semaphore_wait(barrier, count - 1 + len(extra))


class Exchange:
    def __init__(self, count, section, index, source, target, send, recv, local, own_only):
        self.count, self.section, self.index = count, section, index
        self.source, self.target = source, target
        self.send, self.recv, self.local, self.own_only = send, recv, local, own_only

    def piece(self, other):
        return self.source if self.own_only else self.source.at[other]

    def message(self, other, slot):
        return pltpu.make_async_remote_copy(
            src_ref=self.piece(other),
            dst_ref=self.target.at[slot],
            send_sem=self.send.at[other],
            recv_sem=self.recv.at[slot],
            device_id=(self.section, other),
            device_id_type=MESH,
        )

    def start(self):
        def one(step, carry):
            self.message(lax.rem(self.index + step, self.count), self.index).start()
            return carry

        lax.fori_loop(1, self.count, one, 0)
        pltpu.make_async_copy(
            self.piece(self.index), self.target.at[self.index], self.local
        ).start()

    def finish(self):
        def one(step, carry):
            other = lax.rem(self.index + step, self.count)
            self.message(other, self.index).wait_send()
            self.message(other, other).wait_recv()
            return carry

        lax.fori_loop(1, self.count, one, 0)
        pltpu.make_async_copy(
            self.piece(self.index), self.target.at[self.index], self.local
        ).wait()


def share_kernel(count, source, target, send, recv, local):
    section, index, z, y, core = own_place()
    me = section * count + index
    everybody = 2 * count

    def device(step):
        other = lax.rem(me + step, everybody)
        return other, (other // count, lax.rem(other, count))

    def message(other, where, slot):
        return remote_copy(
            source, target.at[slot // count, lax.rem(slot, count)], send.at[other], recv.at[slot], where
        )

    barrier = pltpu.get_barrier_semaphore()

    def greet_one(step, carry):
        pl.semaphore_signal(barrier, inc=1, device_id=device(step)[1], device_id_type=MESH)
        return carry

    def start_one(step, carry):
        other, where = device(step)
        message(other, where, me).start()
        return carry

    def finish_one(step, carry):
        other, where = device(step)
        message(other, where, me).wait_send()
        message(other, where, other).wait_recv()
        return carry

    lax.fori_loop(1, everybody, greet_one, 0)
    pl.semaphore_wait(barrier, everybody - 1)
    own = pltpu.make_async_copy(source, target.at[section, index], local)
    own.start()
    lax.fori_loop(1, everybody, start_one, 0)
    lax.fori_loop(1, everybody, finish_one, 0)
    own.wait()


def share_small(count, values):
    return pl.pallas_call(
        functools.partial(share_kernel, count),
        out_shape=jax.ShapeDtypeStruct((2, count) + values.shape, values.dtype),
        in_specs=[pl.BlockSpec(memory_space=pl.ANY)],
        out_specs=pl.BlockSpec(memory_space=pl.ANY),
        scratch_shapes=[DMA((2 * count,)), DMA((2 * count,)), DMA],
        compiler_params=pltpu.CompilerParams(collective_id=0, has_side_effects=True),
        name="share_small",
    )(values)


def gather_kernel(count, images, arrays, items, stride, *refs):
    total = len(items)
    modes = [item[0] >= 4 for item in items]
    first = [item[4] for item in items]
    starts = [item[5] for item in items]
    refs = list(refs)

    def take(amount):
        taken = refs[:amount]
        del refs[:amount]
        return taken

    part, x_ref, bias = take(3)
    src = take(arrays)
    part_out, mod_out = take(2)
    dst = take(arrays)
    kept_out = take(11)
    part_send, part_recv, part_local, local_sem, send_core, send_y, send_x, send_up, send_down, recv = take(10)
    weight_refs = take(4)
    kept = take(11)
    part_in, blend, part_sem, weight_sem, kept_sem, hidden_send, hidden_recv = refs
    depth = count // 4
    section, me, z, y, c = own_place()
    up, down = (section, me + 4), (section, me - 4)
    across, partner = (section, index_of(z, 1 - y, c)), (section, index_of(z, y, 1 - c))
    other = (1 - section, me)
    greet_section(count, section, me, (other,))
    parts = Exchange(count, section, me, part, part_out, part_send, part_recv, part_local, False)
    parts.start()

    def cut(w):
        _, axis, start, size = items[w][:4]
        return (pl.ds(start, size),) if axis == 0 else (slice(None), pl.ds(start, size))

    def slot(w, sec, blk):
        place = (sec, blk) if modes[w] else (blk,)
        return dst[items[w][0]].at[place + cut(w)]

    def source_of(w):
        return src[items[w][0]].at[cut(w)]

    def copy(w, sec, blk, target, sem, src_ref=None):
        here = slot(w, sec, blk)
        return pltpu.make_async_remote_copy(
            src_ref=here if src_ref is None else src_ref,
            dst_ref=here,
            send_sem=sem,
            recv_sem=recv.at[w, sec if modes[w] else 0, blk],
            device_id=target,
            device_id_type=MESH,
        )

    def arrived(w, sec, blk):
        copy(w, sec, blk, partner, send_core.at[w, 0, 0, 0]).wait_recv()

    def pass_on(w, zz, side, go_up, go_down, go_across, source=None):
        blk = index_of(zz, y if side == 0 else 1 - y, c)
        if go_up is not None:

            @pl.when(go_up)
            def _():
                copy(w, section, blk, up, send_up.at[w, side, zz], source).start()

        if go_down is not None:

            @pl.when(go_down)
            def _():
                copy(w, section, blk, down, send_down.at[w, side, zz], source).start()

        if go_across:
            copy(w, section, blk, across, send_y.at[w, zz], source).start()
        if modes[w]:

            @pl.when(section == 1)
            def _():
                copy(w, section, blk, other, send_x.at[w, side, zz], source).start()

        copy(w, section, blk, partner, send_core.at[w, 0, side, zz], source).start()

    def depart(w):
        pass_on(w, z, 0, z < depth - 1, z > 0, True, source_of(w))
        pltpu.make_async_copy(source_of(w), slot(w, section, me), local_sem.at[w]).start()

    def near(w, k):
        if k >= depth:
            return

        @pl.when(z >= k)
        def _():
            arrived(w, section, index_of(z - k, y, c))
            pass_on(w, z - k, 0, z < depth - 1, None, not first[w])

        @pl.when(z + k < depth)
        def _():
            arrived(w, section, index_of(z + k, y, c))
            pass_on(w, z + k, 0, None, z > 0, not first[w])

    def far(w, k):
        @pl.when(z >= k)
        def _():
            arrived(w, section, index_of(z - k, 1 - y, c))
            if first[w]:
                pass_on(w, z - k, 1, z < depth - 1, (z > 0) if k == 0 else None, False)
            else:
                pass_on(w, z - k, 1, None, None, False)

        if k > 0:

            @pl.when(z + k < depth)
            def _():
                arrived(w, section, index_of(z + k, 1 - y, c))
                pass_on(w, z + k, 1, None, (z > 0) if first[w] else None, False)

    def complete(w):
        pltpu.make_async_copy(source_of(w), slot(w, section, me), local_sem.at[w]).wait()
        for side in range(2):

            def one(zz, carry):
                arrived(w, section, index_of(zz, y if side == 0 else 1 - y, 1 - c))
                return carry

            lax.fori_loop(0, depth, one, 0)

    def load(w):
        return pltpu.make_async_copy(dst[w], weight_refs[w], weight_sem.at[w])

    def modulate():
        parts.finish()
        copy_in = pltpu.make_async_copy(part_out, part_in, part_sem)
        copy_in.start()
        copy_in.wait()
        total_mod = wide(part_in[0])
        for device in range(1, count):
            total_mod = total_mod + wide(part_in[device])
        chunks = x_ref.shape[1] // LANES
        for image in range(images):
            for q in range(chunks):
                at = (image * chunks + q) * 6
                cols = slice(q * LANES, (q + 1) * LANES)
                mod_out[image, 0:6, cols] = total_mod[at : at + 6]
            for k in range(6):
                start = (9 + k) * x_ref.shape[1]
                mod_out[image, k : k + 1, :] += bias[:, start : start + x_ref.shape[1]]

    store, wait_stored = stored(kept, kept_out, kept_sem)
    forward = Forward(
        images, x_ref, mod_out, bias_parts(bias), kept, blend,
        [flat(ref) for ref in weight_refs], store,
    )

    def on_first(action):
        @pl.when(section == 0)
        def _():
            action()

    def load_array(a):
        on_first(lambda: load(a).start())

    last_item = [max(w for w in range(total) if items[w][0] == a) for a in range(4)]
    events = []
    for t in range(max(starts) + stride * depth + 1):
        for w in range(total):
            k, rest = divmod(t - starts[w], stride)
            if rest or k < 0 or k > depth:
                continue
            if k == 0:
                events.append((t, functools.partial(depart, w), None))
                continue
            if first[w]:
                events.append((t, functools.partial(far, w, k - 1), None))
                events.append((t, functools.partial(near, w, k), None))
            else:
                events.append((t, functools.partial(near, w, k), None))
                events.append((t, functools.partial(far, w, k - 1), None))
            if k == depth and not modes[w]:
                events.append((t, functools.partial(complete, w), None))
                a = items[w][0]
                if w == last_item[a]:
                    events.append((t, functools.partial(load_array, a), a))
    def finish_block():
        forward.leave()
        remote_copy(kept[10], kept_out[10], hidden_send, hidden_recv, other).start()

    groups = [
        [forward.project_all, forward.attend_all],
        [forward.middle],
        [forward.feed],
        [finish_block],
    ]

    def run_group(w):
        load(w).wait()
        for chunk in groups[w]:
            chunk()

    modulated = False
    for i, (t, event, ready) in enumerate(events):
        event()
        if not modulated and t == stride and events[i + 1][0] > stride:
            modulated = True
            modulate()
            on_first(forward.enter)
        if ready is not None:
            on_first(functools.partial(run_group, ready))

    for w in range(total):
        if modes[w]:
            complete(w)

            @pl.when(section == 0)
            def _():
                for side in range(2):

                    def from_x(zz, carry):
                        blk = index_of(zz, y if side == 0 else 1 - y, c)
                        arrived(w, 1, blk)
                        copy(w, 1, blk, partner, send_core.at[w, 1, side, zz]).start()
                        return carry

                    lax.fori_loop(0, depth, from_x, 0)

    for w in range(total):
        for side in range(2):

            def finish(zz, carry):
                copy(w, section, me, partner, send_core.at[w, 0, side, zz]).wait_send()
                if modes[w]:

                    @pl.when(section == 1)
                    def _():
                        copy(w, section, me, other, send_x.at[w, side, zz]).wait_send()

                    @pl.when(section == 0)
                    def _():
                        blk = index_of(zz, y if side == 0 else 1 - y, 1 - c)
                        arrived(w, 1, blk)
                        copy(w, 1, blk, partner, send_core.at[w, 1, side, zz]).wait_send()

                if side == 0:

                    @pl.when((zz == z) if first[w] else (zz >= 0))
                    def _():
                        copy(w, section, me, across, send_y.at[w, zz]).wait_send()

                if side == 0 or first[w]:

                    @pl.when((z < depth - 1) & (zz <= z))
                    def _():
                        copy(w, section, me, up, send_up.at[w, side, zz]).wait_send()

                    @pl.when((z > 0) & (zz >= z))
                    def _():
                        copy(w, section, me, down, send_down.at[w, side, zz]).wait_send()

                return carry

            lax.fori_loop(0, depth, finish, 0)
    hidden_copy = remote_copy(kept[10], kept_out[10], hidden_send, hidden_recv, other)

    @pl.when(section == 0)
    def _():
        hidden_copy.wait_send()
        wait_stored()

    @pl.when(section == 1)
    def _():
        hidden_copy.wait_recv()


def gather_forward(count, parts, inputs, images, bias, own, both, items, stride):
    arrays = list(own) + list(both)
    modes = [False] * len(own) + [True] * len(both)
    total, depth, n_arrays = len(items), count // 4, len(arrays)
    rows, width = inputs.shape
    anywhere, vmem = pl.BlockSpec(memory_space=pl.ANY), pl.BlockSpec(memory_space=pltpu.VMEM)
    shapes = [((2, count) if m else (count,)) + a.shape for a, m in zip(arrays, modes)]
    kept = kept_shapes(rows, width, images, own[2].shape[1])
    results = pl.pallas_call(
        functools.partial(gather_kernel, count, images, n_arrays, items, stride),
        out_shape=[
            jax.ShapeDtypeStruct(parts.shape, parts.dtype),
            jax.ShapeDtypeStruct((images, 8, width), jnp.float32),
        ]
        + [jax.ShapeDtypeStruct(s, a.dtype) for s, a in zip(shapes, arrays)]
        + kept,
        in_specs=[anywhere] + [vmem] * 2 + [anywhere] * n_arrays,
        out_specs=[anywhere, vmem] + [anywhere] * (n_arrays + 11),
        scratch_shapes=[
            DMA((count,)),
            DMA((count,)),
            DMA,
            DMA((total,)),
            DMA((total, 2, 2, depth)),
            DMA((total, depth)),
            DMA((total, 2, depth)),
            DMA((total, 2, depth)),
            DMA((total, 2, depth)),
            DMA((total, 2, count)),
        ]
        + [pltpu.VMEM((count,) + a.shape, a.dtype) for a in own]
        + [pltpu.VMEM(s.shape, s.dtype) for s in kept]
        + [
            pltpu.VMEM(parts.shape, parts.dtype),
            pltpu.VMEM((rows // images, width), jnp.float32),
            DMA,
            DMA((4,)),
            DMA((11,)),
            DMA,
            DMA,
        ],
        compiler_params=pltpu.CompilerParams(
            collective_id=1, has_side_effects=True, vmem_limit_bytes=63 * 2**20
        ),
        name="gather_forward",
    )(parts, inputs, bias, *arrays)
    return results[1], results[2 : 2 + n_arrays], results[2 + n_arrays :]


class Chain:
    def __init__(self, place, depth, z_first, sums, y_in, z_in, sems, out):
        self.section, self.z, self.y, self.c = place
        self.depth, self.z_first = depth, z_first
        self.sums, self.y_in, self.z_in, self.out = sums, y_in, z_in, out
        self.y_send, self.y_recv, self.z_send, self.z_recv = sems
        me = index_of(self.z, self.y, self.c)
        self.up, self.down = (self.section, me + 4), (self.section, me - 4)
        self.across = (self.section, index_of(self.z, 1 - self.y, self.c))

    def part(self, p, to):
        ref, lead = self.sums(p)
        return ref, lead + ((to,) if self.z_first else (to, self.y))

    def y_copy(self, p):
        ref, lead = self.sums(p)
        whole = self.z if self.z_first else slice(None)
        return remote_copy(
            ref.at[lead + (whole, 1 - self.y)],
            self.y_in(p),
            self.y_send.at[p],
            self.y_recv.at[p],
            self.across,
        )

    def z_copy(self, p, to, where, device):
        ref, place = self.part(p, to)
        return remote_copy(
            ref.at[place], self.z_in(p).at[where], self.z_send.at[p, to], self.z_recv.at[p, where], device
        )

    def add_z(self, p, to, where):
        self.z_copy(p, 0, where, self.across).wait_recv()
        ref, place = self.part(p, to)
        z_in = self.z_in(p)
        if self.z_first:
            for side in range(2):
                ref[place + (side,)] = half(wide(ref[place + (side,)]) + wide(z_in[where, side]))
        else:
            ref[place] = half(wide(ref[place]) + wide(z_in[where]))

    def hop(self, p, h):
        @pl.when((self.z == h) & (self.z < self.depth - 1))
        def _():
            def one(back, carry):
                to = self.depth - 1 - back
                if h > 0:
                    self.add_z(p, to, to)
                self.z_copy(p, to, to, self.up).start()
                return carry

            lax.fori_loop(0, self.depth - 1 - self.z, one, 0)

        @pl.when((self.depth - 1 - self.z == h) & (self.z > 0))
        def _():
            def one(to, carry):
                if h > 0:
                    self.add_z(p, to, to)
                self.z_copy(p, to, jnp.where(to == self.z - 1, self.depth, to), self.down).start()
                return carry

            lax.fori_loop(0, self.z, one, 0)

    def join(self, p):
        @pl.when(self.z > 0)
        def _():
            self.add_z(p, self.z, self.z)

        @pl.when(self.z < self.depth - 1)
        def _():
            self.add_z(p, self.z, self.depth)

    def begin(self, p):
        if self.z_first:
            self.hop(p, 0)
        else:
            self.y_copy(p).start()

    def move(self, p, step):
        if self.z_first:
            if step < self.depth - 1:
                self.hop(p, step)
            else:
                self.join(p)
                self.y_copy(p).start()
            return
        if step == 1:
            self.y_copy(p).wait_recv()
            y_in = self.y_in(p)

            def one(to, carry):
                ref, place = self.part(p, to)
                ref[place] = half(wide(ref[place]) + wide(y_in[to]))
                return carry

            lax.fori_loop(0, self.depth, one, 0)
        self.hop(p, step - 1)

    def last(self, p):
        ref, lead = self.sums(p)
        if self.z_first:
            self.y_copy(p).wait_recv()
            total = wide(ref[lead + (self.z, self.y)]) + wide(self.y_in(p)[...])
            self.out(p)[...] = half(total)
        else:
            self.join(p)
            self.out(p)[...] = ref[lead + (self.z, self.y)]

    def finish(self, p):
        self.y_copy(p).wait_send()

        def one(to, carry):
            @pl.when(to != self.z)
            def _():
                self.z_copy(p, to, to, self.across).wait_send()

            return carry

        lax.fori_loop(0, self.depth, one, 0)


def chain_slots(depth, first, shape):
    y_shape = shape if first else (depth,) + shape
    z_shape = (depth + 1, 2) + shape if first else (depth + 1,) + shape
    return y_shape, z_shape


def remote_copy(source, target, send, recv, device):
    return pltpu.make_async_remote_copy(
        src_ref=source,
        dst_ref=target,
        send_sem=send,
        recv_sem=recv,
        device_id=device,
        device_id_type=MESH,
    )


def reduce_kernel(count, ready, pairs, plan, far_first, far_steps, stride, *refs):
    depth = count // 4
    far_total = len(far_first)
    near_total = ready + len(plan)
    refs = list(refs)

    def take(amount):
        taken = refs[:amount]
        del refs[:amount]
        return taken

    act_src, branch_src, wanted = take(3)
    left_src, right_src = take(pairs), take(pairs)
    far_src = take(far_total)
    mod_src, bias_src = take(2)
    (near_out,) = take(1)
    far_out = take(far_total)
    mod_out, bias_out = take(2)
    left, right, chunk, picked, made, core_in, y_in, z_in, tail_y_in, tail_z_in = take(10)
    far_core_in, far_y_in, far_z_in = take(far_total), take(far_total), take(far_total)
    (
        left_sem, right_sem, chunk_sem, core_send, core_recv, y_send, y_recv, z_send, z_recv,
        far_local, far_send, far_recv,
        far_y_send, far_y_recv, far_z_send, far_z_recv,
        mod_send, mod_recv, mod_local, bias_send, bias_recv, bias_local,
    ) = refs
    section, me, z, y, c = own_place()
    partner = (section, index_of(z, y, 1 - c))
    other = (1 - section, me)
    barrier = pltpu.get_barrier_semaphore()

    def greet_one(step, carry):
        target = (section, lax.rem(me + step, count))
        pl.semaphore_signal(barrier, inc=1, device_id=target, device_id_type=MESH)
        return carry

    lax.fori_loop(1, count, greet_one, 0)

    @pl.when(section == 1)
    def _():
        pl.semaphore_signal(barrier, inc=1, device_id=other, device_id_type=MESH)
        pl.semaphore_wait(barrier, count - 1)

    @pl.when(section == 0)
    def _():
        pl.semaphore_wait(barrier, count)

    rows, width = made.shape[-2:]
    mods = Exchange(count, section, me, mod_src, mod_out, mod_send, mod_recv, mod_local, True)
    biases = Exchange(count, section, me, bias_src, bias_out, bias_send, bias_recv, bias_local, False)

    base = near_total - 2
    order = [near_total - 1, base] + list(range(ready, base)) + list(range(ready))

    def operands(p, slot):
        pair, row, column = plan[p - ready]
        return (
            pltpu.make_async_copy(
                left_src[pair].at[:, pl.ds(row * width, width)], left.at[slot], left_sem.at[slot]
            ),
            pltpu.make_async_copy(
                right_src[pair].at[:, pl.ds(column * width, width)], right.at[slot], right_sem.at[slot]
            ),
        )

    def branch_copy(slot):
        return pltpu.make_async_copy(branch_src, right.at[slot], right_sem.at[slot])

    def chunk_copy(w):
        return pltpu.make_async_copy(
            act_src.at[:, pl.ds(w * width, width)], chunk.at[w % 2], chunk_sem.at[w % 2]
        )

    def pick(p, slot):
        chunks = act_src.shape[1] // width
        picked[...] = jnp.zeros(picked.shape, jnp.float32)
        chunk_copy(0).start()
        row = wanted[pl.ds(p, 1), :]
        for w in range(chunks):
            if w + 1 < chunks:
                chunk_copy(w + 1).start()
            start = w * width // chunks // LANES * LANES
            stop = -(-((w + 1) * width // chunks) // LANES) * LANES
            window = slice(start, stop)
            at = lax.broadcasted_iota(jnp.int32, (width, stop - start), 0) + w * width
            picks = half(jnp.where(at == row[:, window], 1.0, 0.0))
            chunk_copy(w).wait()
            picked[:, window] += dot_plain(chunk[w % 2], picks)
        left[slot] = half(picked[...])

    def core_copy(p, slot):
        return remote_copy(
            made.at[slot, :, :, 1 - c], core_in.at[p], core_send.at[p], core_recv.at[p], partner
        )

    def fetch(t, slot):
        for i, p in enumerate(order):

            @pl.when(t == i)
            def _():
                if p < ready:
                    branch_copy(slot).start()
                else:
                    for copy in operands(p, slot):
                        copy.start()

    def piece_of(t):
        return jnp.where(t < 2, near_total - 1 - t, lax.rem(t - 2 + ready, base))

    def make(t):
        slot = lax.rem(t, 2)
        p = piece_of(t)

        @pl.when(t >= 2)
        def _():
            core_copy(piece_of(t - 2), slot).wait_send()

        @pl.when(t + 1 < near_total)
        def _():
            fetch(t + 1, 1 - slot)

        @pl.when(p < ready)
        def _():
            pick(p, slot)
            branch_copy(slot).wait()

        @pl.when(p >= ready)
        def _():
            for copy in operands(ready, slot):
                copy.wait()

        tile = 3 * LANES
        for at in range(0, width, tile):
            cols = slice(at, at + tile)
            product = dot_down(left[slot], right[slot, :, cols])
            made[slot, :, :, :, :, cols] = half(product).reshape(depth, 2, 2, rows, tile)
        core_copy(p, slot).start()

    near = Chain(
        (section, z, y, c), depth, False,
        lambda p: (core_in, (p,)), lambda p: y_in.at[p], lambda p: z_in.at[p],
        (y_send, y_recv, z_send, z_recv), lambda p: near_out.at[p],
    )
    tail = Chain(
        (section, z, y, c), depth, True,
        lambda p: (core_in, (p,)), lambda p: tail_y_in.at[p - base], lambda p: tail_z_in.at[p - base],
        (y_send, y_recv, z_send, z_recv), lambda p: near_out.at[p],
    )
    far = [
        Chain(
            (section, z, y, c), depth, far_first[i],
            lambda p: (far_core_in[p], ()), lambda p: far_y_in[p], lambda p: far_z_in[p],
            (far_y_send, far_y_recv, far_z_send, far_z_recv), lambda p: far_out[p],
        )
        for i in range(far_total)
    ]

    def begin(t):
        slot = lax.rem(t, 2)
        p = piece_of(t)
        core_copy(p, slot).wait_recv()

        def add_side(side):
            def one(to, carry):
                core_in[p, to, side] = half(
                    wide(core_in[p, to, side]) + wide(made[slot, to, side, c])
                )
                return carry

            lax.fori_loop(0, depth, one, 0)

        add_side(1 - y)

        @pl.when(p < base)
        def _():
            near.begin(p)

        add_side(y)

        @pl.when(p >= base)
        def _():
            tail.begin(p)

    def far_columns(i, late):
        size = far_core_in[i].shape[-1]
        start, stop = {0: (size, size), 1: (0, size), 2: (size // 2, size)}[i]
        start, stop = (start, stop) if late else (0, start)
        return (slice(None),) * 3 + (pl.ds(start, stop - start),)

    def far_lies(i):
        at = far_columns(i, False)
        return pltpu.make_async_copy(far_src[i].at[at], far_core_in[i].at[at], far_local.at[i])

    def far_comes(i):
        at = far_columns(i, True)
        return remote_copy(
            far_src[i].at[at], far_core_in[i].at[at], far_send.at[i], far_recv.at[i], other
        )

    fetch(0, 0)

    @pl.when(section == 0)
    def _():
        for i in (1, 2):
            far_comes(i).start()

    @pl.when(section == 1)
    def _():
        for i in (0, 2):
            far_lies(i).start()

    mods.start()
    biases.start()

    def step(t, carry):
        @pl.when(t < near_total)
        def _():
            make(t)

        @pl.when((t >= 1) & (t <= near_total))
        def _():
            begin(t - 1)

        for i in range(far_total):

            @pl.when((t == far_steps[i]) & (section == 1))
            def _():
                if i != 1:
                    far_lies(i).wait()
                if i != 0:
                    far_comes(i).wait_recv()
                far[i].begin(i)

            for k in range(1, depth):

                @pl.when((t == far_steps[i] + stride * k) & (section == 1))
                def _():
                    far[i].move(i, k)

            @pl.when((t == far_steps[i] + stride * depth) & (section == 1))
            def _():
                far[i].last(i)

        for k in range(1, depth):
            p = t - 3 - stride * k

            @pl.when((p >= 0) & (p < base))
            def _():
                near.move(lax.rem(p + ready, base), k)

            for q in range(2):

                @pl.when(t == 1 + q + stride * k)
                def _():
                    tail.move(near_total - 1 - q, k)

        p = t - 3 - stride * depth

        @pl.when((p >= 0) & (p < base))
        def _():
            near.last(lax.rem(p + ready, base))

        for q in range(2):

            @pl.when(t == 1 + q + stride * depth)
            def _():
                tail.last(near_total - 1 - q)

        return carry

    lax.fori_loop(0, max(near_total + 1, max(far_steps) + 1) + stride * depth, step, 0)
    for t in (near_total - 2, near_total - 1):
        core_copy(order[t], t % 2).wait_send()

    @pl.when(section == 0)
    def _():
        for i in (1, 2):
            far_comes(i).wait_send()

    @pl.when(section == 1)
    def _():
        for i in range(far_total):
            far[i].finish(i)

    def near_finish(p, carry):
        near.finish(p)
        return carry

    lax.fori_loop(0, base, near_finish, 0)
    for q in range(2):
        tail.finish(near_total - 1 - q)
    mods.finish()
    biases.finish()


def reduce_grads(count, rows, act, branch, pairs, plan, far, far_first, far_steps, stride, mods, biases):
    depth = count // 4
    tokens, width = branch.shape
    pieces = act.shape[1] // (count * rows)
    near_total = pieces + len(plan)
    lane = jnp.arange(width, dtype=jnp.int32)
    wanted = jnp.stack([(lane // rows * pieces + j) * rows + lane % rows for j in range(pieces)])
    far_shapes = [a.shape[2:] for a in far]
    kind = jnp.bfloat16
    anywhere, vmem = pl.BlockSpec(memory_space=pl.ANY), pl.BlockSpec(memory_space=pltpu.VMEM)
    n_far = len(far)
    lefts, rights = [a for a, _ in pairs], [b for _, b in pairs]

    far_slots = [chain_slots(depth, f, s) for f, s in zip(far_first, far_shapes)]
    results = pl.pallas_call(
        functools.partial(reduce_kernel, count, pieces, len(pairs), plan, far_first, far_steps, stride),
        out_shape=[jax.ShapeDtypeStruct((near_total, rows, width), kind)]
        + [jax.ShapeDtypeStruct(s, kind) for s in far_shapes]
        + [
            jax.ShapeDtypeStruct((count,) + mods.shape, mods.dtype),
            jax.ShapeDtypeStruct(biases.shape, biases.dtype),
        ],
        in_specs=[anywhere] * 2 + [vmem] + [anywhere] * (2 * len(pairs) + n_far + 2),
        out_specs=[vmem] * (1 + n_far) + [anywhere] * 2,
        scratch_shapes=[
            pltpu.VMEM((2, tokens, width), kind),
            pltpu.VMEM((2, tokens, width), kind),
            pltpu.VMEM((2, tokens, width), kind),
            pltpu.VMEM((tokens, width), jnp.float32),
            pltpu.VMEM((2, depth, 2, 2, rows, width), kind),
            pltpu.VMEM((near_total, depth, 2, rows, width), kind),
            pltpu.VMEM((near_total - 2, depth, rows, width), kind),
            pltpu.VMEM((near_total - 2, depth + 1, rows, width), kind),
            pltpu.VMEM((2, rows, width), kind),
            pltpu.VMEM((2, depth + 1, 2, rows, width), kind),
        ]
        + [pltpu.VMEM((depth, 2) + s, kind) for s in far_shapes]
        + [pltpu.VMEM(s[0], kind) for s in far_slots]
        + [pltpu.VMEM(s[1], kind) for s in far_slots]
        + [
            DMA((2,)),
            DMA((2,)),
            DMA((2,)),
            DMA((near_total,)),
            DMA((near_total,)),
            DMA((near_total,)),
            DMA((near_total,)),
            DMA((near_total, depth)),
            DMA((near_total, depth + 1)),
            DMA((n_far,)),
            DMA((n_far,)),
            DMA((n_far,)),
            DMA((n_far,)),
            DMA((n_far,)),
            DMA((n_far, depth)),
            DMA((n_far, depth + 1)),
            DMA((count,)),
            DMA((count,)),
            DMA,
            DMA((count,)),
            DMA((count,)),
            DMA,
        ],
        compiler_params=pltpu.CompilerParams(
            collective_id=2, has_side_effects=True, vmem_limit_bytes=63 * 2**20
        ),
        name="reduce_grads",
    )(act, branch, wanted, *lefts, *rights, *far, mods, biases)
    return results[0], results[1 : 1 + n_far], results[1 + n_far], results[2 + n_far]


def padded(values, rows):
    flat = values.reshape(values.shape[0], -1)
    room = rows * LANES - flat.shape[1]
    return jnp.pad(flat, ((0, 0), (0, room))).reshape(values.shape[0], rows, LANES)


def rows_for(amount, unit):
    rows = -(-amount // LANES)
    return -(-rows // unit) * unit


def split_at(flat, sizes):
    pieces, start = [], 0
    for size in sizes:
        pieces.append(flat[..., start : start + size])
        start += size
    return pieces


def gather_plan(own, both):
    width = own[1].shape[1]
    parts = [(0, 1, j * width, width, False) for j in range(own[0].shape[1] // width)]
    parts.append((1, 1, 0, width, True))
    parts += [(2, 1, j * width, width, False) for j in range(own[2].shape[1] // width)]
    third = own[3].shape[0] // 3
    parts += [(3, 0, j * third, third, False) for j in range(3)]
    parts.append((4, 1, 0, both[0].shape[1], False))
    wide_two = both[1].shape[1] // 2
    parts += [(5, 1, j * wide_two, wide_two, True) for j in range(2)]
    parts.append((6, 1, 0, both[2].shape[1], False))
    return tuple(part + (i // 2,) for i, part in enumerate(parts))


def body(
    tokens,
    time_bins,
    labels,
    dino_feats,
    cotangent,
    time_table,
    class_table,
    ada_weight,
    ada_bias,
    qkv_weight,
    qkv_bias,
    out_weight,
    out_bias,
    mlp_in_weight,
    mlp_in_bias,
    mlp_out_weight,
    mlp_out_bias,
    align_weight_one,
    align_bias_one,
    align_weight_two,
    align_bias_two,
    align_weight_three,
    align_bias_three,
):
    count = lax.axis_size("dp")
    first_section = lax.axis_index("section") == 0
    index = lax.axis_index("dp")
    images, _, image_rows, model_width = tokens.shape
    rows_all = images * image_rows
    shard = out_weight.shape[1]
    kernels = count % 4 == 0 and shard % 8 == 0

    block_biases = (qkv_bias, out_bias, mlp_in_bias, mlp_out_bias, ada_bias)
    align_biases = (align_bias_one, align_bias_two, align_bias_three)
    block_sizes = [b.size for b in block_biases]
    align_sizes = [b.size for b in align_biases]
    indices = jnp.concatenate([time_bins, labels], 1).reshape(-1)
    pack = jnp.concatenate(
        [wide(half(b.reshape(-1))) for b in block_biases + align_biases] + [wide(indices)]
    )
    pack = padded(pack[None], rows_for(pack.size, 8))[0]
    if kernels:
        packs = share_small(count, pack).reshape(2, count, -1)
    else:
        packs = lax.all_gather(pack.reshape(-1), ("section", "dp")).reshape(2, count, -1)
    own_pack = jnp.where(first_section, packs[0], packs[1])
    block_full = [b.reshape(-1) for b in split_at(own_pack[:, : sum(block_sizes)], block_sizes)]
    bias_row = jnp.concatenate(
        [block_full[0][:model_width], jnp.zeros((model_width,), jnp.float32), block_full[0][model_width:]]
        + block_full[1:]
    )[None]
    start = sum(block_sizes)
    align_bias_full = [
        b.reshape(-1) for b in split_at(packs[:, :, start : start + sum(align_sizes)], align_sizes)
    ]
    start = start + sum(align_sizes)
    pairs = own_pack[:, start : start + 2 * images].astype(jnp.int32).reshape(count * images, 2)

    time_hot = pairs[:, :1] == jnp.arange(time_table.shape[0], dtype=jnp.int32)[None]
    class_hot = pairs[:, 1:] == jnp.arange(class_table.shape[0], dtype=jnp.int32)[None]
    cond = matmul(half(time_hot), half(time_table)) + matmul(half(class_hot), half(class_table))
    cond_act = half(jax.nn.silu(cond))
    ada_half = half(ada_weight[0])
    mod_wide = ada_half.shape[1]
    mod_parts = half(matmul(cond_act, ada_half)).reshape(count, images, mod_wide)
    mod_rows = rows_for(images * mod_wide, 16)

    start_rows = tokens.reshape(rows_all, model_width)
    own = [half(w[0]) for w in (qkv_weight, out_weight, mlp_in_weight, mlp_out_weight)]
    both = [half(w) for w in (align_weight_one, align_weight_two, align_weight_three)]
    one_rows = both[0].shape[0]
    one_padded = -(-one_rows // 16) * 16
    both[0] = jnp.pad(both[0], ((0, one_padded - one_rows), (0, 0)))
    place = jnp.arange(2 * count * one_padded, dtype=jnp.int32)
    owner, row = place // one_padded, place % one_padded
    wanted = jnp.where(row < one_rows, owner * one_rows + row, -1)[None]
    if kernels:
        chunked = mod_parts.reshape(count, images, 6, model_width // LANES, LANES)
        parts = padded(jnp.swapaxes(chunked, 2, 3).reshape(count, -1), mod_rows)
        modulation, gathered, kept = gather_forward(
            count, parts, start_rows, images, bias_row, own, both, gather_plan(own, both), 2
        )
        weights = [g.reshape(-1, g.shape[-1]) for g in gathered[:4]]
        align_weights = [g.reshape(-1, g.shape[-1]) for g in gathered[4:]]
        hidden = kept[10]
    else:
        modulation = lax.psum_scatter(wide(mod_parts), "dp", scatter_dimension=0, tiled=True)
        modulation = modulation.reshape(images, 6, model_width) + block_full[4].reshape(6, model_width)
        modulation = jnp.pad(modulation, ((0, 0), (0, 2), (0, 0)))
        weights = [lax.all_gather(w, "dp", axis=0, tiled=True) for w in own]
        align_weights = [lax.all_gather(w, ("section", "dp"), axis=0, tiled=True) for w in both]
        blank = kept_shapes(rows_all, model_width, images, weights[2].shape[1])
        blank = [jnp.zeros(b.shape, b.dtype) for b in blank[:10]]
        kept = block_forward(0, start_rows, modulation, bias_row, weights, blank)
        received = lax.ppermute(kept[10], "section", [(0, 1)])
        hidden = jnp.where(first_section, kept[10], received)
    aligner = (
        align_weights[0], align_bias_full[0], align_weights[1], align_bias_full[1],
        align_weights[2], align_bias_full[2],
    )

    target = dino_feats.reshape(rows_all, -1)
    *kept, final = block_forward(1, hidden, modulation, bias_row, weights, kept[:10])
    align_hidden, final = lax.optimization_barrier((hidden, final))
    grad_align, align_sums, align_grads = project_align(align_hidden, target, wanted, aligner, loss_weight)
    attn_input, qkv_rows, probs, mixed, attn_branch, after, mlp_input, slope, mlp_act, mlp_branch = kept

    def sources(block_input, grad):
        return (block_input, grad, mlp_branch, slope, after, attn_branch, probs, qkv_rows)

    last_sources = sources(hidden, cotangent.reshape(rows_all, model_width))
    if kernels:
        far = [g.reshape(2, count // 4, 2, 2, *w.shape) for g, w in zip(align_grads, both)]
        far = [far[2], far[0], far[1]]
        results = block_backward(count, 1, modulation, last_sources, weights, grad_align, far)
        grads, far_first_sum, far_halves = results[:10], results[10:13], results[13:]
    else:
        blank = block_backward(count, 0, modulation, last_sources, weights)
        grads = block_backward(count, 1, modulation, last_sources, weights, previous=blank)
        received = lax.ppermute(grad_align, "section", [(0, 1)])
        grad_hidden = half(wide(grads[0]) + wide(received))
        received = lax.ppermute(grad_hidden, "section", [(1, 0)])
        grads = [jnp.where(first_section, received, grad_hidden)] + list(grads[1:])
    grads = block_backward(
        count, 0, modulation, sources(start_rows, grads[0]), weights, previous=grads
    )
    in_grads, grad_qkv, grad_attn, grad_pre, grad_branch, grad_mod = grads[:6]
    outputs = jnp.where(first_section, hidden, final)
    grad_mod = half(grad_mod[:, :6])
    sums = [g[0] for g in grads[6:]]
    sums[0] = jnp.concatenate([sums[0][:model_width], sums[0][2 * model_width :]])
    align_bias_grads = [jnp.where(first_section, g, 0.0) for g in align_sums]
    align_sums = [jnp.moveaxis(g.reshape(2, count, -1), 0, 1).reshape(count, -1) for g in align_bias_grads]
    bias_flat = jnp.concatenate([g.reshape(count, -1) for g in sums] + align_sums, 1)
    if kernels:
        tall = mlp_act.shape[1] // (count * shard)
        n_qkv, n_in = 3, weights[2].shape[1] // model_width
        products = ((mlp_input, grad_pre), (attn_input, grad_qkv), (mixed, grad_attn))
        plan = [(0, 0, j) for j in range(n_in)] + [(1, 0, j) for j in range(n_qkv)] + [(2, 0, 0)]
        bias_grad_rows = rows_for(bias_flat.shape[1], 8)
        near_sum, far_sum, mods, bias_parts_sum = reduce_grads(
            count, shard, mlp_act, grad_branch, products, plan, far_halves, (False, True, False), (3, 8, 10), 3,
            padded(grad_mod.reshape(1, -1), mod_rows)[0], padded(bias_flat, bias_grad_rows),
        )
        grad_mods = mods.reshape(count, -1)[:, : images * mod_wide]
        bias_sum = jnp.sum(bias_parts_sum, 0).reshape(-1)
        grad_down_weight = wide(near_sum[:tall]).reshape(-1, model_width)
        grad_in_weight = wide(jnp.concatenate([near_sum[tall + j] for j in range(n_in)], 1))
        grad_qkv_weight = wide(jnp.concatenate([near_sum[tall + n_in + j] for j in range(n_qkv)], 1))
        grad_out_weight = wide(near_sum[tall + n_in + n_qkv])
        far_sum = [wide(jnp.where(first_section, a, b)) for a, b in zip(far_first_sum, far_sum)]
        align_out = [far_sum[1][:one_rows], far_sum[2], far_sum[0]]
    else:
        grad_mods = lax.all_gather(grad_mod.reshape(-1), "dp")
        bias_sum = lax.psum_scatter(bias_flat, "dp", scatter_dimension=0, tiled=True).reshape(-1)
        weight_grads = (
            transposed(attn_input, grad_qkv),
            transposed(mixed, grad_attn),
            transposed(mlp_input, grad_pre),
            transposed(mlp_act, grad_branch),
        )
        reduced = [
            lax.psum_scatter(g, "dp", scatter_dimension=0, tiled=True) for g in weight_grads
        ]
        grad_qkv_weight, grad_out_weight, grad_in_weight, grad_down_weight = reduced
        align_out = [
            lax.psum_scatter(
                jnp.where(first_section, wide(g), 0.0), ("section", "dp"), scatter_dimension=0, tiled=True
            )
            for g in align_grads
        ]
        align_out[0] = align_out[0][:one_rows]

    grad_mods = grad_mods.reshape(count * images, mod_wide)
    grad_ada = transposed(cond_act, grad_mods)
    mod_sums = jnp.sum(wide(grad_mods), 0)
    ada_share = mod_wide // count
    grad_ada_bias = lax.dynamic_slice(mod_sums, (index * ada_share,), (ada_share,))
    cond_part = times_transpose(grad_mods, ada_half)
    block_sum = sum(block_sizes[:4])
    grad_biases = split_at(bias_sum[:block_sum], block_sizes[:4])
    align_share = split_at(bias_sum[block_sum : block_sum + 2 * sum(align_sizes)], [2 * a for a in align_sizes])
    align_share = jnp.concatenate([a.reshape(2, -1) for a in align_share], 1)
    packet = jnp.concatenate([cond_part.reshape(-1), align_share.reshape(-1)])
    packet = packet + lax.ppermute(packet, "section", [(0, 1), (1, 0)])
    cond_grad = packet[: cond_part.size].reshape(cond_part.shape)
    align_share = packet[cond_part.size :].reshape(2, -1)
    align_share = jnp.where(first_section, align_share[0], align_share[1])
    align_bias_out = split_at(align_share, align_sizes)
    cond_grad = local_grad(jax.nn.silu, cond, cond_grad)

    def table_grad(hot):
        return lax.dot_general(
            wide(hot),
            cond_grad,
            (((0,), (0,)), ((), ())),
            precision=lax.Precision.HIGHEST,
            preferred_element_type=jnp.float32,
        )

    whole_rows = (1, images, 1, image_rows, model_width)
    return (
        outputs.reshape(whole_rows),
        in_grads.reshape(whole_rows),
        table_grad(time_hot),
        table_grad(class_hot),
        grad_ada[None],
        grad_ada_bias[None],
        grad_qkv_weight[None],
        grad_biases[0][None],
        grad_out_weight[None],
        grad_biases[1][None],
        grad_in_weight[None],
        grad_biases[2][None],
        grad_down_weight[None],
        grad_biases[3][None],
        align_out[0],
        align_bias_out[0],
        align_out[1],
        align_bias_out[1],
        align_out[2],
        align_bias_out[2],
    )


def solution(mesh):
    placed = (
        P(None, "dp", None, None),
        P(None, "dp"),
        P(None, "dp"),
        P(None, "dp", None, None),
        P(None, "dp", None, None),
        P(None, "dp"),
        P(None, "dp"),
        P("section", "dp", None),
        P("section", "dp"),
        P("section", "dp", None),
        P("section", "dp"),
        P("section", "dp", None),
        P("section", "dp"),
        P("section", "dp", None),
        P("section", "dp"),
        P("section", "dp", None),
        P("section", "dp"),
        P(("section", "dp"), None),
        P(("section", "dp")),
        P(("section", "dp"), None),
        P(("section", "dp")),
        P(("section", "dp"), None),
        P(("section", "dp")),
    )
    return jax.shard_map(
        body,
        mesh=mesh,
        in_specs=placed,
        out_specs=(
            P("section", None, "dp", None, None),
            P("section", None, "dp", None, None),
        )
        + placed[5:],
        check_vma=False,
    )
```

```python
import functools

import jax
import jax.numpy as jnp
from jax import lax
from jax.experimental import pallas as pl
from jax.experimental.pallas import tpu as pltpu
from jax.sharding import PartitionSpec as P

HEADS = 16
HD = 72
LANES = 128
MESH = pl.DeviceIdType.MESH
DMA = pltpu.SemaphoreType.DMA

epsilon = 1e-06
loss_weight = 0.5


def matmul(left, right):
    return jnp.dot(left, right, preferred_element_type=jnp.float32)


def transposed(left, right):
    return lax.dot_general(
        left, right, (((0,), (0,)), ((), ())), preferred_element_type=jnp.float32
    )


def times_transpose(grad_rows, weight):
    return lax.dot_general(
        grad_rows, weight, (((1,), (1,)), ((), ())), preferred_element_type=jnp.float32
    )


def local_grad(function, point, grad_value):
    return jax.vjp(function, point)[1](grad_value)[0]


def half(values):
    return values.astype(jnp.bfloat16)


def wide(values):
    return values.astype(jnp.float32)


GELU_SLOPE = 0.7978845608028654
GELU_CUBE = 0.044715


def dot_plain(left, right):
    return lax.dot_general(left, right, (((1,), (0,)), ((), ())), preferred_element_type=jnp.float32)


def dot_across(left, right):
    return lax.dot_general(left, right, (((1,), (1,)), ((), ())), preferred_element_type=jnp.float32)


def dot_down(left, right):
    return lax.dot_general(left, right, (((0,), (0,)), ((), ())), preferred_element_type=jnp.float32)


class Loads:
    def __init__(self, sems):
        self.sems, self.copies = sems, []

    def add(self, source, target, axis, tiles):
        size = source.shape[axis] // tiles
        first = len(self.copies)
        for j in range(tiles):
            place = (pl.ds(j * size, size),) if axis == 0 else (slice(None), pl.ds(j * size, size))
            self.copies.append(
                pltpu.make_async_copy(source.at[place], target.at[place], self.sems.at[first + j])
            )
        return list(range(first, first + tiles))

    def start(self):
        for copy in self.copies:
            copy.start()

    def wait(self, places):
        for place in places:
            self.copies[place].wait()


def head_window(head):
    low = head * HD
    start = low // LANES * LANES
    stop = -(-(low + HD) // LANES) * LANES
    return low, start, stop - start


def head_mask(head, rows):
    low, start, size = head_window(head)
    lane = lax.broadcasted_iota(jnp.int32, (rows, size), 1) + start
    return (lane >= low) & (lane < low + HD)


def masked(mask, values):
    return jnp.where(mask, values, jnp.zeros_like(values))


def row_norm(values):
    centred = values - jnp.mean(values, -1, keepdims=True)
    inverse = lax.rsqrt(jnp.mean(centred * centred, -1, keepdims=True) + epsilon)
    return centred * inverse, inverse


def row_norm_back(grad, normed, inverse):
    return inverse * (
        grad
        - jnp.mean(grad, -1, keepdims=True)
        - normed * jnp.mean(grad * normed, -1, keepdims=True)
    )


def column_tiles(total, tile):
    return [(at, min(tile, total - at)) for at in range(0, total, tile)]


class Forward:
    def __init__(self, images, x_ref, mod_ref, biases, kept, blend, weights, store):
        self.images, self.x_ref, self.mod_ref = images, x_ref, mod_ref
        self.qkv_bias, self.out_bias, self.in_bias, self.down_bias = biases
        (
            self.attn_in, self.qkv, self.probs, self.mixed, self.attn_branch, self.after,
            self.mlp_in, self.slope, self.act, self.mlp_branch, self.output,
        ) = kept
        self.blend, self.weights, self.store = blend, weights, store
        self.rows, self.width = x_ref.shape
        self.each = self.rows // images

    def at(self, image):
        return pl.ds(pl.multiple_of(image * self.each, self.each), self.each)

    def mod(self, image, k):
        return self.mod_ref[image, pl.ds(k, 1), :]

    def per_image(self, action):
        def one(image, carry):
            action(image, self.at(image))
            return carry

        lax.fori_loop(0, self.images, one, 0)

    def enter(self):
        def one(image, at):
            normed, _ = row_norm(wide(self.x_ref[at, :]))
            self.attn_in[at, :] = half(normed * (1.0 + self.mod(image, 1)) + self.mod(image, 0))

        self.per_image(one)
        self.store(0)

    def project_all(self, ready=None):
        def one(part, carry):
            if ready is not None:
                for third in range(3):

                    @pl.when(part == third)
                    def _():
                        ready(third)

            cols = pl.ds(pl.multiple_of(part * self.width, LANES), self.width)
            product = dot_plain(self.attn_in[...], self.weights[0](cols))
            self.qkv[:, cols] = half(product + self.qkv_bias[:, cols])
            return carry

        lax.fori_loop(0, 3, one, 0)
        self.store(1)

    def attend(self, image):
        at, each, width = self.at(image), self.each, self.width
        for head in range(HEADS):
            low, start, size = head_window(head)
            mask = head_mask(head, each)
            cols = [slice(part * width + start, part * width + start + size) for part in range(3)]
            queries = masked(mask, self.qkv[at, cols[0]])
            scores = dot_across(queries, self.qkv[at, cols[1]]) * HD ** (-0.5)
            powers = jnp.exp(scores - jnp.max(scores, -1, keepdims=True))
            soft = half(powers * (1.0 / jnp.sum(powers, -1, keepdims=True)))
            self.probs[image, head] = soft
            fresh = dot_plain(soft, self.qkv[at, cols[2]])
            window = slice(start, start + size)
            self.blend[:, window] = jnp.where(mask, fresh, self.blend[:, window])
        self.mixed[at, :] = half(self.blend[...])

    def attend_all(self):
        def one(image, carry):
            self.attend(image)
            return carry

        lax.fori_loop(0, self.images, one, 0)
        self.attended()

    def attended(self):
        self.store(2)
        self.store(3)

    def middle(self):
        branch = dot_plain(self.mixed[...], self.weights[1](slice(0, self.width))) + self.out_bias[...]
        self.attn_branch[...] = half(branch)
        self.store(4)

        def one(image, at):
            joined = wide(self.x_ref[at, :]) + self.mod(image, 2) * wide(self.attn_branch[at, :])
            self.after[at, :] = joined
            normed, _ = row_norm(joined)
            self.mlp_in[at, :] = half(normed * (1.0 + self.mod(image, 4)) + self.mod(image, 3))

        self.per_image(one)
        self.store(5)
        self.store(6)

    def feed(self, ready=None, tile=512):
        feeds = self.act.shape[1] // tile

        def one(j, carry):
            if ready is not None:
                for third in range(3):

                    @pl.when(j == feeds * third // 3)
                    def _():
                        ready(third)

            cols = pl.ds(pl.multiple_of(j * tile, tile), tile)
            pre = dot_plain(self.mlp_in[...], self.weights[2](cols)) + self.in_bias[:, cols]
            square = pre * pre
            bend = jnp.tanh(GELU_SLOPE * pre * (1.0 + GELU_CUBE * square))
            self.act[:, cols] = half(0.5 * pre * (1.0 + bend))
            self.slope[:, cols] = half(
                0.5 * (1.0 + bend)
                + 0.5 * pre * (1.0 - bend * bend) * (GELU_SLOPE + 3.0 * GELU_SLOPE * GELU_CUBE * square)
            )
            return carry

        lax.fori_loop(0, feeds, one, 0)
        self.store(7)
        self.store(8)

    def leave(self):
        branch = dot_plain(self.act[...], self.weights[3](slice(0, self.width))) + self.down_bias[...]
        self.mlp_branch[...] = half(branch)
        self.store(9)

        def one(image, at):
            self.output[at, :] = half(
                self.after[at, :] + self.mod(image, 5) * wide(self.mlp_branch[at, :])
            )

        self.per_image(one)
        self.store(10)


def kept_shapes(rows, width, images, hidden_width):
    each = rows // images
    thin = jax.ShapeDtypeStruct((rows, width), jnp.bfloat16)
    fat = jax.ShapeDtypeStruct((rows, hidden_width), jnp.bfloat16)
    return [
        thin, jax.ShapeDtypeStruct((rows, 3 * width), jnp.bfloat16),
        jax.ShapeDtypeStruct((images, HEADS, each, each), jnp.bfloat16), thin, thin,
        jax.ShapeDtypeStruct((rows, width), jnp.float32), thin, fat, fat, thin, thin,
    ]


def stored(refs, places, sems):
    copies = [pltpu.make_async_copy(a, b, sems.at[k]) for k, (a, b) in enumerate(zip(refs, places))]

    def wait():
        for copy in copies:
            copy.wait()

    return lambda k: copies[k].start(), wait


def flat(ref):
    def columns(cols):
        values = ref[:, :, cols]
        return values.reshape(values.shape[0] * values.shape[1], values.shape[2])

    return columns


def forward_kernel(images, own_section, *refs):
    x_hbm, mod_ref, bias = refs[:3]
    weights_hbm = refs[3:7]
    kept_out = refs[17:28]
    weights = refs[28:32]
    x_ref, *kept = refs[32:44]
    blend, load_sem, kept_sem = refs[44:]

    @pl.when(lax.axis_index("section") == own_section)
    def _():
        loads = Loads(load_sem)
        x_at = loads.add(x_hbm, x_ref, 0, 1)
        qkv_at = loads.add(weights_hbm[0], weights[0], 1, 3)
        out_at = loads.add(weights_hbm[1], weights[1], 0, 1)
        in_at = loads.add(weights_hbm[2], weights[2], 1, 3)
        down_at = loads.add(weights_hbm[3], weights[3], 0, 3)
        loads.start()
        store, wait_stored = stored(kept, kept_out, kept_sem)
        columns = [functools.partial(lambda ref, cols: ref[:, cols], ref) for ref in weights]
        forward = Forward(images, x_ref, mod_ref, bias_parts(bias), kept, blend, columns, store)
        loads.wait(x_at)
        forward.enter()
        forward.project_all(lambda part: loads.wait([qkv_at[part]]))
        forward.attend_all()
        loads.wait(out_at)
        forward.middle()
        forward.feed(lambda third: loads.wait([in_at[third]]))
        loads.wait(down_at)
        forward.leave()
        wait_stored()


def bias_parts(bias):
    width = bias.shape[1] // 15
    places = ((0, 3), (3, 1), (4, 4), (8, 1))
    return [bias.at[:, start * width : (start + size) * width] for start, size in places]


def block_forward(own_section, inputs, modulation, bias, weights, previous):
    rows, width = inputs.shape
    images = modulation.shape[0]
    each = rows // images
    kept = kept_shapes(rows, width, images, weights[2].shape[1])
    vmem, anywhere = pl.BlockSpec(memory_space=pltpu.VMEM), pl.BlockSpec(memory_space=pl.ANY)
    return pl.pallas_call(
        functools.partial(forward_kernel, images, own_section),
        out_shape=kept,
        in_specs=[anywhere, vmem, vmem] + [anywhere] * 14,
        out_specs=[anywhere] * 11,
        scratch_shapes=[pltpu.VMEM(w.shape, w.dtype) for w in weights]
        + [pltpu.VMEM(inputs.shape, inputs.dtype)]
        + [pltpu.VMEM(s.shape, s.dtype) for s in kept]
        + [pltpu.VMEM((each, width), jnp.float32), DMA((11,)), DMA((11,))],
        input_output_aliases={7 + k: k for k in range(10)},
        compiler_params=pltpu.CompilerParams(vmem_limit_bytes=63 * 2**20),
        name="block_forward",
    )(inputs, modulation, bias, *weights, *previous)


def backward_kernel(count, images, own_section, fresh, kept, *refs):
    refs = list(refs)

    def take(amount):
        taken = refs[:amount]
        del refs[:amount]
        return taken

    (mod_ref,) = take(1)
    sources = take(8)
    weights_hbm = take(4)
    if fresh:
        (extra_hbm,) = take(1)
        far_src = take(3)
    if kept:
        take(10)
    out_hbm = take(10)
    if fresh:
        far_out, half_out = take(3), take(3)
    held = take(8)
    in_w, down_w = take(2)
    outs = take(9)
    wide_grad, blend, load_sem, out_sem, late_sem = take(5)
    x_ref, dout, mlp_branch, slope, after, attn_branch, probs, qkv_ref = held
    dx_half, d_qkv, d_attn, d_branch, d_mod, qkv_sum, attn_sum, pre_sum, branch_sum = outs
    d_pre, half_grad = slope, dx_half
    if kept:
        sources[1] = out_hbm[0]
    out_refs = [dx_half, d_qkv, d_attn, d_pre, d_branch, d_mod, qkv_sum, attn_sum, pre_sum, branch_sum]
    rows, width = x_ref.shape
    each = rows // images
    hidden_width = in_w.shape[1]
    tile = 512
    section = lax.axis_index("section")
    dx_ref = wide_grad.at[1]
    grad_ref = wide_grad.at[0]

    feeds = hidden_width // tile
    if fresh:
        extra, extra_send, extra_recv, grad_send, grad_recv = take(5)
        place = own_place()
        other = (1 - section, place[1])
        greet_section(count, section, place[1], (other,))
        extra_copy = remote_copy(extra_hbm, extra, extra_send, extra_recv, other)

        def grad_copy(image):
            at = pl.ds(pl.multiple_of(image * each, each), each)
            return remote_copy(
                dx_half.at[at], out_hbm[0].at[at], grad_send.at[image], grad_recv.at[image], other
            )

        @pl.when(section != own_section)
        def _():
            extra_copy.start()
            far_sums(count, place, far_src, far_out, half_out, refs)
            extra_copy.wait_send()

            def one(image, carry):
                grad_copy(image).wait_recv()
                return carry

            lax.fori_loop(0, images, one, 0)

    @pl.when(section == own_section)
    def _():
        loads = Loads(load_sem)
        places = {}
        qkv_w = in_w.at[:, pl.ds(0, weights_hbm[0].shape[1])]
        out_w = down_w.at[pl.ds(0, width)]
        out_load = pltpu.make_async_copy(weights_hbm[1], out_w, late_sem.at[0])
        qkv_load = pltpu.make_async_copy(weights_hbm[0], qkv_w, late_sem.at[1])
        for name in (1, 2, "down", 3, "in", 4, 5, 6, 7, 0):
            if name == "down":
                places[name] = loads.add(weights_hbm[3], down_w, 0, 3)
            elif name == "in":
                places[name] = loads.add(weights_hbm[2], in_w, 0, 3)
            else:
                places[name] = loads.add(sources[name], held[name], 0, 1)
        loads.start()
        store, wait_stored = stored(out_refs, out_hbm, out_sem)

        def per_image(action):
            def one(image, carry):
                action(image, pl.ds(pl.multiple_of(image * each, each), each))
                return carry

            lax.fori_loop(0, images, one, 0)

        def mod(image, k):
            return mod_ref[image, pl.ds(k, 1), :]

        def sums(image, k, values):
            d_mod[image, pl.ds(k, 1), :] = jnp.sum(values, 0, keepdims=True)

        def enter(image, at):
            grad = wide(dout[at, :])
            d_branch[at, :] = half(grad * mod(image, 5))
            sums(image, 5, grad * wide(mlp_branch[at, :]))

        loads.wait(places[1] + places[2])
        per_image(enter)
        branch_sum[...] = jnp.sum(wide(d_branch[...]), 0, keepdims=True)
        store(4)
        store(9)
        loads.wait(places[3])

        def feed(j, carry):
            for third in range(3):

                @pl.when(j == feeds * third // 3)
                def _():
                    loads.wait([places["down"][third]])

            cols = pl.ds(pl.multiple_of(j * tile, tile), tile)
            grad = half(dot_across(d_branch[...], down_w[cols, :]) * wide(slope[:, cols]))
            d_pre[:, cols] = grad
            pre_sum[:, cols] = jnp.sum(wide(grad), 0, keepdims=True)
            return carry

        lax.fori_loop(0, feeds, feed, 0)
        out_load.start()
        store(3)
        store(8)
        loads.wait(places["in"])
        for start, size in column_tiles(width, 512):
            grad_ref[:, start : start + size] = dot_across(d_pre[...], in_w[start : start + size, :])
        qkv_load.start()

        def middle(image, at):
            grad_in = grad_ref[at, :]
            normed, inverse = row_norm(after[at, :])
            sums(image, 4, grad_in * normed)
            sums(image, 3, grad_in)
            grad = wide(dout[at, :]) + row_norm_back(grad_in * (1.0 + mod(image, 4)), normed, inverse)
            dx_ref[at, :] = grad
            d_attn[at, :] = half(grad * mod(image, 2))
            sums(image, 2, grad * wide(attn_branch[at, :]))

        loads.wait(places[4] + places[5])
        per_image(middle)
        attn_sum[...] = jnp.sum(wide(d_attn[...]), 0, keepdims=True)
        store(2)
        store(7)
        out_load.wait()
        half_grad[...] = half(dot_across(d_attn[...], out_w[...]))
        loads.wait(places[6] + places[7])

        def attend(image, at):
            for head in range(HEADS):
                low, start, size = head_window(head)
                mask = head_mask(head, each)
                window = slice(start, start + size)
                cols = [slice(part * width + start, part * width + start + size) for part in range(3)]
                grad = masked(mask, half_grad[at, window])
                soft = probs[image, head]
                grad_soft = dot_across(grad, qkv_ref[at, cols[2]])
                weighed = wide(soft) * grad_soft
                grad_scores = half(weighed - wide(soft) * jnp.sum(weighed, -1, keepdims=True))
                made = (
                    dot_plain(grad_scores, qkv_ref[at, cols[1]]) * HD ** (-0.5),
                    dot_down(grad_scores, qkv_ref[at, cols[0]]) * HD ** (-0.5),
                    dot_down(soft, grad),
                )
                for part in range(3):
                    blend[:, cols[part]] = jnp.where(mask, made[part], blend[:, cols[part]])
            d_qkv[at, :] = half(blend[...])

        def leave(image, at):
            grad_in = grad_ref[at, :]
            normed, inverse = row_norm(wide(x_ref[at, :]))
            sums(image, 1, grad_in * normed)
            sums(image, 0, grad_in)
            grad = dx_ref[at, :] + row_norm_back(grad_in * (1.0 + mod(image, 1)), normed, inverse)
            if fresh:
                grad = grad + wide(extra[at, :])
            dx_half[at, :] = half(grad)

        loads.wait(places[0])
        qkv_load.wait()
        if fresh:
            extra_copy.wait_recv()

            def finish(image, at):
                attend(image, at)
                for start, size in column_tiles(width, 512):
                    grad_ref[at, start : start + size] = dot_across(
                        d_qkv[at, :], qkv_w[start : start + size, :]
                    )
                leave(image, at)
                grad_copy(image).start()

            per_image(finish)
            store(1)
        else:
            per_image(attend)
            store(1)
            for start, size in column_tiles(width, 512):
                grad_ref[:, start : start + size] = dot_across(
                    d_qkv[...], qkv_w[start : start + size, :]
                )
            per_image(leave)
        store(0)
        qkv_sum[...] = jnp.sum(wide(d_qkv[...]), 0, keepdims=True)
        store(5)
        store(6)
        wait_stored()
        if fresh:

            def one(image, carry):
                grad_copy(image).wait_send()
                return carry

            lax.fori_loop(0, images, one, 0)
            total = len(FAR_CUTS)
            sems = refs[3 * total + 4 : 3 * total + 6]
            for i in range(total):
                if i in FAR_EARLY:
                    far_half_copy(i, None, half_out, sems, other).wait_recv()


FAR_CUTS = ((0, 1, 0, True), (2, 2, 0, False), (2, 2, 1, False), (1, 2, 0, False), (1, 2, 1, False))
FAR_EARLY = (0, 1)


def far_shape(cut, shapes):
    rows, columns = shapes[cut[0]]
    return (rows, columns // cut[1])


def far_place(cut, shapes):
    size = far_shape(cut, shapes)[1]
    return (slice(None), pl.ds(cut[2] * size, size))


def far_scratch(count, shapes):
    depth, kind, total = count // 4, jnp.bfloat16, len(FAR_CUTS)
    parts = [far_shape(cut, shapes) for cut in FAR_CUTS]
    tall, wide_most = max(s[0] for s in parts), max(s[1] for s in parts)
    slots = [chain_slots(depth, cut[3], s) for cut, s in zip(FAR_CUTS, parts)]
    return (
        [pltpu.VMEM((2, depth, 2) + s, kind) for s in parts]
        + [pltpu.VMEM((depth, 2, tall, wide_most), kind)]
        + [pltpu.VMEM(s[0], kind) for s in slots]
        + [pltpu.VMEM(s[1], kind) for s in slots]
        + [DMA, DMA((2, total)), DMA((2, total)), DMA((total,)), DMA((total,))]
        + [DMA((total,)), DMA((total,)), DMA((total, depth)), DMA((total, depth + 1))]
    )


def far_half_copy(i, source, half_out, sems, other):
    cut = FAR_CUTS[i]
    shapes = [ref.shape[2:] for ref in half_out]
    place = half_out[cut[0]].at[(slice(None), slice(None)) + far_place(cut, shapes)]
    if i not in FAR_EARLY:
        return pltpu.make_async_copy(place if source is None else source, place, sems[0].at[i])
    return remote_copy(
        place if source is None else source, place, sems[0].at[i], sems[1].at[i], other
    )


def far_sums(count, place, far_src, far_out, half_out, refs):
    depth, total = count // 4, len(FAR_CUTS)
    refs = list(refs)

    def take(amount):
        taken = refs[:amount]
        del refs[:amount]
        return taken

    core_in, held, y_in, z_in = take(total), take(1)[0], take(total), take(total)
    held_sem, core_send, core_recv, x_send, x_recv, y_send, y_recv, z_send, z_recv = refs
    section, me, z, y, c = place
    partner, other = (section, index_of(z, y, 1 - c)), (1 - section, me)
    shapes = [ref.shape for ref in far_out]
    places = [far_place(cut, shapes) for cut in FAR_CUTS]
    chains = [
        Chain(
            (section, z, y, c), depth, cut[3],
            lambda p: (core_in[p], (0,)), lambda p: y_in[p], lambda p: z_in[p],
            (y_send, y_recv, z_send, z_recv), lambda p: far_out[FAR_CUTS[p][0]].at[places[p]],
        )
        for cut in FAR_CUTS
    ]

    def core_copy(i, owner):
        source = far_src[FAR_CUTS[i][0]].at[(owner, slice(None), slice(None), 1 - c) + places[i]]
        return remote_copy(
            source, core_in[i].at[owner], core_send.at[owner, i], core_recv.at[owner, i], partner
        )

    def add_core(i, owner):
        ref = core_in[i]
        tile = (pl.ds(0, ref.shape[-2]), pl.ds(0, ref.shape[-1]))
        load = pltpu.make_async_copy(
            far_src[FAR_CUTS[i][0]].at[(owner, slice(None), slice(None), c) + places[i]],
            held.at[(slice(None), slice(None)) + tile],
            held_sem,
        )
        load.start()
        load.wait()
        core_copy(i, owner).wait_recv()

        def one(at, carry):
            to, side = at // 2, lax.rem(at, 2)
            ref[owner, to, side] = half(wide(ref[owner, to, side]) + wide(held[(to, side) + tile]))
            return carry

        lax.fori_loop(0, 2 * depth, one, 0)

    def leave(i):
        return far_half_copy(i, core_in[i].at[1], half_out, (x_send, x_recv), other)

    for owner in (0, 1):
        for i in range(total):
            core_copy(i, owner).start()
    for i in range(total):
        add_core(i, 0)
        chains[i].begin(i)
    for i in FAR_EARLY:
        add_core(i, 1)
        leave(i).start()
    later = [i for i in range(total) if i not in FAR_EARLY]
    for step in range(total + depth):
        for i in range(total):
            k = step - i + 1
            if 1 <= k < depth:
                chains[i].move(i, k)
            elif k == depth:
                chains[i].last(i)
        if later:
            i = later.pop(0)
            add_core(i, 1)
            leave(i).start()
    for i in range(total):
        chains[i].finish(i)
        core_copy(i, 0).wait_send()
        core_copy(i, 1).wait_send()
        if i in FAR_EARLY:
            leave(i).wait_send()
        else:
            leave(i).wait()


def block_backward(count, own_section, modulation, sources, weights, extra=None, far=(), previous=None):
    fresh = extra is not None
    rows, width = sources[0].shape
    images = modulation.shape[0]
    each = rows // images
    hidden_width = weights[2].shape[1]
    vmem, anywhere = pl.BlockSpec(memory_space=pltpu.VMEM), pl.BlockSpec(memory_space=pl.ANY)

    def shape(columns, kind=jnp.bfloat16, count=rows):
        return jax.ShapeDtypeStruct((count, columns), kind)

    outs = [
        shape(width), shape(3 * width), shape(width), shape(hidden_width), shape(width),
        jax.ShapeDtypeStruct((images, 8, width), jnp.float32),
        shape(3 * width, jnp.float32, 1), shape(width, jnp.float32, 1),
        shape(hidden_width, jnp.float32, 1), shape(width, jnp.float32, 1),
    ]
    scratch = [pltpu.VMEM(a.shape, a.dtype) for a in list(sources) + list(weights[2:])]
    scratch += [pltpu.VMEM(s.shape, s.dtype) for k, s in enumerate(outs) if k != 3]
    scratch += [
        pltpu.VMEM((2, rows, width), jnp.float32),
        pltpu.VMEM((each, 3 * width), jnp.float32), DMA((14,)), DMA((10,)), DMA((2,)),
    ]
    extra_in, extra_out, aliases = [], [], {}
    params = {}
    if fresh:
        extra_in = [extra] + list(far)
        scratch += [pltpu.VMEM(extra.shape, extra.dtype), DMA, DMA, DMA((images,)), DMA((images,))]
        shapes = [a.shape[4:] for a in far]
        extra_out = [jax.ShapeDtypeStruct(s, jnp.bfloat16) for s in shapes]
        extra_out += [jax.ShapeDtypeStruct((count // 4, 2) + s, jnp.bfloat16) for s in shapes]
        scratch += far_scratch(count, shapes)
        params = {"collective_id": 3, "has_side_effects": True}
    elif previous is not None:
        extra_in = list(previous)
        aliases = {13 + k: k for k in range(10)}
    return pl.pallas_call(
        functools.partial(
            backward_kernel, count, images, own_section, fresh, previous is not None
        ),
        out_shape=outs + extra_out,
        in_specs=[vmem] + [anywhere] * (12 + len(extra_in)),
        out_specs=[anywhere] * 10 + ([vmem] * 3 + [anywhere] * 3 if fresh else []),
        scratch_shapes=scratch,
        input_output_aliases=aliases,
        compiler_params=pltpu.CompilerParams(vmem_limit_bytes=63 * 2**20, **params),
        name="block_backward",
    )(modulation, *sources, *weights, *extra_in)


def sigmoid_parts(values):
    gate = 1.0 / (1.0 + jnp.exp(-values))
    return values * gate, gate * (1.0 + values * (1.0 - gate))


def align_kernel(
    loss,
    wanted, bias_one, bias_two, bias_three, x_hbm, target_hbm, one_hbm, two_hbm, three_hbm,
    dx_hbm, one_sum, two_sum, three_sum, one_grad, two_grad, three_grad,
    x_ref, target, dx_ref, one_w, two_w, three_w, padded_x, act_one, act_two, d_one, d_two, d_latent, slope_one, slope_two,
    product, sems, product_sem, dx_sem,
):
    tile = 512

    def layer(source, weight, bias, act, slope):
        def one(j, carry):
            cols = pl.ds(pl.multiple_of(j * tile, tile), tile)
            pre = dot_plain(source[...], weight[:, cols]) + bias[:, cols]
            value, bend = sigmoid_parts(pre)
            act[:, cols] = half(value)
            slope[:, cols] = half(bend)
            return carry

        lax.fori_loop(0, weight.shape[1] // tile, one, 0)

    def back(grad, weight, slope, target_ref, sum_ref):
        def one(j, carry):
            cols = pl.ds(pl.multiple_of(j * tile, tile), tile)
            value = half(dot_across(grad[...], weight[cols, :]) * wide(slope[:, cols]))
            target_ref[:, cols] = value
            sum_ref[:, cols] = jnp.sum(wide(value), 0, keepdims=True)
            return carry

        lax.fori_loop(0, weight.shape[0] // tile, one, 0)

    def picks(cols, size):
        row = lax.broadcasted_iota(jnp.int32, (x_ref.shape[1], size), 0)
        return half(jnp.where(row == wanted[:, cols], 1.0, 0.0))

    @pl.when(lax.axis_index("section") == 0)
    def _():
        loads = Loads(sems)
        x_at = loads.add(x_hbm, x_ref, 0, 1)
        target_at = loads.add(target_hbm, target, 0, 1)
        one_at = loads.add(one_hbm, one_w, 0, 1)
        two_at = loads.add(two_hbm, two_w, 0, 1)
        three_at = loads.add(three_hbm, three_w, 0, 1)
        loads.start()
        loads.wait(x_at)
        padded_width = one_w.shape[0]
        for start, size in column_tiles(padded_width, tile):
            cols = slice(start, start + size)
            padded_x[:, cols] = half(dot_plain(x_ref[...], picks(cols, size)))
        loads.wait(one_at)
        layer(padded_x, one_w, bias_one, act_one, slope_one)
        loads.wait(two_at)
        layer(act_one, two_w, bias_two, act_two, slope_two)
        loads.wait(three_at + target_at)
        latent = dot_plain(act_two[...], three_w[...]) + bias_three[...]
        features = wide(target[...])
        root_latent = lax.rsqrt(jnp.sum(latent * latent, -1, keepdims=True) + epsilon)
        root_target = lax.rsqrt(jnp.sum(features * features, -1, keepdims=True) + epsilon)
        crossed = jnp.sum(latent * features, -1, keepdims=True)
        grad = half(
            -loss
            * (
                features * (root_latent * root_target)
                - (crossed * root_target * root_latent * root_latent * root_latent) * latent
            )
        )
        d_latent[...] = grad
        three_sum[...] = jnp.sum(wide(grad), 0, keepdims=True)
        back(d_latent, three_w, slope_two, d_two, two_sum)
        back(d_two, two_w, slope_one, d_one, one_sum)
        total = jnp.zeros(x_ref.shape, jnp.float32)
        for start, size in column_tiles(padded_width, tile):
            cols = slice(start, start + size)
            value = half(dot_across(d_one[...], one_w[start : start + size, :]))
            total = total + dot_across(value, picks(cols, size))
        dx_ref[...] = half(total)
        dx_copy = pltpu.make_async_copy(dx_ref, dx_hbm, dx_sem)
        dx_copy.start()

        jobs = []
        for left, right, place in (
            (act_two, d_latent, three_grad), (padded_x, d_one, one_grad), (act_one, d_two, two_grad),
        ):
            for start, size in column_tiles(left.shape[1], tile):
                jobs.append((left, right, place, start, size))
        copies = []
        for k, (left, right, place, start, size) in enumerate(jobs):
            if k >= 2:
                copies[k - 2].wait()
            held = product.at[k % 2, pl.ds(0, size), pl.ds(0, right.shape[1])]
            held[...] = half(dot_down(left[:, start : start + size], right[...]))
            copies.append(
                pltpu.make_async_copy(held, place.at[pl.ds(start, size)], product_sem.at[k % 2])
            )
            copies[k].start()
        copies[-2].wait()
        copies[-1].wait()
        dx_copy.wait()


def project_align(hidden, target, wanted, aligner, loss):
    weight_one, bias_one, weight_two, bias_two, weight_three, bias_three = aligner
    rows, width = hidden.shape
    first, second, third = weight_one.shape[1], weight_two.shape[1], weight_three.shape[1]
    vmem, anywhere = pl.BlockSpec(memory_space=pltpu.VMEM), pl.BlockSpec(memory_space=pl.ANY)

    def shape(columns, kind=jnp.bfloat16, count=rows):
        return jax.ShapeDtypeStruct((count, columns), kind)

    weights = (weight_one, weight_two, weight_three)
    results = pl.pallas_call(
        functools.partial(align_kernel, loss),
        out_shape=[
            shape(width),
            shape(first, jnp.float32, 1), shape(second, jnp.float32, 1), shape(third, jnp.float32, 1),
        ]
        + [jax.ShapeDtypeStruct(w.shape, jnp.bfloat16) for w in weights],
        in_specs=[vmem] * 4 + [anywhere] * 5,
        out_specs=[anywhere] + [vmem] * 3 + [anywhere] * 3,
        scratch_shapes=[pltpu.VMEM(a.shape, a.dtype) for a in (hidden, target, hidden) + weights]
        + [
            pltpu.VMEM((rows, k), jnp.bfloat16)
            for k in (weight_one.shape[0], first, second, first, second, third, first, second)
        ]
        + [pltpu.VMEM((2, 512, max(first, second, third)), jnp.bfloat16), DMA((5,)), DMA((2,)), DMA],
        compiler_params=pltpu.CompilerParams(vmem_limit_bytes=62 * 2**20),
        name="project_align",
    )(
        wanted, bias_one[None], bias_two[None], bias_three[None], hidden, target, *weights
    )
    return results[0], results[1:4], results[4:]


def own_place():
    section = lax.axis_index("section")
    index = lax.axis_index("dp")
    return section, index, index // 4, lax.rem(index // 2, 2), lax.rem(index, 2)


def index_of(z, y, core):
    return z * 4 + y * 2 + core


def greet(targets):
    barrier = pltpu.get_barrier_semaphore()
    for target in targets:
        pl.semaphore_signal(barrier, inc=1, device_id=target, device_id_type=MESH)
    pl.semaphore_wait(barrier, len(targets))


def greet_section(count, section, index, extra=()):
    barrier = pltpu.get_barrier_semaphore()

    def one(step, carry):
        target = (section, lax.rem(index + step, count))
        pl.semaphore_signal(barrier, inc=1, device_id=target, device_id_type=MESH)
        return carry

    lax.fori_loop(1, count, one, 0)
    for target in extra:
        pl.semaphore_signal(barrier, inc=1, device_id=target, device_id_type=MESH)
    pl.semaphore_wait(barrier, count - 1 + len(extra))


class Exchange:
    def __init__(self, count, section, index, source, target, send, recv, local, own_only):
        self.count, self.section, self.index = count, section, index
        self.source, self.target = source, target
        self.send, self.recv, self.local, self.own_only = send, recv, local, own_only

    def piece(self, other):
        return self.source if self.own_only else self.source.at[other]

    def message(self, other, slot):
        return pltpu.make_async_remote_copy(
            src_ref=self.piece(other),
            dst_ref=self.target.at[slot],
            send_sem=self.send.at[other],
            recv_sem=self.recv.at[slot],
            device_id=(self.section, other),
            device_id_type=MESH,
        )

    def start(self):
        def one(step, carry):
            self.message(lax.rem(self.index + step, self.count), self.index).start()
            return carry

        lax.fori_loop(1, self.count, one, 0)
        pltpu.make_async_copy(
            self.piece(self.index), self.target.at[self.index], self.local
        ).start()

    def finish(self):
        def one(step, carry):
            other = lax.rem(self.index + step, self.count)
            self.message(other, self.index).wait_send()
            self.message(other, other).wait_recv()
            return carry

        lax.fori_loop(1, self.count, one, 0)
        pltpu.make_async_copy(
            self.piece(self.index), self.target.at[self.index], self.local
        ).wait()


def share_kernel(count, source, target, send, recv, local):
    section, index, z, y, core = own_place()
    me = section * count + index
    everybody = 2 * count

    def device(step):
        other = lax.rem(me + step, everybody)
        return other, (other // count, lax.rem(other, count))

    def message(other, where, slot):
        return remote_copy(
            source, target.at[slot // count, lax.rem(slot, count)], send.at[other], recv.at[slot], where
        )

    barrier = pltpu.get_barrier_semaphore()

    def greet_one(step, carry):
        pl.semaphore_signal(barrier, inc=1, device_id=device(step)[1], device_id_type=MESH)
        return carry

    def start_one(step, carry):
        other, where = device(step)
        message(other, where, me).start()
        return carry

    def finish_one(step, carry):
        other, where = device(step)
        message(other, where, me).wait_send()
        message(other, where, other).wait_recv()
        return carry

    lax.fori_loop(1, everybody, greet_one, 0)
    pl.semaphore_wait(barrier, everybody - 1)
    own = pltpu.make_async_copy(source, target.at[section, index], local)
    own.start()
    lax.fori_loop(1, everybody, start_one, 0)
    lax.fori_loop(1, everybody, finish_one, 0)
    own.wait()


def share_small(count, values):
    return pl.pallas_call(
        functools.partial(share_kernel, count),
        out_shape=jax.ShapeDtypeStruct((2, count) + values.shape, values.dtype),
        in_specs=[pl.BlockSpec(memory_space=pl.ANY)],
        out_specs=pl.BlockSpec(memory_space=pl.ANY),
        scratch_shapes=[DMA((2 * count,)), DMA((2 * count,)), DMA],
        compiler_params=pltpu.CompilerParams(collective_id=0, has_side_effects=True),
        name="share_small",
    )(values)


def gather_kernel(count, images, arrays, items, stride, *refs):
    total = len(items)
    modes = [item[0] >= 4 for item in items]
    first = [item[4] for item in items]
    starts = [item[5] for item in items]
    refs = list(refs)

    def take(amount):
        taken = refs[:amount]
        del refs[:amount]
        return taken

    part, x_ref, bias = take(3)
    src = take(arrays)
    part_out, mod_out = take(2)
    dst = take(arrays)
    kept_out = take(11)
    part_send, part_recv, part_local, local_sem, send_core, send_y, send_x, send_up, send_down, recv = take(10)
    weight_refs = take(4)
    kept = take(11)
    part_in, blend, part_sem, weight_sem, kept_sem, hidden_send, hidden_recv = refs
    depth = count // 4
    section, me, z, y, c = own_place()
    up, down = (section, me + 4), (section, me - 4)
    across, partner = (section, index_of(z, 1 - y, c)), (section, index_of(z, y, 1 - c))
    other = (1 - section, me)
    greet_section(count, section, me, (other,))
    parts = Exchange(count, section, me, part, part_out, part_send, part_recv, part_local, False)
    parts.start()

    def cut(w):
        _, axis, start, size = items[w][:4]
        return (pl.ds(start, size),) if axis == 0 else (slice(None), pl.ds(start, size))

    def slot(w, sec, blk):
        place = (sec, blk) if modes[w] else (blk,)
        return dst[items[w][0]].at[place + cut(w)]

    def source_of(w):
        return src[items[w][0]].at[cut(w)]

    def copy(w, sec, blk, target, sem, src_ref=None):
        here = slot(w, sec, blk)
        return pltpu.make_async_remote_copy(
            src_ref=here if src_ref is None else src_ref,
            dst_ref=here,
            send_sem=sem,
            recv_sem=recv.at[w, sec if modes[w] else 0, blk],
            device_id=target,
            device_id_type=MESH,
        )

    def arrived(w, sec, blk):
        copy(w, sec, blk, partner, send_core.at[w, 0, 0, 0]).wait_recv()

    def pass_on(w, zz, side, go_up, go_down, go_across, source=None):
        blk = index_of(zz, y if side == 0 else 1 - y, c)
        if go_up is not None:

            @pl.when(go_up)
            def _():
                copy(w, section, blk, up, send_up.at[w, side, zz], source).start()

        if go_down is not None:

            @pl.when(go_down)
            def _():
                copy(w, section, blk, down, send_down.at[w, side, zz], source).start()

        if go_across:
            copy(w, section, blk, across, send_y.at[w, zz], source).start()
        if modes[w]:

            @pl.when(section == 1)
            def _():
                copy(w, section, blk, other, send_x.at[w, side, zz], source).start()

        copy(w, section, blk, partner, send_core.at[w, 0, side, zz], source).start()

    def depart(w):
        pass_on(w, z, 0, z < depth - 1, z > 0, True, source_of(w))
        pltpu.make_async_copy(source_of(w), slot(w, section, me), local_sem.at[w]).start()

    def near(w, k):
        if k >= depth:
            return

        @pl.when(z >= k)
        def _():
            arrived(w, section, index_of(z - k, y, c))
            pass_on(w, z - k, 0, z < depth - 1, None, not first[w])

        @pl.when(z + k < depth)
        def _():
            arrived(w, section, index_of(z + k, y, c))
            pass_on(w, z + k, 0, None, z > 0, not first[w])

    def far(w, k):
        @pl.when(z >= k)
        def _():
            arrived(w, section, index_of(z - k, 1 - y, c))
            if first[w]:
                pass_on(w, z - k, 1, z < depth - 1, (z > 0) if k == 0 else None, False)
            else:
                pass_on(w, z - k, 1, None, None, False)

        if k > 0:

            @pl.when(z + k < depth)
            def _():
                arrived(w, section, index_of(z + k, 1 - y, c))
                pass_on(w, z + k, 1, None, (z > 0) if first[w] else None, False)

    def complete(w):
        pltpu.make_async_copy(source_of(w), slot(w, section, me), local_sem.at[w]).wait()
        for side in range(2):

            def one(zz, carry):
                arrived(w, section, index_of(zz, y if side == 0 else 1 - y, 1 - c))
                return carry

            lax.fori_loop(0, depth, one, 0)

    def load(w):
        return pltpu.make_async_copy(dst[w], weight_refs[w], weight_sem.at[w])

    def modulate():
        parts.finish()
        copy_in = pltpu.make_async_copy(part_out, part_in, part_sem)
        copy_in.start()
        copy_in.wait()
        total_mod = wide(part_in[0])
        for device in range(1, count):
            total_mod = total_mod + wide(part_in[device])
        chunks = x_ref.shape[1] // LANES
        for image in range(images):
            for q in range(chunks):
                at = (image * chunks + q) * 6
                cols = slice(q * LANES, (q + 1) * LANES)
                mod_out[image, 0:6, cols] = total_mod[at : at + 6]
            for k in range(6):
                start = (9 + k) * x_ref.shape[1]
                mod_out[image, k : k + 1, :] += bias[:, start : start + x_ref.shape[1]]

    store, wait_stored = stored(kept, kept_out, kept_sem)
    forward = Forward(
        images, x_ref, mod_out, bias_parts(bias), kept, blend,
        [flat(ref) for ref in weight_refs], store,
    )

    def on_first(action):
        @pl.when(section == 0)
        def _():
            action()

    def load_array(a):
        on_first(lambda: load(a).start())

    last_item = [max(w for w in range(total) if items[w][0] == a) for a in range(4)]
    events = []
    for t in range(max(starts) + stride * depth + 1):
        for w in range(total):
            k, rest = divmod(t - starts[w], stride)
            if rest or k < 0 or k > depth:
                continue
            if k == 0:
                events.append((t, functools.partial(depart, w), None))
                continue
            if first[w]:
                events.append((t, functools.partial(far, w, k - 1), None))
                events.append((t, functools.partial(near, w, k), None))
            else:
                events.append((t, functools.partial(near, w, k), None))
                events.append((t, functools.partial(far, w, k - 1), None))
            if k == depth and not modes[w]:
                events.append((t, functools.partial(complete, w), None))
                a = items[w][0]
                if w == last_item[a]:
                    events.append((t, functools.partial(load_array, a), a))
    def finish_block():
        forward.leave()
        remote_copy(kept[10], kept_out[10], hidden_send, hidden_recv, other).start()

    groups = [
        [forward.project_all, forward.attend_all],
        [forward.middle],
        [forward.feed],
        [finish_block],
    ]

    def run_group(w):
        load(w).wait()
        for chunk in groups[w]:
            chunk()

    modulated = False
    for i, (t, event, ready) in enumerate(events):
        event()
        if not modulated and t == stride and events[i + 1][0] > stride:
            modulated = True
            modulate()
            on_first(forward.enter)
        if ready is not None:
            on_first(functools.partial(run_group, ready))

    for w in range(total):
        if modes[w]:
            complete(w)

            @pl.when(section == 0)
            def _():
                for side in range(2):

                    def from_x(zz, carry):
                        blk = index_of(zz, y if side == 0 else 1 - y, c)
                        arrived(w, 1, blk)
                        copy(w, 1, blk, partner, send_core.at[w, 1, side, zz]).start()
                        return carry

                    lax.fori_loop(0, depth, from_x, 0)

    for w in range(total):
        for side in range(2):

            def finish(zz, carry):
                copy(w, section, me, partner, send_core.at[w, 0, side, zz]).wait_send()
                if modes[w]:

                    @pl.when(section == 1)
                    def _():
                        copy(w, section, me, other, send_x.at[w, side, zz]).wait_send()

                    @pl.when(section == 0)
                    def _():
                        blk = index_of(zz, y if side == 0 else 1 - y, 1 - c)
                        arrived(w, 1, blk)
                        copy(w, 1, blk, partner, send_core.at[w, 1, side, zz]).wait_send()

                if side == 0:

                    @pl.when((zz == z) if first[w] else (zz >= 0))
                    def _():
                        copy(w, section, me, across, send_y.at[w, zz]).wait_send()

                if side == 0 or first[w]:

                    @pl.when((z < depth - 1) & (zz <= z))
                    def _():
                        copy(w, section, me, up, send_up.at[w, side, zz]).wait_send()

                    @pl.when((z > 0) & (zz >= z))
                    def _():
                        copy(w, section, me, down, send_down.at[w, side, zz]).wait_send()

                return carry

            lax.fori_loop(0, depth, finish, 0)
    hidden_copy = remote_copy(kept[10], kept_out[10], hidden_send, hidden_recv, other)

    @pl.when(section == 0)
    def _():
        hidden_copy.wait_send()
        wait_stored()

    @pl.when(section == 1)
    def _():
        hidden_copy.wait_recv()


def gather_forward(count, parts, inputs, images, bias, own, both, items, stride):
    arrays = list(own) + list(both)
    modes = [False] * len(own) + [True] * len(both)
    total, depth, n_arrays = len(items), count // 4, len(arrays)
    rows, width = inputs.shape
    anywhere, vmem = pl.BlockSpec(memory_space=pl.ANY), pl.BlockSpec(memory_space=pltpu.VMEM)
    shapes = [((2, count) if m else (count,)) + a.shape for a, m in zip(arrays, modes)]
    kept = kept_shapes(rows, width, images, own[2].shape[1])
    results = pl.pallas_call(
        functools.partial(gather_kernel, count, images, n_arrays, items, stride),
        out_shape=[
            jax.ShapeDtypeStruct(parts.shape, parts.dtype),
            jax.ShapeDtypeStruct((images, 8, width), jnp.float32),
        ]
        + [jax.ShapeDtypeStruct(s, a.dtype) for s, a in zip(shapes, arrays)]
        + kept,
        in_specs=[anywhere] + [vmem] * 2 + [anywhere] * n_arrays,
        out_specs=[anywhere, vmem] + [anywhere] * (n_arrays + 11),
        scratch_shapes=[
            DMA((count,)),
            DMA((count,)),
            DMA,
            DMA((total,)),
            DMA((total, 2, 2, depth)),
            DMA((total, depth)),
            DMA((total, 2, depth)),
            DMA((total, 2, depth)),
            DMA((total, 2, depth)),
            DMA((total, 2, count)),
        ]
        + [pltpu.VMEM((count,) + a.shape, a.dtype) for a in own]
        + [pltpu.VMEM(s.shape, s.dtype) for s in kept]
        + [
            pltpu.VMEM(parts.shape, parts.dtype),
            pltpu.VMEM((rows // images, width), jnp.float32),
            DMA,
            DMA((4,)),
            DMA((11,)),
            DMA,
            DMA,
        ],
        compiler_params=pltpu.CompilerParams(
            collective_id=1, has_side_effects=True, vmem_limit_bytes=63 * 2**20
        ),
        name="gather_forward",
    )(parts, inputs, bias, *arrays)
    return results[1], results[2 : 2 + n_arrays], results[2 + n_arrays :]


class Chain:
    def __init__(self, place, depth, z_first, sums, y_in, z_in, sems, out):
        self.section, self.z, self.y, self.c = place
        self.depth, self.z_first = depth, z_first
        self.sums, self.y_in, self.z_in, self.out = sums, y_in, z_in, out
        self.y_send, self.y_recv, self.z_send, self.z_recv = sems
        me = index_of(self.z, self.y, self.c)
        self.up, self.down = (self.section, me + 4), (self.section, me - 4)
        self.across = (self.section, index_of(self.z, 1 - self.y, self.c))

    def part(self, p, to):
        ref, lead = self.sums(p)
        return ref, lead + ((to,) if self.z_first else (to, self.y))

    def y_copy(self, p):
        ref, lead = self.sums(p)
        whole = self.z if self.z_first else slice(None)
        return remote_copy(
            ref.at[lead + (whole, 1 - self.y)],
            self.y_in(p),
            self.y_send.at[p],
            self.y_recv.at[p],
            self.across,
        )

    def z_copy(self, p, to, where, device):
        ref, place = self.part(p, to)
        return remote_copy(
            ref.at[place], self.z_in(p).at[where], self.z_send.at[p, to], self.z_recv.at[p, where], device
        )

    def add_z(self, p, to, where):
        self.z_copy(p, 0, where, self.across).wait_recv()
        ref, place = self.part(p, to)
        z_in = self.z_in(p)
        if self.z_first:
            for side in range(2):
                ref[place + (side,)] = half(wide(ref[place + (side,)]) + wide(z_in[where, side]))
        else:
            ref[place] = half(wide(ref[place]) + wide(z_in[where]))

    def hop(self, p, h):
        @pl.when((self.z == h) & (self.z < self.depth - 1))
        def _():
            def one(back, carry):
                to = self.depth - 1 - back
                if h > 0:
                    self.add_z(p, to, to)
                self.z_copy(p, to, to, self.up).start()
                return carry

            lax.fori_loop(0, self.depth - 1 - self.z, one, 0)

        @pl.when((self.depth - 1 - self.z == h) & (self.z > 0))
        def _():
            def one(to, carry):
                if h > 0:
                    self.add_z(p, to, to)
                self.z_copy(p, to, jnp.where(to == self.z - 1, self.depth, to), self.down).start()
                return carry

            lax.fori_loop(0, self.z, one, 0)

    def join(self, p):
        @pl.when(self.z > 0)
        def _():
            self.add_z(p, self.z, self.z)

        @pl.when(self.z < self.depth - 1)
        def _():
            self.add_z(p, self.z, self.depth)

    def begin(self, p):
        if self.z_first:
            self.hop(p, 0)
        else:
            self.y_copy(p).start()

    def move(self, p, step):
        if self.z_first:
            if step < self.depth - 1:
                self.hop(p, step)
            else:
                self.join(p)
                self.y_copy(p).start()
            return
        if step == 1:
            self.y_copy(p).wait_recv()
            y_in = self.y_in(p)

            def one(to, carry):
                ref, place = self.part(p, to)
                ref[place] = half(wide(ref[place]) + wide(y_in[to]))
                return carry

            lax.fori_loop(0, self.depth, one, 0)
        self.hop(p, step - 1)

    def last(self, p):
        ref, lead = self.sums(p)
        if self.z_first:
            self.y_copy(p).wait_recv()
            total = wide(ref[lead + (self.z, self.y)]) + wide(self.y_in(p)[...])
            self.out(p)[...] = half(total)
        else:
            self.join(p)
            self.out(p)[...] = ref[lead + (self.z, self.y)]

    def finish(self, p):
        self.y_copy(p).wait_send()

        def one(to, carry):
            @pl.when(to != self.z)
            def _():
                self.z_copy(p, to, to, self.across).wait_send()

            return carry

        lax.fori_loop(0, self.depth, one, 0)


def chain_slots(depth, first, shape):
    y_shape = shape if first else (depth,) + shape
    z_shape = (depth + 1, 2) + shape if first else (depth + 1,) + shape
    return y_shape, z_shape


def remote_copy(source, target, send, recv, device):
    return pltpu.make_async_remote_copy(
        src_ref=source,
        dst_ref=target,
        send_sem=send,
        recv_sem=recv,
        device_id=device,
        device_id_type=MESH,
    )


def reduce_kernel(count, ready, pairs, plan, far_first, far_steps, stride, *refs):
    depth = count // 4
    far_total = len(far_first)
    near_total = ready + len(plan)
    refs = list(refs)

    def take(amount):
        taken = refs[:amount]
        del refs[:amount]
        return taken

    act_src, branch_src, wanted = take(3)
    left_src, right_src = take(pairs), take(pairs)
    far_src = take(far_total)
    mod_src, bias_src = take(2)
    (near_out,) = take(1)
    far_out = take(far_total)
    mod_out, bias_out = take(2)
    left, right, chunk, picked, made, core_in, y_in, z_in, tail_y_in, tail_z_in = take(10)
    far_core_in, far_y_in, far_z_in = take(far_total), take(far_total), take(far_total)
    (
        left_sem, right_sem, chunk_sem, core_send, core_recv, y_send, y_recv, z_send, z_recv,
        far_local, far_send, far_recv,
        far_y_send, far_y_recv, far_z_send, far_z_recv,
        mod_send, mod_recv, mod_local, bias_send, bias_recv, bias_local,
    ) = refs
    section, me, z, y, c = own_place()
    partner = (section, index_of(z, y, 1 - c))
    other = (1 - section, me)
    barrier = pltpu.get_barrier_semaphore()

    def greet_one(step, carry):
        target = (section, lax.rem(me + step, count))
        pl.semaphore_signal(barrier, inc=1, device_id=target, device_id_type=MESH)
        return carry

    lax.fori_loop(1, count, greet_one, 0)

    @pl.when(section == 1)
    def _():
        pl.semaphore_signal(barrier, inc=1, device_id=other, device_id_type=MESH)
        pl.semaphore_wait(barrier, count - 1)

    @pl.when(section == 0)
    def _():
        pl.semaphore_wait(barrier, count)

    rows, width = made.shape[-2:]
    mods = Exchange(count, section, me, mod_src, mod_out, mod_send, mod_recv, mod_local, True)
    biases = Exchange(count, section, me, bias_src, bias_out, bias_send, bias_recv, bias_local, False)

    base = near_total - 2
    order = [near_total - 1, base] + list(range(ready, base)) + list(range(ready))

    def operands(p, slot):
        pair, row, column = plan[p - ready]
        return (
            pltpu.make_async_copy(
                left_src[pair].at[:, pl.ds(row * width, width)], left.at[slot], left_sem.at[slot]
            ),
            pltpu.make_async_copy(
                right_src[pair].at[:, pl.ds(column * width, width)], right.at[slot], right_sem.at[slot]
            ),
        )

    def branch_copy(slot):
        return pltpu.make_async_copy(branch_src, right.at[slot], right_sem.at[slot])

    def chunk_copy(w):
        return pltpu.make_async_copy(
            act_src.at[:, pl.ds(w * width, width)], chunk.at[w % 2], chunk_sem.at[w % 2]
        )

    def pick(p, slot):
        chunks = act_src.shape[1] // width
        picked[...] = jnp.zeros(picked.shape, jnp.float32)
        chunk_copy(0).start()
        row = wanted[pl.ds(p, 1), :]
        for w in range(chunks):
            if w + 1 < chunks:
                chunk_copy(w + 1).start()
            start = w * width // chunks // LANES * LANES
            stop = -(-((w + 1) * width // chunks) // LANES) * LANES
            window = slice(start, stop)
            at = lax.broadcasted_iota(jnp.int32, (width, stop - start), 0) + w * width
            picks = half(jnp.where(at == row[:, window], 1.0, 0.0))
            chunk_copy(w).wait()
            picked[:, window] += dot_plain(chunk[w % 2], picks)
        left[slot] = half(picked[...])

    def core_copy(p, slot):
        return remote_copy(
            made.at[slot, :, :, 1 - c], core_in.at[p], core_send.at[p], core_recv.at[p], partner
        )

    def fetch(t, slot):
        for i, p in enumerate(order):

            @pl.when(t == i)
            def _():
                if p < ready:
                    branch_copy(slot).start()
                else:
                    for copy in operands(p, slot):
                        copy.start()

    def piece_of(t):
        return jnp.where(t < 2, near_total - 1 - t, lax.rem(t - 2 + ready, base))

    def make(t):
        slot = lax.rem(t, 2)
        p = piece_of(t)

        @pl.when(t >= 2)
        def _():
            core_copy(piece_of(t - 2), slot).wait_send()

        @pl.when(t + 1 < near_total)
        def _():
            fetch(t + 1, 1 - slot)

        @pl.when(p < ready)
        def _():
            pick(p, slot)
            branch_copy(slot).wait()

        @pl.when(p >= ready)
        def _():
            for copy in operands(ready, slot):
                copy.wait()

        tile = 3 * LANES
        for at in range(0, width, tile):
            cols = slice(at, at + tile)
            product = dot_down(left[slot], right[slot, :, cols])
            made[slot, :, :, :, :, cols] = half(product).reshape(depth, 2, 2, rows, tile)
        core_copy(p, slot).start()

    near = Chain(
        (section, z, y, c), depth, False,
        lambda p: (core_in, (p,)), lambda p: y_in.at[p], lambda p: z_in.at[p],
        (y_send, y_recv, z_send, z_recv), lambda p: near_out.at[p],
    )
    tail = Chain(
        (section, z, y, c), depth, True,
        lambda p: (core_in, (p,)), lambda p: tail_y_in.at[p - base], lambda p: tail_z_in.at[p - base],
        (y_send, y_recv, z_send, z_recv), lambda p: near_out.at[p],
    )
    far = [
        Chain(
            (section, z, y, c), depth, far_first[i],
            lambda p: (far_core_in[p], ()), lambda p: far_y_in[p], lambda p: far_z_in[p],
            (far_y_send, far_y_recv, far_z_send, far_z_recv), lambda p: far_out[p],
        )
        for i in range(far_total)
    ]

    def begin(t):
        slot = lax.rem(t, 2)
        p = piece_of(t)
        core_copy(p, slot).wait_recv()

        def add_side(side):
            def one(to, carry):
                core_in[p, to, side] = half(
                    wide(core_in[p, to, side]) + wide(made[slot, to, side, c])
                )
                return carry

            lax.fori_loop(0, depth, one, 0)

        add_side(1 - y)

        @pl.when(p < base)
        def _():
            near.begin(p)

        add_side(y)

        @pl.when(p >= base)
        def _():
            tail.begin(p)

    def far_columns(i, late):
        size = far_core_in[i].shape[-1]
        start, stop = {0: (size, size), 1: (0, size), 2: (size // 2, size)}[i]
        start, stop = (start, stop) if late else (0, start)
        return (slice(None),) * 3 + (pl.ds(start, stop - start),)

    def far_lies(i):
        at = far_columns(i, False)
        return pltpu.make_async_copy(far_src[i].at[at], far_core_in[i].at[at], far_local.at[i])

    def far_comes(i):
        at = far_columns(i, True)
        return remote_copy(
            far_src[i].at[at], far_core_in[i].at[at], far_send.at[i], far_recv.at[i], other
        )

    fetch(0, 0)

    @pl.when(section == 0)
    def _():
        for i in (1, 2):
            far_comes(i).start()

    @pl.when(section == 1)
    def _():
        for i in (0, 2):
            far_lies(i).start()

    mods.start()
    biases.start()

    def step(t, carry):
        @pl.when(t < near_total)
        def _():
            make(t)

        @pl.when((t >= 1) & (t <= near_total))
        def _():
            begin(t - 1)

        for i in range(far_total):

            @pl.when((t == far_steps[i]) & (section == 1))
            def _():
                if i != 1:
                    far_lies(i).wait()
                if i != 0:
                    far_comes(i).wait_recv()
                far[i].begin(i)

            for k in range(1, depth):

                @pl.when((t == far_steps[i] + stride * k) & (section == 1))
                def _():
                    far[i].move(i, k)

            @pl.when((t == far_steps[i] + stride * depth) & (section == 1))
            def _():
                far[i].last(i)

        for k in range(1, depth):
            p = t - 3 - stride * k

            @pl.when((p >= 0) & (p < base))
            def _():
                near.move(lax.rem(p + ready, base), k)

            for q in range(2):

                @pl.when(t == 1 + q + stride * k)
                def _():
                    tail.move(near_total - 1 - q, k)

        p = t - 3 - stride * depth

        @pl.when((p >= 0) & (p < base))
        def _():
            near.last(lax.rem(p + ready, base))

        for q in range(2):

            @pl.when(t == 1 + q + stride * depth)
            def _():
                tail.last(near_total - 1 - q)

        return carry

    lax.fori_loop(0, max(near_total + 1, max(far_steps) + 1) + stride * depth, step, 0)
    for t in (near_total - 2, near_total - 1):
        core_copy(order[t], t % 2).wait_send()

    @pl.when(section == 0)
    def _():
        for i in (1, 2):
            far_comes(i).wait_send()

    @pl.when(section == 1)
    def _():
        for i in range(far_total):
            far[i].finish(i)

    def near_finish(p, carry):
        near.finish(p)
        return carry

    lax.fori_loop(0, base, near_finish, 0)
    for q in range(2):
        tail.finish(near_total - 1 - q)
    mods.finish()
    biases.finish()


def reduce_grads(count, rows, act, branch, pairs, plan, far, far_first, far_steps, stride, mods, biases):
    depth = count // 4
    tokens, width = branch.shape
    pieces = act.shape[1] // (count * rows)
    near_total = pieces + len(plan)
    lane = jnp.arange(width, dtype=jnp.int32)
    wanted = jnp.stack([(lane // rows * pieces + j) * rows + lane % rows for j in range(pieces)])
    far_shapes = [a.shape[2:] for a in far]
    kind = jnp.bfloat16
    anywhere, vmem = pl.BlockSpec(memory_space=pl.ANY), pl.BlockSpec(memory_space=pltpu.VMEM)
    n_far = len(far)
    lefts, rights = [a for a, _ in pairs], [b for _, b in pairs]

    far_slots = [chain_slots(depth, f, s) for f, s in zip(far_first, far_shapes)]
    results = pl.pallas_call(
        functools.partial(reduce_kernel, count, pieces, len(pairs), plan, far_first, far_steps, stride),
        out_shape=[jax.ShapeDtypeStruct((near_total, rows, width), kind)]
        + [jax.ShapeDtypeStruct(s, kind) for s in far_shapes]
        + [
            jax.ShapeDtypeStruct((count,) + mods.shape, mods.dtype),
            jax.ShapeDtypeStruct(biases.shape, biases.dtype),
        ],
        in_specs=[anywhere] * 2 + [vmem] + [anywhere] * (2 * len(pairs) + n_far + 2),
        out_specs=[vmem] * (1 + n_far) + [anywhere] * 2,
        scratch_shapes=[
            pltpu.VMEM((2, tokens, width), kind),
            pltpu.VMEM((2, tokens, width), kind),
            pltpu.VMEM((2, tokens, width), kind),
            pltpu.VMEM((tokens, width), jnp.float32),
            pltpu.VMEM((2, depth, 2, 2, rows, width), kind),
            pltpu.VMEM((near_total, depth, 2, rows, width), kind),
            pltpu.VMEM((near_total - 2, depth, rows, width), kind),
            pltpu.VMEM((near_total - 2, depth + 1, rows, width), kind),
            pltpu.VMEM((2, rows, width), kind),
            pltpu.VMEM((2, depth + 1, 2, rows, width), kind),
        ]
        + [pltpu.VMEM((depth, 2) + s, kind) for s in far_shapes]
        + [pltpu.VMEM(s[0], kind) for s in far_slots]
        + [pltpu.VMEM(s[1], kind) for s in far_slots]
        + [
            DMA((2,)),
            DMA((2,)),
            DMA((2,)),
            DMA((near_total,)),
            DMA((near_total,)),
            DMA((near_total,)),
            DMA((near_total,)),
            DMA((near_total, depth)),
            DMA((near_total, depth + 1)),
            DMA((n_far,)),
            DMA((n_far,)),
            DMA((n_far,)),
            DMA((n_far,)),
            DMA((n_far,)),
            DMA((n_far, depth)),
            DMA((n_far, depth + 1)),
            DMA((count,)),
            DMA((count,)),
            DMA,
            DMA((count,)),
            DMA((count,)),
            DMA,
        ],
        compiler_params=pltpu.CompilerParams(
            collective_id=2, has_side_effects=True, vmem_limit_bytes=63 * 2**20
        ),
        name="reduce_grads",
    )(act, branch, wanted, *lefts, *rights, *far, mods, biases)
    return results[0], results[1 : 1 + n_far], results[1 + n_far], results[2 + n_far]


def padded(values, rows):
    flat = values.reshape(values.shape[0], -1)
    room = rows * LANES - flat.shape[1]
    return jnp.pad(flat, ((0, 0), (0, room))).reshape(values.shape[0], rows, LANES)


def rows_for(amount, unit):
    rows = -(-amount // LANES)
    return -(-rows // unit) * unit


def split_at(flat, sizes):
    pieces, start = [], 0
    for size in sizes:
        pieces.append(flat[..., start : start + size])
        start += size
    return pieces


def gather_plan(own, both):
    width = own[1].shape[1]
    parts = [(0, 1, j * width, width, False) for j in range(own[0].shape[1] // width)]
    parts.append((1, 1, 0, width, True))
    parts += [(2, 1, j * width, width, False) for j in range(own[2].shape[1] // width)]
    third = own[3].shape[0] // 3
    parts += [(3, 0, j * third, third, False) for j in range(3)]
    parts.append((4, 1, 0, both[0].shape[1], False))
    wide_two = both[1].shape[1] // 2
    parts += [(5, 1, j * wide_two, wide_two, True) for j in range(2)]
    parts.append((6, 1, 0, both[2].shape[1], False))
    return tuple(part + (i // 2,) for i, part in enumerate(parts))


def body(
    tokens,
    time_bins,
    labels,
    dino_feats,
    cotangent,
    time_table,
    class_table,
    ada_weight,
    ada_bias,
    qkv_weight,
    qkv_bias,
    out_weight,
    out_bias,
    mlp_in_weight,
    mlp_in_bias,
    mlp_out_weight,
    mlp_out_bias,
    align_weight_one,
    align_bias_one,
    align_weight_two,
    align_bias_two,
    align_weight_three,
    align_bias_three,
):
    count = lax.axis_size("dp")
    first_section = lax.axis_index("section") == 0
    index = lax.axis_index("dp")
    images, _, image_rows, model_width = tokens.shape
    rows_all = images * image_rows
    shard = out_weight.shape[1]
    kernels = count % 4 == 0 and shard % 8 == 0

    block_biases = (qkv_bias, out_bias, mlp_in_bias, mlp_out_bias, ada_bias)
    align_biases = (align_bias_one, align_bias_two, align_bias_three)
    block_sizes = [b.size for b in block_biases]
    align_sizes = [b.size for b in align_biases]
    indices = jnp.concatenate([time_bins, labels], 1).reshape(-1)
    pack = jnp.concatenate(
        [wide(half(b.reshape(-1))) for b in block_biases + align_biases] + [wide(indices)]
    )
    pack = padded(pack[None], rows_for(pack.size, 8))[0]
    if kernels:
        packs = share_small(count, pack).reshape(2, count, -1)
    else:
        packs = lax.all_gather(pack.reshape(-1), ("section", "dp")).reshape(2, count, -1)
    own_pack = jnp.where(first_section, packs[0], packs[1])
    block_full = [b.reshape(-1) for b in split_at(own_pack[:, : sum(block_sizes)], block_sizes)]
    bias_row = jnp.concatenate(
        [block_full[0][:model_width], jnp.zeros((model_width,), jnp.float32), block_full[0][model_width:]]
        + block_full[1:]
    )[None]
    start = sum(block_sizes)
    align_bias_full = [
        b.reshape(-1) for b in split_at(packs[:, :, start : start + sum(align_sizes)], align_sizes)
    ]
    start = start + sum(align_sizes)
    pairs = own_pack[:, start : start + 2 * images].astype(jnp.int32).reshape(count * images, 2)

    time_hot = pairs[:, :1] == jnp.arange(time_table.shape[0], dtype=jnp.int32)[None]
    class_hot = pairs[:, 1:] == jnp.arange(class_table.shape[0], dtype=jnp.int32)[None]
    cond = matmul(half(time_hot), half(time_table)) + matmul(half(class_hot), half(class_table))
    cond_act = half(jax.nn.silu(cond))
    ada_half = half(ada_weight[0])
    mod_wide = ada_half.shape[1]
    mod_parts = half(matmul(cond_act, ada_half)).reshape(count, images, mod_wide)
    mod_rows = rows_for(images * mod_wide, 16)

    start_rows = tokens.reshape(rows_all, model_width)
    own = [half(w[0]) for w in (qkv_weight, out_weight, mlp_in_weight, mlp_out_weight)]
    both = [half(w) for w in (align_weight_one, align_weight_two, align_weight_three)]
    one_rows = both[0].shape[0]
    one_padded = -(-one_rows // 16) * 16
    both[0] = jnp.pad(both[0], ((0, one_padded - one_rows), (0, 0)))
    place = jnp.arange(2 * count * one_padded, dtype=jnp.int32)
    owner, row = place // one_padded, place % one_padded
    wanted = jnp.where(row < one_rows, owner * one_rows + row, -1)[None]
    if kernels:
        chunked = mod_parts.reshape(count, images, 6, model_width // LANES, LANES)
        parts = padded(jnp.swapaxes(chunked, 2, 3).reshape(count, -1), mod_rows)
        modulation, gathered, kept = gather_forward(
            count, parts, start_rows, images, bias_row, own, both, gather_plan(own, both), 2
        )
        weights = [g.reshape(-1, g.shape[-1]) for g in gathered[:4]]
        align_weights = [g.reshape(-1, g.shape[-1]) for g in gathered[4:]]
        hidden = kept[10]
    else:
        modulation = lax.psum_scatter(wide(mod_parts), "dp", scatter_dimension=0, tiled=True)
        modulation = modulation.reshape(images, 6, model_width) + block_full[4].reshape(6, model_width)
        modulation = jnp.pad(modulation, ((0, 0), (0, 2), (0, 0)))
        weights = [lax.all_gather(w, "dp", axis=0, tiled=True) for w in own]
        align_weights = [lax.all_gather(w, ("section", "dp"), axis=0, tiled=True) for w in both]
        blank = kept_shapes(rows_all, model_width, images, weights[2].shape[1])
        blank = [jnp.zeros(b.shape, b.dtype) for b in blank[:10]]
        kept = block_forward(0, start_rows, modulation, bias_row, weights, blank)
        received = lax.ppermute(kept[10], "section", [(0, 1)])
        hidden = jnp.where(first_section, kept[10], received)
    aligner = (
        align_weights[0], align_bias_full[0], align_weights[1], align_bias_full[1],
        align_weights[2], align_bias_full[2],
    )

    target = dino_feats.reshape(rows_all, -1)
    *kept, final = block_forward(1, hidden, modulation, bias_row, weights, kept[:10])
    align_hidden, final = lax.optimization_barrier((hidden, final))
    grad_align, align_sums, align_grads = project_align(align_hidden, target, wanted, aligner, loss_weight)
    attn_input, qkv_rows, probs, mixed, attn_branch, after, mlp_input, slope, mlp_act, mlp_branch = kept

    def sources(block_input, grad):
        return (block_input, grad, mlp_branch, slope, after, attn_branch, probs, qkv_rows)

    last_sources = sources(hidden, cotangent.reshape(rows_all, model_width))
    if kernels:
        far = [g.reshape(2, count // 4, 2, 2, *w.shape) for g, w in zip(align_grads, both)]
        far = [far[2], far[0], far[1]]
        results = block_backward(count, 1, modulation, last_sources, weights, grad_align, far)
        grads, far_first_sum, far_halves = results[:10], results[10:13], results[13:]
    else:
        blank = block_backward(count, 0, modulation, last_sources, weights)
        blank = [last_sources[1]] + list(blank[1:])
        grads = block_backward(count, 1, modulation, last_sources, weights, previous=blank)
        received = lax.ppermute(grad_align, "section", [(0, 1)])
        grad_hidden = half(wide(grads[0]) + wide(received))
        received = lax.ppermute(grad_hidden, "section", [(1, 0)])
        grads = [jnp.where(first_section, received, grad_hidden)] + list(grads[1:])
    grads = block_backward(
        count, 0, modulation, sources(start_rows, start_rows), weights, previous=grads
    )
    in_grads, grad_qkv, grad_attn, grad_pre, grad_branch, grad_mod = grads[:6]
    outputs = jnp.where(first_section, hidden, final)
    grad_mod = half(grad_mod[:, :6])
    sums = [g[0] for g in grads[6:]]
    sums[0] = jnp.concatenate([sums[0][:model_width], sums[0][2 * model_width :]])
    align_bias_grads = [jnp.where(first_section, g, 0.0) for g in align_sums]
    align_sums = [jnp.moveaxis(g.reshape(2, count, -1), 0, 1).reshape(count, -1) for g in align_bias_grads]
    bias_flat = jnp.concatenate([g.reshape(count, -1) for g in sums] + align_sums, 1)
    if kernels:
        tall = mlp_act.shape[1] // (count * shard)
        n_qkv, n_in = 3, weights[2].shape[1] // model_width
        products = ((mlp_input, grad_pre), (attn_input, grad_qkv), (mixed, grad_attn))
        plan = [(0, 0, j) for j in range(n_in)] + [(1, 0, j) for j in range(n_qkv)] + [(2, 0, 0)]
        bias_grad_rows = rows_for(bias_flat.shape[1], 8)
        near_sum, far_sum, mods, bias_parts_sum = reduce_grads(
            count, shard, mlp_act, grad_branch, products, plan, far_halves, (False, True, False), (3, 8, 10), 3,
            padded(grad_mod.reshape(1, -1), mod_rows)[0], padded(bias_flat, bias_grad_rows),
        )
        grad_mods = mods.reshape(count, -1)[:, : images * mod_wide]
        bias_sum = jnp.sum(bias_parts_sum, 0).reshape(-1)
        grad_down_weight = wide(near_sum[:tall]).reshape(-1, model_width)
        grad_in_weight = wide(jnp.concatenate([near_sum[tall + j] for j in range(n_in)], 1))
        grad_qkv_weight = wide(jnp.concatenate([near_sum[tall + n_in + j] for j in range(n_qkv)], 1))
        grad_out_weight = wide(near_sum[tall + n_in + n_qkv])
        far_sum = [wide(jnp.where(first_section, a, b)) for a, b in zip(far_first_sum, far_sum)]
        align_out = [far_sum[1][:one_rows], far_sum[2], far_sum[0]]
    else:
        grad_mods = lax.all_gather(grad_mod.reshape(-1), "dp")
        bias_sum = lax.psum_scatter(bias_flat, "dp", scatter_dimension=0, tiled=True).reshape(-1)
        weight_grads = (
            transposed(attn_input, grad_qkv),
            transposed(mixed, grad_attn),
            transposed(mlp_input, grad_pre),
            transposed(mlp_act, grad_branch),
        )
        reduced = [
            lax.psum_scatter(g, "dp", scatter_dimension=0, tiled=True) for g in weight_grads
        ]
        grad_qkv_weight, grad_out_weight, grad_in_weight, grad_down_weight = reduced
        align_out = [
            lax.psum_scatter(
                jnp.where(first_section, wide(g), 0.0), ("section", "dp"), scatter_dimension=0, tiled=True
            )
            for g in align_grads
        ]
        align_out[0] = align_out[0][:one_rows]

    grad_mods = grad_mods.reshape(count * images, mod_wide)
    grad_ada = transposed(cond_act, grad_mods)
    mod_sums = jnp.sum(wide(grad_mods), 0)
    ada_share = mod_wide // count
    grad_ada_bias = lax.dynamic_slice(mod_sums, (index * ada_share,), (ada_share,))
    cond_part = times_transpose(grad_mods, ada_half)
    block_sum = sum(block_sizes[:4])
    grad_biases = split_at(bias_sum[:block_sum], block_sizes[:4])
    align_share = split_at(bias_sum[block_sum : block_sum + 2 * sum(align_sizes)], [2 * a for a in align_sizes])
    align_share = jnp.concatenate([a.reshape(2, -1) for a in align_share], 1)
    packet = jnp.concatenate([cond_part.reshape(-1), align_share.reshape(-1)])
    packet = packet + lax.ppermute(packet, "section", [(0, 1), (1, 0)])
    cond_grad = packet[: cond_part.size].reshape(cond_part.shape)
    align_share = packet[cond_part.size :].reshape(2, -1)
    align_share = jnp.where(first_section, align_share[0], align_share[1])
    align_bias_out = split_at(align_share, align_sizes)
    cond_grad = local_grad(jax.nn.silu, cond, cond_grad)

    def table_grad(hot):
        return lax.dot_general(
            wide(hot),
            cond_grad,
            (((0,), (0,)), ((), ())),
            precision=lax.Precision.HIGHEST,
            preferred_element_type=jnp.float32,
        )

    whole_rows = (1, images, 1, image_rows, model_width)
    return (
        outputs.reshape(whole_rows),
        in_grads.reshape(whole_rows),
        table_grad(time_hot),
        table_grad(class_hot),
        grad_ada[None],
        grad_ada_bias[None],
        grad_qkv_weight[None],
        grad_biases[0][None],
        grad_out_weight[None],
        grad_biases[1][None],
        grad_in_weight[None],
        grad_biases[2][None],
        grad_down_weight[None],
        grad_biases[3][None],
        align_out[0],
        align_bias_out[0],
        align_out[1],
        align_bias_out[1],
        align_out[2],
        align_bias_out[2],
    )


def solution(mesh):
    placed = (
        P(None, "dp", None, None),
        P(None, "dp"),
        P(None, "dp"),
        P(None, "dp", None, None),
        P(None, "dp", None, None),
        P(None, "dp"),
        P(None, "dp"),
        P("section", "dp", None),
        P("section", "dp"),
        P("section", "dp", None),
        P("section", "dp"),
        P("section", "dp", None),
        P("section", "dp"),
        P("section", "dp", None),
        P("section", "dp"),
        P("section", "dp", None),
        P("section", "dp"),
        P(("section", "dp"), None),
        P(("section", "dp")),
        P(("section", "dp"), None),
        P(("section", "dp")),
        P(("section", "dp"), None),
        P(("section", "dp")),
    )
    return jax.shard_map(
        body,
        mesh=mesh,
        in_specs=placed,
        out_specs=(
            P("section", None, "dp", None, None),
            P("section", None, "dp", None, None),
        )
        + placed[5:],
        check_vma=False,
    )
```
